32 devices in a mesh: head: 4 (over y, x), blk: 8 (over z, core).
Axes of the slice: x: 2, y: 2, z: 4, core: 2. Of those that a mesh axis runs over, the one named last changes fastest.
Arguments:
- tokens: bfloat16 [8, 2048, 768], P(None, ('head', 'blk')), may hold values from -6 to 6
- lengths: int32 [8], replicated, may hold values from 256 to 2048, as said below
- first_gain: bfloat16 [768], P(('head', 'blk')), may hold values from 0.25 to 1.75
- first_bias: bfloat16 [768], P(('head', 'blk')), may hold values from -1.25 to 1.25
- joint_weight: bfloat16 [768, 2304], P(('head', 'blk')), may hold values from -0.21875 to 0.21875
- query_bias: bfloat16 [768], P(('head', 'blk')), may hold values from -3 to 3
- value_bias: bfloat16 [768], P(('head', 'blk')), may hold values from -0.125 to 0.125
- output_weight: bfloat16 [768, 768], P(('head', 'blk')), may hold values from -6 to 6
- output_bias: bfloat16 [768], P(('head', 'blk')), may hold values from -1.25 to 1.25
- second_gain: bfloat16 [768], P(('head', 'blk')), may hold values from 0.25 to 1.75
- second_bias: bfloat16 [768], P(('head', 'blk')), may hold values from -1.25 to 1.25
- inner_weight: bfloat16 [768, 3072], P(('head', 'blk')), may hold values from -0.21875 to 0.21875
- inner_bias: bfloat16 [3072], P(('head', 'blk')), may hold values from -1.25 to 1.25
- outer_weight: bfloat16 [3072, 768], P(('head', 'blk')), may hold values from -0.4375 to 0.4375
- outer_bias: bfloat16 [768], P(('head', 'blk')), may hold values from -3 to 3
- cotangent: bfloat16 [8, 2048, 768], P(None, ('head', 'blk')), may hold values from -6 to 6
Outputs:
- output: bfloat16 [8, 2048, 768], P(None, ('head', 'blk'))
- tokens_gradient: bfloat16 [8, 2048, 768], P(None, ('head', 'blk'))
- first_gain_gradient: float32 [768], P(('head', 'blk'))
- first_bias_gradient: float32 [768], P(('head', 'blk'))
- joint_weight_gradient: float32 [768, 2304], P(('head', 'blk'))
- query_bias_gradient: float32 [768], P(('head', 'blk'))
- value_bias_gradient: float32 [768], P(('head', 'blk'))
- output_weight_gradient: float32 [768, 768], P(('head', 'blk'))
- output_bias_gradient: float32 [768], P(('head', 'blk'))
- second_gain_gradient: float32 [768], P(('head', 'blk'))
- second_bias_gradient: float32 [768], P(('head', 'blk'))
- inner_weight_gradient: float32 [768, 3072], P(('head', 'blk'))
- inner_bias_gradient: float32 [3072], P(('head', 'blk'))
- outer_weight_gradient: float32 [3072, 768], P(('head', 'blk'))
- outer_bias_gradient: float32 [768], P(('head', 'blk'))
- stats: float32 [3], replicated
The draws below stay inside these ranges and needn't reach their ends.
Inputs may be any that keep to these rules, and one draw needn't show every extreme that they name: `lengths`: one slot, chosen by the seed, is full (2048).
All inputs are finite; a program needn't handle non-finite values.
Results may differ from the reference program's by a relative error of at most 0.02.
Values may be sent and summed in bfloat16 or wider, within the bound.
A program may use at most 128 MiB of HBM per device.

```python
import math
import jax
import jax.numpy as jnp
from jax import lax

D = 768
H = 12
DH = 64
FF = 3072
SEQS = 8
SEQ_LEN = 2048


def draw_lengths(key, part):
    first, second = jax.random.split(jax.random.fold_in(key, 7))
    drawn = jax.random.randint(first, (SEQS,), SEQ_LEN // 8, SEQ_LEN + 1)
    chosen = jax.random.randint(second, (), 0, SEQS)
    slots = jnp.arange(SEQS)
    drawn = jnp.where(slots == chosen, SEQ_LEN, drawn)
    return drawn.astype(jnp.int32)


def block_scale(stream_key, shape, shards, smallest, largest):
    factor_of = 1.0
    for axis_at, blocks in shards:
        draws = jax.random.uniform(jax.random.fold_in(jax.random.fold_in(stream_key, 6), axis_at), (blocks,), jnp.float32, smallest / len(shards), largest / len(shards))
        factor_of = factor_of * jnp.repeat(jnp.exp(draws), shape[axis_at] // blocks).reshape((-1,) + (1,) * (len(shape) - 1 - axis_at))
    return factor_of


def bell_draw(stream_key, shape, width, most, shards=(), held_as=jnp.bfloat16):
    level = block_scale(stream_key, shape, shards, -0.22, 0.18) if shards else 1.0
    values = jax.random.normal(stream_key, shape, jnp.float32) * width * level
    return jnp.minimum(jnp.maximum(values, -most), most).astype(held_as)


def setup_inputs(seed: int = 0) -> dict:
    seeds = jax.random.split(jax.random.key(seed), 17)
    tokens = bell_draw(seeds[0], (SEQS, SEQ_LEN, D), 1.0, 6.0, ((1, 32),))
    lengths = draw_lengths(jax.random.fold_in(seeds[16], 71), 0)
    first_gain = jnp.clip(1.0 + 0.15 * jax.random.normal(seeds[2], (D,), jnp.float32), 0.25, 1.75).astype(jnp.bfloat16)
    first_bias = bell_draw(seeds[3], (D,), 0.2, 1.25, ((0, 32),))
    joint_weight = bell_draw(seeds[4], (D, 3 * D), D ** -0.5, 0.21875, ((0, 32),))
    query_bias = bell_draw(seeds[5], (D,), 0.5, 3.0, ((0, 32),))
    value_bias = bell_draw(seeds[6], (D,), 0.02, 0.125, ((0, 32),))
    output_weight = bell_draw(seeds[7], (D, D), 1 ** -0.5, 6.0, ((0, 32),))
    output_bias = bell_draw(seeds[8], (D,), 0.2, 1.25, ((0, 32),))
    second_gain = jnp.clip(1.0 + 0.15 * jax.random.normal(seeds[9], (D,), jnp.float32), 0.25, 1.75).astype(jnp.bfloat16)
    second_bias = bell_draw(seeds[10], (D,), 0.2, 1.25, ((0, 32),))
    inner_weight = bell_draw(seeds[11], (D, FF), D ** -0.5, 0.21875, ((0, 32),))
    inner_bias = bell_draw(seeds[12], (FF,), 0.2, 1.25, ((0, 32),))
    outer_weight = bell_draw(seeds[13], (FF, D), (FF // 16) ** -0.5, 0.4375, ((0, 32),))
    outer_bias = bell_draw(seeds[14], (D,), 0.5, 3.0, ((0, 32),))
    cotangent = bell_draw(seeds[15], (SEQS, SEQ_LEN, D), 1.0, 6.0, ((1, 32),))
    return {"tokens": tokens, "lengths": lengths, "first_gain": first_gain, "first_bias": first_bias, "joint_weight": joint_weight, "query_bias": query_bias, "value_bias": value_bias, "output_weight": output_weight, "output_bias": output_bias, "second_gain": second_gain, "second_bias": second_bias, "inner_weight": inner_weight, "inner_bias": inner_bias, "outer_weight": outer_weight, "outer_bias": outer_bias, "cotangent": cotangent}


@jax.custom_vjp
def low(v):
    return lax.optimization_barrier(v.astype(jnp.bfloat16)).astype(jnp.float32)

@jax.custom_vjp
def low_back(v):
    return v

def low_keep(v):
    return (low(v), None)

def low_pass(kept, grad):
    return (grad,)

def back_keep(v):
    return (v, None)

def back_low(kept, grad):
    return (low(grad),)
low.defvjp(low_keep, low_pass)
low_back.defvjp(back_keep, back_low)
EPS = 1e-12
NEG = -1e+30
HIGH = lax.Precision.HIGHEST

def layer_norm(values, gain, shift):
    average = lax.optimization_barrier(jnp.mean(values, axis=-1, keepdims=True))
    centered = values - average
    variance = lax.optimization_barrier(jnp.mean(centered * centered, axis=-1, keepdims=True))
    return centered * lax.rsqrt(variance + EPS) * gain + shift

def gelu_exact(values):
    return jax.nn.gelu(values, approximate=False)

def attention(query_rows, key_rows, value_rows, valid):
    length = query_rows.shape[0]
    block_rows = math.gcd(length, 512)
    blocks = length // block_rows
    query_blocks = query_rows.reshape(blocks, block_rows, H, DH)
    key_heads = key_rows.reshape(length, H, DH)
    value_heads = value_rows.reshape(length, H, DH)

    def one_block(query_block):
        scores = jnp.einsum('qhd,khd->hqk', query_block, key_heads, precision=HIGH) * DH ** (-0.5)
        scores = low_back(scores)
        scores = jnp.where(valid[None, None, :], scores, NEG)
        highest = lax.optimization_barrier(jnp.max(scores, axis=-1, keepdims=True))
        weights = jnp.exp(scores - highest)
        probs = low(weights / lax.optimization_barrier(jnp.sum(weights, axis=-1, keepdims=True)))
        return jnp.einsum('hqk,khd->qhd', probs, value_heads, precision=HIGH).reshape(block_rows, D)
    return lax.map(jax.checkpoint(one_block), query_blocks).reshape(length, D)

def layer(inputs, weights_all, valid):
    first_gain, first_bias, joint_weight, query_bias, value_bias, output_weight, output_bias, second_gain, second_bias, inner_weight, inner_bias, outer_weight, outer_bias = weights_all
    first_low = low(layer_norm(inputs, first_gain, first_bias))
    joint = jnp.dot(first_low, joint_weight, precision=HIGH)
    query_rows = low(low_back(joint[:, :D] + query_bias))
    key_rows = low(low_back(joint[:, D:2 * D]))
    value_rows = low(low_back(joint[:, 2 * D:] + value_bias))
    context = low(low_back(attention(query_rows, key_rows, value_rows, valid)))
    branch = low_back(jnp.dot(context, output_weight, precision=HIGH) + output_bias)
    residual = inputs + branch
    second_low = low(layer_norm(residual, second_gain, second_bias))
    inner = low_back(jnp.dot(second_low, inner_weight, precision=HIGH) + inner_bias)
    activated = low(gelu_exact(inner))
    feed = low_back(jnp.dot(activated, outer_weight, precision=HIGH) + outer_bias)
    result = residual + feed
    keep = valid[:, None]
    squares = jnp.stack([jnp.sum(jnp.where(keep, result * result, 0.0)), jnp.sum(jnp.where(keep, branch * branch, 0.0)), jnp.sum(jnp.where(keep, feed * feed, 0.0))])
    return (jnp.where(keep, result, 0.0), squares)

def reference(tokens, lengths, first_gain, first_bias, joint_weight, query_bias, value_bias, output_weight, output_bias, second_gain, second_bias, inner_weight, inner_bias, outer_weight, outer_bias, cotangent):
    weights_all = tuple((item.astype(jnp.float32) for item in (first_gain, first_bias, joint_weight, query_bias, value_bias, output_weight, output_bias, second_gain, second_bias, inner_weight, inner_bias, outer_weight, outer_bias)))
    positions = jnp.arange(SEQ_LEN, dtype=jnp.int32)

    def one_sequence(carry, item):
        gradients, sums = carry
        seq_tokens, seq_cotangent, seq_length = item
        valid = positions < seq_length

        def forward(inputs, weights_now):
            return layer(inputs, weights_now, valid)
        result, pull, seq_sums = jax.vjp(forward, seq_tokens.astype(jnp.float32), weights_all, has_aux=True)
        grad_inputs, grad_weights = pull(seq_cotangent.astype(jnp.float32))
        gradients = jax.tree.map(jnp.add, gradients, grad_weights)
        return ((gradients, sums + seq_sums), (result.astype(jnp.bfloat16), grad_inputs.astype(jnp.bfloat16)))
    start = (tuple((jnp.zeros(item.shape, jnp.float32) for item in weights_all)), jnp.zeros((3,), jnp.float32))
    (gradients, sums), (output, tokens_gradient) = lax.scan(one_sequence, start, (tokens, cotangent, lengths))
    count = jnp.sum(lengths).astype(jnp.float32) * D
    stats = jnp.sqrt(sums / count + 1e-06)
    return (output, tokens_gradient, gradients[0], gradients[1], gradients[2], gradients[3], gradients[4], gradients[5], gradients[6], gradients[7], gradients[8], gradients[9], gradients[10], gradients[11], gradients[12], stats)
```

```python
import jax
import jax.numpy as jnp
from jax import lax
from jax.experimental import pallas as pl
from jax.experimental.pallas import tpu as pltpu
from jax.sharding import PartitionSpec as P

H = 12
DH = 64


EPS = 1e-12
NEG = -1e30


def passed_along(value, axis, steps):
    count = lax.axis_size(axis)
    pairs = [(source, (source + steps) % count) for source in range(count)]
    return lax.ppermute(value, axis, pairs)


def normalize(values, gain, shift):
    average = jnp.mean(values, axis=-1, keepdims=True)
    centered = values - average
    inverse = lax.rsqrt(jnp.mean(centered * centered, axis=-1, keepdims=True) + EPS)
    normed = centered * inverse
    return (normed * gain + shift, normed, inverse)


def normalize_back(incoming, normed, inverse, gain):
    scaled = incoming * gain
    inner = (
        scaled
        - jnp.mean(scaled, axis=-1, keepdims=True)
        - normed * jnp.mean(scaled * normed, axis=-1, keepdims=True)
    )
    return (
        inner * inverse,
        jnp.sum(incoming * normed, axis=(0, 1)),
        jnp.sum(incoming, axis=(0, 1)),
    )


def gelu_exact(values):
    return jax.nn.gelu(values, approximate=False)


def key_mask(lengths, source, piece_rows, block_count, head_count):
    rows_here = jnp.arange(head_count * piece_rows, dtype=jnp.int32)
    position = (
        rows_here // piece_rows * block_count + source
    ) * piece_rows + rows_here % piece_rows
    return position[None, :] < lengths[:, None]


def attend(query_part, state, keys_block, values_block, mask):
    best, total, running = state
    scores = jnp.einsum(
        "sqhd,skhd->sqhk", query_part, keys_block, preferred_element_type=jnp.float32
    ) * DH ** (-0.5)
    scores = jnp.where(mask[:, None, None, :], scores, NEG)
    fresh = jnp.maximum(best, jnp.max(scores, axis=-1))
    decay = jnp.exp(best - fresh)
    weights = jnp.exp(scores - fresh[..., None])
    total = total * decay + jnp.sum(weights, axis=-1)
    running = running * decay[..., None] + jnp.einsum(
        "sqhk,skhd->sqhd",
        weights.astype(jnp.bfloat16),
        values_block,
        preferred_element_type=jnp.float32,
    )
    return (fresh, total, running)


def block_grads(query_part, back_part, total_part, spread_part, keys_block, values_block, mask):
    scale = DH ** (-0.5)
    scores = (
        jnp.einsum("sqhd,skhd->sqhk", query_part, keys_block, preferred_element_type=jnp.float32)
        * scale
    )
    scores = jnp.where(mask[:, None, None, :], scores, NEG)
    chances = jnp.exp(scores - total_part[..., None])
    back_chances = jnp.einsum(
        "sqhd,skhd->sqhk", back_part, values_block, preferred_element_type=jnp.float32
    )
    back_scores = (chances * (back_chances - spread_part[..., None])).astype(jnp.bfloat16)
    query_step = (
        jnp.einsum("sqhk,skhd->sqhd", back_scores, keys_block, preferred_element_type=jnp.float32)
        * scale
    )
    key_step = (
        jnp.einsum("sqhk,sqhd->skhd", back_scores, query_part, preferred_element_type=jnp.float32)
        * scale
    )
    value_step = jnp.einsum(
        "sqhk,sqhd->skhd",
        chances.astype(jnp.bfloat16),
        back_part,
        preferred_element_type=jnp.float32,
    )
    return (query_step, key_step, value_step)


def on_device(
    tokens,
    lengths,
    first_gain,
    first_bias,
    joint_weight,
    query_bias,
    value_bias,
    output_weight,
    output_bias,
    second_gain,
    second_bias,
    inner_weight,
    inner_bias,
    outer_weight,
    outer_bias,
    cotangent,
):
    head_count = lax.axis_size("head")
    block_count = lax.axis_size("blk")
    block = lax.axis_index("blk")
    quarter = lax.axis_index("head")
    (
        gain_one,
        shift_one,
        joint_full,
        query_shift,
        value_shift,
        output_full,
        output_shift,
        gain_two,
        shift_two,
        inner_full,
        inner_shift,
        outer_full,
        outer_shift,
    ) = (
        lax.all_gather(first_gain, ("head", "blk"), axis=0, tiled=True),
        lax.all_gather(first_bias, ("head", "blk"), axis=0, tiled=True),
        lax.all_gather(joint_weight, ("head", "blk"), axis=0, tiled=True),
        lax.all_gather(query_bias, ("head", "blk"), axis=0, tiled=True),
        lax.all_gather(value_bias, ("head", "blk"), axis=0, tiled=True),
        lax.all_gather(output_weight, ("head", "blk"), axis=0, tiled=True),
        lax.all_gather(output_bias, ("head", "blk"), axis=0, tiled=True),
        lax.all_gather(second_gain, ("head", "blk"), axis=0, tiled=True),
        lax.all_gather(second_bias, ("head", "blk"), axis=0, tiled=True),
        lax.all_gather(inner_weight, ("head", "blk"), axis=0, tiled=True),
        lax.all_gather(inner_bias, ("head", "blk"), axis=0, tiled=True),
        lax.all_gather(outer_weight, ("head", "blk"), axis=0, tiled=True),
        lax.all_gather(outer_bias, ("head", "blk"), axis=0, tiled=True),
    )
    sequences, piece_rows, width = tokens.shape
    heads_here = H // head_count
    head_width = heads_here * DH
    rows = head_count * piece_rows
    shape_heads = (sequences, rows, heads_here, DH)
    shape_flat = (sequences, rows, head_width)
    own_position = (quarter * block_count + block) * piece_rows + jnp.arange(
        piece_rows, dtype=jnp.int32
    )
    valid = own_position[None, :] < lengths[:, None]
    keep = valid[..., None]
    inputs = tokens.astype(jnp.float32)
    gain_one_wide = gain_one.astype(jnp.float32)
    gain_two_wide = gain_two.astype(jnp.float32)
    first_out, first_unit, first_scale = normalize(
        inputs, gain_one_wide, shift_one.astype(jnp.float32)
    )
    first_low = first_out.astype(jnp.bfloat16)
    joint = jnp.einsum("scd,de->sce", first_low, joint_full, preferred_element_type=jnp.float32)
    query_flat = (joint[..., :width] + query_shift.astype(jnp.float32)).astype(jnp.bfloat16)
    key_flat = joint[..., width : 2 * width].astype(jnp.bfloat16)
    value_flat = (joint[..., 2 * width :] + value_shift.astype(jnp.float32)).astype(jnp.bfloat16)
    query_flat, key_flat, value_flat = (
        lax.all_to_all(query_flat, "head", split_axis=2, concat_axis=1, tiled=True),
        lax.all_to_all(key_flat, "head", split_axis=2, concat_axis=1, tiled=True),
        lax.all_to_all(value_flat, "head", split_axis=2, concat_axis=1, tiled=True),
    )
    query_rows = query_flat.reshape(shape_heads)
    key_rows = key_flat.reshape(shape_heads)
    value_rows = value_flat.reshape(shape_heads)

    def visit(carry):
        keys_block, values_block, source, state = carry
        keys_block, values_block = passed_along((keys_block, values_block), "blk", 1)
        source = (source - 1) % block_count
        mask = key_mask(lengths, source, piece_rows, block_count, head_count)
        return (
            keys_block,
            values_block,
            source,
            attend(query_rows, state, keys_block, values_block, mask),
        )

    start_state = (
        jnp.full((sequences, rows, heads_here), NEG, jnp.float32),
        jnp.zeros((sequences, rows, heads_here), jnp.float32),
        jnp.zeros(shape_heads, jnp.float32),
    )
    first_state = attend(
        query_rows,
        start_state,
        key_rows,
        value_rows,
        key_mask(lengths, block, piece_rows, block_count, head_count),
    )
    carry = (key_rows, value_rows, block, first_state)
    carry = lax.fori_loop(0, block_count // 2 - 1, lambda turn, state: visit(visit(state)), carry)
    best, total, running = visit(carry)[3]
    context = running / total[..., None]
    log_total = best + jnp.log(total)
    context_low = context.astype(jnp.bfloat16).reshape(shape_flat)
    context_tokens = lax.all_to_all(context_low, "head", split_axis=1, concat_axis=2, tiled=True)
    branch = jnp.einsum(
        "sce,ed->scd", context_tokens, output_full, preferred_element_type=jnp.float32
    ) + output_shift.astype(jnp.float32)
    residual = inputs + branch
    second_out, second_unit, second_scale = normalize(
        residual, gain_two_wide, shift_two.astype(jnp.float32)
    )
    second_low = second_out.astype(jnp.bfloat16)
    inner = jnp.einsum(
        "scd,df->scf", second_low, inner_full, preferred_element_type=jnp.float32
    ) + inner_shift.astype(jnp.float32)
    activated = gelu_exact(inner).astype(jnp.bfloat16)
    feed = jnp.einsum(
        "scf,fd->scd", activated, outer_full, preferred_element_type=jnp.float32
    ) + outer_shift.astype(jnp.float32)
    result = residual + feed
    output = jnp.where(keep, result, 0.0).astype(jnp.bfloat16)
    sums = lax.psum(
        (
            jnp.sum(jnp.where(keep, result * result, 0.0)),
            jnp.sum(jnp.where(keep, branch * branch, 0.0)),
            jnp.sum(jnp.where(keep, feed * feed, 0.0)),
        ),
        ("head", "blk"),
    )
    count = jnp.sum(lengths).astype(jnp.float32) * width
    stats = jnp.sqrt(jnp.stack(sums) / count + 1e-06)
    back_result = jnp.where(keep, cotangent.astype(jnp.float32), 0.0)
    back_feed = back_result.astype(jnp.bfloat16)
    outer_gradient = jnp.einsum(
        "scf,scd->fd", activated, back_feed, preferred_element_type=jnp.float32
    )
    outer_shift_gradient = jnp.sum(back_feed.astype(jnp.float32), axis=(0, 1))
    back_active = jnp.einsum(
        "scd,fd->scf", back_feed, outer_full, preferred_element_type=jnp.float32
    )
    back_inner = jax.vjp(gelu_exact, inner)[1](back_active)[0].astype(jnp.bfloat16)
    inner_gradient = jnp.einsum(
        "scd,scf->df", second_low, back_inner, preferred_element_type=jnp.float32
    )
    inner_shift_gradient = jnp.sum(back_inner.astype(jnp.float32), axis=(0, 1))
    back_second = jnp.einsum(
        "scf,df->scd", back_inner, inner_full, preferred_element_type=jnp.float32
    )
    back_norm_two, gain_two_gradient, shift_two_gradient = normalize_back(
        back_second, second_unit, second_scale, gain_two_wide
    )
    back_residual = back_result + back_norm_two
    back_branch = back_residual.astype(jnp.bfloat16)
    output_gradient = jnp.einsum(
        "sce,scd->ed", context_tokens, back_branch, preferred_element_type=jnp.float32
    )
    output_shift_gradient = jnp.sum(back_branch.astype(jnp.float32), axis=(0, 1))
    back_context = jnp.einsum(
        "scd,ed->sce", back_branch, output_full, preferred_element_type=jnp.float32
    ).astype(jnp.bfloat16)
    back_context = lax.all_to_all(back_context, "head", split_axis=2, concat_axis=1, tiled=True)
    back_heads = back_context.reshape(shape_heads)
    spread = jnp.sum(back_heads.astype(jnp.float32) * context, axis=-1)
    zero_heads = jnp.zeros(shape_heads, jnp.float32)

    def pass_keys(carry):
        keys_block, values_block, key_sum, value_sum, query_sum, source = carry
        mask = key_mask(lengths, source, piece_rows, block_count, head_count)
        query_step, key_step, value_step = block_grads(
            query_rows, back_heads, log_total, spread, keys_block, values_block, mask
        )
        keys_block, values_block = passed_along((keys_block, values_block), "blk", 1)
        key_sum, value_sum = passed_along((key_sum + key_step, value_sum + value_step), "blk", 1)
        return (
            keys_block,
            values_block,
            key_sum,
            value_sum,
            query_sum + query_step,
            (source - 1) % block_count,
        )

    carry = (key_rows, value_rows, zero_heads, zero_heads, zero_heads, block)
    carry = lax.fori_loop(
        0, block_count // 2, lambda turn, state: pass_keys(pass_keys(state)), carry
    )
    key_sum, value_sum, query_sum = (carry[2], carry[3], carry[4])
    back_query, back_key, back_value = (
        lax.all_to_all(
            query_sum.astype(jnp.bfloat16).reshape(shape_flat),
            "head",
            split_axis=1,
            concat_axis=2,
            tiled=True,
        ),
        lax.all_to_all(
            key_sum.astype(jnp.bfloat16).reshape(shape_flat),
            "head",
            split_axis=1,
            concat_axis=2,
            tiled=True,
        ),
        lax.all_to_all(
            value_sum.astype(jnp.bfloat16).reshape(shape_flat),
            "head",
            split_axis=1,
            concat_axis=2,
            tiled=True,
        ),
    )
    back_joint = jnp.concatenate([back_query, back_key, back_value], axis=-1)
    joint_gradient = jnp.einsum(
        "scd,sce->de", first_low, back_joint, preferred_element_type=jnp.float32
    )
    query_shift_gradient = jnp.sum(back_query.astype(jnp.float32), axis=(0, 1))
    value_shift_gradient = jnp.sum(back_value.astype(jnp.float32), axis=(0, 1))
    back_first = jnp.einsum(
        "sce,de->scd", back_joint, joint_full, preferred_element_type=jnp.float32
    )
    back_norm_one, gain_one_gradient, shift_one_gradient = normalize_back(
        back_first, first_unit, first_scale, gain_one_wide
    )
    tokens_gradient = (back_residual + back_norm_one).astype(jnp.bfloat16)
    shards = (
        lax.psum_scatter(gain_one_gradient, ("head", "blk"), scatter_dimension=0, tiled=True),
        lax.psum_scatter(shift_one_gradient, ("head", "blk"), scatter_dimension=0, tiled=True),
        lax.psum_scatter(joint_gradient, ("head", "blk"), scatter_dimension=0, tiled=True),
        lax.psum_scatter(query_shift_gradient, ("head", "blk"), scatter_dimension=0, tiled=True),
        lax.psum_scatter(value_shift_gradient, ("head", "blk"), scatter_dimension=0, tiled=True),
        lax.psum_scatter(output_gradient, ("head", "blk"), scatter_dimension=0, tiled=True),
        lax.psum_scatter(output_shift_gradient, ("head", "blk"), scatter_dimension=0, tiled=True),
        lax.psum_scatter(gain_two_gradient, ("head", "blk"), scatter_dimension=0, tiled=True),
        lax.psum_scatter(shift_two_gradient, ("head", "blk"), scatter_dimension=0, tiled=True),
        lax.psum_scatter(inner_gradient, ("head", "blk"), scatter_dimension=0, tiled=True),
        lax.psum_scatter(inner_shift_gradient, ("head", "blk"), scatter_dimension=0, tiled=True),
        lax.psum_scatter(outer_gradient, ("head", "blk"), scatter_dimension=0, tiled=True),
        lax.psum_scatter(outer_shift_gradient, ("head", "blk"), scatter_dimension=0, tiled=True),
    )
    return (
        output,
        tokens_gradient,
        shards[0],
        shards[1],
        shards[2],
        shards[3],
        shards[4],
        shards[5],
        shards[6],
        shards[7],
        shards[8],
        shards[9],
        shards[10],
        shards[11],
        shards[12],
        stats,
    )


MESH = pl.DeviceIdType.MESH
WIDTH = H * DH
GROUP = 3 * DH
NT = (((1,), (1,)), ((), ()))
NN = (((1,), (0,)), ((), ()))


def place():
    head = lax.axis_index("head")
    blk = lax.axis_index("blk")
    return head // 2, lax.rem(head, 2), blk // 2, lax.rem(blk, 2)


def at(y, x, z, c):
    return (y * 2 + x, z * 2 + c)


def number(y, x, z, c):
    return y * 16 + x * 8 + z * 2 + c


def column(t):
    return t // 4, lax.rem(t, 4)


def meet(peers):
    barrier = pltpu.get_barrier_semaphore()
    for peer in peers:
        pl.semaphore_signal(barrier, inc=1, device_id=peer, device_id_type=MESH)
    pl.semaphore_wait(barrier, len(peers))


class Mover:
    def __init__(self, send_sem, local_sem, anyone):
        self.send_sem = send_sem
        self.local_sem = local_sem
        self.anyone = anyone
        self.sent = []
        self.local = []

    def push(self, source, target, sem, device):
        copy = pltpu.make_async_remote_copy(
            src_ref=source,
            dst_ref=target,
            send_sem=self.send_sem.at[len(self.sent)],
            recv_sem=sem,
            device_id=device,
            device_id_type=MESH,
        )
        copy.start()
        self.sent.append(copy)

    def keep(self, source, target):
        copy = pltpu.make_async_copy(source, target, self.local_sem.at[len(self.local)])
        copy.start()
        self.local.append(copy)
        return copy

    def landed(self, target, sem):
        pltpu.make_async_remote_copy(
            src_ref=target,
            dst_ref=target,
            send_sem=self.send_sem.at[0],
            recv_sem=sem,
            device_id=self.anyone,
            device_id_type=MESH,
        ).wait_recv()

    def finish(self):
        for copy in self.sent:
            copy.wait_send()
        for copy in self.local:
            copy.wait()


def spread_kernel(
    tokens, cotangent, wj, wo, wi, wu, small,
    tok_all, cot_own, wj_all, wo_all, wi_all, wu_all, small_all,
    send_sem, local_sem, tok_sem, cot_sem, weight_sem,
):
    y, x, z, c = place()
    mine = number(y, x, z, c)
    spot = y * 4 + z
    other_core = at(y, x, z, 1 - c)
    across = at(y, 1 - x, z, c)
    y1, x1 = jnp.where(c == 0, y, 1 - y), jnp.where(c == 0, 1 - x, x)
    y2, x2 = jnp.where(c == 0, 1 - y, y), jnp.where(c == 0, x, 1 - x)
    first, second = at(y1, x1, z, c), at(y2, x2, z, c)
    spots = [column(lax.rem(spot + k, 8)) for k in range(1, 8)]
    peers = [at(yy, x, zz, c) for yy, zz in spots] + [across, other_core]
    meet(peers)
    move = Mover(send_sem, local_sem, other_core)
    sources = (wj, wo, wi, wu, small)
    wholes = (wj_all, wo_all, wi_all, wu_all, small_all)

    for yy, zz in spots:
        move.push(tokens.at[yy * 4 + zz], tok_all.at[mine], tok_sem.at[mine], at(yy, x, zz, c))
    move.push(tokens.at[spot], tok_all.at[mine], tok_sem.at[mine], across)
    move.push(tokens.at[spot], tok_all.at[mine], tok_sem.at[mine], other_core)
    move.keep(tokens.at[spot], tok_all.at[mine])

    def hand(block, own, device):
        for i, (source, whole) in enumerate(zip(sources, wholes)):
            move.push(
                source if own else whole.at[block], whole.at[block], weight_sem.at[i, block], device
            )

    def arrive(block):
        for i, whole in enumerate(wholes):
            move.landed(whole.at[block], weight_sem.at[i, block])

    for k in range(1, 4):
        hand(mine, True, at(y, x, lax.rem(z + k, 4), c))
    for source, whole in zip(sources, wholes):
        move.keep(source, whole.at[mine])
    hand(mine, True, first)
    hand(mine, True, second)
    hand(mine, True, other_core)
    for yy, zz in spots:
        move.push(cotangent.at[yy * 4 + zz], cot_own.at[spot], cot_sem.at[spot], at(yy, x, zz, c))
    move.keep(cotangent.at[spot], cot_own.at[spot])

    back_spots = [column(lax.rem(spot + 8 - k, 8)) for k in range(1, 8)]
    for yy, zz in back_spots:
        block = number(yy, x, zz, c)
        move.landed(tok_all.at[block], tok_sem.at[block])
        move.push(tok_all.at[block], tok_all.at[block], tok_sem.at[block], across)
        move.push(tok_all.at[block], tok_all.at[block], tok_sem.at[block], other_core)
    lines = [lax.rem(z + 4 - k, 4) for k in range(4)]
    for zz in lines[1:]:
        block = number(y, x, zz, c)
        arrive(block)
        hand(block, False, first)
        hand(block, False, second)
        hand(block, False, other_core)
    for yy, zz in [(y, z)] + back_spots:
        block = number(yy, 1 - x, zz, c)
        move.landed(tok_all.at[block], tok_sem.at[block])
        move.push(tok_all.at[block], tok_all.at[block], tok_sem.at[block], other_core)
    for zz in lines:
        block = number(y1, x1, zz, c)
        arrive(block)
        hand(block, False, second)
        hand(block, False, other_core)
    for yy, xx in ((y2, x2), (1 - y, 1 - x)):
        for zz in lines:
            block = number(yy, xx, zz, c)
            arrive(block)
            hand(block, False, other_core)
    for yy, zz in [(y, z)] + back_spots:
        for xx in (x, 1 - x):
            block = number(yy, xx, zz, 1 - c)
            move.landed(tok_all.at[block], tok_sem.at[block])
    for yy, zz in back_spots:
        move.landed(cot_own.at[yy * 4 + zz], cot_sem.at[yy * 4 + zz])
    for yy in range(2):
        for xx in range(2):
            for zz in range(4):
                arrive(number(yy, xx, zz, 1 - c))
    move.finish()


def comm_call(kernel, outs, args, sends, locals_, sems, scratch, ident, space=None):
    space = space or [pltpu.HBM] * len(args)
    return pl.pallas_call(
        kernel,
        out_shape=[jax.ShapeDtypeStruct(shape, dtype) for shape, dtype, _ in outs],
        in_specs=[pl.BlockSpec(memory_space=one) for one in space],
        out_specs=[pl.BlockSpec(memory_space=one) for _, _, one in outs],
        scratch_shapes=[
            pltpu.SemaphoreType.DMA((sends,)),
            pltpu.SemaphoreType.DMA((max(locals_, 1),)),
            *[pltpu.SemaphoreType.DMA(shape) for shape in sems],
            *scratch,
        ],
        compiler_params=pltpu.CompilerParams(
            collective_id=ident, has_side_effects=True, vmem_limit_bytes=56 * 1024 * 1024
        ),
    )(*args)


def quad(x, c):
    return [(lax.rem(x + dx, 2), lax.rem(c + dc, 2)) for dx, dc in ((0, 1), (1, 0), (1, 1))]


def to_rows_kernel(source, target, send_sem, local_sem, recv_sem):
    y, x, z, c = place()
    mine = x * 2 + c
    meet([at(y, xx, z, cc) for xx, cc in quad(x, c)])
    move = Mover(send_sem, local_sem, at(y, x, z, 1 - c))
    for xx, cc in quad(x, c)[::-1]:
        for yy in range(2):
            move.push(
                source.at[yy, xx, :, cc], target.at[mine, yy], recv_sem.at[mine, yy], at(y, xx, z, cc)
            )
    for yy in range(2):
        move.keep(source.at[yy, x, :, c], target.at[mine, yy])
    for xx, cc in quad(x, c):
        for yy in range(2):
            move.landed(target.at[xx * 2 + cc, yy], recv_sem.at[xx * 2 + cc, yy])
    move.finish()


def to_heads_kernel(source, target, send_sem, local_sem, recv_sem):
    y, x, z, c = place()
    mine = x * 2 + c
    meet([at(y, xx, z, cc) for xx, cc in quad(x, c)])
    move = Mover(send_sem, local_sem, at(y, x, z, 1 - c))
    for xx, cc in quad(x, c)[::-1]:
        for yy in range(2):
            move.push(
                source.at[xx * 2 + cc, yy],
                target.at[yy, x, :, c],
                recv_sem.at[mine, yy],
                at(y, xx, z, cc),
            )
    for yy in range(2):
        move.keep(source.at[mine, yy], target.at[yy, x, :, c])
    for xx, cc in quad(x, c):
        for yy in range(2):
            move.landed(target.at[yy, xx, :, cc], recv_sem.at[xx * 2 + cc, yy])
    move.finish()


def wide(value):
    return value.astype(jnp.float32)


def reduce_kernel(
    go, gi, gu, gs, outgoing,
    out_o, out_i, out_u, out_s, output,
    send_sem, local_sem, sem1, sem2, sem3, sem4, sem_out,
    *held,
):
    y, x, z, c = place()
    spot = y * 4 + z
    other_core = at(y, x, z, 1 - c)
    across = at(y, 1 - x, z, c)
    y1, x1 = jnp.where(c == 0, y, 1 - y), jnp.where(c == 0, 1 - x, x)
    y2, x2 = jnp.where(c == 0, 1 - y, y), jnp.where(c == 0, x, 1 - x)
    first, second = at(y1, x1, z, c), at(y2, x2, z, c)
    spots = [column(lax.rem(spot + k, 8)) for k in range(1, 8)]
    meet([at(yy, x, zz, c) for yy, zz in spots] + [across, other_core])
    move = Mover(send_sem, local_sem, other_core)
    parts = (gu, gi, go, gs)
    results = (out_u, out_i, out_o, out_s)
    r1, r2, r3, r4 = held[0:4], held[4:8], held[8:12], held[12:16]
    own, near1, near2 = y * 2 + x, y1 * 2 + x1, y2 * 2 + x2
    far = (1 - y) * 2 + 1 - x
    order = (far, near1, near2, own)
    for i in range(4):
        for quarter in order:
            move.push(
                parts[i].at[quarter, :, 1 - c], r1[i].at[quarter], sem1.at[i, quarter], other_core
            )
    for yy, zz in spots:
        move.push(outgoing.at[yy * 4 + zz], output.at[spot], sem_out.at[spot], at(yy, x, zz, c))
    move.keep(outgoing.at[spot], output.at[spot])

    def gather(i, quarter):
        move.landed(r1[i].at[quarter], sem1.at[i, quarter])
        r1[i][quarter] = (wide(r1[i][quarter]) + wide(parts[i][quarter, :, c])).astype(r1[i].dtype)

    def stage2(i):
        for slot, quarter in ((1, far), (0, near1)):
            gather(i, quarter)
            move.push(r1[i].at[quarter], r2[i].at[slot], sem2.at[i, slot], first)

    def stage3(i):
        gather(i, near2)
        move.landed(r2[i].at[1], sem2.at[i, 1])
        r1[i][near2] = (wide(r1[i][near2]) + wide(r2[i][1])).astype(r1[i].dtype)
        move.push(r1[i].at[near2], r3[i], sem3.at[i], second)

    def stage4(i):
        gather(i, own)
        move.landed(r2[i].at[0], sem2.at[i, 0])
        move.landed(r3[i], sem3.at[i])
        r1[i][own] = (wide(r1[i][own]) + wide(r2[i][0]) + wide(r3[i][...])).astype(r1[i].dtype)
        for k in range(1, 4):
            zz = lax.rem(z + k, 4)
            move.push(r1[i].at[own, zz], r4[i].at[k - 1], sem4.at[i, k - 1], at(y, x, zz, c))

    def stage5(i):
        total = wide(r1[i][own, z])
        for k in range(1, 4):
            move.landed(r4[i].at[k - 1], sem4.at[i, k - 1])
            total = total + wide(r4[i][k - 1])
        results[i][...] = total

    stages = (stage2, stage3, stage4, stage5)
    for turn in range(7):
        for depth in range(3, -1, -1):
            i = turn - depth
            if 0 <= i < 4:
                stages[depth](i)
    for k in range(1, 8):
        t = lax.rem(spot + 8 - k, 8)
        move.landed(output.at[t], sem_out.at[t])
    move.finish()


def last_kernel(
    gj, bf, out_j, out_b,
    send_sem, local_sem, sem_y, sem_z, sem_g, sem_c, sem_x,
    ry, rz, sj, rc, rx,
):
    y, x, z, c = place()
    other_core = at(y, x, z, 1 - c)
    across = at(y, 1 - x, z, c)
    down = at(1 - y, x, z, c)
    line = [lax.rem(z + k, 4) for k in range(1, 4)]
    group = quad(x, c)
    meet([at(y, xx, z, cc) for xx, cc in group] + [down] + [at(y, x, zz, c) for zz in line])
    move = Mover(send_sem, local_sem, other_core)
    move.push(gj.at[1 - y], ry, sem_y, down)
    quarters = [(yy, xx) for xx in (1 - x, x) for yy in range(2)]
    for yy, xx in quarters:
        move.push(bf.at[yy, xx, :, 1 - c], rc.at[yy, xx], sem_c.at[yy, xx], other_core)
    for yy, xx in quarters[:2]:
        move.landed(rc.at[yy, xx], sem_c.at[yy, xx])
        rc[yy, xx] = (wide(rc[yy, xx]) + wide(bf[yy, xx, :, c])).astype(rc.dtype)
        move.push(rc.at[yy, xx], rx.at[yy], sem_x.at[yy], across)
    move.landed(ry, sem_y)
    ry[...] = (wide(ry[...]) + wide(gj[y])).astype(ry.dtype)
    for k in range(3):
        move.push(ry.at[:, line[k]], rz.at[k], sem_z.at[k], at(y, x, line[k], c))
    for yy, xx in quarters[2:]:
        move.landed(rc.at[yy, xx], sem_c.at[yy, xx])
    total = wide(ry[:, z])
    for k in range(3):
        move.landed(rz.at[k], sem_z.at[k])
        total = total + wide(rz[k])
    sj[...] = total
    mine = x * 2 + c
    for xx, cc in group:
        move.push(sj.at[xx, cc], out_j.at[mine], sem_g.at[mine], at(y, xx, z, cc))
    move.keep(sj.at[x, c], out_j.at[mine])
    for yy in range(2):
        move.landed(rx.at[yy], sem_x.at[yy])
        out_b[yy] = wide(rc[yy, x]) + wide(bf[yy, x, :, c]) + wide(rx[yy])
    for xx, cc in group:
        move.landed(out_j.at[xx * 2 + cc], sem_g.at[xx * 2 + cc])
    move.finish()


def return_kernel(grads, small, out, small_all, send_sem, local_sem, sem_t, sem_s):
    y, x, z, c = place()
    spot = y * 4 + z
    mine = number(y, x, z, c)
    others = []
    for k in range(1, 32):
        t = lax.rem(mine + k, 32)
        others.append((t, (t // 8, lax.rem(t, 8))))
    meet([device for _, device in others])
    move = Mover(send_sem, local_sem, at(y, x, z, 1 - c))
    for k in range(1, 8):
        yy, zz = column(lax.rem(spot + k, 8))
        move.push(grads.at[yy * 4 + zz], out.at[spot], sem_t.at[spot], at(yy, x, zz, c))
    move.keep(grads.at[spot], out.at[spot])
    for t, device in others:
        move.push(small.at[t], small_all.at[mine], sem_s.at[mine], device)
    move.keep(small.at[mine], small_all.at[mine])
    for k in range(1, 8):
        t = lax.rem(spot + 8 - k, 8)
        move.landed(out.at[t], sem_t.at[t])
    for t, device in others:
        move.landed(small_all.at[t], sem_s.at[t])
    move.finish()


def dot(a, b, dims=NN):
    return lax.dot_general(a, b, dims, preferred_element_type=jnp.float32)


ROWS = 256


def attend_kernel(
    length, tok, wj, gain, shift, query_shift, value_shift, first, query, key, value, context, context_turned, log_total
):
    rows = tok.shape[0]

    def project(i, _):
        here = pl.ds(i * ROWS, ROWS)
        normed = normalize(wide(tok[here, :]), gain[...], shift[...])[0].astype(jnp.bfloat16)
        first[here, :] = normed
        joint = dot(normed, wj[...])
        low_q = (joint[:, :GROUP] + query_shift[...]).astype(jnp.bfloat16)
        low_k = joint[:, GROUP : 2 * GROUP].astype(jnp.bfloat16)
        low_v = (joint[:, 2 * GROUP :] + value_shift[...]).astype(jnp.bfloat16)
        for h in range(3):
            query[h, here, :] = low_q[:, h * DH : (h + 1) * DH]
            key[h, here, :] = low_k[:, h * DH : (h + 1) * DH]
            value[h, here, :] = low_v[:, h * DH : (h + 1) * DH]
        return 0

    lax.fori_loop(0, rows // ROWS, project, 0)
    keep = lax.broadcasted_iota(jnp.int32, (rows, 1), 0) < length[0]
    eye = jnp.eye(DH, dtype=jnp.bfloat16)
    for h in range(3):
        turned = dot(eye, value[h], NT).astype(jnp.bfloat16)

        def block(i, _):
            here = pl.ds(i * ROWS, ROWS)
            scores = dot(key[h], query[h, here, :], NT) * DH ** (-0.5)
            scores = jnp.where(keep, scores, NEG)
            best = jnp.max(scores, axis=0, keepdims=True)
            weights = jnp.exp(scores - best)
            total = jnp.sum(weights, axis=0, keepdims=True)
            mixed = dot(turned, weights.astype(jnp.bfloat16)) / total
            context_turned[h, :, here] = mixed
            log_total[h, :, here] = best + jnp.log(total)
            context[here, h * DH : (h + 1) * DH] = mixed.T.astype(jnp.bfloat16)
            return 0

        lax.fori_loop(0, rows // ROWS, block, 0)


def attend_back_kernel(
    length, query, key, value, back_context, context_turned, log_total, joint, key_sum, value_sum
):
    rows = query.shape[1]
    scale = DH ** (-0.5)
    keep = lax.broadcasted_iota(jnp.int32, (rows, 1), 0) < length[0]
    eye = jnp.eye(DH, dtype=jnp.bfloat16)
    for h in range(3):
        turned = dot(eye, key[h], NT).astype(jnp.bfloat16)
        key_sum[...] = jnp.zeros_like(key_sum)
        value_sum[...] = jnp.zeros_like(value_sum)

        def block(i, _):
            here = pl.ds(i * ROWS, ROWS)
            queries = query[h, here, :]
            backs = back_context[here, h * DH : (h + 1) * DH]
            scores = dot(key[h], queries, NT) * scale
            scores = jnp.where(keep, scores, NEG)
            chances = jnp.exp(scores - log_total[h, :, here])
            spread = jnp.sum(dot(eye, backs, NT) * context_turned[h, :, here], axis=0, keepdims=True)
            back_scores = (chances * (dot(value[h], backs, NT) - spread)).astype(jnp.bfloat16)
            joint[here, h * DH : (h + 1) * DH] = (dot(turned, back_scores) * scale).T.astype(jnp.bfloat16)
            key_sum[...] += dot(back_scores, queries)
            value_sum[...] += dot(chances.astype(jnp.bfloat16), backs)
            return 0

        lax.fori_loop(0, rows // ROWS, block, 0)
        joint[:, GROUP + h * DH : GROUP + (h + 1) * DH] = (key_sum[...] * scale).astype(jnp.bfloat16)
        joint[:, 2 * GROUP + h * DH : 2 * GROUP + (h + 1) * DH] = value_sum[...].astype(jnp.bfloat16)


def local_call(kernel, outs, args, scratch=(), smem=1):
    return pl.pallas_call(
        kernel,
        out_shape=[jax.ShapeDtypeStruct(shape, dtype) for shape, dtype in outs],
        in_specs=[pl.BlockSpec(memory_space=pltpu.SMEM)] * smem
        + [pl.BlockSpec(memory_space=pltpu.VMEM)] * (len(args) - smem),
        out_specs=[pl.BlockSpec(memory_space=pltpu.VMEM)] * len(outs),
        scratch_shapes=list(scratch),
        compiler_params=pltpu.CompilerParams(vmem_limit_bytes=56 * 1024 * 1024),
    )(*args)


def packed(vectors, blocks, dtype, tile):
    rows = [jnp.pad(v.reshape(blocks, 1, -1), ((0, 0), (0, 0), (0, 128 - v.size // blocks))) for v in vectors]
    whole = jnp.concatenate(rows, axis=1).astype(dtype)
    return jnp.pad(whole, ((0, 0), (0, tile - whole.shape[1]), (0, 0)))


def owner_device(
    tokens,
    lengths,
    first_gain,
    first_bias,
    joint_weight,
    query_bias,
    value_bias,
    output_weight,
    output_bias,
    second_gain,
    second_bias,
    inner_weight,
    inner_bias,
    outer_weight,
    outer_bias,
    cotangent,
):
    bf16, f32 = jnp.bfloat16, jnp.float32
    y, x, z, c = place()
    mine = x * 2 + c
    slots, piece, width = tokens.shape
    ff = inner_weight.shape[1]
    small = packed(
        [first_gain, first_bias, query_bias, value_bias, output_bias, second_gain, second_bias, outer_bias, inner_bias],
        1, bf16, 16,
    )[0]
    hbm, vmem = pltpu.HBM, pltpu.VMEM
    tok_all, cot_own, wj_all, wo_all, wi_all, wu_all, small_all = comm_call(
        spread_kernel,
        [
            ((32, piece, width), bf16, hbm),
            ((8, piece, width), bf16, hbm),
            ((32,) + joint_weight.shape, bf16, hbm),
            ((32,) + output_weight.shape, bf16, hbm),
            ((32,) + inner_weight.shape, bf16, hbm),
            ((32,) + outer_weight.shape, bf16, hbm),
            ((32, 16, 128), bf16, hbm),
        ],
        (tokens, cotangent, joint_weight, output_weight, inner_weight, outer_weight, small),
        200, 8, [(32,), (8,), (5, 32)], [], 0,
    )
    vectors = jnp.transpose(small_all[:, :8, :24], (1, 0, 2)).reshape(8, width).astype(f32)
    inner_shift = small_all[:, 8, :96].reshape(1, ff).astype(f32)
    gain_one, shift_one, query_shift, value_shift, output_shift, gain_two, shift_two, outer_shift = (
        vectors[i : i + 1] for i in range(8)
    )
    length = lax.dynamic_slice(lengths, (y * 4 + z,), (1,))
    joint_full = wj_all.reshape(width, 3, 4, GROUP)
    joint_here = lax.dynamic_index_in_dim(joint_full, mine, 2, keepdims=False).reshape(width, 3 * GROUP)
    rows_all = 32 * piece
    tok_flat = tok_all.reshape(rows_all, width)
    first_low, query, key, value, context, context_turned, log_total = local_call(
        attend_kernel,
        [
            ((rows_all, width), bf16),
            ((3, rows_all, DH), bf16),
            ((3, rows_all, DH), bf16),
            ((3, rows_all, DH), bf16),
            ((rows_all, GROUP), bf16),
            ((3, DH, rows_all), f32),
            ((3, 1, rows_all), f32),
        ],
        (
            length, tok_flat, joint_here, gain_one, shift_one,
            lax.dynamic_slice(query_shift, (0, mine * GROUP), (1, GROUP)),
            lax.dynamic_slice(value_shift, (0, mine * GROUP), (1, GROUP)),
        ),
    )
    natural = (2, 2, 4, 2, piece)
    (context_rows,) = comm_call(
        to_rows_kernel,
        [((4, 2, 4, piece, GROUP), bf16, hbm)],
        (context.reshape(natural + (GROUP,)),),
        6, 2, [(4, 2)], [], 1,
    )
    rows = 8 * piece
    context_low = jnp.transpose(context_rows.reshape(4, rows, GROUP), (1, 0, 2)).reshape(rows, width)

    def own_rows(whole):
        whole = lax.dynamic_index_in_dim(whole.reshape(natural + (-1,)), x, 1, keepdims=False)
        return lax.dynamic_index_in_dim(whole, c, 2, keepdims=False).reshape(rows, -1)

    spots = jnp.arange(8, dtype=jnp.int32)
    position = (
        number(spots // 4, x, spots % 4, c)[:, None] * piece + jnp.arange(piece, dtype=jnp.int32)
    ).reshape(rows, 1)
    keep = position < length[0]
    inputs = own_rows(tok_all).astype(f32)
    output_full = wo_all.reshape(width, width)
    inner_full = wi_all.reshape(width, ff)
    outer_full = wu_all.reshape(ff, width)
    branch = dot(context_low, output_full) + output_shift
    residual = inputs + branch
    second_out, second_unit, second_scale = normalize(residual, gain_two, shift_two)
    second_low = second_out.astype(bf16)
    inner = dot(second_low, inner_full) + inner_shift
    activated = gelu_exact(inner).astype(bf16)
    feed = dot(activated, outer_full) + outer_shift
    result = residual + feed
    output_here = jnp.where(keep, result, 0.0).astype(bf16)
    sums = [jnp.sum(jnp.where(keep, item * item, 0.0)) for item in (result, branch, feed)]
    back_result = jnp.where(keep, cot_own.reshape(rows, width).astype(f32), 0.0)
    back_feed = back_result.astype(bf16)
    turn = (((0,), (0,)), ((), ()))
    outer_gradient = dot(activated, back_feed, turn).astype(bf16)
    outer_shift_gradient = jnp.sum(back_feed.astype(f32), axis=0)
    back_active = dot(back_feed, outer_full, NT)
    back_inner = jax.vjp(gelu_exact, inner)[1](back_active)[0].astype(bf16)
    inner_gradient = dot(second_low, back_inner, turn).astype(bf16)
    inner_shift_gradient = jnp.sum(back_inner.astype(f32), axis=0)
    back_second = dot(back_inner, inner_full, NT)
    back_norm_two, gain_two_gradient, shift_two_gradient = normalize_back(
        back_second[None], second_unit[None], second_scale[None], gain_two
    )
    back_residual = back_result + back_norm_two[0]
    back_branch = back_residual.astype(bf16)
    output_gradient = dot(context_low, back_branch, turn).astype(bf16)
    output_shift_gradient = jnp.sum(back_branch.astype(f32), axis=0)
    back_context = jnp.einsum(
        "rd,ged->gre", back_branch, output_full.reshape(4, GROUP, width), preferred_element_type=f32
    ).astype(bf16)
    (back_heads,) = comm_call(
        to_heads_kernel,
        [(natural + (GROUP,), bf16, hbm)],
        (back_context.reshape(4, 2, 4, piece, GROUP),),
        6, 2, [(4, 2)], [], 2,
    )
    (back_joint,) = local_call(
        attend_back_kernel,
        [((rows_all, 3 * GROUP), bf16)],
        (length, query, key, value, back_heads.reshape(rows_all, GROUP), context_turned, log_total),
        scratch=[vmem((rows_all, DH), f32), vmem((rows_all, DH), f32)],
    )
    stat_row = jnp.broadcast_to(jnp.stack(sums), (32, 3)).reshape(-1)
    small_one = packed(
        [outer_shift_gradient, gain_two_gradient, shift_two_gradient, output_shift_gradient, inner_shift_gradient, stat_row],
        32, f32, 8,
    )
    grid = (4, 4, 2)
    owned = [
        (output_gradient, output_weight.shape, bf16),
        (inner_gradient, inner_weight.shape, bf16),
        (outer_gradient, outer_weight.shape, bf16),
        (small_one, (8, 128), f32),
    ]
    order = [owned[2], owned[1], owned[0], owned[3]]
    out_o, out_i, out_u, out_s, output = comm_call(
        reduce_kernel,
        [(shape, f32, vmem) for _, shape, _ in owned] + [(tokens.shape, bf16, hbm)],
        tuple(item.reshape(grid + shape) for item, shape, _ in owned)
        + (output_here.reshape(8, piece, width),),
        63, 1, [(4, 4), (4, 2), (4,), (4, 3), (8,)],
        [vmem((4, 4) + shape, dtype) for _, shape, dtype in order]
        + [vmem((2, 4) + shape, dtype) for _, shape, dtype in order]
        + [vmem((4,) + shape, dtype) for _, shape, dtype in order]
        + [vmem((3,) + shape, dtype) for _, shape, dtype in order],
        3,
        [vmem] * 4 + [hbm],
    )
    joint_gradient = dot(first_low, back_joint, turn).astype(bf16)
    back_first_part = dot(back_joint, joint_here, NT).astype(bf16)
    lead = joint_weight.shape[0]
    joint_parts, back_first = comm_call(
        last_kernel,
        [((4, lead, 3 * GROUP), f32, vmem), ((2, 4, piece, width), f32, vmem)],
        (joint_gradient.reshape(2, 2, 4, 2, lead, 3 * GROUP), back_first_part.reshape(natural + (width,))),
        13, 1, [(), (3,), (4,), (2, 2), (2,)],
        [
            vmem((2, 4, 2, lead, 3 * GROUP), bf16),
            vmem((3, 2, 2, lead, 3 * GROUP), bf16),
            vmem((2, 2, lead, 3 * GROUP), f32),
            vmem((2, 2, 4, piece, width), bf16),
            vmem((2, 4, piece, width), bf16),
        ],
        4,
        [vmem] * 2,
    )
    joint_shard = jnp.transpose(joint_parts.reshape(4, lead, 3, GROUP), (1, 2, 0, 3)).reshape(lead, 3 * width)
    _, first_unit, first_scale = normalize(inputs, gain_one, shift_one)
    back_norm_one, gain_one_gradient, shift_one_gradient = normalize_back(
        back_first.reshape(1, rows, width), first_unit[None], first_scale[None], gain_one
    )
    grads_here = (back_residual + back_norm_one[0]).astype(bf16)
    shifts = jnp.sum(back_joint.astype(f32), axis=0)
    zero = jnp.zeros((width,), f32)
    query_shift_gradient = lax.dynamic_update_slice(zero, shifts[:GROUP], (mine * GROUP,))
    value_shift_gradient = lax.dynamic_update_slice(zero, shifts[2 * GROUP :], (mine * GROUP,))
    small_two = packed(
        [gain_one_gradient, shift_one_gradient, query_shift_gradient, value_shift_gradient], 32, f32, 8
    )
    tokens_gradient, small_back = comm_call(
        return_kernel,
        [(tokens.shape, bf16, hbm), ((32, 8, 128), f32, hbm)],
        (grads_here.reshape(8, piece, width), small_two),
        38, 2, [(8,), (32,)], [], 5,
    )
    late = jnp.sum(small_back, axis=0)
    count = jnp.sum(lengths).astype(f32) * width
    stats = jnp.sqrt(out_s[5, :3] / count + 1e-06)
    return (
        output,
        tokens_gradient,
        late[0, :lead],
        late[1, :lead],
        joint_shard,
        late[2, :lead],
        late[3, :lead],
        out_o,
        out_s[3, :lead],
        out_s[1, :lead],
        out_s[2, :lead],
        out_i,
        out_s[4, : inner_bias.shape[0]],
        out_u,
        out_s[0, :lead],
        stats,
    )


def solution(mesh):
    in_specs = (
        P(None, ("head", "blk"), None),
        P(),
        P(("head", "blk")),
        P(("head", "blk")),
        P(("head", "blk"), None),
        P(("head", "blk")),
        P(("head", "blk")),
        P(("head", "blk"), None),
        P(("head", "blk")),
        P(("head", "blk")),
        P(("head", "blk")),
        P(("head", "blk"), None),
        P(("head", "blk")),
        P(("head", "blk"), None),
        P(("head", "blk")),
        P(None, ("head", "blk"), None),
    )
    out_specs = (
        P(None, ("head", "blk"), None),
        P(None, ("head", "blk"), None),
        P(("head", "blk")),
        P(("head", "blk")),
        P(("head", "blk"), None),
        P(("head", "blk")),
        P(("head", "blk")),
        P(("head", "blk"), None),
        P(("head", "blk")),
        P(("head", "blk")),
        P(("head", "blk")),
        P(("head", "blk"), None),
        P(("head", "blk")),
        P(("head", "blk"), None),
        P(("head", "blk")),
        P(),
    )
    small_slice = dict(mesh.shape) == {"head": 4, "blk": 8}
    device_work = owner_device if small_slice else on_device
    return jax.shard_map(
        device_work, mesh=mesh, in_specs=in_specs, out_specs=out_specs, check_vma=False
    )
```

```python
import jax
import jax.numpy as jnp
from jax import lax
from jax.experimental import pallas as pl
from jax.experimental.pallas import tpu as pltpu
from jax.sharding import PartitionSpec as P

H = 12
DH = 64


EPS = 1e-12
NEG = -1e30


def passed_along(value, axis, steps):
    count = lax.axis_size(axis)
    pairs = [(source, (source + steps) % count) for source in range(count)]
    return lax.ppermute(value, axis, pairs)


def normalize(values, gain, shift):
    average = jnp.mean(values, axis=-1, keepdims=True)
    centered = values - average
    inverse = lax.rsqrt(jnp.mean(centered * centered, axis=-1, keepdims=True) + EPS)
    normed = centered * inverse
    return (normed * gain + shift, normed, inverse)


def normalize_back(incoming, normed, inverse, gain):
    scaled = incoming * gain
    inner = (
        scaled
        - jnp.mean(scaled, axis=-1, keepdims=True)
        - normed * jnp.mean(scaled * normed, axis=-1, keepdims=True)
    )
    return (
        inner * inverse,
        jnp.sum(incoming * normed, axis=(0, 1)),
        jnp.sum(incoming, axis=(0, 1)),
    )


def gelu_exact(values):
    return jax.nn.gelu(values, approximate=False)


def key_mask(lengths, source, piece_rows, block_count, head_count):
    rows_here = jnp.arange(head_count * piece_rows, dtype=jnp.int32)
    position = (
        rows_here // piece_rows * block_count + source
    ) * piece_rows + rows_here % piece_rows
    return position[None, :] < lengths[:, None]


def attend(query_part, state, keys_block, values_block, mask):
    best, total, running = state
    scores = jnp.einsum(
        "sqhd,skhd->sqhk", query_part, keys_block, preferred_element_type=jnp.float32
    ) * DH ** (-0.5)
    scores = jnp.where(mask[:, None, None, :], scores, NEG)
    fresh = jnp.maximum(best, jnp.max(scores, axis=-1))
    decay = jnp.exp(best - fresh)
    weights = jnp.exp(scores - fresh[..., None])
    total = total * decay + jnp.sum(weights, axis=-1)
    running = running * decay[..., None] + jnp.einsum(
        "sqhk,skhd->sqhd",
        weights.astype(jnp.bfloat16),
        values_block,
        preferred_element_type=jnp.float32,
    )
    return (fresh, total, running)


def block_grads(query_part, back_part, total_part, spread_part, keys_block, values_block, mask):
    scale = DH ** (-0.5)
    scores = (
        jnp.einsum("sqhd,skhd->sqhk", query_part, keys_block, preferred_element_type=jnp.float32)
        * scale
    )
    scores = jnp.where(mask[:, None, None, :], scores, NEG)
    chances = jnp.exp(scores - total_part[..., None])
    back_chances = jnp.einsum(
        "sqhd,skhd->sqhk", back_part, values_block, preferred_element_type=jnp.float32
    )
    back_scores = (chances * (back_chances - spread_part[..., None])).astype(jnp.bfloat16)
    query_step = (
        jnp.einsum("sqhk,skhd->sqhd", back_scores, keys_block, preferred_element_type=jnp.float32)
        * scale
    )
    key_step = (
        jnp.einsum("sqhk,sqhd->skhd", back_scores, query_part, preferred_element_type=jnp.float32)
        * scale
    )
    value_step = jnp.einsum(
        "sqhk,sqhd->skhd",
        chances.astype(jnp.bfloat16),
        back_part,
        preferred_element_type=jnp.float32,
    )
    return (query_step, key_step, value_step)


def on_device(
    tokens,
    lengths,
    first_gain,
    first_bias,
    joint_weight,
    query_bias,
    value_bias,
    output_weight,
    output_bias,
    second_gain,
    second_bias,
    inner_weight,
    inner_bias,
    outer_weight,
    outer_bias,
    cotangent,
):
    head_count = lax.axis_size("head")
    block_count = lax.axis_size("blk")
    block = lax.axis_index("blk")
    quarter = lax.axis_index("head")
    (
        gain_one,
        shift_one,
        joint_full,
        query_shift,
        value_shift,
        output_full,
        output_shift,
        gain_two,
        shift_two,
        inner_full,
        inner_shift,
        outer_full,
        outer_shift,
    ) = (
        lax.all_gather(first_gain, ("head", "blk"), axis=0, tiled=True),
        lax.all_gather(first_bias, ("head", "blk"), axis=0, tiled=True),
        lax.all_gather(joint_weight, ("head", "blk"), axis=0, tiled=True),
        lax.all_gather(query_bias, ("head", "blk"), axis=0, tiled=True),
        lax.all_gather(value_bias, ("head", "blk"), axis=0, tiled=True),
        lax.all_gather(output_weight, ("head", "blk"), axis=0, tiled=True),
        lax.all_gather(output_bias, ("head", "blk"), axis=0, tiled=True),
        lax.all_gather(second_gain, ("head", "blk"), axis=0, tiled=True),
        lax.all_gather(second_bias, ("head", "blk"), axis=0, tiled=True),
        lax.all_gather(inner_weight, ("head", "blk"), axis=0, tiled=True),
        lax.all_gather(inner_bias, ("head", "blk"), axis=0, tiled=True),
        lax.all_gather(outer_weight, ("head", "blk"), axis=0, tiled=True),
        lax.all_gather(outer_bias, ("head", "blk"), axis=0, tiled=True),
    )
    sequences, piece_rows, width = tokens.shape
    heads_here = H // head_count
    head_width = heads_here * DH
    rows = head_count * piece_rows
    shape_heads = (sequences, rows, heads_here, DH)
    shape_flat = (sequences, rows, head_width)
    own_position = (quarter * block_count + block) * piece_rows + jnp.arange(
        piece_rows, dtype=jnp.int32
    )
    valid = own_position[None, :] < lengths[:, None]
    keep = valid[..., None]
    inputs = tokens.astype(jnp.float32)
    gain_one_wide = gain_one.astype(jnp.float32)
    gain_two_wide = gain_two.astype(jnp.float32)
    first_out, first_unit, first_scale = normalize(
        inputs, gain_one_wide, shift_one.astype(jnp.float32)
    )
    first_low = first_out.astype(jnp.bfloat16)
    joint = jnp.einsum("scd,de->sce", first_low, joint_full, preferred_element_type=jnp.float32)
    query_flat = (joint[..., :width] + query_shift.astype(jnp.float32)).astype(jnp.bfloat16)
    key_flat = joint[..., width : 2 * width].astype(jnp.bfloat16)
    value_flat = (joint[..., 2 * width :] + value_shift.astype(jnp.float32)).astype(jnp.bfloat16)
    query_flat, key_flat, value_flat = (
        lax.all_to_all(query_flat, "head", split_axis=2, concat_axis=1, tiled=True),
        lax.all_to_all(key_flat, "head", split_axis=2, concat_axis=1, tiled=True),
        lax.all_to_all(value_flat, "head", split_axis=2, concat_axis=1, tiled=True),
    )
    query_rows = query_flat.reshape(shape_heads)
    key_rows = key_flat.reshape(shape_heads)
    value_rows = value_flat.reshape(shape_heads)

    def visit(carry):
        keys_block, values_block, source, state = carry
        keys_block, values_block = passed_along((keys_block, values_block), "blk", 1)
        source = (source - 1) % block_count
        mask = key_mask(lengths, source, piece_rows, block_count, head_count)
        return (
            keys_block,
            values_block,
            source,
            attend(query_rows, state, keys_block, values_block, mask),
        )

    start_state = (
        jnp.full((sequences, rows, heads_here), NEG, jnp.float32),
        jnp.zeros((sequences, rows, heads_here), jnp.float32),
        jnp.zeros(shape_heads, jnp.float32),
    )
    first_state = attend(
        query_rows,
        start_state,
        key_rows,
        value_rows,
        key_mask(lengths, block, piece_rows, block_count, head_count),
    )
    carry = (key_rows, value_rows, block, first_state)
    carry = lax.fori_loop(0, block_count // 2 - 1, lambda turn, state: visit(visit(state)), carry)
    best, total, running = visit(carry)[3]
    context = running / total[..., None]
    log_total = best + jnp.log(total)
    context_low = context.astype(jnp.bfloat16).reshape(shape_flat)
    context_tokens = lax.all_to_all(context_low, "head", split_axis=1, concat_axis=2, tiled=True)
    branch = jnp.einsum(
        "sce,ed->scd", context_tokens, output_full, preferred_element_type=jnp.float32
    ) + output_shift.astype(jnp.float32)
    residual = inputs + branch
    second_out, second_unit, second_scale = normalize(
        residual, gain_two_wide, shift_two.astype(jnp.float32)
    )
    second_low = second_out.astype(jnp.bfloat16)
    inner = jnp.einsum(
        "scd,df->scf", second_low, inner_full, preferred_element_type=jnp.float32
    ) + inner_shift.astype(jnp.float32)
    activated = gelu_exact(inner).astype(jnp.bfloat16)
    feed = jnp.einsum(
        "scf,fd->scd", activated, outer_full, preferred_element_type=jnp.float32
    ) + outer_shift.astype(jnp.float32)
    result = residual + feed
    output = jnp.where(keep, result, 0.0).astype(jnp.bfloat16)
    sums = lax.psum(
        (
            jnp.sum(jnp.where(keep, result * result, 0.0)),
            jnp.sum(jnp.where(keep, branch * branch, 0.0)),
            jnp.sum(jnp.where(keep, feed * feed, 0.0)),
        ),
        ("head", "blk"),
    )
    count = jnp.sum(lengths).astype(jnp.float32) * width
    stats = jnp.sqrt(jnp.stack(sums) / count + 1e-06)
    back_result = jnp.where(keep, cotangent.astype(jnp.float32), 0.0)
    back_feed = back_result.astype(jnp.bfloat16)
    outer_gradient = jnp.einsum(
        "scf,scd->fd", activated, back_feed, preferred_element_type=jnp.float32
    )
    outer_shift_gradient = jnp.sum(back_feed.astype(jnp.float32), axis=(0, 1))
    back_active = jnp.einsum(
        "scd,fd->scf", back_feed, outer_full, preferred_element_type=jnp.float32
    )
    back_inner = jax.vjp(gelu_exact, inner)[1](back_active)[0].astype(jnp.bfloat16)
    inner_gradient = jnp.einsum(
        "scd,scf->df", second_low, back_inner, preferred_element_type=jnp.float32
    )
    inner_shift_gradient = jnp.sum(back_inner.astype(jnp.float32), axis=(0, 1))
    back_second = jnp.einsum(
        "scf,df->scd", back_inner, inner_full, preferred_element_type=jnp.float32
    )
    back_norm_two, gain_two_gradient, shift_two_gradient = normalize_back(
        back_second, second_unit, second_scale, gain_two_wide
    )
    back_residual = back_result + back_norm_two
    back_branch = back_residual.astype(jnp.bfloat16)
    output_gradient = jnp.einsum(
        "sce,scd->ed", context_tokens, back_branch, preferred_element_type=jnp.float32
    )
    output_shift_gradient = jnp.sum(back_branch.astype(jnp.float32), axis=(0, 1))
    back_context = jnp.einsum(
        "scd,ed->sce", back_branch, output_full, preferred_element_type=jnp.float32
    ).astype(jnp.bfloat16)
    back_context = lax.all_to_all(back_context, "head", split_axis=2, concat_axis=1, tiled=True)
    back_heads = back_context.reshape(shape_heads)
    spread = jnp.sum(back_heads.astype(jnp.float32) * context, axis=-1)
    zero_heads = jnp.zeros(shape_heads, jnp.float32)

    def pass_keys(carry):
        keys_block, values_block, key_sum, value_sum, query_sum, source = carry
        mask = key_mask(lengths, source, piece_rows, block_count, head_count)
        query_step, key_step, value_step = block_grads(
            query_rows, back_heads, log_total, spread, keys_block, values_block, mask
        )
        keys_block, values_block = passed_along((keys_block, values_block), "blk", 1)
        key_sum, value_sum = passed_along((key_sum + key_step, value_sum + value_step), "blk", 1)
        return (
            keys_block,
            values_block,
            key_sum,
            value_sum,
            query_sum + query_step,
            (source - 1) % block_count,
        )

    carry = (key_rows, value_rows, zero_heads, zero_heads, zero_heads, block)
    carry = lax.fori_loop(
        0, block_count // 2, lambda turn, state: pass_keys(pass_keys(state)), carry
    )
    key_sum, value_sum, query_sum = (carry[2], carry[3], carry[4])
    back_query, back_key, back_value = (
        lax.all_to_all(
            query_sum.astype(jnp.bfloat16).reshape(shape_flat),
            "head",
            split_axis=1,
            concat_axis=2,
            tiled=True,
        ),
        lax.all_to_all(
            key_sum.astype(jnp.bfloat16).reshape(shape_flat),
            "head",
            split_axis=1,
            concat_axis=2,
            tiled=True,
        ),
        lax.all_to_all(
            value_sum.astype(jnp.bfloat16).reshape(shape_flat),
            "head",
            split_axis=1,
            concat_axis=2,
            tiled=True,
        ),
    )
    back_joint = jnp.concatenate([back_query, back_key, back_value], axis=-1)
    joint_gradient = jnp.einsum(
        "scd,sce->de", first_low, back_joint, preferred_element_type=jnp.float32
    )
    query_shift_gradient = jnp.sum(back_query.astype(jnp.float32), axis=(0, 1))
    value_shift_gradient = jnp.sum(back_value.astype(jnp.float32), axis=(0, 1))
    back_first = jnp.einsum(
        "sce,de->scd", back_joint, joint_full, preferred_element_type=jnp.float32
    )
    back_norm_one, gain_one_gradient, shift_one_gradient = normalize_back(
        back_first, first_unit, first_scale, gain_one_wide
    )
    tokens_gradient = (back_residual + back_norm_one).astype(jnp.bfloat16)
    shards = (
        lax.psum_scatter(gain_one_gradient, ("head", "blk"), scatter_dimension=0, tiled=True),
        lax.psum_scatter(shift_one_gradient, ("head", "blk"), scatter_dimension=0, tiled=True),
        lax.psum_scatter(joint_gradient, ("head", "blk"), scatter_dimension=0, tiled=True),
        lax.psum_scatter(query_shift_gradient, ("head", "blk"), scatter_dimension=0, tiled=True),
        lax.psum_scatter(value_shift_gradient, ("head", "blk"), scatter_dimension=0, tiled=True),
        lax.psum_scatter(output_gradient, ("head", "blk"), scatter_dimension=0, tiled=True),
        lax.psum_scatter(output_shift_gradient, ("head", "blk"), scatter_dimension=0, tiled=True),
        lax.psum_scatter(gain_two_gradient, ("head", "blk"), scatter_dimension=0, tiled=True),
        lax.psum_scatter(shift_two_gradient, ("head", "blk"), scatter_dimension=0, tiled=True),
        lax.psum_scatter(inner_gradient, ("head", "blk"), scatter_dimension=0, tiled=True),
        lax.psum_scatter(inner_shift_gradient, ("head", "blk"), scatter_dimension=0, tiled=True),
        lax.psum_scatter(outer_gradient, ("head", "blk"), scatter_dimension=0, tiled=True),
        lax.psum_scatter(outer_shift_gradient, ("head", "blk"), scatter_dimension=0, tiled=True),
    )
    return (
        output,
        tokens_gradient,
        shards[0],
        shards[1],
        shards[2],
        shards[3],
        shards[4],
        shards[5],
        shards[6],
        shards[7],
        shards[8],
        shards[9],
        shards[10],
        shards[11],
        shards[12],
        stats,
    )


MESH = pl.DeviceIdType.MESH
WIDTH = H * DH
GROUP = 3 * DH
NT = (((1,), (1,)), ((), ()))
NN = (((1,), (0,)), ((), ()))


def place():
    head = lax.axis_index("head")
    blk = lax.axis_index("blk")
    return head // 2, lax.rem(head, 2), blk // 2, lax.rem(blk, 2)


def at(y, x, z, c):
    return (y * 2 + x, z * 2 + c)


def number(y, x, z, c):
    return y * 16 + x * 8 + z * 2 + c


def column(t):
    return t // 4, lax.rem(t, 4)


def meet(peers):
    barrier = pltpu.get_barrier_semaphore()
    for peer in peers:
        pl.semaphore_signal(barrier, inc=1, device_id=peer, device_id_type=MESH)
    pl.semaphore_wait(barrier, len(peers))


class Mover:
    def __init__(self, send_sem, local_sem, anyone):
        self.send_sem = send_sem
        self.local_sem = local_sem
        self.anyone = anyone
        self.zero = anyone[0] * 0
        self.sent = []
        self.local = []

    def push(self, source, target, sem, device):
        self.sent.append((source, target, len(self.sent), sem, device))
        self.start(*self.sent[-1])

    def start(self, source, target, spot, sem, device):
        sem = sem[0].at[self.zero + sem[1], sem[2]] if isinstance(sem, tuple) else sem
        remote(source, target, self.send_sem.at[self.zero + spot], sem, device).start()

    def sent_off(self, source, target, spot, sem, device):
        sem = sem[0].at[self.zero + sem[1], sem[2]] if isinstance(sem, tuple) else sem
        remote(source, target, self.send_sem.at[self.zero + spot], sem, device).wait_send()

    def keep(self, source, target):
        parts = (source, target, self.local_sem.at[len(self.local)])
        pltpu.make_async_copy(*parts).start()
        self.local.append(parts)

    def landed(self, target, sem):
        remote(target, target, self.send_sem.at[self.zero], sem, self.anyone).wait_recv()

    def finish(self):
        for parts in self.sent:
            self.sent_off(*parts)
        for parts in self.local:
            pltpu.make_async_copy(*parts).wait()


def remote(source, target, send_sem, recv_sem, device):
    return pltpu.make_async_remote_copy(
        src_ref=source,
        dst_ref=target,
        send_sem=send_sem,
        recv_sem=recv_sem,
        device_id=device,
        device_id_type=MESH,
    )


def unpack(small_all, vectors):
    for block in range(32):
        tile = wide(small_all[block])
        vectors[:, block * 24 : block * 24 + 24] = tile[:8, :24]


def forward_kernel(
    length, tokens, cotangent, wj, wo, wi, wu, small,
    first_low, query, key, value, context, context_rows, cot_own, tok_own, wo_all, wi_all, wu_all, small_all, wj_flat,
    send_sem, local_sem, tok_sem, cot_sem, weight_sem, small_sem, wja_sem, wjb_sem, wjc_sem, ctx_send, ctx_recv,
    ctx_local, tok_all, wj_all, vectors, turned, mixed_low,
):
    y, x, z, c = place()
    mine = number(y, x, z, c)
    quarter = x * 2 + c
    spot = y * 4 + z
    other_core = at(y, x, z, 1 - c)
    across = at(y, 1 - x, z, c)
    diagonal = at(y, 1 - x, z, 1 - c)
    down = at(1 - y, x, z, c)
    y1, x1 = jnp.where(c == 0, y, 1 - y), jnp.where(c == 0, 1 - x, x)
    y2, x2 = jnp.where(c == 0, 1 - y, y), jnp.where(c == 0, x, 1 - x)
    first, second = at(y1, x1, z, c), at(y2, x2, z, c)
    spots = [column(lax.rem(spot + k, 8)) for k in range(1, 8)]
    back_spots = [column(lax.rem(spot + 8 - k, 8)) for k in range(1, 8)]
    lines = [lax.rem(z + 4 - k, 4) for k in range(4)]
    ahead = [at(y, x, lax.rem(z + k, 4), c) for k in range(1, 4)]
    line_blocks = [number(y, x, zz, c) for zz in lines]
    first_blocks = [number(y1, x1, zz, c) for zz in lines]
    second_blocks = [number(yy, xx, zz, c) for yy, xx in ((y2, x2), (1 - y, 1 - x)) for zz in lines]
    core_blocks = [number(yy, xx, zz, 1 - c) for yy in range(2) for xx in range(2) for zz in range(4)]
    group = quad(x, c)
    meet([at(yy, x, zz, c) for yy, zz in spots] + [across, other_core, diagonal])
    move = Mover(send_sem, local_sem, other_core)
    sources = (wo, wi, wu)
    wholes = (wo_all, wi_all, wu_all)

    for yy, zz in spots:
        move.push(tokens.at[yy * 4 + zz], tok_all.at[mine], tok_sem.at[mine], at(yy, x, zz, c))
    for xx, cc in group:
        move.push(wj.at[xx * 2 + cc], wj_all.at[y, x, z, c], wja_sem.at[quarter], at(y, xx, z, cc))
    move.keep(wj.at[quarter], wj_all.at[y, x, z, c])
    move.push(tokens.at[spot], tok_all.at[mine], tok_sem.at[mine], across)
    move.push(tokens.at[spot], tok_all.at[mine], tok_sem.at[mine], other_core)
    move.keep(tokens.at[spot], tok_all.at[mine])
    for device in ahead + [first, second, other_core]:
        move.push(small, small_all.at[mine], small_sem.at[mine], device)
    move.keep(small, small_all.at[mine])

    def hand(block, own, device):
        for i in range(3):
            move.push(
                sources[i] if own else wholes[i].at[block],
                wholes[i].at[block],
                (weight_sem, i, block),
                device,
            )

    def arrive(block):
        for i in range(3):
            move.landed(wholes[i].at[block], weight_sem.at[i, block])

    def pass_small(blocks, devices):
        for block in blocks:
            move.landed(small_all.at[block], small_sem.at[block])
            for device in devices:
                move.push(small_all.at[block], small_all.at[block], small_sem.at[block], device)

    for device in ahead:
        hand(mine, True, device)
    for source, whole in zip(sources, wholes):
        move.keep(source, whole.at[mine])
    hand(mine, True, first)
    hand(mine, True, second)
    hand(mine, True, other_core)

    for xx, cc in group:
        move.landed(wj_all.at[y, xx, z, cc], wja_sem.at[xx * 2 + cc])
    pltpu.make_async_copy(*move.local[0]).wait()
    for device in ahead:
        move.push(wj_all.at[y, :, z], wj_all.at[y, :, z], wjb_sem.at[z], device)
    move.push(wj_all.at[y, :, z], wj_all.at[y, :, z], wjc_sem.at[z], down)
    pass_small(line_blocks[1:], (first, second, other_core))
    for yy, zz in back_spots:
        block = number(yy, x, zz, c)
        move.landed(tok_all.at[block], tok_sem.at[block])
        move.push(tok_all.at[block], tok_all.at[block], tok_sem.at[block], across)
        move.push(tok_all.at[block], tok_all.at[block], tok_sem.at[block], other_core)
    for zz in lines[1:]:
        move.landed(wj_all.at[y, :, zz], wjb_sem.at[zz])
        move.push(wj_all.at[y, :, zz], wj_all.at[y, :, zz], wjc_sem.at[zz], down)
    for yy, zz in spots:
        move.push(cotangent.at[yy * 4 + zz], cot_own.at[spot], cot_sem.at[spot], at(yy, x, zz, c))
    move.keep(cotangent.at[spot], cot_own.at[spot])
    pass_small(first_blocks, (second, other_core))
    pass_small(second_blocks, (other_core,))
    for yy, zz in [(y, z)] + back_spots:
        block = number(yy, 1 - x, zz, c)
        move.landed(tok_all.at[block], tok_sem.at[block])
        move.push(tok_all.at[block], tok_all.at[block], tok_sem.at[block], other_core)
    for block in line_blocks[1:]:
        arrive(block)
        hand(block, False, first)
        hand(block, False, second)
        hand(block, False, other_core)
    for block in core_blocks:
        move.landed(small_all.at[block], small_sem.at[block])
    for zz in lines:
        move.landed(wj_all.at[1 - y, :, zz], wjc_sem.at[zz])
    for yy, zz in [(y, z)] + back_spots:
        for xx in (x, 1 - x):
            block = number(yy, xx, zz, 1 - c)
            move.landed(tok_all.at[block], tok_sem.at[block])
    for parts in move.local[1:3]:
        pltpu.make_async_copy(*parts).wait()

    unpack(small_all, vectors)
    rows = query.shape[1]
    for yy in range(2):
        for xx in range(2):
            for zz in range(4):
                pair = jnp.concatenate([wide(wj_all[yy, xx, zz, cc]) for cc in range(2)], axis=0)
                row = number(yy, xx, zz, 0) * 24
                wj_flat[row : row + 48, :] = pair.astype(jnp.bfloat16)
    lane = lax.broadcasted_iota(jnp.int32, (ROWS, DH), 1)
    row_at = lax.broadcasted_iota(jnp.int32, (ROWS, DH), 0)
    one_lane = jnp.where(lane == 0, 1.0, 0.0).astype(jnp.bfloat16)
    three_lanes = jnp.where(lane < 3, 1.0, 0.0).astype(jnp.bfloat16)
    gain, shift = vectors[0:1, :], vectors[1:2, :]
    query_all, value_all = vectors[2:3, :], vectors[3:4, :]

    def chosen(whole):
        total = jnp.zeros((1, GROUP), jnp.float32)
        for q in range(4):
            total = jnp.where(quarter == q, whole[:, q * GROUP : (q + 1) * GROUP], total)
        return total

    query_shift, value_shift = chosen(query_all), chosen(value_all)
    blocks = ROWS // tokens.shape[1]

    def project(i, _):
        here = pl.ds(i * ROWS, ROWS)
        raw = tok_all[pl.ds(i * blocks, blocks)].reshape(ROWS, WIDTH)
        normed = normalize(wide(raw), gain, shift)[0].astype(jnp.bfloat16)
        first_low[here, :] = normed
        joint = dot(normed, wj_flat[...])
        low_q = ((joint[:, :GROUP] + query_shift).astype(jnp.bfloat16) * DH ** (-0.5)).astype(jnp.bfloat16)
        low_k = joint[:, GROUP : 2 * GROUP].astype(jnp.bfloat16)
        low_v = (joint[:, 2 * GROUP :] + value_shift).astype(jnp.bfloat16)
        mask = jnp.where(row_at + i * ROWS < length[0], 0.0, NEG)
        key_side = jnp.where(lane == 0, mask, jnp.where(lane < 4, 1.0, 0.0)).astype(jnp.bfloat16)
        for h in range(3):
            here_h = slice(h * DH, (h + 1) * DH)
            query[h, here, :] = jnp.concatenate([low_q[:, here_h], one_lane], axis=1)
            key[h, here, :] = jnp.concatenate([low_k[:, here_h], key_side], axis=1)
            value[h, here, :] = jnp.concatenate([low_v[:, here_h], three_lanes], axis=1)
        return 0

    lax.fori_loop(0, rows // ROWS, project, 0)
    eye = jnp.eye(72, 2 * DH, dtype=jnp.bfloat16)
    for h in range(3):
        turned[h] = dot(eye, value[h], NT).astype(jnp.bfloat16)
    side = lax.broadcasted_iota(jnp.int32, (DH, ROWS), 0)

    def ctx_piece(j, cc):
        yy, xx, zz = j // 4, lax.rem(j // 2, 2), pl.ds(lax.rem(j, 2) * 2, 2)
        return mixed_low.at[yy, xx, zz, cc], context_rows.at[quarter, yy, zz]

    def block(j, _):
        here = pl.ds(j * ROWS, ROWS)
        whole = []
        for h in range(3):
            scores = dot(key[h], query[h, here, :], NT)
            best = jnp.max(scores, axis=0, keepdims=True)
            weights = jnp.exp(scores - best).astype(jnp.bfloat16)
            mixed = dot(turned[h], weights)
            total = mixed[DH : DH + 1, :]
            mixed = mixed[:DH, :] / total
            log_total = best + jnp.log(total)
            high = log_total.astype(jnp.bfloat16).astype(jnp.float32)
            middle = (log_total - high).astype(jnp.bfloat16).astype(jnp.float32)
            low = log_total - high - middle
            extra = jnp.where(
                side == 0, 1.0, jnp.where(side == 1, -high, jnp.where(side == 2, -middle, jnp.where(side == 3, -low, 0.0)))
            )
            straight = jnp.concatenate([mixed, extra], axis=0).T
            query[h, here, DH:] = straight[:, DH:].astype(jnp.bfloat16)
            whole.append(straight[:, :DH])
        mixed = jnp.concatenate(whole, axis=1)
        context[here, :] = mixed
        yy, xx, zz = j // 4, lax.rem(j // 2, 2), lax.rem(j, 2) * 2
        low = mixed.astype(jnp.bfloat16)
        piece = tokens.shape[1]
        for k in range(2):
            for cc in range(2):
                start = (k * 2 + cc) * piece
                mixed_low[yy, xx, zz + k, cc] = low[start : start + piece]
        for cc in range(2):
            source, target = ctx_piece(j, cc)

            @pl.when(jnp.logical_and(xx == x, c == cc))
            def _():
                pltpu.make_async_copy(source, target, ctx_local.at[j]).start()

            @pl.when(jnp.logical_not(jnp.logical_and(xx == x, c == cc)))
            def _():
                remote(source, target, ctx_send.at[j, cc], ctx_recv.at[quarter, j], at(y, xx, z, cc)).start()

        @pl.when(j == 2)
        def _():
            for b in first_blocks:
                arrive(b)
                hand(b, False, second)
                hand(b, False, other_core)

        @pl.when(j == 6)
        def _():
            for b in second_blocks:
                arrive(b)
                hand(b, False, other_core)

        return 0

    lax.fori_loop(0, rows // ROWS, block, 0)
    for yy, zz in back_spots:
        move.landed(cot_own.at[yy * 4 + zz], cot_sem.at[yy * 4 + zz])
    for b in core_blocks:
        arrive(b)
    tok_copies = []
    for i in range(8):
        yy, zz = i // 4, i % 4
        tok_copies.append(pltpu.make_async_copy(tok_all.at[number(yy, x, zz, c)], tok_own.at[i], local_sem.at[8 + i]))
        tok_copies[-1].start()

    def settle(j, _):
        xx = lax.rem(j // 2, 2)
        for cc in range(2):
            source, target = ctx_piece(j, cc)

            @pl.when(jnp.logical_and(xx == x, c == cc))
            def _():
                pltpu.make_async_copy(source, target, ctx_local.at[j]).wait()

            @pl.when(jnp.logical_not(jnp.logical_and(xx == x, c == cc)))
            def _():
                remote(source, target, ctx_send.at[j, cc], ctx_recv.at[quarter, j], at(y, xx, z, cc)).wait_send()

        return 0

    lax.fori_loop(0, rows // ROWS, settle, 0)
    for xx, cc in group:
        for yy in range(2):
            for half in range(2):
                j = yy * 4 + x * 2 + half
                target = context_rows.at[xx * 2 + cc, yy, pl.ds(half * 2, 2)]
                move.landed(target, ctx_recv.at[xx * 2 + cc, j])
    for parts in move.sent:
        move.sent_off(*parts)
    for parts in move.local[3:]:
        pltpu.make_async_copy(*parts).wait()
    for copy in tok_copies:
        copy.wait()


def comm_call(kernel, outs, args, sends, locals_, sems, scratch, ident, space=None):
    space = space or [pltpu.HBM] * len(args)
    return pl.pallas_call(
        kernel,
        out_shape=[jax.ShapeDtypeStruct(shape, dtype) for shape, dtype, _ in outs],
        in_specs=[pl.BlockSpec(memory_space=one) for one in space],
        out_specs=[pl.BlockSpec(memory_space=one) for _, _, one in outs],
        scratch_shapes=[
            pltpu.SemaphoreType.DMA((sends,)),
            pltpu.SemaphoreType.DMA((max(locals_, 1),)),
            *[pltpu.SemaphoreType.DMA(shape) for shape in sems],
            *scratch,
        ],
        compiler_params=pltpu.CompilerParams(
            collective_id=ident, has_side_effects=True, vmem_limit_bytes=56 * 1024 * 1024
        ),
    )(*args)


def quad(x, c):
    return [(lax.rem(x + dx, 2), lax.rem(c + dc, 2)) for dx, dc in ((0, 1), (1, 0), (1, 1))]


def to_heads_kernel(source, target, send_sem, local_sem, recv_sem):
    y, x, z, c = place()
    mine = x * 2 + c
    meet([at(y, xx, z, cc) for xx, cc in quad(x, c)])
    move = Mover(send_sem, local_sem, at(y, x, z, 1 - c))
    for xx, cc in quad(x, c)[::-1]:
        for yy in range(2):
            move.push(
                source.at[xx * 2 + cc, yy],
                target.at[yy, x, :, c],
                recv_sem.at[mine, yy],
                at(y, xx, z, cc),
            )
    for yy in range(2):
        move.keep(source.at[mine, yy], target.at[yy, x, :, c])
    for xx, cc in quad(x, c):
        for yy in range(2):
            move.landed(target.at[yy, xx, :, cc], recv_sem.at[xx * 2 + cc, yy])
    move.finish()


def wide(value):
    return value.astype(jnp.float32)


def reduce_kernel(
    go, gi, gu, gs, outgoing,
    out_o, out_i, out_u, out_s, output,
    send_sem, local_sem, sem1, sem2, sem3, sem4, sem_out,
    *held,
):
    y, x, z, c = place()
    spot = y * 4 + z
    other_core = at(y, x, z, 1 - c)
    across = at(y, 1 - x, z, c)
    y1, x1 = jnp.where(c == 0, y, 1 - y), jnp.where(c == 0, 1 - x, x)
    y2, x2 = jnp.where(c == 0, 1 - y, y), jnp.where(c == 0, x, 1 - x)
    first, second = at(y1, x1, z, c), at(y2, x2, z, c)
    spots = [column(lax.rem(spot + k, 8)) for k in range(1, 8)]
    meet([at(yy, x, zz, c) for yy, zz in spots] + [across, other_core])
    move = Mover(send_sem, local_sem, other_core)
    parts = (gu, gi, go, gs)
    results = (out_u, out_i, out_o, out_s)
    r1, r2, r3, r4 = held[0:4], held[4:8], held[8:12], held[12:16]
    own, near1, near2 = y * 2 + x, y1 * 2 + x1, y2 * 2 + x2
    far = (1 - y) * 2 + 1 - x
    order = (far, near1, near2, own)
    for i in range(4):
        for quarter in order:
            move.push(
                parts[i].at[quarter, :, 1 - c], r1[i].at[quarter], sem1.at[i, quarter], other_core
            )
    for yy, zz in spots:
        move.push(outgoing.at[yy * 4 + zz], output.at[spot], sem_out.at[spot], at(yy, x, zz, c))
    move.keep(outgoing.at[spot], output.at[spot])

    def gather(i, quarter):
        move.landed(r1[i].at[quarter], sem1.at[i, quarter])
        r1[i][quarter] = (wide(r1[i][quarter]) + wide(parts[i][quarter, :, c])).astype(r1[i].dtype)

    def stage2(i):
        for slot, quarter in ((1, far), (0, near1)):
            gather(i, quarter)
            move.push(r1[i].at[quarter], r2[i].at[slot], sem2.at[i, slot], first)

    def stage3(i):
        gather(i, near2)
        move.landed(r2[i].at[1], sem2.at[i, 1])
        r1[i][near2] = (wide(r1[i][near2]) + wide(r2[i][1])).astype(r1[i].dtype)
        move.push(r1[i].at[near2], r3[i], sem3.at[i], second)

    def stage4(i):
        gather(i, own)
        move.landed(r2[i].at[0], sem2.at[i, 0])
        move.landed(r3[i], sem3.at[i])
        r1[i][own] = (wide(r1[i][own]) + wide(r2[i][0]) + wide(r3[i][...])).astype(r1[i].dtype)
        for k in range(1, 4):
            zz = lax.rem(z + k, 4)
            move.push(r1[i].at[own, zz], r4[i].at[k - 1], sem4.at[i, k - 1], at(y, x, zz, c))

    def stage5(i):
        total = wide(r1[i][own, z])
        for k in range(1, 4):
            move.landed(r4[i].at[k - 1], sem4.at[i, k - 1])
            total = total + wide(r4[i][k - 1])
        results[i][...] = total

    stages = (stage2, stage3, stage4, stage5)
    for turn in range(7):
        for depth in range(3, -1, -1):
            i = turn - depth
            if 0 <= i < 4:
                stages[depth](i)
    for k in range(1, 8):
        t = lax.rem(spot + 8 - k, 8)
        move.landed(output.at[t], sem_out.at[t])
    move.finish()


def last_kernel(
    gj, bf, out_j, out_b,
    send_sem, local_sem, sem_y, sem_z, sem_g, sem_c, sem_x,
    ry, rz, sj, rc, rx,
):
    y, x, z, c = place()
    other_core = at(y, x, z, 1 - c)
    across = at(y, 1 - x, z, c)
    down = at(1 - y, x, z, c)
    line = [lax.rem(z + k, 4) for k in range(1, 4)]
    group = quad(x, c)
    meet([at(y, xx, z, cc) for xx, cc in group] + [down] + [at(y, x, zz, c) for zz in line])
    move = Mover(send_sem, local_sem, other_core)
    move.push(gj.at[1 - y], ry, sem_y, down)
    quarters = [(yy, xx) for xx in (1 - x, x) for yy in range(2)]
    for yy, xx in quarters:
        move.push(bf.at[yy, xx, :, 1 - c], rc.at[yy, xx], sem_c.at[yy, xx], other_core)
    for yy, xx in quarters[:2]:
        move.landed(rc.at[yy, xx], sem_c.at[yy, xx])
        rc[yy, xx] = (wide(rc[yy, xx]) + wide(bf[yy, xx, :, c])).astype(rc.dtype)
        move.push(rc.at[yy, xx], rx.at[yy], sem_x.at[yy], across)
    move.landed(ry, sem_y)
    ry[...] = (wide(ry[...]) + wide(gj[y])).astype(ry.dtype)
    for k in range(3):
        move.push(ry.at[:, line[k]], rz.at[k], sem_z.at[k], at(y, x, line[k], c))
    for yy, xx in quarters[2:]:
        move.landed(rc.at[yy, xx], sem_c.at[yy, xx])
    total = wide(ry[:, z])
    for k in range(3):
        move.landed(rz.at[k], sem_z.at[k])
        total = total + wide(rz[k])
    sj[...] = total
    mine = x * 2 + c
    for xx, cc in group:
        move.push(sj.at[xx, cc], out_j.at[mine], sem_g.at[mine], at(y, xx, z, cc))
    move.keep(sj.at[x, c], out_j.at[mine])
    for yy in range(2):
        move.landed(rx.at[yy], sem_x.at[yy])
        out_b[yy] = wide(rc[yy, x]) + wide(bf[yy, x, :, c]) + wide(rx[yy])
    for xx, cc in group:
        move.landed(out_j.at[xx * 2 + cc], sem_g.at[xx * 2 + cc])
    move.finish()


def return_kernel(grads, small, out, small_all, send_sem, local_sem, sem_t, sem_s):
    y, x, z, c = place()
    spot = y * 4 + z
    mine = number(y, x, z, c)
    others = []
    for k in range(1, 32):
        t = lax.rem(mine + k, 32)
        others.append((t, (t // 8, lax.rem(t, 8))))
    meet([device for _, device in others])
    move = Mover(send_sem, local_sem, at(y, x, z, 1 - c))
    for k in range(1, 8):
        yy, zz = column(lax.rem(spot + k, 8))
        move.push(grads.at[yy * 4 + zz], out.at[spot], sem_t.at[spot], at(yy, x, zz, c))
    move.keep(grads.at[spot], out.at[spot])
    for t, device in others:
        move.push(small.at[t], small_all.at[mine], sem_s.at[mine], device)
    move.keep(small.at[mine], small_all.at[mine])
    for k in range(1, 8):
        t = lax.rem(spot + 8 - k, 8)
        move.landed(out.at[t], sem_t.at[t])
    for t, device in others:
        move.landed(small_all.at[t], sem_s.at[t])
    move.finish()


def dot(a, b, dims=NN):
    return lax.dot_general(a, b, dims, preferred_element_type=jnp.float32)


ROWS = 256


def attend_back_kernel(query, key, value, back_context, context, joint, key_sum, value_sum):
    rows = query.shape[1]
    scale = DH ** (-0.5)
    eye = jnp.eye(DH, 2 * DH, dtype=jnp.bfloat16)
    lane = lax.broadcasted_iota(jnp.int32, (ROWS, DH), 1)
    for h in range(3):
        turned = dot(eye, key[h], NT).astype(jnp.bfloat16)
        key_sum[...] = jnp.zeros_like(key_sum)
        value_sum[...] = jnp.zeros_like(value_sum)

        def block(i, _):
            here = pl.ds(i * ROWS, ROWS)
            queries = query[h, here, :]
            backs = back_context[here, h * DH : (h + 1) * DH]
            spread = jnp.sum(wide(backs) * context[here, h * DH : (h + 1) * DH], axis=1, keepdims=True)
            high = spread.astype(jnp.bfloat16).astype(jnp.float32)
            middle = (spread - high).astype(jnp.bfloat16).astype(jnp.float32)
            low = spread - high - middle
            side = jnp.where(lane == 0, -high, jnp.where(lane == 1, -middle, jnp.where(lane == 2, -low, 0.0)))
            widened = jnp.concatenate([backs, side.astype(jnp.bfloat16)], axis=1)
            chances = jnp.exp(dot(key[h], queries, NT))
            back_scores = (chances * dot(value[h], widened, NT)).astype(jnp.bfloat16)
            joint[here, h * DH : (h + 1) * DH] = (dot(turned, back_scores) * scale).T.astype(jnp.bfloat16)
            key_sum[...] += dot(back_scores, queries[:, :DH])
            value_sum[...] += dot(chances.astype(jnp.bfloat16), backs)
            return 0

        lax.fori_loop(0, rows // ROWS, block, 0)
        joint[:, GROUP + h * DH : GROUP + (h + 1) * DH] = key_sum[...].astype(jnp.bfloat16)
        joint[:, 2 * GROUP + h * DH : 2 * GROUP + (h + 1) * DH] = value_sum[...].astype(jnp.bfloat16)


def local_call(kernel, outs, args, scratch=(), smem=1):
    return pl.pallas_call(
        kernel,
        out_shape=[jax.ShapeDtypeStruct(shape, dtype) for shape, dtype in outs],
        in_specs=[pl.BlockSpec(memory_space=pltpu.SMEM)] * smem
        + [pl.BlockSpec(memory_space=pltpu.VMEM)] * (len(args) - smem),
        out_specs=[pl.BlockSpec(memory_space=pltpu.VMEM)] * len(outs),
        scratch_shapes=list(scratch),
        compiler_params=pltpu.CompilerParams(vmem_limit_bytes=56 * 1024 * 1024),
    )(*args)


def packed(vectors, blocks, dtype, tile):
    rows = [jnp.pad(v.reshape(blocks, 1, -1), ((0, 0), (0, 0), (0, 128 - v.size // blocks))) for v in vectors]
    whole = jnp.concatenate(rows, axis=1).astype(dtype)
    return jnp.pad(whole, ((0, 0), (0, tile - whole.shape[1]), (0, 0)))


def owner_device(
    tokens,
    lengths,
    first_gain,
    first_bias,
    joint_weight,
    query_bias,
    value_bias,
    output_weight,
    output_bias,
    second_gain,
    second_bias,
    inner_weight,
    inner_bias,
    outer_weight,
    outer_bias,
    cotangent,
):
    bf16, f32 = jnp.bfloat16, jnp.float32
    y, x, z, c = place()
    mine = x * 2 + c
    slots, piece, width = tokens.shape
    ff = inner_weight.shape[1]
    short = jnp.stack(
        [first_gain, first_bias, query_bias, value_bias, output_bias, second_gain, second_bias, outer_bias]
    )
    lead = short.shape[1]
    ff_piece = inner_bias.shape[0]
    small = jnp.concatenate(
        [
            jnp.pad(short, ((0, 0), (0, ff_piece - lead))),
            jnp.broadcast_to(inner_bias, (8, ff_piece)),
        ],
        axis=0,
    )
    hbm, vmem = pltpu.HBM, pltpu.VMEM
    dma, regular = pltpu.SemaphoreType.DMA, pltpu.SemaphoreType.REGULAR
    rows_all = 32 * piece
    natural = (2, 2, 4, 2, piece)
    length = lax.dynamic_slice(lengths, (y * 4 + z,), (1,))
    joint_four = jnp.transpose(joint_weight.reshape(lead, 3, 4, GROUP), (2, 0, 1, 3)).reshape(4, lead, 3 * GROUP)
    forward_outs = [
        ((rows_all, width), bf16, vmem),
        ((3, rows_all, 2 * DH), bf16, vmem),
        ((3, rows_all, 2 * DH), bf16, vmem),
        ((3, rows_all, 2 * DH), bf16, vmem),
        ((rows_all, GROUP), f32, vmem),
        ((4, 2, 4, piece, GROUP), bf16, vmem),
        ((8, piece, width), bf16, hbm),
        ((8, piece, width), bf16, hbm),
        ((32,) + output_weight.shape, bf16, hbm),
        ((32,) + inner_weight.shape, bf16, hbm),
        ((32,) + outer_weight.shape, bf16, hbm),
        ((32,) + small.shape, bf16, vmem),
        ((width, 3 * GROUP), bf16, vmem),
    ]
    (
        first_low, query, key, value, context, context_rows, cot_own, tok_own, wo_all, wi_all, wu_all, small_all, joint_here
    ) = comm_call(
        forward_kernel,
        forward_outs,
        (length, tokens, cotangent, joint_four, output_weight, inner_weight, outer_weight, small),
        220, 16,
        [(32,), (8,), (3, 32), (32,), (4,), (4,), (4,), (8, 2), (4, 8), (8,)],
        [
            vmem((32, piece, width), bf16),
            vmem((2, 2, 4, 2, lead, 3 * GROUP), bf16),
            vmem((8, width), f32),
            vmem((3, 72, rows_all), bf16),
            vmem(natural + (GROUP,), bf16),
        ],
        0,
        [pltpu.SMEM, hbm, hbm, hbm, hbm, hbm, hbm, hbm],
    )
    vectors = jnp.transpose(small_all[:, :8, :lead], (1, 0, 2)).reshape(8, width).astype(f32)
    inner_shift = small_all[:, 8, :ff_piece].reshape(1, ff).astype(f32)
    gain_one, shift_one, query_shift, value_shift, output_shift, gain_two, shift_two, outer_shift = (
        vectors[i : i + 1] for i in range(8)
    )
    rows = 8 * piece
    context_low = jnp.transpose(context_rows.reshape(4, rows, GROUP), (1, 0, 2)).reshape(rows, width)

    spots = jnp.arange(8, dtype=jnp.int32)
    position = (
        number(spots // 4, x, spots % 4, c)[:, None] * piece + jnp.arange(piece, dtype=jnp.int32)
    ).reshape(rows, 1)
    keep = position < length[0]
    inputs = tok_own.reshape(rows, width).astype(f32)
    output_full = wo_all.reshape(width, width)
    inner_full = wi_all.reshape(width, ff)
    outer_full = wu_all.reshape(ff, width)
    branch = dot(context_low, output_full) + output_shift
    residual = inputs + branch
    second_out, second_unit, second_scale = normalize(residual, gain_two, shift_two)
    second_low = second_out.astype(bf16)
    inner = dot(second_low, inner_full) + inner_shift
    activated = gelu_exact(inner).astype(bf16)
    feed = dot(activated, outer_full) + outer_shift
    result = residual + feed
    output_here = jnp.where(keep, result, 0.0).astype(bf16)
    sums = [jnp.sum(jnp.where(keep, item * item, 0.0)) for item in (result, branch, feed)]
    back_result = jnp.where(keep, cot_own.reshape(rows, width).astype(f32), 0.0)
    back_feed = back_result.astype(bf16)
    turn = (((0,), (0,)), ((), ()))
    outer_gradient = dot(activated, back_feed, turn).astype(bf16)
    outer_shift_gradient = jnp.sum(back_feed.astype(f32), axis=0)
    back_active = dot(back_feed, outer_full, NT)
    back_inner = jax.vjp(gelu_exact, inner)[1](back_active)[0].astype(bf16)
    inner_gradient = dot(second_low, back_inner, turn).astype(bf16)
    inner_shift_gradient = jnp.sum(back_inner.astype(f32), axis=0)
    back_second = dot(back_inner, inner_full, NT)
    back_norm_two, gain_two_gradient, shift_two_gradient = normalize_back(
        back_second[None], second_unit[None], second_scale[None], gain_two
    )
    back_residual = back_result + back_norm_two[0]
    back_branch = back_residual.astype(bf16)
    output_gradient = dot(context_low, back_branch, turn).astype(bf16)
    output_shift_gradient = jnp.sum(back_branch.astype(f32), axis=0)
    back_context = jnp.einsum(
        "rd,ged->gre", back_branch, output_full.reshape(4, GROUP, width), preferred_element_type=f32
    ).astype(bf16)
    (back_heads,) = comm_call(
        to_heads_kernel,
        [(natural + (GROUP,), bf16, hbm)],
        (back_context.reshape(4, 2, 4, piece, GROUP),),
        6, 2, [(4, 2)], [], 2,
    )
    (back_joint,) = local_call(
        attend_back_kernel,
        [((rows_all, 3 * GROUP), bf16)],
        (query, key, value, back_heads.reshape(rows_all, GROUP), context),
        scratch=[vmem((rows_all, DH), f32), vmem((rows_all, DH), f32)],
        smem=0,
    )
    stat_row = jnp.broadcast_to(jnp.stack(sums), (32, 3)).reshape(-1)
    small_one = packed(
        [outer_shift_gradient, gain_two_gradient, shift_two_gradient, output_shift_gradient, inner_shift_gradient, stat_row],
        32, f32, 8,
    )
    grid = (4, 4, 2)
    owned = [
        (output_gradient, output_weight.shape, bf16),
        (inner_gradient, inner_weight.shape, bf16),
        (outer_gradient, outer_weight.shape, bf16),
        (small_one, (8, 128), f32),
    ]
    order = [owned[2], owned[1], owned[0], owned[3]]
    out_o, out_i, out_u, out_s, output = comm_call(
        reduce_kernel,
        [(shape, f32, vmem) for _, shape, _ in owned] + [(tokens.shape, bf16, hbm)],
        tuple(item.reshape(grid + shape) for item, shape, _ in owned)
        + (output_here.reshape(8, piece, width),),
        63, 1, [(4, 4), (4, 2), (4,), (4, 3), (8,)],
        [vmem((4, 4) + shape, dtype) for _, shape, dtype in order]
        + [vmem((2, 4) + shape, dtype) for _, shape, dtype in order]
        + [vmem((4,) + shape, dtype) for _, shape, dtype in order]
        + [vmem((3,) + shape, dtype) for _, shape, dtype in order],
        3,
        [vmem] * 4 + [hbm],
    )
    joint_gradient = dot(first_low, back_joint, turn).astype(bf16)
    back_first_part = dot(back_joint, joint_here, NT).astype(bf16)
    joint_parts, back_first = comm_call(
        last_kernel,
        [((4, lead, 3 * GROUP), f32, vmem), ((2, 4, piece, width), f32, vmem)],
        (joint_gradient.reshape(2, 2, 4, 2, lead, 3 * GROUP), back_first_part.reshape(natural + (width,))),
        13, 1, [(), (3,), (4,), (2, 2), (2,)],
        [
            vmem((2, 4, 2, lead, 3 * GROUP), bf16),
            vmem((3, 2, 2, lead, 3 * GROUP), bf16),
            vmem((2, 2, lead, 3 * GROUP), f32),
            vmem((2, 2, 4, piece, width), bf16),
            vmem((2, 4, piece, width), bf16),
        ],
        4,
        [vmem] * 2,
    )
    joint_shard = jnp.transpose(joint_parts.reshape(4, lead, 3, GROUP), (1, 2, 0, 3)).reshape(lead, 3 * width)
    _, first_unit, first_scale = normalize(inputs, gain_one, shift_one)
    back_norm_one, gain_one_gradient, shift_one_gradient = normalize_back(
        back_first.reshape(1, rows, width), first_unit[None], first_scale[None], gain_one
    )
    grads_here = (back_residual + back_norm_one[0]).astype(bf16)
    shifts = jnp.sum(back_joint.astype(f32), axis=0)
    zero = jnp.zeros((width,), f32)
    query_shift_gradient = lax.dynamic_update_slice(zero, shifts[:GROUP], (mine * GROUP,))
    value_shift_gradient = lax.dynamic_update_slice(zero, shifts[2 * GROUP :], (mine * GROUP,))
    small_two = packed(
        [gain_one_gradient, shift_one_gradient, query_shift_gradient, value_shift_gradient], 32, f32, 8
    )
    tokens_gradient, small_back = comm_call(
        return_kernel,
        [(tokens.shape, bf16, hbm), ((32, 8, 128), f32, hbm)],
        (grads_here.reshape(8, piece, width), small_two),
        38, 2, [(8,), (32,)], [], 5,
    )
    late = jnp.sum(small_back, axis=0)
    count = jnp.sum(lengths).astype(f32) * width
    stats = jnp.sqrt(out_s[5, :3] / count + 1e-06)
    return (
        output,
        tokens_gradient,
        late[0, :lead],
        late[1, :lead],
        joint_shard,
        late[2, :lead],
        late[3, :lead],
        out_o,
        out_s[3, :lead],
        out_s[1, :lead],
        out_s[2, :lead],
        out_i,
        out_s[4, : inner_bias.shape[0]],
        out_u,
        out_s[0, :lead],
        stats,
    )


def solution(mesh):
    in_specs = (
        P(None, ("head", "blk"), None),
        P(),
        P(("head", "blk")),
        P(("head", "blk")),
        P(("head", "blk"), None),
        P(("head", "blk")),
        P(("head", "blk")),
        P(("head", "blk"), None),
        P(("head", "blk")),
        P(("head", "blk")),
        P(("head", "blk")),
        P(("head", "blk"), None),
        P(("head", "blk")),
        P(("head", "blk"), None),
        P(("head", "blk")),
        P(None, ("head", "blk"), None),
    )
    out_specs = (
        P(None, ("head", "blk"), None),
        P(None, ("head", "blk"), None),
        P(("head", "blk")),
        P(("head", "blk")),
        P(("head", "blk"), None),
        P(("head", "blk")),
        P(("head", "blk")),
        P(("head", "blk"), None),
        P(("head", "blk")),
        P(("head", "blk")),
        P(("head", "blk")),
        P(("head", "blk"), None),
        P(("head", "blk")),
        P(("head", "blk"), None),
        P(("head", "blk")),
        P(),
    )
    small_slice = dict(mesh.shape) == {"head": 4, "blk": 8}
    device_work = owner_device if small_slice else on_device
    return jax.shard_map(
        device_work, mesh=mesh, in_specs=in_specs, out_specs=out_specs, check_vma=False
    )
```

```python
import jax
import jax.numpy as jnp
from jax import lax
from jax.experimental import pallas as pl
from jax.experimental.pallas import tpu as pltpu
from jax.sharding import PartitionSpec as P

H = 12
DH = 64


EPS = 1e-12
NEG = -1e30


def passed_along(value, axis, steps):
    count = lax.axis_size(axis)
    pairs = [(source, (source + steps) % count) for source in range(count)]
    return lax.ppermute(value, axis, pairs)


def normalize(values, gain, shift):
    average = jnp.mean(values, axis=-1, keepdims=True)
    centered = values - average
    inverse = lax.rsqrt(jnp.mean(centered * centered, axis=-1, keepdims=True) + EPS)
    normed = centered * inverse
    return (normed * gain + shift, normed, inverse)


def normalize_back(incoming, normed, inverse, gain):
    scaled = incoming * gain
    inner = (
        scaled
        - jnp.mean(scaled, axis=-1, keepdims=True)
        - normed * jnp.mean(scaled * normed, axis=-1, keepdims=True)
    )
    return (
        inner * inverse,
        jnp.sum(incoming * normed, axis=(0, 1)),
        jnp.sum(incoming, axis=(0, 1)),
    )


def gelu_exact(values):
    return jax.nn.gelu(values, approximate=False)


def key_mask(lengths, source, piece_rows, block_count, head_count):
    rows_here = jnp.arange(head_count * piece_rows, dtype=jnp.int32)
    position = (
        rows_here // piece_rows * block_count + source
    ) * piece_rows + rows_here % piece_rows
    return position[None, :] < lengths[:, None]


def attend(query_part, state, keys_block, values_block, mask):
    best, total, running = state
    scores = jnp.einsum(
        "sqhd,skhd->sqhk", query_part, keys_block, preferred_element_type=jnp.float32
    ) * DH ** (-0.5)
    scores = jnp.where(mask[:, None, None, :], scores, NEG)
    fresh = jnp.maximum(best, jnp.max(scores, axis=-1))
    decay = jnp.exp(best - fresh)
    weights = jnp.exp(scores - fresh[..., None])
    total = total * decay + jnp.sum(weights, axis=-1)
    running = running * decay[..., None] + jnp.einsum(
        "sqhk,skhd->sqhd",
        weights.astype(jnp.bfloat16),
        values_block,
        preferred_element_type=jnp.float32,
    )
    return (fresh, total, running)


def block_grads(query_part, back_part, total_part, spread_part, keys_block, values_block, mask):
    scale = DH ** (-0.5)
    scores = (
        jnp.einsum("sqhd,skhd->sqhk", query_part, keys_block, preferred_element_type=jnp.float32)
        * scale
    )
    scores = jnp.where(mask[:, None, None, :], scores, NEG)
    chances = jnp.exp(scores - total_part[..., None])
    back_chances = jnp.einsum(
        "sqhd,skhd->sqhk", back_part, values_block, preferred_element_type=jnp.float32
    )
    back_scores = (chances * (back_chances - spread_part[..., None])).astype(jnp.bfloat16)
    query_step = (
        jnp.einsum("sqhk,skhd->sqhd", back_scores, keys_block, preferred_element_type=jnp.float32)
        * scale
    )
    key_step = (
        jnp.einsum("sqhk,sqhd->skhd", back_scores, query_part, preferred_element_type=jnp.float32)
        * scale
    )
    value_step = jnp.einsum(
        "sqhk,sqhd->skhd",
        chances.astype(jnp.bfloat16),
        back_part,
        preferred_element_type=jnp.float32,
    )
    return (query_step, key_step, value_step)


def on_device(
    tokens,
    lengths,
    first_gain,
    first_bias,
    joint_weight,
    query_bias,
    value_bias,
    output_weight,
    output_bias,
    second_gain,
    second_bias,
    inner_weight,
    inner_bias,
    outer_weight,
    outer_bias,
    cotangent,
):
    head_count = lax.axis_size("head")
    block_count = lax.axis_size("blk")
    block = lax.axis_index("blk")
    quarter = lax.axis_index("head")
    (
        gain_one,
        shift_one,
        joint_full,
        query_shift,
        value_shift,
        output_full,
        output_shift,
        gain_two,
        shift_two,
        inner_full,
        inner_shift,
        outer_full,
        outer_shift,
    ) = (
        lax.all_gather(first_gain, ("head", "blk"), axis=0, tiled=True),
        lax.all_gather(first_bias, ("head", "blk"), axis=0, tiled=True),
        lax.all_gather(joint_weight, ("head", "blk"), axis=0, tiled=True),
        lax.all_gather(query_bias, ("head", "blk"), axis=0, tiled=True),
        lax.all_gather(value_bias, ("head", "blk"), axis=0, tiled=True),
        lax.all_gather(output_weight, ("head", "blk"), axis=0, tiled=True),
        lax.all_gather(output_bias, ("head", "blk"), axis=0, tiled=True),
        lax.all_gather(second_gain, ("head", "blk"), axis=0, tiled=True),
        lax.all_gather(second_bias, ("head", "blk"), axis=0, tiled=True),
        lax.all_gather(inner_weight, ("head", "blk"), axis=0, tiled=True),
        lax.all_gather(inner_bias, ("head", "blk"), axis=0, tiled=True),
        lax.all_gather(outer_weight, ("head", "blk"), axis=0, tiled=True),
        lax.all_gather(outer_bias, ("head", "blk"), axis=0, tiled=True),
    )
    sequences, piece_rows, width = tokens.shape
    heads_here = H // head_count
    head_width = heads_here * DH
    rows = head_count * piece_rows
    shape_heads = (sequences, rows, heads_here, DH)
    shape_flat = (sequences, rows, head_width)
    own_position = (quarter * block_count + block) * piece_rows + jnp.arange(
        piece_rows, dtype=jnp.int32
    )
    valid = own_position[None, :] < lengths[:, None]
    keep = valid[..., None]
    inputs = tokens.astype(jnp.float32)
    gain_one_wide = gain_one.astype(jnp.float32)
    gain_two_wide = gain_two.astype(jnp.float32)
    first_out, first_unit, first_scale = normalize(
        inputs, gain_one_wide, shift_one.astype(jnp.float32)
    )
    first_low = first_out.astype(jnp.bfloat16)
    joint = jnp.einsum("scd,de->sce", first_low, joint_full, preferred_element_type=jnp.float32)
    query_flat = (joint[..., :width] + query_shift.astype(jnp.float32)).astype(jnp.bfloat16)
    key_flat = joint[..., width : 2 * width].astype(jnp.bfloat16)
    value_flat = (joint[..., 2 * width :] + value_shift.astype(jnp.float32)).astype(jnp.bfloat16)
    query_flat, key_flat, value_flat = (
        lax.all_to_all(query_flat, "head", split_axis=2, concat_axis=1, tiled=True),
        lax.all_to_all(key_flat, "head", split_axis=2, concat_axis=1, tiled=True),
        lax.all_to_all(value_flat, "head", split_axis=2, concat_axis=1, tiled=True),
    )
    query_rows = query_flat.reshape(shape_heads)
    key_rows = key_flat.reshape(shape_heads)
    value_rows = value_flat.reshape(shape_heads)

    def visit(carry):
        keys_block, values_block, source, state = carry
        keys_block, values_block = passed_along((keys_block, values_block), "blk", 1)
        source = (source - 1) % block_count
        mask = key_mask(lengths, source, piece_rows, block_count, head_count)
        return (
            keys_block,
            values_block,
            source,
            attend(query_rows, state, keys_block, values_block, mask),
        )

    start_state = (
        jnp.full((sequences, rows, heads_here), NEG, jnp.float32),
        jnp.zeros((sequences, rows, heads_here), jnp.float32),
        jnp.zeros(shape_heads, jnp.float32),
    )
    first_state = attend(
        query_rows,
        start_state,
        key_rows,
        value_rows,
        key_mask(lengths, block, piece_rows, block_count, head_count),
    )
    carry = (key_rows, value_rows, block, first_state)
    carry = lax.fori_loop(0, block_count // 2 - 1, lambda turn, state: visit(visit(state)), carry)
    best, total, running = visit(carry)[3]
    context = running / total[..., None]
    log_total = best + jnp.log(total)
    context_low = context.astype(jnp.bfloat16).reshape(shape_flat)
    context_tokens = lax.all_to_all(context_low, "head", split_axis=1, concat_axis=2, tiled=True)
    branch = jnp.einsum(
        "sce,ed->scd", context_tokens, output_full, preferred_element_type=jnp.float32
    ) + output_shift.astype(jnp.float32)
    residual = inputs + branch
    second_out, second_unit, second_scale = normalize(
        residual, gain_two_wide, shift_two.astype(jnp.float32)
    )
    second_low = second_out.astype(jnp.bfloat16)
    inner = jnp.einsum(
        "scd,df->scf", second_low, inner_full, preferred_element_type=jnp.float32
    ) + inner_shift.astype(jnp.float32)
    activated = gelu_exact(inner).astype(jnp.bfloat16)
    feed = jnp.einsum(
        "scf,fd->scd", activated, outer_full, preferred_element_type=jnp.float32
    ) + outer_shift.astype(jnp.float32)
    result = residual + feed
    output = jnp.where(keep, result, 0.0).astype(jnp.bfloat16)
    sums = lax.psum(
        (
            jnp.sum(jnp.where(keep, result * result, 0.0)),
            jnp.sum(jnp.where(keep, branch * branch, 0.0)),
            jnp.sum(jnp.where(keep, feed * feed, 0.0)),
        ),
        ("head", "blk"),
    )
    count = jnp.sum(lengths).astype(jnp.float32) * width
    stats = jnp.sqrt(jnp.stack(sums) / count + 1e-06)
    back_result = jnp.where(keep, cotangent.astype(jnp.float32), 0.0)
    back_feed = back_result.astype(jnp.bfloat16)
    outer_gradient = jnp.einsum(
        "scf,scd->fd", activated, back_feed, preferred_element_type=jnp.float32
    )
    outer_shift_gradient = jnp.sum(back_feed.astype(jnp.float32), axis=(0, 1))
    back_active = jnp.einsum(
        "scd,fd->scf", back_feed, outer_full, preferred_element_type=jnp.float32
    )
    back_inner = jax.vjp(gelu_exact, inner)[1](back_active)[0].astype(jnp.bfloat16)
    inner_gradient = jnp.einsum(
        "scd,scf->df", second_low, back_inner, preferred_element_type=jnp.float32
    )
    inner_shift_gradient = jnp.sum(back_inner.astype(jnp.float32), axis=(0, 1))
    back_second = jnp.einsum(
        "scf,df->scd", back_inner, inner_full, preferred_element_type=jnp.float32
    )
    back_norm_two, gain_two_gradient, shift_two_gradient = normalize_back(
        back_second, second_unit, second_scale, gain_two_wide
    )
    back_residual = back_result + back_norm_two
    back_branch = back_residual.astype(jnp.bfloat16)
    output_gradient = jnp.einsum(
        "sce,scd->ed", context_tokens, back_branch, preferred_element_type=jnp.float32
    )
    output_shift_gradient = jnp.sum(back_branch.astype(jnp.float32), axis=(0, 1))
    back_context = jnp.einsum(
        "scd,ed->sce", back_branch, output_full, preferred_element_type=jnp.float32
    ).astype(jnp.bfloat16)
    back_context = lax.all_to_all(back_context, "head", split_axis=2, concat_axis=1, tiled=True)
    back_heads = back_context.reshape(shape_heads)
    spread = jnp.sum(back_heads.astype(jnp.float32) * context, axis=-1)
    zero_heads = jnp.zeros(shape_heads, jnp.float32)

    def pass_keys(carry):
        keys_block, values_block, key_sum, value_sum, query_sum, source = carry
        mask = key_mask(lengths, source, piece_rows, block_count, head_count)
        query_step, key_step, value_step = block_grads(
            query_rows, back_heads, log_total, spread, keys_block, values_block, mask
        )
        keys_block, values_block = passed_along((keys_block, values_block), "blk", 1)
        key_sum, value_sum = passed_along((key_sum + key_step, value_sum + value_step), "blk", 1)
        return (
            keys_block,
            values_block,
            key_sum,
            value_sum,
            query_sum + query_step,
            (source - 1) % block_count,
        )

    carry = (key_rows, value_rows, zero_heads, zero_heads, zero_heads, block)
    carry = lax.fori_loop(
        0, block_count // 2, lambda turn, state: pass_keys(pass_keys(state)), carry
    )
    key_sum, value_sum, query_sum = (carry[2], carry[3], carry[4])
    back_query, back_key, back_value = (
        lax.all_to_all(
            query_sum.astype(jnp.bfloat16).reshape(shape_flat),
            "head",
            split_axis=1,
            concat_axis=2,
            tiled=True,
        ),
        lax.all_to_all(
            key_sum.astype(jnp.bfloat16).reshape(shape_flat),
            "head",
            split_axis=1,
            concat_axis=2,
            tiled=True,
        ),
        lax.all_to_all(
            value_sum.astype(jnp.bfloat16).reshape(shape_flat),
            "head",
            split_axis=1,
            concat_axis=2,
            tiled=True,
        ),
    )
    back_joint = jnp.concatenate([back_query, back_key, back_value], axis=-1)
    joint_gradient = jnp.einsum(
        "scd,sce->de", first_low, back_joint, preferred_element_type=jnp.float32
    )
    query_shift_gradient = jnp.sum(back_query.astype(jnp.float32), axis=(0, 1))
    value_shift_gradient = jnp.sum(back_value.astype(jnp.float32), axis=(0, 1))
    back_first = jnp.einsum(
        "sce,de->scd", back_joint, joint_full, preferred_element_type=jnp.float32
    )
    back_norm_one, gain_one_gradient, shift_one_gradient = normalize_back(
        back_first, first_unit, first_scale, gain_one_wide
    )
    tokens_gradient = (back_residual + back_norm_one).astype(jnp.bfloat16)
    shards = (
        lax.psum_scatter(gain_one_gradient, ("head", "blk"), scatter_dimension=0, tiled=True),
        lax.psum_scatter(shift_one_gradient, ("head", "blk"), scatter_dimension=0, tiled=True),
        lax.psum_scatter(joint_gradient, ("head", "blk"), scatter_dimension=0, tiled=True),
        lax.psum_scatter(query_shift_gradient, ("head", "blk"), scatter_dimension=0, tiled=True),
        lax.psum_scatter(value_shift_gradient, ("head", "blk"), scatter_dimension=0, tiled=True),
        lax.psum_scatter(output_gradient, ("head", "blk"), scatter_dimension=0, tiled=True),
        lax.psum_scatter(output_shift_gradient, ("head", "blk"), scatter_dimension=0, tiled=True),
        lax.psum_scatter(gain_two_gradient, ("head", "blk"), scatter_dimension=0, tiled=True),
        lax.psum_scatter(shift_two_gradient, ("head", "blk"), scatter_dimension=0, tiled=True),
        lax.psum_scatter(inner_gradient, ("head", "blk"), scatter_dimension=0, tiled=True),
        lax.psum_scatter(inner_shift_gradient, ("head", "blk"), scatter_dimension=0, tiled=True),
        lax.psum_scatter(outer_gradient, ("head", "blk"), scatter_dimension=0, tiled=True),
        lax.psum_scatter(outer_shift_gradient, ("head", "blk"), scatter_dimension=0, tiled=True),
    )
    return (
        output,
        tokens_gradient,
        shards[0],
        shards[1],
        shards[2],
        shards[3],
        shards[4],
        shards[5],
        shards[6],
        shards[7],
        shards[8],
        shards[9],
        shards[10],
        shards[11],
        shards[12],
        stats,
    )


MESH = pl.DeviceIdType.MESH
WIDTH = H * DH
GROUP = 3 * DH
NT = (((1,), (1,)), ((), ()))
NN = (((1,), (0,)), ((), ()))


def place():
    head = lax.axis_index("head")
    blk = lax.axis_index("blk")
    return head // 2, lax.rem(head, 2), blk // 2, lax.rem(blk, 2)


def at(y, x, z, c):
    return (y * 2 + x, z * 2 + c)


def number(y, x, z, c):
    return y * 16 + x * 8 + z * 2 + c


def column(t):
    return t // 4, lax.rem(t, 4)


def meet(peers):
    barrier = pltpu.get_barrier_semaphore()
    for peer in peers:
        pl.semaphore_signal(barrier, inc=1, device_id=peer, device_id_type=MESH)
    pl.semaphore_wait(barrier, len(peers))


class Mover:
    def __init__(self, send_sem, local_sem, anyone):
        self.send_sem = send_sem
        self.local_sem = local_sem
        self.anyone = anyone
        self.zero = anyone[0] * 0
        self.sent = []
        self.local = []

    def push(self, source, target, sem, device):
        self.sent.append((source, target, len(self.sent), sem, device))
        self.start(*self.sent[-1])

    def start(self, source, target, spot, sem, device):
        sem = sem[0].at[self.zero + sem[1], sem[2]] if isinstance(sem, tuple) else sem
        remote(source, target, self.send_sem.at[self.zero + spot], sem, device).start()

    def sent_off(self, source, target, spot, sem, device):
        sem = sem[0].at[self.zero + sem[1], sem[2]] if isinstance(sem, tuple) else sem
        remote(source, target, self.send_sem.at[self.zero + spot], sem, device).wait_send()

    def keep(self, source, target):
        parts = (source, target, self.local_sem.at[len(self.local)])
        pltpu.make_async_copy(*parts).start()
        self.local.append(parts)

    def landed(self, target, sem):
        remote(target, target, self.send_sem.at[self.zero], sem, self.anyone).wait_recv()

    def finish(self):
        for parts in self.sent:
            self.sent_off(*parts)
        for parts in self.local:
            pltpu.make_async_copy(*parts).wait()


def remote(source, target, send_sem, recv_sem, device):
    return pltpu.make_async_remote_copy(
        src_ref=source,
        dst_ref=target,
        send_sem=send_sem,
        recv_sem=recv_sem,
        device_id=device,
        device_id_type=MESH,
    )


def unpack(small_all, vectors):
    for block in range(32):
        tile = wide(small_all[block])
        vectors[:, block * 24 : block * 24 + 24] = tile[:8, :24]


def forward_kernel(
    length, tokens, cotangent, wj, wo, wi, wu, small,
    first_low, query, key, value, context, context_rows, cot_own, tok_own, wo_all, wi_all, wu_all, small_all, wj_flat,
    send_sem, local_sem, tok_sem, cot_sem, weight_sem, small_sem, wja_sem, wjb_sem, wjc_sem, ctx_send, ctx_recv,
    ctx_local, tok_all, wj_all, vectors, turned, mixed_low,
):
    y, x, z, c = place()
    mine = number(y, x, z, c)
    quarter = x * 2 + c
    spot = y * 4 + z
    other_core = at(y, x, z, 1 - c)
    across = at(y, 1 - x, z, c)
    diagonal = at(y, 1 - x, z, 1 - c)
    down = at(1 - y, x, z, c)
    y1, x1 = jnp.where(c == 0, y, 1 - y), jnp.where(c == 0, 1 - x, x)
    y2, x2 = jnp.where(c == 0, 1 - y, y), jnp.where(c == 0, x, 1 - x)
    first, second = at(y1, x1, z, c), at(y2, x2, z, c)
    spots = [column(lax.rem(spot + k, 8)) for k in range(1, 8)]
    back_spots = [column(lax.rem(spot + 8 - k, 8)) for k in range(1, 8)]
    lines = [lax.rem(z + 4 - k, 4) for k in range(4)]
    ahead = [at(y, x, lax.rem(z + k, 4), c) for k in range(1, 4)]
    line_blocks = [number(y, x, zz, c) for zz in lines]
    first_blocks = [number(y1, x1, zz, c) for zz in lines]
    second_blocks = [number(yy, xx, zz, c) for yy, xx in ((y2, x2), (1 - y, 1 - x)) for zz in lines]
    core_blocks = [number(yy, xx, zz, 1 - c) for yy in range(2) for xx in range(2) for zz in range(4)]
    group = quad(x, c)
    meet([at(yy, x, zz, c) for yy, zz in spots] + [across, other_core, diagonal])
    move = Mover(send_sem, local_sem, other_core)
    sources = (wo, wi, wu)
    wholes = (wo_all, wi_all, wu_all)

    for yy, zz in spots:
        move.push(tokens.at[yy * 4 + zz], tok_all.at[mine], tok_sem.at[mine], at(yy, x, zz, c))
    for xx, cc in group:
        move.push(wj.at[xx * 2 + cc], wj_all.at[y, x, z, c], wja_sem.at[quarter], at(y, xx, z, cc))
    move.keep(wj.at[quarter], wj_all.at[y, x, z, c])
    move.push(tokens.at[spot], tok_all.at[mine], tok_sem.at[mine], across)
    move.push(tokens.at[spot], tok_all.at[mine], tok_sem.at[mine], other_core)
    move.keep(tokens.at[spot], tok_all.at[mine])
    for device in ahead + [first, second, other_core]:
        move.push(small, small_all.at[mine], small_sem.at[mine], device)
    move.keep(small, small_all.at[mine])

    def hand(block, own, device):
        for i in range(3):
            move.push(
                sources[i] if own else wholes[i].at[block],
                wholes[i].at[block],
                (weight_sem, i, block),
                device,
            )

    def arrive(block):
        for i in range(3):
            move.landed(wholes[i].at[block], weight_sem.at[i, block])

    def pass_small(blocks, devices):
        for block in blocks:
            move.landed(small_all.at[block], small_sem.at[block])
            for device in devices:
                move.push(small_all.at[block], small_all.at[block], small_sem.at[block], device)

    for device in ahead:
        hand(mine, True, device)
    for source, whole in zip(sources, wholes):
        move.keep(source, whole.at[mine])
    hand(mine, True, first)
    hand(mine, True, second)
    hand(mine, True, other_core)

    for xx, cc in group:
        move.landed(wj_all.at[y, xx, z, cc], wja_sem.at[xx * 2 + cc])
    pltpu.make_async_copy(*move.local[0]).wait()
    for device in ahead:
        move.push(wj_all.at[y, :, z], wj_all.at[y, :, z], wjb_sem.at[z], device)
    move.push(wj_all.at[y, :, z], wj_all.at[y, :, z], wjc_sem.at[z], down)
    pass_small(line_blocks[1:], (first, second, other_core))
    for yy, zz in back_spots:
        block = number(yy, x, zz, c)
        move.landed(tok_all.at[block], tok_sem.at[block])
        move.push(tok_all.at[block], tok_all.at[block], tok_sem.at[block], across)
        move.push(tok_all.at[block], tok_all.at[block], tok_sem.at[block], other_core)
    for zz in lines[1:]:
        move.landed(wj_all.at[y, :, zz], wjb_sem.at[zz])
        move.push(wj_all.at[y, :, zz], wj_all.at[y, :, zz], wjc_sem.at[zz], down)
    for yy, zz in spots:
        move.push(cotangent.at[yy * 4 + zz], cot_own.at[spot], cot_sem.at[spot], at(yy, x, zz, c))
    move.keep(cotangent.at[spot], cot_own.at[spot])
    pass_small(first_blocks, (second, other_core))
    pass_small(second_blocks, (other_core,))
    for yy, zz in [(y, z)] + back_spots:
        block = number(yy, 1 - x, zz, c)
        move.landed(tok_all.at[block], tok_sem.at[block])
        move.push(tok_all.at[block], tok_all.at[block], tok_sem.at[block], other_core)
    for block in line_blocks[1:]:
        arrive(block)
        hand(block, False, first)
        hand(block, False, second)
        hand(block, False, other_core)
    for block in core_blocks:
        move.landed(small_all.at[block], small_sem.at[block])
    for zz in lines:
        move.landed(wj_all.at[1 - y, :, zz], wjc_sem.at[zz])
    for yy, zz in [(y, z)] + back_spots:
        for xx in (x, 1 - x):
            block = number(yy, xx, zz, 1 - c)
            move.landed(tok_all.at[block], tok_sem.at[block])
    for parts in move.local[1:3]:
        pltpu.make_async_copy(*parts).wait()

    unpack(small_all, vectors)
    rows = query.shape[1]
    for yy in range(2):
        for xx in range(2):
            for zz in range(4):
                pair = jnp.concatenate([wide(wj_all[yy, xx, zz, cc]) for cc in range(2)], axis=0)
                row = number(yy, xx, zz, 0) * 24
                wj_flat[row : row + 48, :] = pair.astype(jnp.bfloat16)
    lane = lax.broadcasted_iota(jnp.int32, (ROWS, DH), 1)
    row_at = lax.broadcasted_iota(jnp.int32, (ROWS, DH), 0)
    one_lane = jnp.where(lane == 0, 1.0, 0.0).astype(jnp.bfloat16)
    three_lanes = jnp.where(lane < 3, 1.0, 0.0).astype(jnp.bfloat16)
    gain, shift = vectors[0:1, :], vectors[1:2, :]
    query_all, value_all = vectors[2:3, :], vectors[3:4, :]

    def chosen(whole):
        total = jnp.zeros((1, GROUP), jnp.float32)
        for q in range(4):
            total = jnp.where(quarter == q, whole[:, q * GROUP : (q + 1) * GROUP], total)
        return total

    query_shift, value_shift = chosen(query_all), chosen(value_all)
    blocks = ROWS // tokens.shape[1]

    def project(i, _):
        here = pl.ds(i * ROWS, ROWS)
        raw = tok_all[pl.ds(i * blocks, blocks)].reshape(ROWS, WIDTH)
        normed = normalize(wide(raw), gain, shift)[0].astype(jnp.bfloat16)
        first_low[here, :] = normed
        joint = dot(normed, wj_flat[...])
        low_q = ((joint[:, :GROUP] + query_shift).astype(jnp.bfloat16) * DH ** (-0.5)).astype(jnp.bfloat16)
        low_k = joint[:, GROUP : 2 * GROUP].astype(jnp.bfloat16)
        low_v = (joint[:, 2 * GROUP :] + value_shift).astype(jnp.bfloat16)
        mask = jnp.where(row_at + i * ROWS < length[0], 0.0, NEG)
        key_side = jnp.where(lane == 0, mask, jnp.where(lane < 4, 1.0, 0.0)).astype(jnp.bfloat16)
        for h in range(3):
            here_h = slice(h * DH, (h + 1) * DH)
            query[h, here, :] = jnp.concatenate([low_q[:, here_h], one_lane], axis=1)
            key[h, here, :] = jnp.concatenate([low_k[:, here_h], key_side], axis=1)
            value[h, here, :] = jnp.concatenate([low_v[:, here_h], three_lanes], axis=1)
        return 0

    lax.fori_loop(0, rows // ROWS, project, 0)
    eye = jnp.eye(72, 2 * DH, dtype=jnp.bfloat16)
    for h in range(3):
        turned[h] = dot(eye, value[h], NT).astype(jnp.bfloat16)
    side = lax.broadcasted_iota(jnp.int32, (DH, ROWS), 0)

    def ctx_piece(j, cc):
        yy, xx, zz = j // 4, lax.rem(j // 2, 2), pl.ds(lax.rem(j, 2) * 2, 2)
        return mixed_low.at[yy, xx, zz, cc], context_rows.at[quarter, yy, zz]

    def block(j, _):
        here = pl.ds(j * ROWS, ROWS)
        whole = []
        for h in range(3):
            scores = dot(key[h], query[h, here, :], NT)
            best = jnp.max(scores, axis=0, keepdims=True)
            weights = jnp.exp(scores - best).astype(jnp.bfloat16)
            mixed = dot(turned[h], weights)
            total = mixed[DH : DH + 1, :]
            mixed = mixed[:DH, :] / total
            log_total = best + jnp.log(total)
            high = log_total.astype(jnp.bfloat16).astype(jnp.float32)
            middle = (log_total - high).astype(jnp.bfloat16).astype(jnp.float32)
            low = log_total - high - middle
            extra = jnp.where(
                side == 0, 1.0, jnp.where(side == 1, -high, jnp.where(side == 2, -middle, jnp.where(side == 3, -low, 0.0)))
            )
            straight = jnp.concatenate([mixed, extra], axis=0).T
            query[h, here, DH:] = straight[:, DH:].astype(jnp.bfloat16)
            whole.append(straight[:, :DH])
        mixed = jnp.concatenate(whole, axis=1)
        yy, xx, zz = j // 4, lax.rem(j // 2, 2), lax.rem(j, 2) * 2
        low = mixed.astype(jnp.bfloat16)
        context[here, :] = low
        piece = tokens.shape[1]
        for k in range(2):
            for cc in range(2):
                start = (k * 2 + cc) * piece
                mixed_low[yy, xx, zz + k, cc] = low[start : start + piece]
        for cc in range(2):
            source, target = ctx_piece(j, cc)

            @pl.when(jnp.logical_and(xx == x, c == cc))
            def _():
                pltpu.make_async_copy(source, target, ctx_local.at[j]).start()

            @pl.when(jnp.logical_not(jnp.logical_and(xx == x, c == cc)))
            def _():
                remote(source, target, ctx_send.at[j, cc], ctx_recv.at[quarter, j], at(y, xx, z, cc)).start()

        @pl.when(j == 2)
        def _():
            for b in first_blocks:
                arrive(b)
                hand(b, False, second)
                hand(b, False, other_core)

        @pl.when(j == 6)
        def _():
            for b in second_blocks:
                arrive(b)
                hand(b, False, other_core)

        return 0

    lax.fori_loop(0, rows // ROWS, block, 0)
    for yy, zz in back_spots:
        move.landed(cot_own.at[yy * 4 + zz], cot_sem.at[yy * 4 + zz])
    for b in core_blocks:
        arrive(b)
    tok_copies = []
    for i in range(8):
        yy, zz = i // 4, i % 4
        tok_copies.append(pltpu.make_async_copy(tok_all.at[number(yy, x, zz, c)], tok_own.at[i], local_sem.at[8 + i]))
        tok_copies[-1].start()

    def settle(j, _):
        xx = lax.rem(j // 2, 2)
        for cc in range(2):
            source, target = ctx_piece(j, cc)

            @pl.when(jnp.logical_and(xx == x, c == cc))
            def _():
                pltpu.make_async_copy(source, target, ctx_local.at[j]).wait()

            @pl.when(jnp.logical_not(jnp.logical_and(xx == x, c == cc)))
            def _():
                remote(source, target, ctx_send.at[j, cc], ctx_recv.at[quarter, j], at(y, xx, z, cc)).wait_send()

        return 0

    lax.fori_loop(0, rows // ROWS, settle, 0)
    for xx, cc in group:
        for yy in range(2):
            for half in range(2):
                j = yy * 4 + x * 2 + half
                target = context_rows.at[xx * 2 + cc, yy, pl.ds(half * 2, 2)]
                move.landed(target, ctx_recv.at[xx * 2 + cc, j])
    for parts in move.sent:
        move.sent_off(*parts)
    for parts in move.local[3:]:
        pltpu.make_async_copy(*parts).wait()
    for copy in tok_copies:
        copy.wait()


def comm_call(kernel, outs, args, sends, locals_, sems, scratch, ident, space=None):
    space = space or [pltpu.HBM] * len(args)
    return pl.pallas_call(
        kernel,
        out_shape=[jax.ShapeDtypeStruct(shape, dtype) for shape, dtype, _ in outs],
        in_specs=[pl.BlockSpec(memory_space=one) for one in space],
        out_specs=[pl.BlockSpec(memory_space=one) for _, _, one in outs],
        scratch_shapes=[
            pltpu.SemaphoreType.DMA((sends,)),
            pltpu.SemaphoreType.DMA((max(locals_, 1),)),
            *[pltpu.SemaphoreType.DMA(shape) for shape in sems],
            *scratch,
        ],
        compiler_params=pltpu.CompilerParams(
            collective_id=ident, has_side_effects=True, vmem_limit_bytes=61 * 1024 * 1024
        ),
    )(*args)


def quad(x, c):
    return [(lax.rem(x + dx, 2), lax.rem(c + dc, 2)) for dx, dc in ((0, 1), (1, 0), (1, 1))]


def wide(value):
    return value.astype(jnp.float32)


def last_kernel(
    gj, bf, out_j, out_b,
    send_sem, local_sem, sem_y, sem_z, sem_g, sem_c, sem_x,
    ry, rz, sj, rc, rx,
):
    y, x, z, c = place()
    other_core = at(y, x, z, 1 - c)
    across = at(y, 1 - x, z, c)
    down = at(1 - y, x, z, c)
    line = [lax.rem(z + k, 4) for k in range(1, 4)]
    group = quad(x, c)
    meet([at(y, xx, z, cc) for xx, cc in group] + [down] + [at(y, x, zz, c) for zz in line])
    move = Mover(send_sem, local_sem, other_core)
    move.push(gj.at[1 - y], ry, sem_y, down)
    quarters = [(yy, xx) for xx in (1 - x, x) for yy in range(2)]
    for yy, xx in quarters:
        move.push(bf.at[yy, xx, :, 1 - c], rc.at[yy, xx], sem_c.at[yy, xx], other_core)
    for yy, xx in quarters[:2]:
        move.landed(rc.at[yy, xx], sem_c.at[yy, xx])
        rc[yy, xx] = (wide(rc[yy, xx]) + wide(bf[yy, xx, :, c])).astype(rc.dtype)
        move.push(rc.at[yy, xx], rx.at[yy], sem_x.at[yy], across)
    move.landed(ry, sem_y)
    ry[...] = (wide(ry[...]) + wide(gj[y])).astype(ry.dtype)
    for k in range(3):
        move.push(ry.at[:, line[k]], rz.at[k], sem_z.at[k], at(y, x, line[k], c))
    for yy, xx in quarters[2:]:
        move.landed(rc.at[yy, xx], sem_c.at[yy, xx])
    total = wide(ry[:, z])
    for k in range(3):
        move.landed(rz.at[k], sem_z.at[k])
        total = total + wide(rz[k])
    sj[...] = total
    mine = x * 2 + c
    for xx, cc in group:
        move.push(sj.at[xx, cc], out_j.at[mine], sem_g.at[mine], at(y, xx, z, cc))
    move.keep(sj.at[x, c], out_j.at[mine])
    for yy in range(2):
        move.landed(rx.at[yy], sem_x.at[yy])
        out_b[yy] = wide(rc[yy, x]) + wide(bf[yy, x, :, c]) + wide(rx[yy])
    for xx, cc in group:
        move.landed(out_j.at[xx * 2 + cc], sem_g.at[xx * 2 + cc])
    move.finish()


def return_kernel(grads, small, out, small_all, send_sem, local_sem, sem_t, sem_s):
    y, x, z, c = place()
    spot = y * 4 + z
    mine = number(y, x, z, c)
    others = []
    for k in range(1, 32):
        t = lax.rem(mine + k, 32)
        others.append((t, (t // 8, lax.rem(t, 8))))
    meet([device for _, device in others])
    move = Mover(send_sem, local_sem, at(y, x, z, 1 - c))
    for k in range(1, 8):
        yy, zz = column(lax.rem(spot + k, 8))
        move.push(grads.at[yy * 4 + zz], out.at[spot], sem_t.at[spot], at(yy, x, zz, c))
    move.keep(grads.at[spot], out.at[spot])
    for t, device in others:
        move.push(small.at[t], small_all.at[mine], sem_s.at[mine], device)
    move.keep(small.at[mine], small_all.at[mine])
    for k in range(1, 8):
        t = lax.rem(spot + 8 - k, 8)
        move.landed(out.at[t], sem_t.at[t])
    for t, device in others:
        move.landed(small_all.at[t], sem_s.at[t])
    move.finish()


def dot(a, b, dims=NN):
    return lax.dot_general(a, b, dims, preferred_element_type=jnp.float32)


ROWS = 256


TN = (((0,), (0,)), ((), ()))
BACK_ROWS = 512
KEY_ROWS = 1024


def three(value):
    high = value.astype(jnp.bfloat16).astype(jnp.float32)
    middle = (value - high).astype(jnp.bfloat16).astype(jnp.float32)
    return high, middle, value - high - middle


def mean_of(value):
    return jnp.mean(value, axis=-1, keepdims=True)


def backward_kernel(
    length, context_rows, tok_own, cot_own, wo, small_all, wi_far, wu_far, query_far, key_far, value_far, context_far,
    out_o, out_i, out_u, out_s, output, joint, back_residual,
    send_sem, local_sem, sem1, sem2, sem3, sem4, sem_out, sem_back,
    r1u, r1i, r1o, r1s, r2u, r2i, r2o, r2s, r3u, r3i, r3o, r3s, r4u, r4i, r4o, r4s,
    gu, gi, go, gs, shared, context, back_near, back_context, vectors, inner_shift,
    active, back_inner, output_low, sums, turned,
):
    bf16, f32 = jnp.bfloat16, jnp.float32
    y, x, z, c = place()
    spot = y * 4 + z
    mine = x * 2 + c
    other_core = at(y, x, z, 1 - c)
    across = at(y, 1 - x, z, c)
    diagonal = at(y, 1 - x, z, 1 - c)
    y1, x1 = jnp.where(c == 0, y, 1 - y), jnp.where(c == 0, 1 - x, x)
    y2, x2 = jnp.where(c == 0, 1 - y, y), jnp.where(c == 0, x, 1 - x)
    first, second = at(y1, x1, z, c), at(y2, x2, z, c)
    spots = [column(lax.rem(spot + k, 8)) for k in range(1, 8)]
    line = [lax.rem(z + k, 4) for k in range(1, 4)]
    own, near1, near2 = y * 2 + x, y1 * 2 + x1, y2 * 2 + x2
    far = (1 - y) * 2 + 1 - x
    order = (far, near1, near2, own)
    group = quad(x, c)
    meet([at(yy, x, zz, c) for yy, zz in spots] + [across, other_core, diagonal])
    move = Mover(send_sem, local_sem, other_core)
    width = wo.shape[0]
    ff = wi_far.shape[1]
    lanes_here = shared.shape[1]
    tiles = ff // lanes_here
    for t in range(tiles):
        move.keep(wi_far.at[:, t * lanes_here : (t + 1) * lanes_here], shared.at[pl.ds(t * width, width)])
    move.keep(wu_far, gu)
    move.keep(context_far, context)

    def fetched(n):
        pltpu.make_async_copy(*move.local[n]).wait()

    piece = tok_own.shape[1]
    rows = tok_own.shape[0] * piece
    steps = ff // width
    per_step = width // lanes_here

    def wi_columns(step):
        return jnp.concatenate(
            [
                shared[pl.ds(pl.multiple_of((step * per_step + k) * width, width), width), :]
                for k in range(per_step)
            ],
            axis=1,
        )

    unpack(small_all, vectors)
    ff_piece = ff // 32
    for block in range(32):
        inner_shift[:, block * ff_piece : (block + 1) * ff_piece] = wide(small_all[block])[8:9, :ff_piece]

    spot_at = lax.broadcasted_iota(jnp.int32, (8, piece, 1), 0)
    position = number(spot_at // 4, x, lax.rem(spot_at, 4), c) * piece
    position = position + lax.broadcasted_iota(jnp.int32, (8, piece, 1), 1)
    keep = jnp.where(position < length[0], 1.0, 0.0).reshape(rows, 1) > 0.5

    def column_sum(item):
        return jnp.sum(item, axis=0, keepdims=True)

    def square(item):
        return jnp.sum(item * item)

    branch = vectors[4:5, :] + dot(context_rows[0].reshape(rows, GROUP), wo[:GROUP, :])
    for g in range(1, 4):
        branch = branch + dot(context_rows[g].reshape(rows, GROUP), wo[g * GROUP : (g + 1) * GROUP, :])
    residual = wide(tok_own[...].reshape(rows, width)) + branch
    branch_total = square(jnp.where(keep, branch, 0.0))
    average = mean_of(residual)
    centered = residual - average
    inverse = lax.rsqrt(mean_of(centered * centered) + EPS)
    unit = centered * inverse
    second_low = (unit * vectors[5:6, :] + vectors[6:7, :]).astype(bf16)
    back_result = jnp.where(keep, wide(cot_own[...].reshape(rows, width)), 0.0)
    back_feed = back_result.astype(bf16)
    for n in range(tiles + 1):
        fetched(n)

    def middle(step, sums_here):
        back_second, feed = sums_here
        cols = pl.ds(pl.multiple_of(step * width, width), width)
        wi_here = wi_columns(step)
        inner = dot(second_low, wi_here) + inner_shift[:, cols]
        chance = 0.5 * (1.0 + lax.erf(inner * 0.7071067811865476))
        low = (inner * chance).astype(bf16)
        active[:, cols] = low
        wu_here = gu[step].reshape(width, width)
        slope = chance + inner * jnp.exp(inner * inner * -0.5) * 0.3989422804014327
        back = (dot(back_feed, wu_here, NT) * slope).astype(bf16)
        back_inner[:, cols] = back
        return back_second + dot(back, wi_here, NT), feed + dot(low, wu_here)

    zero = jnp.zeros((rows, width), f32)
    back_second, feed = lax.fori_loop(0, steps, middle, (zero, zero))
    heads_rows = query_far.shape[1]
    for kind, source in enumerate((query_far, key_far, value_far)):
        for h in range(3):
            move.keep(source.at[h], shared.at[pl.ds((kind * 3 + h) * heads_rows, heads_rows)])
    scaled = back_second * vectors[5:6, :]
    back_res = back_result + inverse * (scaled - mean_of(scaled) - unit * mean_of(scaled * unit))
    back_residual[...] = back_res
    back_branch = back_res.astype(bf16)
    short = jnp.concatenate(
        [
            column_sum(wide(back_feed)), column_sum(back_second * unit), column_sum(back_second),
            column_sum(wide(back_branch)), jnp.zeros((4, width), f32),
        ],
        axis=0,
    )
    for g in range(4):
        back_near[g] = dot(back_branch, wo[g * GROUP : (g + 1) * GROUP, :], NT).astype(bf16).reshape(8, piece, GROUP)
    for xx, cc in group[::-1]:
        for yy in range(2):
            move.push(
                back_near.at[xx * 2 + cc, pl.ds(yy * 4, 4)],
                back_context.at[yy, x, :, c],
                sem_back.at[mine, yy],
                at(y, xx, z, cc),
            )
    for yy in range(2):
        move.keep(back_near.at[mine, pl.ds(yy * 4, 4)], back_context.at[yy, x, :, c])

    feed = feed + vectors[7:8, :]
    result = jnp.where(keep, residual + feed, 0.0)
    output_low[...] = result.astype(bf16).reshape(8, piece, width)
    for yy, zz in spots:
        move.push(output_low.at[yy * 4 + zz], output.at[spot], sem_out.at[spot], at(yy, x, zz, c))
    move.keep(output_low.at[spot], output.at[spot])

    totals = (square(result), branch_total, square(jnp.where(keep, feed, 0.0)))
    lane = lax.broadcasted_iota(jnp.int32, (1, 128), 1)
    stat_row = jnp.where(lane == 0, totals[0], jnp.where(lane == 1, totals[1], jnp.where(lane == 2, totals[2], 0.0)))
    parts = (gu, gi, go, gs)
    results = (out_u, out_i, out_o, out_s)
    r1, r2 = (r1u, r1i, r1o, r1s), (r2u, r2i, r2o, r2s)
    r3, r4 = (r3u, r3i, r3o, r3s), (r4u, r4i, r4o, r4s)

    def to_core(i, quarter):
        move.push(parts[i].at[quarter, :, 1 - c], r1[i].at[quarter], sem1.at[i, quarter], other_core)

    lead = width // 32
    wide_piece = ff // 32
    for step in range(steps):
        grad = dot(active[:, step * width : (step + 1) * width], back_feed, TN).astype(bf16)
        for zz in range(4):
            for cc in range(2):
                row = (zz * 2 + cc) * wide_piece
                gu[step, zz, cc] = grad[row : row + wide_piece, :]
        to_core(0, step)
    for step in range(steps):
        grad = dot(second_low, back_inner[:, step * width : (step + 1) * width], TN)
        for block in range(32):
            gi[block // 8, block % 8 // 2, block % 2, :, step * width : (step + 1) * width] = grad[
                block * lead : (block + 1) * lead, :
            ].astype(bf16)
    for quarter in order:
        to_core(1, quarter)
    for g in range(4):
        grad = dot(context_rows[g].reshape(rows, GROUP), back_branch, TN)
        for zz in range(4):
            for cc in range(2):
                row = (zz * 2 + cc) * lead
                go[g, zz, cc] = grad[row : row + lead, :].astype(bf16)
        to_core(2, g)

    long = column_sum(wide(back_inner[...]))
    for block in range(32):
        at_block = (block // 8, block % 8 // 2, block % 2)
        gs[at_block] = jnp.zeros((8, 128), f32)
        gs[at_block + (slice(0, 8), slice(0, lead))] = short[:, block * lead : (block + 1) * lead]
        gs[at_block + (slice(4, 5), slice(0, wide_piece))] = long[:, block * wide_piece : (block + 1) * wide_piece]
        gs[at_block + (slice(5, 6), slice(None))] = stat_row
    for quarter in order:
        to_core(3, quarter)

    def gather(i, quarter):
        move.landed(r1[i].at[quarter], sem1.at[i, quarter])
        r1[i][quarter] = (wide(r1[i][quarter]) + wide(parts[i][quarter, :, c])).astype(r1[i].dtype)

    def stage2(i):
        for slot, quarter in ((1, far), (0, near1)):
            gather(i, quarter)
            move.push(r1[i].at[quarter], r2[i].at[slot], sem2.at[i, slot], first)

    def stage3(i):
        gather(i, near2)
        move.landed(r2[i].at[1], sem2.at[i, 1])
        r1[i][near2] = (wide(r1[i][near2]) + wide(r2[i][1])).astype(r1[i].dtype)
        move.push(r1[i].at[near2], r3[i], sem3.at[i], second)

    def stage4(i):
        gather(i, own)
        move.landed(r2[i].at[0], sem2.at[i, 0])
        move.landed(r3[i], sem3.at[i])
        r1[i][own] = (wide(r1[i][own]) + wide(r2[i][0]) + wide(r3[i][...])).astype(r1[i].dtype)
        for k in range(3):
            move.push(r1[i].at[own, line[k]], r4[i].at[k], sem4.at[i, k], at(y, x, line[k], c))

    def stage5(i):
        total = wide(r1[i][own, z])
        for k in range(3):
            move.landed(r4[i].at[k], sem4.at[i, k])
            total = total + wide(r4[i][k])
        results[i][...] = total

    for i in range(4):
        stage2(i)
    for xx, cc in group:
        for yy in range(2):
            move.landed(back_context.at[yy, xx, :, cc], sem_back.at[xx * 2 + cc, yy])
    for n in range(tiles + 1, tiles + 13):
        fetched(n)

    rows_all = heads_rows
    scale = DH ** (-0.5)
    eye = jnp.eye(DH, 2 * DH, dtype=bf16)
    side_lane = lax.broadcasted_iota(jnp.int32, (BACK_ROWS, DH), 1)
    blocks = BACK_ROWS // piece // 8
    between = {0: [lambda: stage3(0)], 1: [lambda: stage4(0), lambda: stage3(1)], 2: []}
    for h in range(3):
        for k in range(rows_all // KEY_ROWS):
            start = (3 + h) * rows_all + k * KEY_ROWS
            turned[k] = dot(eye, shared[start : start + KEY_ROWS, :], NT).astype(bf16)
        sums[...] = jnp.zeros_like(sums)
        lanes = slice(h * DH, (h + 1) * DH)

        def block(i, _):
            here = pl.ds(i * BACK_ROWS, BACK_ROWS)
            queries = shared[pl.ds(h * rows_all + i * BACK_ROWS, BACK_ROWS), :]
            yy, xx = i // 2, lax.rem(i, 2)
            backs = back_context[yy, xx].reshape(BACK_ROWS, GROUP)[:, lanes]
            spread = jnp.sum(wide(backs) * wide(context[here, lanes]), axis=1, keepdims=True)
            high, mid, low = three(spread)
            side = jnp.where(
                side_lane == 0, -high, jnp.where(side_lane == 1, -mid, jnp.where(side_lane == 2, -low, 0.0))
            )
            widened = jnp.concatenate([backs, side.astype(bf16)], axis=1)

            def part(k, back_query):
                keys = pl.ds(k * KEY_ROWS, KEY_ROWS)
                key = shared[pl.ds((3 + h) * rows_all + k * KEY_ROWS, KEY_ROWS), :]
                value = shared[pl.ds((6 + h) * rows_all + k * KEY_ROWS, KEY_ROWS), :]
                chances = jnp.exp(dot(key, queries, NT))
                back_scores = (chances * dot(value, widened, NT)).astype(bf16)
                sums[keys, :DH] += dot(back_scores, queries[:, :DH])
                sums[keys, DH:] += dot(chances.astype(bf16), backs)
                return back_query + dot(turned[k], back_scores)

            back_query = jnp.zeros((DH, BACK_ROWS), f32)
            back_query = lax.fori_loop(0, rows_all // KEY_ROWS, part, back_query)
            joint[here, lanes] = (back_query * scale).T.astype(bf16)
            return 0

        lax.fori_loop(0, rows_all // BACK_ROWS, block, 0)
        joint[:, GROUP + h * DH : GROUP + (h + 1) * DH] = sums[:, :DH].astype(bf16)
        joint[:, 2 * GROUP + h * DH : 2 * GROUP + (h + 1) * DH] = sums[:, DH:].astype(bf16)
        for action in between[h]:
            action()
    for action in (
        lambda: stage4(1), lambda: stage3(2), lambda: stage3(3), lambda: stage4(2), lambda: stage4(3),
        lambda: stage5(0), lambda: stage5(1), lambda: stage5(2), lambda: stage5(3),
    ):
        action()
    for k in range(1, 8):
        t = lax.rem(spot + 8 - k, 8)
        move.landed(output.at[t], sem_out.at[t])
    for parts_sent in move.sent:
        move.sent_off(*parts_sent)
    fetched(tiles + 13)


def local_call(kernel, outs, args, scratch=(), smem=1):
    return pl.pallas_call(
        kernel,
        out_shape=[jax.ShapeDtypeStruct(shape, dtype) for shape, dtype in outs],
        in_specs=[pl.BlockSpec(memory_space=pltpu.SMEM)] * smem
        + [pl.BlockSpec(memory_space=pltpu.VMEM)] * (len(args) - smem),
        out_specs=[pl.BlockSpec(memory_space=pltpu.VMEM)] * len(outs),
        scratch_shapes=list(scratch),
        compiler_params=pltpu.CompilerParams(vmem_limit_bytes=56 * 1024 * 1024),
    )(*args)


def packed(vectors, blocks, dtype, tile):
    rows = [jnp.pad(v.reshape(blocks, 1, -1), ((0, 0), (0, 0), (0, 128 - v.size // blocks))) for v in vectors]
    whole = jnp.concatenate(rows, axis=1).astype(dtype)
    return jnp.pad(whole, ((0, 0), (0, tile - whole.shape[1]), (0, 0)))


def owner_device(
    tokens,
    lengths,
    first_gain,
    first_bias,
    joint_weight,
    query_bias,
    value_bias,
    output_weight,
    output_bias,
    second_gain,
    second_bias,
    inner_weight,
    inner_bias,
    outer_weight,
    outer_bias,
    cotangent,
):
    bf16, f32 = jnp.bfloat16, jnp.float32
    y, x, z, c = place()
    mine = x * 2 + c
    slots, piece, width = tokens.shape
    ff = inner_weight.shape[1]
    short = jnp.stack(
        [first_gain, first_bias, query_bias, value_bias, output_bias, second_gain, second_bias, outer_bias]
    )
    lead = short.shape[1]
    ff_piece = inner_bias.shape[0]
    small = jnp.concatenate(
        [
            jnp.pad(short, ((0, 0), (0, ff_piece - lead))),
            jnp.broadcast_to(inner_bias, (8, ff_piece)),
        ],
        axis=0,
    )
    hbm, vmem = pltpu.HBM, pltpu.VMEM
    dma, regular = pltpu.SemaphoreType.DMA, pltpu.SemaphoreType.REGULAR
    rows_all = 32 * piece
    natural = (2, 2, 4, 2, piece)
    length = lax.dynamic_slice(lengths, (y * 4 + z,), (1,))
    joint_four = jnp.transpose(joint_weight.reshape(lead, 3, 4, GROUP), (2, 0, 1, 3)).reshape(4, lead, 3 * GROUP)
    forward_outs = [
        ((rows_all, width), bf16, vmem),
        ((3, rows_all, 2 * DH), bf16, vmem),
        ((3, rows_all, 2 * DH), bf16, vmem),
        ((3, rows_all, 2 * DH), bf16, vmem),
        ((rows_all, GROUP), bf16, vmem),
        ((4, 2, 4, piece, GROUP), bf16, vmem),
        ((8, piece, width), bf16, hbm),
        ((8, piece, width), bf16, hbm),
        ((32,) + output_weight.shape, bf16, hbm),
        ((32,) + inner_weight.shape, bf16, hbm),
        ((32,) + outer_weight.shape, bf16, hbm),
        ((32,) + small.shape, bf16, vmem),
        ((width, 3 * GROUP), bf16, vmem),
    ]
    (
        first_low, query, key, value, context, context_rows, cot_own, tok_own, wo_all, wi_all, wu_all, small_all, joint_here
    ) = comm_call(
        forward_kernel,
        forward_outs,
        (length, tokens, cotangent, joint_four, output_weight, inner_weight, outer_weight, small),
        220, 16,
        [(32,), (8,), (3, 32), (32,), (4,), (4,), (4,), (8, 2), (4, 8), (8,)],
        [
            vmem((32, piece, width), bf16),
            vmem((2, 2, 4, 2, lead, 3 * GROUP), bf16),
            vmem((8, width), f32),
            vmem((3, 72, rows_all), bf16),
            vmem(natural + (GROUP,), bf16),
        ],
        0,
        [pltpu.SMEM, hbm, hbm, hbm, hbm, hbm, hbm, hbm],
    )
    vectors = jnp.transpose(small_all[:, :2, :lead], (1, 0, 2)).reshape(2, width).astype(f32)
    gain_one, shift_one = vectors[0:1], vectors[1:2]
    rows = 8 * piece
    turn = (((0,), (0,)), ((), ()))
    grid = (4, 4, 2)
    kinds = [
        (outer_weight.shape, bf16),
        (inner_weight.shape, bf16),
        (output_weight.shape, bf16),
        ((8, 128), f32),
    ]
    out_o, out_i, out_u, out_s, output, back_joint, back_residual = comm_call(
        backward_kernel,
        [
            (output_weight.shape, f32, vmem),
            (inner_weight.shape, f32, vmem),
            (outer_weight.shape, f32, vmem),
            ((8, 128), f32, vmem),
            (tokens.shape, bf16, hbm),
            ((rows_all, 3 * GROUP), bf16, vmem),
            ((rows, width), f32, vmem),
        ],
        (
            length, context_rows.reshape(4, 8, piece, GROUP), tok_own, cot_own, wo_all.reshape(width, width), small_all,
            wi_all.reshape(width, ff), wu_all.reshape(grid + outer_weight.shape), query, key, value, context,
        ),
        80, 48, [(4, 4), (4, 2), (4,), (4, 3), (8,), (4, 2)],
        [vmem((4, 4) + shape, dtype) for shape, dtype in kinds]
        + [vmem((2, 4) + shape, dtype) for shape, dtype in kinds]
        + [vmem((4,) + shape, dtype) for shape, dtype in kinds]
        + [vmem((3,) + shape, dtype) for shape, dtype in kinds]
        + [vmem(grid + shape, dtype) for shape, dtype in kinds]
        + [
            vmem((width * ff // 128, 128), bf16),
            vmem(context.shape, bf16),
            vmem((4, 8, piece, GROUP), bf16),
            vmem(natural + (GROUP,), bf16),
            vmem((8, width), f32),
            vmem((1, ff), f32),
            vmem((rows, ff), bf16),
            vmem((rows, ff), bf16),
            vmem((8, piece, width), bf16),
            vmem((rows_all, 2 * DH), f32),
            vmem((rows_all // KEY_ROWS, DH, KEY_ROWS), bf16),
        ],
        1,
        [pltpu.SMEM] + [vmem] * 5 + [hbm] * 6,
    )
    inputs = tok_own.reshape(rows, width).astype(f32)
    joint_gradient = dot(first_low, back_joint, turn).astype(bf16)
    back_first_part = dot(back_joint, joint_here, NT).astype(bf16)
    joint_parts, back_first = comm_call(
        last_kernel,
        [((4, lead, 3 * GROUP), f32, vmem), ((2, 4, piece, width), f32, vmem)],
        (joint_gradient.reshape(2, 2, 4, 2, lead, 3 * GROUP), back_first_part.reshape(natural + (width,))),
        13, 1, [(), (3,), (4,), (2, 2), (2,)],
        [
            vmem((2, 4, 2, lead, 3 * GROUP), bf16),
            vmem((3, 2, 2, lead, 3 * GROUP), bf16),
            vmem((2, 2, lead, 3 * GROUP), f32),
            vmem((2, 2, 4, piece, width), bf16),
            vmem((2, 4, piece, width), bf16),
        ],
        4,
        [vmem] * 2,
    )
    joint_shard = jnp.transpose(joint_parts.reshape(4, lead, 3, GROUP), (1, 2, 0, 3)).reshape(lead, 3 * width)
    _, first_unit, first_scale = normalize(inputs, gain_one, shift_one)
    back_norm_one, gain_one_gradient, shift_one_gradient = normalize_back(
        back_first.reshape(1, rows, width), first_unit[None], first_scale[None], gain_one
    )
    grads_here = (back_residual + back_norm_one[0]).astype(bf16)
    shifts = jnp.sum(back_joint.astype(f32), axis=0)
    zero = jnp.zeros((width,), f32)
    query_shift_gradient = lax.dynamic_update_slice(zero, shifts[:GROUP], (mine * GROUP,))
    value_shift_gradient = lax.dynamic_update_slice(zero, shifts[2 * GROUP :], (mine * GROUP,))
    small_two = packed(
        [gain_one_gradient, shift_one_gradient, query_shift_gradient, value_shift_gradient], 32, f32, 8
    )
    tokens_gradient, small_back = comm_call(
        return_kernel,
        [(tokens.shape, bf16, hbm), ((32, 8, 128), f32, hbm)],
        (grads_here.reshape(8, piece, width), small_two),
        38, 2, [(8,), (32,)], [], 5,
    )
    late = jnp.sum(small_back, axis=0)
    count = jnp.sum(lengths).astype(f32) * width
    stats = jnp.sqrt(out_s[5, :3] / count + 1e-06)
    return (
        output,
        tokens_gradient,
        late[0, :lead],
        late[1, :lead],
        joint_shard,
        late[2, :lead],
        late[3, :lead],
        out_o,
        out_s[3, :lead],
        out_s[1, :lead],
        out_s[2, :lead],
        out_i,
        out_s[4, : inner_bias.shape[0]],
        out_u,
        out_s[0, :lead],
        stats,
    )


def solution(mesh):
    in_specs = (
        P(None, ("head", "blk"), None),
        P(),
        P(("head", "blk")),
        P(("head", "blk")),
        P(("head", "blk"), None),
        P(("head", "blk")),
        P(("head", "blk")),
        P(("head", "blk"), None),
        P(("head", "blk")),
        P(("head", "blk")),
        P(("head", "blk")),
        P(("head", "blk"), None),
        P(("head", "blk")),
        P(("head", "blk"), None),
        P(("head", "blk")),
        P(None, ("head", "blk"), None),
    )
    out_specs = (
        P(None, ("head", "blk"), None),
        P(None, ("head", "blk"), None),
        P(("head", "blk")),
        P(("head", "blk")),
        P(("head", "blk"), None),
        P(("head", "blk")),
        P(("head", "blk")),
        P(("head", "blk"), None),
        P(("head", "blk")),
        P(("head", "blk")),
        P(("head", "blk")),
        P(("head", "blk"), None),
        P(("head", "blk")),
        P(("head", "blk"), None),
        P(("head", "blk")),
        P(),
    )
    small_slice = dict(mesh.shape) == {"head": 4, "blk": 8}
    device_work = owner_device if small_slice else on_device
    return jax.shard_map(
        device_work, mesh=mesh, in_specs=in_specs, out_specs=out_specs, check_vma=False
    )
```

```python
import jax
import jax.numpy as jnp
from jax import lax
from jax.experimental import pallas as pl
from jax.experimental.pallas import tpu as pltpu
from jax.sharding import PartitionSpec as P

H = 12
DH = 64


EPS = 1e-12
NEG = -1e30


def passed_along(value, axis, steps):
    count = lax.axis_size(axis)
    pairs = [(source, (source + steps) % count) for source in range(count)]
    return lax.ppermute(value, axis, pairs)


def normalize(values, gain, shift):
    average = jnp.mean(values, axis=-1, keepdims=True)
    centered = values - average
    inverse = lax.rsqrt(jnp.mean(centered * centered, axis=-1, keepdims=True) + EPS)
    normed = centered * inverse
    return (normed * gain + shift, normed, inverse)


def normalize_back(incoming, normed, inverse, gain):
    scaled = incoming * gain
    inner = (
        scaled
        - jnp.mean(scaled, axis=-1, keepdims=True)
        - normed * jnp.mean(scaled * normed, axis=-1, keepdims=True)
    )
    return (
        inner * inverse,
        jnp.sum(incoming * normed, axis=(0, 1)),
        jnp.sum(incoming, axis=(0, 1)),
    )


def gelu_exact(values):
    return jax.nn.gelu(values, approximate=False)


def key_mask(lengths, source, piece_rows, block_count, head_count):
    rows_here = jnp.arange(head_count * piece_rows, dtype=jnp.int32)
    position = (
        rows_here // piece_rows * block_count + source
    ) * piece_rows + rows_here % piece_rows
    return position[None, :] < lengths[:, None]


def attend(query_part, state, keys_block, values_block, mask):
    best, total, running = state
    scores = jnp.einsum(
        "sqhd,skhd->sqhk", query_part, keys_block, preferred_element_type=jnp.float32
    ) * DH ** (-0.5)
    scores = jnp.where(mask[:, None, None, :], scores, NEG)
    fresh = jnp.maximum(best, jnp.max(scores, axis=-1))
    decay = jnp.exp(best - fresh)
    weights = jnp.exp(scores - fresh[..., None])
    total = total * decay + jnp.sum(weights, axis=-1)
    running = running * decay[..., None] + jnp.einsum(
        "sqhk,skhd->sqhd",
        weights.astype(jnp.bfloat16),
        values_block,
        preferred_element_type=jnp.float32,
    )
    return (fresh, total, running)


def block_grads(query_part, back_part, total_part, spread_part, keys_block, values_block, mask):
    scale = DH ** (-0.5)
    scores = (
        jnp.einsum("sqhd,skhd->sqhk", query_part, keys_block, preferred_element_type=jnp.float32)
        * scale
    )
    scores = jnp.where(mask[:, None, None, :], scores, NEG)
    chances = jnp.exp(scores - total_part[..., None])
    back_chances = jnp.einsum(
        "sqhd,skhd->sqhk", back_part, values_block, preferred_element_type=jnp.float32
    )
    back_scores = (chances * (back_chances - spread_part[..., None])).astype(jnp.bfloat16)
    query_step = (
        jnp.einsum("sqhk,skhd->sqhd", back_scores, keys_block, preferred_element_type=jnp.float32)
        * scale
    )
    key_step = (
        jnp.einsum("sqhk,sqhd->skhd", back_scores, query_part, preferred_element_type=jnp.float32)
        * scale
    )
    value_step = jnp.einsum(
        "sqhk,sqhd->skhd",
        chances.astype(jnp.bfloat16),
        back_part,
        preferred_element_type=jnp.float32,
    )
    return (query_step, key_step, value_step)


def on_device(
    tokens,
    lengths,
    first_gain,
    first_bias,
    joint_weight,
    query_bias,
    value_bias,
    output_weight,
    output_bias,
    second_gain,
    second_bias,
    inner_weight,
    inner_bias,
    outer_weight,
    outer_bias,
    cotangent,
):
    head_count = lax.axis_size("head")
    block_count = lax.axis_size("blk")
    block = lax.axis_index("blk")
    quarter = lax.axis_index("head")
    (
        gain_one,
        shift_one,
        joint_full,
        query_shift,
        value_shift,
        output_full,
        output_shift,
        gain_two,
        shift_two,
        inner_full,
        inner_shift,
        outer_full,
        outer_shift,
    ) = (
        lax.all_gather(first_gain, ("head", "blk"), axis=0, tiled=True),
        lax.all_gather(first_bias, ("head", "blk"), axis=0, tiled=True),
        lax.all_gather(joint_weight, ("head", "blk"), axis=0, tiled=True),
        lax.all_gather(query_bias, ("head", "blk"), axis=0, tiled=True),
        lax.all_gather(value_bias, ("head", "blk"), axis=0, tiled=True),
        lax.all_gather(output_weight, ("head", "blk"), axis=0, tiled=True),
        lax.all_gather(output_bias, ("head", "blk"), axis=0, tiled=True),
        lax.all_gather(second_gain, ("head", "blk"), axis=0, tiled=True),
        lax.all_gather(second_bias, ("head", "blk"), axis=0, tiled=True),
        lax.all_gather(inner_weight, ("head", "blk"), axis=0, tiled=True),
        lax.all_gather(inner_bias, ("head", "blk"), axis=0, tiled=True),
        lax.all_gather(outer_weight, ("head", "blk"), axis=0, tiled=True),
        lax.all_gather(outer_bias, ("head", "blk"), axis=0, tiled=True),
    )
    sequences, piece_rows, width = tokens.shape
    heads_here = H // head_count
    head_width = heads_here * DH
    rows = head_count * piece_rows
    shape_heads = (sequences, rows, heads_here, DH)
    shape_flat = (sequences, rows, head_width)
    own_position = (quarter * block_count + block) * piece_rows + jnp.arange(
        piece_rows, dtype=jnp.int32
    )
    valid = own_position[None, :] < lengths[:, None]
    keep = valid[..., None]
    inputs = tokens.astype(jnp.float32)
    gain_one_wide = gain_one.astype(jnp.float32)
    gain_two_wide = gain_two.astype(jnp.float32)
    first_out, first_unit, first_scale = normalize(
        inputs, gain_one_wide, shift_one.astype(jnp.float32)
    )
    first_low = first_out.astype(jnp.bfloat16)
    joint = jnp.einsum("scd,de->sce", first_low, joint_full, preferred_element_type=jnp.float32)
    query_flat = (joint[..., :width] + query_shift.astype(jnp.float32)).astype(jnp.bfloat16)
    key_flat = joint[..., width : 2 * width].astype(jnp.bfloat16)
    value_flat = (joint[..., 2 * width :] + value_shift.astype(jnp.float32)).astype(jnp.bfloat16)
    query_flat, key_flat, value_flat = (
        lax.all_to_all(query_flat, "head", split_axis=2, concat_axis=1, tiled=True),
        lax.all_to_all(key_flat, "head", split_axis=2, concat_axis=1, tiled=True),
        lax.all_to_all(value_flat, "head", split_axis=2, concat_axis=1, tiled=True),
    )
    query_rows = query_flat.reshape(shape_heads)
    key_rows = key_flat.reshape(shape_heads)
    value_rows = value_flat.reshape(shape_heads)

    def visit(carry):
        keys_block, values_block, source, state = carry
        keys_block, values_block = passed_along((keys_block, values_block), "blk", 1)
        source = (source - 1) % block_count
        mask = key_mask(lengths, source, piece_rows, block_count, head_count)
        return (
            keys_block,
            values_block,
            source,
            attend(query_rows, state, keys_block, values_block, mask),
        )

    start_state = (
        jnp.full((sequences, rows, heads_here), NEG, jnp.float32),
        jnp.zeros((sequences, rows, heads_here), jnp.float32),
        jnp.zeros(shape_heads, jnp.float32),
    )
    first_state = attend(
        query_rows,
        start_state,
        key_rows,
        value_rows,
        key_mask(lengths, block, piece_rows, block_count, head_count),
    )
    carry = (key_rows, value_rows, block, first_state)
    carry = lax.fori_loop(0, block_count // 2 - 1, lambda turn, state: visit(visit(state)), carry)
    best, total, running = visit(carry)[3]
    context = running / total[..., None]
    log_total = best + jnp.log(total)
    context_low = context.astype(jnp.bfloat16).reshape(shape_flat)
    context_tokens = lax.all_to_all(context_low, "head", split_axis=1, concat_axis=2, tiled=True)
    branch = jnp.einsum(
        "sce,ed->scd", context_tokens, output_full, preferred_element_type=jnp.float32
    ) + output_shift.astype(jnp.float32)
    residual = inputs + branch
    second_out, second_unit, second_scale = normalize(
        residual, gain_two_wide, shift_two.astype(jnp.float32)
    )
    second_low = second_out.astype(jnp.bfloat16)
    inner = jnp.einsum(
        "scd,df->scf", second_low, inner_full, preferred_element_type=jnp.float32
    ) + inner_shift.astype(jnp.float32)
    activated = gelu_exact(inner).astype(jnp.bfloat16)
    feed = jnp.einsum(
        "scf,fd->scd", activated, outer_full, preferred_element_type=jnp.float32
    ) + outer_shift.astype(jnp.float32)
    result = residual + feed
    output = jnp.where(keep, result, 0.0).astype(jnp.bfloat16)
    sums = lax.psum(
        (
            jnp.sum(jnp.where(keep, result * result, 0.0)),
            jnp.sum(jnp.where(keep, branch * branch, 0.0)),
            jnp.sum(jnp.where(keep, feed * feed, 0.0)),
        ),
        ("head", "blk"),
    )
    count = jnp.sum(lengths).astype(jnp.float32) * width
    stats = jnp.sqrt(jnp.stack(sums) / count + 1e-06)
    back_result = jnp.where(keep, cotangent.astype(jnp.float32), 0.0)
    back_feed = back_result.astype(jnp.bfloat16)
    outer_gradient = jnp.einsum(
        "scf,scd->fd", activated, back_feed, preferred_element_type=jnp.float32
    )
    outer_shift_gradient = jnp.sum(back_feed.astype(jnp.float32), axis=(0, 1))
    back_active = jnp.einsum(
        "scd,fd->scf", back_feed, outer_full, preferred_element_type=jnp.float32
    )
    back_inner = jax.vjp(gelu_exact, inner)[1](back_active)[0].astype(jnp.bfloat16)
    inner_gradient = jnp.einsum(
        "scd,scf->df", second_low, back_inner, preferred_element_type=jnp.float32
    )
    inner_shift_gradient = jnp.sum(back_inner.astype(jnp.float32), axis=(0, 1))
    back_second = jnp.einsum(
        "scf,df->scd", back_inner, inner_full, preferred_element_type=jnp.float32
    )
    back_norm_two, gain_two_gradient, shift_two_gradient = normalize_back(
        back_second, second_unit, second_scale, gain_two_wide
    )
    back_residual = back_result + back_norm_two
    back_branch = back_residual.astype(jnp.bfloat16)
    output_gradient = jnp.einsum(
        "sce,scd->ed", context_tokens, back_branch, preferred_element_type=jnp.float32
    )
    output_shift_gradient = jnp.sum(back_branch.astype(jnp.float32), axis=(0, 1))
    back_context = jnp.einsum(
        "scd,ed->sce", back_branch, output_full, preferred_element_type=jnp.float32
    ).astype(jnp.bfloat16)
    back_context = lax.all_to_all(back_context, "head", split_axis=2, concat_axis=1, tiled=True)
    back_heads = back_context.reshape(shape_heads)
    spread = jnp.sum(back_heads.astype(jnp.float32) * context, axis=-1)
    zero_heads = jnp.zeros(shape_heads, jnp.float32)

    def pass_keys(carry):
        keys_block, values_block, key_sum, value_sum, query_sum, source = carry
        mask = key_mask(lengths, source, piece_rows, block_count, head_count)
        query_step, key_step, value_step = block_grads(
            query_rows, back_heads, log_total, spread, keys_block, values_block, mask
        )
        keys_block, values_block = passed_along((keys_block, values_block), "blk", 1)
        key_sum, value_sum = passed_along((key_sum + key_step, value_sum + value_step), "blk", 1)
        return (
            keys_block,
            values_block,
            key_sum,
            value_sum,
            query_sum + query_step,
            (source - 1) % block_count,
        )

    carry = (key_rows, value_rows, zero_heads, zero_heads, zero_heads, block)
    carry = lax.fori_loop(
        0, block_count // 2, lambda turn, state: pass_keys(pass_keys(state)), carry
    )
    key_sum, value_sum, query_sum = (carry[2], carry[3], carry[4])
    back_query, back_key, back_value = (
        lax.all_to_all(
            query_sum.astype(jnp.bfloat16).reshape(shape_flat),
            "head",
            split_axis=1,
            concat_axis=2,
            tiled=True,
        ),
        lax.all_to_all(
            key_sum.astype(jnp.bfloat16).reshape(shape_flat),
            "head",
            split_axis=1,
            concat_axis=2,
            tiled=True,
        ),
        lax.all_to_all(
            value_sum.astype(jnp.bfloat16).reshape(shape_flat),
            "head",
            split_axis=1,
            concat_axis=2,
            tiled=True,
        ),
    )
    back_joint = jnp.concatenate([back_query, back_key, back_value], axis=-1)
    joint_gradient = jnp.einsum(
        "scd,sce->de", first_low, back_joint, preferred_element_type=jnp.float32
    )
    query_shift_gradient = jnp.sum(back_query.astype(jnp.float32), axis=(0, 1))
    value_shift_gradient = jnp.sum(back_value.astype(jnp.float32), axis=(0, 1))
    back_first = jnp.einsum(
        "sce,de->scd", back_joint, joint_full, preferred_element_type=jnp.float32
    )
    back_norm_one, gain_one_gradient, shift_one_gradient = normalize_back(
        back_first, first_unit, first_scale, gain_one_wide
    )
    tokens_gradient = (back_residual + back_norm_one).astype(jnp.bfloat16)
    shards = (
        lax.psum_scatter(gain_one_gradient, ("head", "blk"), scatter_dimension=0, tiled=True),
        lax.psum_scatter(shift_one_gradient, ("head", "blk"), scatter_dimension=0, tiled=True),
        lax.psum_scatter(joint_gradient, ("head", "blk"), scatter_dimension=0, tiled=True),
        lax.psum_scatter(query_shift_gradient, ("head", "blk"), scatter_dimension=0, tiled=True),
        lax.psum_scatter(value_shift_gradient, ("head", "blk"), scatter_dimension=0, tiled=True),
        lax.psum_scatter(output_gradient, ("head", "blk"), scatter_dimension=0, tiled=True),
        lax.psum_scatter(output_shift_gradient, ("head", "blk"), scatter_dimension=0, tiled=True),
        lax.psum_scatter(gain_two_gradient, ("head", "blk"), scatter_dimension=0, tiled=True),
        lax.psum_scatter(shift_two_gradient, ("head", "blk"), scatter_dimension=0, tiled=True),
        lax.psum_scatter(inner_gradient, ("head", "blk"), scatter_dimension=0, tiled=True),
        lax.psum_scatter(inner_shift_gradient, ("head", "blk"), scatter_dimension=0, tiled=True),
        lax.psum_scatter(outer_gradient, ("head", "blk"), scatter_dimension=0, tiled=True),
        lax.psum_scatter(outer_shift_gradient, ("head", "blk"), scatter_dimension=0, tiled=True),
    )
    return (
        output,
        tokens_gradient,
        shards[0],
        shards[1],
        shards[2],
        shards[3],
        shards[4],
        shards[5],
        shards[6],
        shards[7],
        shards[8],
        shards[9],
        shards[10],
        shards[11],
        shards[12],
        stats,
    )


MESH = pl.DeviceIdType.MESH
WIDTH = H * DH
GROUP = 3 * DH
NT = (((1,), (1,)), ((), ()))
NN = (((1,), (0,)), ((), ()))


def place():
    head = lax.axis_index("head")
    blk = lax.axis_index("blk")
    return head // 2, lax.rem(head, 2), blk // 2, lax.rem(blk, 2)


def at(y, x, z, c):
    return (y * 2 + x, z * 2 + c)


def number(y, x, z, c):
    return y * 16 + x * 8 + z * 2 + c


def column(t):
    return t // 4, lax.rem(t, 4)


def meet(peers):
    barrier = pltpu.get_barrier_semaphore()
    for peer in peers:
        pl.semaphore_signal(barrier, inc=1, device_id=peer, device_id_type=MESH)
    pl.semaphore_wait(barrier, len(peers))


class Mover:
    def __init__(self, send_sem, local_sem, anyone):
        self.send_sem = send_sem
        self.local_sem = local_sem
        self.anyone = anyone
        self.zero = anyone[0] * 0
        self.sent = []
        self.local = []

    def push(self, source, target, sem, device):
        self.push_made(lambda: (source, target, sem), device)

    def push_made(self, make, device):
        spot = len(self.sent)
        self.sent.append((make, spot, device))
        self.copy(make, spot, device).start()

    def copy(self, make, spot, device):
        source, target, sem = make()
        return remote(source, target, self.send_sem.at[self.zero + spot], sem, device)

    def keep(self, source, target):
        parts = (source, target, self.local_sem.at[len(self.local)])
        pltpu.make_async_copy(*parts).start()
        self.local.append(parts)
        return len(self.local) - 1

    def kept(self, spot):
        pltpu.make_async_copy(*self.local[spot]).wait()

    def landed(self, target, sem):
        remote(target, target, self.send_sem.at[self.zero], sem, self.anyone).wait_recv()

    def finish(self, kept=()):
        for parts in self.sent:
            self.copy(*parts).wait_send()
        for spot in kept:
            self.kept(spot)


def remote(source, target, send_sem, recv_sem, device):
    return pltpu.make_async_remote_copy(
        src_ref=source,
        dst_ref=target,
        send_sem=send_sem,
        recv_sem=recv_sem,
        device_id=device,
        device_id_type=MESH,
    )


def unpack(small_all, vectors):
    for block in range(32):
        tile = wide(small_all[block])
        vectors[:, block * 24 : block * 24 + 24] = tile[:8, :24]


def forward_kernel(
    length, tokens, cotangent, wj, wo, wi, wu, small,
    first_low, query, key, value, context, context_rows, cot_own, tok_own, wo_all, wi_all, wu_all, small_all, wj_flat,
    send_sem, local_sem, tok_sem, cot_sem, weight_sem, small_sem, wja_sem, wjb_sem, wjc_sem, ctx_send, ctx_recv,
    ctx_local, tok_all, wj_all, vectors, turned, mixed_low,
):
    y, x, z, c = place()
    mine = number(y, x, z, c)
    quarter = x * 2 + c
    spot = y * 4 + z
    other_core = at(y, x, z, 1 - c)
    across = at(y, 1 - x, z, c)
    diagonal = at(y, 1 - x, z, 1 - c)
    down = at(1 - y, x, z, c)
    y1, x1 = jnp.where(c == 0, y, 1 - y), jnp.where(c == 0, 1 - x, x)
    y2, x2 = jnp.where(c == 0, 1 - y, y), jnp.where(c == 0, x, 1 - x)
    first, second = at(y1, x1, z, c), at(y2, x2, z, c)
    spots = [column(lax.rem(spot + k, 8)) for k in range(1, 8)]
    back_spots = [column(lax.rem(spot + 8 - k, 8)) for k in range(1, 8)]
    lines = [lax.rem(z + 4 - k, 4) for k in range(4)]
    ahead = [at(y, x, lax.rem(z + k, 4), c) for k in range(1, 4)]
    line_blocks = [number(y, x, zz, c) for zz in lines]
    first_blocks = [number(y1, x1, zz, c) for zz in lines]
    second_blocks = [number(yy, xx, zz, c) for yy, xx in ((y2, x2), (1 - y, 1 - x)) for zz in lines]
    core_blocks = [number(yy, xx, zz, 1 - c) for yy in range(2) for xx in range(2) for zz in range(4)]
    group = quad(x, c)
    meet([at(yy, x, zz, c) for yy, zz in spots] + [across, other_core, diagonal])
    move = Mover(send_sem, local_sem, other_core)
    sources = (wo, wi, wu)
    wholes = (wo_all, wi_all, wu_all)

    for yy, zz in spots:
        move.push(tokens.at[yy * 4 + zz], tok_all.at[mine], tok_sem.at[mine], at(yy, x, zz, c))
    for xx, cc in group:
        move.push(wj.at[xx * 2 + cc], wj_all.at[y, x, z, c], wja_sem.at[quarter], at(y, xx, z, cc))
    move.keep(wj.at[quarter], wj_all.at[y, x, z, c])
    move.push(tokens.at[spot], tok_all.at[mine], tok_sem.at[mine], across)
    move.push(tokens.at[spot], tok_all.at[mine], tok_sem.at[mine], other_core)
    move.keep(tokens.at[spot], tok_all.at[mine])
    for device in ahead + [first, second, other_core]:
        move.push(small, small_all.at[mine], small_sem.at[mine], device)
    move.keep(small, small_all.at[mine])

    def hand(block, own, device):
        for i in range(3):
            move.push_made(
                lambda i=i: (
                    sources[i] if own else wholes[i].at[block],
                    wholes[i].at[block],
                    weight_sem.at[move.zero + i, block],
                ),
                device,
            )

    def arrive(block):
        for i in range(3):
            move.landed(wholes[i].at[block], weight_sem.at[i, block])

    def pass_small(blocks, devices):
        for block in blocks:
            move.landed(small_all.at[block], small_sem.at[block])
            for device in devices:
                move.push(small_all.at[block], small_all.at[block], small_sem.at[block], device)

    for device in ahead:
        hand(mine, True, device)
    for source, whole in zip(sources, wholes):
        move.keep(source, whole.at[mine])
    hand(mine, True, first)
    hand(mine, True, second)
    hand(mine, True, other_core)

    for xx, cc in group:
        move.landed(wj_all.at[y, xx, z, cc], wja_sem.at[xx * 2 + cc])
    move.kept(0)
    for device in ahead:
        move.push(wj_all.at[y, :, z], wj_all.at[y, :, z], wjb_sem.at[z], device)
    move.push(wj_all.at[y, :, z], wj_all.at[y, :, z], wjc_sem.at[z], down)
    pass_small(line_blocks[1:], (first, second, other_core))
    for yy, zz in back_spots:
        block = number(yy, x, zz, c)
        move.landed(tok_all.at[block], tok_sem.at[block])
        move.push(tok_all.at[block], tok_all.at[block], tok_sem.at[block], across)
        move.push(tok_all.at[block], tok_all.at[block], tok_sem.at[block], other_core)
    for zz in lines[1:]:
        move.landed(wj_all.at[y, :, zz], wjb_sem.at[zz])
        move.push(wj_all.at[y, :, zz], wj_all.at[y, :, zz], wjc_sem.at[zz], down)
    for yy, zz in spots:
        move.push(cotangent.at[yy * 4 + zz], cot_own.at[spot], cot_sem.at[spot], at(yy, x, zz, c))
    move.keep(cotangent.at[spot], cot_own.at[spot])
    pass_small(first_blocks, (second, other_core))
    pass_small(second_blocks, (other_core,))
    for yy, zz in [(y, z)] + back_spots:
        block = number(yy, 1 - x, zz, c)
        move.landed(tok_all.at[block], tok_sem.at[block])
        move.push(tok_all.at[block], tok_all.at[block], tok_sem.at[block], other_core)
    for block in line_blocks[1:]:
        arrive(block)
        hand(block, False, first)
        hand(block, False, second)
        hand(block, False, other_core)
    for block in core_blocks:
        move.landed(small_all.at[block], small_sem.at[block])
    for zz in lines:
        move.landed(wj_all.at[1 - y, :, zz], wjc_sem.at[zz])
    for yy, zz in [(y, z)] + back_spots:
        for xx in (x, 1 - x):
            block = number(yy, xx, zz, 1 - c)
            move.landed(tok_all.at[block], tok_sem.at[block])
    move.kept(1)
    move.kept(2)

    unpack(small_all, vectors)
    rows = query.shape[1]
    for yy in range(2):
        for xx in range(2):
            for zz in range(4):
                pair = jnp.concatenate([wide(wj_all[yy, xx, zz, cc]) for cc in range(2)], axis=0)
                row = number(yy, xx, zz, 0) * 24
                wj_flat[row : row + 48, :] = pair.astype(jnp.bfloat16)
    lane = lax.broadcasted_iota(jnp.int32, (ROWS, DH), 1)
    row_at = lax.broadcasted_iota(jnp.int32, (ROWS, DH), 0)
    one_lane = jnp.where(lane == 0, 1.0, 0.0).astype(jnp.bfloat16)
    three_lanes = jnp.where(lane < 3, 1.0, 0.0).astype(jnp.bfloat16)
    gain, shift = vectors[0:1, :], vectors[1:2, :]
    query_all, value_all = vectors[2:3, :], vectors[3:4, :]

    def chosen(whole):
        total = jnp.zeros((1, GROUP), jnp.float32)
        for q in range(4):
            total = jnp.where(quarter == q, whole[:, q * GROUP : (q + 1) * GROUP], total)
        return total

    query_shift, value_shift = chosen(query_all), chosen(value_all)
    blocks = ROWS // tokens.shape[1]

    def project(i, _):
        here = pl.ds(i * ROWS, ROWS)
        raw = tok_all[pl.ds(i * blocks, blocks)].reshape(ROWS, WIDTH)
        normed = normalize(wide(raw), gain, shift)[0].astype(jnp.bfloat16)
        first_low[here, :] = normed
        joint = dot(normed, wj_flat[...])
        low_q = ((joint[:, :GROUP] + query_shift).astype(jnp.bfloat16) * DH ** (-0.5)).astype(jnp.bfloat16)
        low_k = joint[:, GROUP : 2 * GROUP].astype(jnp.bfloat16)
        low_v = (joint[:, 2 * GROUP :] + value_shift).astype(jnp.bfloat16)
        mask = jnp.where(row_at + i * ROWS < length[0], 0.0, NEG)
        key_side = jnp.where(lane == 0, mask, jnp.where(lane < 4, 1.0, 0.0)).astype(jnp.bfloat16)
        for h in range(3):
            here_h = slice(h * DH, (h + 1) * DH)
            query[h, here, :] = jnp.concatenate([low_q[:, here_h], one_lane], axis=1)
            key[h, here, :] = jnp.concatenate([low_k[:, here_h], key_side], axis=1)
            value[h, here, :] = jnp.concatenate([low_v[:, here_h], three_lanes], axis=1)
        return 0

    lax.fori_loop(0, rows // ROWS, project, 0)
    eye = jnp.eye(72, 2 * DH, dtype=jnp.bfloat16)
    for h in range(3):
        turned[h] = dot(eye, value[h], NT).astype(jnp.bfloat16)
    side = lax.broadcasted_iota(jnp.int32, (DH, ROWS), 0)

    def ctx_piece(j, cc):
        yy, xx, zz = j // 4, lax.rem(j // 2, 2), pl.ds(lax.rem(j, 2) * 2, 2)
        return mixed_low.at[yy, xx, zz, cc], context_rows.at[quarter, yy, zz]

    def block(j, _):
        here = pl.ds(j * ROWS, ROWS)
        whole = []
        for h in range(3):
            scores = dot(key[h], query[h, here, :], NT)
            best = jnp.max(scores, axis=0, keepdims=True)
            weights = jnp.exp(scores - best).astype(jnp.bfloat16)
            mixed = dot(turned[h], weights)
            total = mixed[DH : DH + 1, :]
            mixed = mixed[:DH, :] / total
            log_total = best + jnp.log(total)
            high = log_total.astype(jnp.bfloat16).astype(jnp.float32)
            middle = (log_total - high).astype(jnp.bfloat16).astype(jnp.float32)
            low = log_total - high - middle
            extra = jnp.where(
                side == 0, 1.0, jnp.where(side == 1, -high, jnp.where(side == 2, -middle, jnp.where(side == 3, -low, 0.0)))
            )
            straight = jnp.concatenate([mixed, extra], axis=0).T
            query[h, here, DH:] = straight[:, DH:].astype(jnp.bfloat16)
            whole.append(straight[:, :DH])
        mixed = jnp.concatenate(whole, axis=1)
        yy, xx, zz = j // 4, lax.rem(j // 2, 2), lax.rem(j, 2) * 2
        low = mixed.astype(jnp.bfloat16)
        context[here, :] = low
        piece = tokens.shape[1]
        for k in range(2):
            for cc in range(2):
                start = (k * 2 + cc) * piece
                mixed_low[yy, xx, zz + k, cc] = low[start : start + piece]
        for cc in range(2):
            source, target = ctx_piece(j, cc)

            @pl.when(jnp.logical_and(xx == x, c == cc))
            def _():
                pltpu.make_async_copy(source, target, ctx_local.at[j]).start()

            @pl.when(jnp.logical_not(jnp.logical_and(xx == x, c == cc)))
            def _():
                remote(source, target, ctx_send.at[j, cc], ctx_recv.at[quarter, j], at(y, xx, z, cc)).start()

        @pl.when(j == 2)
        def _():
            for b in first_blocks:
                arrive(b)
                hand(b, False, second)
                hand(b, False, other_core)

        @pl.when(j == 6)
        def _():
            for b in second_blocks:
                arrive(b)
                hand(b, False, other_core)

        return 0

    lax.fori_loop(0, rows // ROWS, block, 0)
    for yy, zz in back_spots:
        move.landed(cot_own.at[yy * 4 + zz], cot_sem.at[yy * 4 + zz])
    for b in core_blocks:
        arrive(b)
    tok_copies = []
    for i in range(8):
        yy, zz = i // 4, i % 4
        tok_copies.append(pltpu.make_async_copy(tok_all.at[number(yy, x, zz, c)], tok_own.at[i], local_sem.at[8 + i]))
        tok_copies[-1].start()

    def settle(j, _):
        xx = lax.rem(j // 2, 2)
        for cc in range(2):
            source, target = ctx_piece(j, cc)

            @pl.when(jnp.logical_and(xx == x, c == cc))
            def _():
                pltpu.make_async_copy(source, target, ctx_local.at[j]).wait()

            @pl.when(jnp.logical_not(jnp.logical_and(xx == x, c == cc)))
            def _():
                remote(source, target, ctx_send.at[j, cc], ctx_recv.at[quarter, j], at(y, xx, z, cc)).wait_send()

        return 0

    lax.fori_loop(0, rows // ROWS, settle, 0)
    for xx, cc in group:
        for yy in range(2):
            for half in range(2):
                j = yy * 4 + x * 2 + half
                target = context_rows.at[xx * 2 + cc, yy, pl.ds(half * 2, 2)]
                move.landed(target, ctx_recv.at[xx * 2 + cc, j])
    move.finish(range(3, len(move.local)))
    for copy in tok_copies:
        copy.wait()


def comm_call(kernel, outs, args, sends, locals_, sems, scratch, ident, space=None):
    space = space or [pltpu.HBM] * len(args)
    return pl.pallas_call(
        kernel,
        out_shape=[jax.ShapeDtypeStruct(shape, dtype) for shape, dtype, _ in outs],
        in_specs=[pl.BlockSpec(memory_space=one) for one in space],
        out_specs=[pl.BlockSpec(memory_space=one) for _, _, one in outs],
        scratch_shapes=[
            pltpu.SemaphoreType.DMA((sends,)),
            pltpu.SemaphoreType.DMA((max(locals_, 1),)),
            *[pltpu.SemaphoreType.DMA(shape) for shape in sems],
            *scratch,
        ],
        compiler_params=pltpu.CompilerParams(
            collective_id=ident, has_side_effects=True, vmem_limit_bytes=61 * 1024 * 1024
        ),
    )(*args)


def quad(x, c):
    return [(lax.rem(x + dx, 2), lax.rem(c + dc, 2)) for dx, dc in ((0, 1), (1, 0), (1, 1))]


def wide(value):
    return value.astype(jnp.float32)


def dot(a, b, dims=NN):
    return lax.dot_general(a, b, dims, preferred_element_type=jnp.float32)


ROWS = 256


TN = (((0,), (0,)), ((), ()))
BACK_ROWS = 512
KEY_ROWS = 1024


def three(value):
    high = value.astype(jnp.bfloat16).astype(jnp.float32)
    middle = (value - high).astype(jnp.bfloat16).astype(jnp.float32)
    return high, middle, value - high - middle


def mean_of(value):
    return jnp.mean(value, axis=-1, keepdims=True)


TN = (((0,), (0,)), ((), ()))
BACK_ROWS = 512
KEY_ROWS = 1024


def three(value):
    high = value.astype(jnp.bfloat16).astype(jnp.float32)
    middle = (value - high).astype(jnp.bfloat16).astype(jnp.float32)
    return high, middle, value - high - middle


def mean_of(value):
    return jnp.mean(value, axis=-1, keepdims=True)


def feed_kernel(
    length, context_rows, tok_own, cot_own, wo, small_all, wi_far, wu_far,
    gu_far, gi_far, go_far, gs_far, output, back_context, back_residual,
    send_sem, local_sem, sem_out, sem_back,
    gu, gi, go, gs, wi, back_near, vectors, inner_shift, active, back_inner, output_low,
):
    bf16, f32 = jnp.bfloat16, jnp.float32
    y, x, z, c = place()
    spot = y * 4 + z
    mine = x * 2 + c
    other_core = at(y, x, z, 1 - c)
    across = at(y, 1 - x, z, c)
    diagonal = at(y, 1 - x, z, 1 - c)
    spots = [column(lax.rem(spot + k, 8)) for k in range(1, 8)]
    group = quad(x, c)
    meet([at(yy, x, zz, c) for yy, zz in spots] + [across, other_core, diagonal])
    move = Mover(send_sem, local_sem, other_core)
    width = wo.shape[0]
    ff = wi.shape[1]
    move.keep(wi_far, wi)
    move.keep(wu_far, gu)

    piece = tok_own.shape[1]
    rows = tok_own.shape[0] * piece
    steps = ff // width
    unpack(small_all, vectors)
    ff_piece = ff // 32
    for block in range(32):
        inner_shift[:, block * ff_piece : (block + 1) * ff_piece] = wide(small_all[block])[8:9, :ff_piece]

    spot_at = lax.broadcasted_iota(jnp.int32, (8, piece, 1), 0)
    position = number(spot_at // 4, x, lax.rem(spot_at, 4), c) * piece
    position = position + lax.broadcasted_iota(jnp.int32, (8, piece, 1), 1)
    keep = jnp.where(position < length[0], 1.0, 0.0).reshape(rows, 1) > 0.5

    def column_sum(item):
        return jnp.sum(item, axis=0, keepdims=True)

    def square(item):
        return jnp.sum(item * item)

    branch = vectors[4:5, :] + dot(context_rows[0].reshape(rows, GROUP), wo[:GROUP, :])
    for g in range(1, 4):
        branch = branch + dot(context_rows[g].reshape(rows, GROUP), wo[g * GROUP : (g + 1) * GROUP, :])
    residual = wide(tok_own[...].reshape(rows, width)) + branch
    branch_total = square(jnp.where(keep, branch, 0.0))
    average = mean_of(residual)
    centered = residual - average
    inverse = lax.rsqrt(mean_of(centered * centered) + EPS)
    unit = centered * inverse
    second_low = (unit * vectors[5:6, :] + vectors[6:7, :]).astype(bf16)
    back_result = jnp.where(keep, wide(cot_own[...].reshape(rows, width)), 0.0)
    back_feed = back_result.astype(bf16)
    move.kept(0)
    move.kept(1)

    def middle(step, sums_here):
        back_second, feed = sums_here
        cols = pl.ds(pl.multiple_of(step * width, width), width)
        wi_here = wi[:, cols]
        inner = dot(second_low, wi_here) + inner_shift[:, cols]
        chance = 0.5 * (1.0 + lax.erf(inner * 0.7071067811865476))
        low = (inner * chance).astype(bf16)
        active[:, cols] = low
        wu_here = gu[step].reshape(width, width)
        slope = chance + inner * jnp.exp(inner * inner * -0.5) * 0.3989422804014327
        back = (dot(back_feed, wu_here, NT) * slope).astype(bf16)
        back_inner[:, cols] = back
        return back_second + dot(back, wi_here, NT), feed + dot(low, wu_here)

    zero = jnp.zeros((rows, width), f32)
    back_second, feed = lax.fori_loop(0, steps, middle, (zero, zero))
    scaled = back_second * vectors[5:6, :]
    back_res = back_result + inverse * (scaled - mean_of(scaled) - unit * mean_of(scaled * unit))
    back_residual[...] = back_res
    back_branch = back_res.astype(bf16)
    short = jnp.concatenate(
        [
            column_sum(wide(back_feed)), column_sum(back_second * unit), column_sum(back_second),
            column_sum(wide(back_branch)), jnp.zeros((4, width), f32),
        ],
        axis=0,
    )
    for g in range(4):
        back_near[g] = dot(back_branch, wo[g * GROUP : (g + 1) * GROUP, :], NT).astype(bf16).reshape(8, piece, GROUP)
    for xx, cc in group[::-1]:
        for yy in range(2):
            move.push(
                back_near.at[xx * 2 + cc, pl.ds(yy * 4, 4)],
                back_context.at[yy, x, :, c],
                sem_back.at[mine, yy],
                at(y, xx, z, cc),
            )
    for yy in range(2):
        move.keep(back_near.at[mine, pl.ds(yy * 4, 4)], back_context.at[yy, x, :, c])

    feed = feed + vectors[7:8, :]
    result = jnp.where(keep, residual + feed, 0.0)
    output_low[...] = result.astype(bf16).reshape(8, piece, width)
    for yy, zz in spots:
        move.push(output_low.at[yy * 4 + zz], output.at[spot], sem_out.at[spot], at(yy, x, zz, c))
    move.keep(output_low.at[spot], output.at[spot])

    totals = (square(result), branch_total, square(jnp.where(keep, feed, 0.0)))
    lane = lax.broadcasted_iota(jnp.int32, (1, 128), 1)
    stat_row = jnp.where(lane == 0, totals[0], jnp.where(lane == 1, totals[1], jnp.where(lane == 2, totals[2], 0.0)))
    lead = width // 32
    wide_piece = ff // 32
    for step in range(steps):
        grad = dot(active[:, step * width : (step + 1) * width], back_feed, TN).astype(bf16)
        for zz in range(4):
            for cc in range(2):
                row = (zz * 2 + cc) * wide_piece
                gu[step, zz, cc] = grad[row : row + wide_piece, :]
        move.keep(gu.at[step], gu_far.at[step])
    for step in range(steps):
        grad = dot(second_low, back_inner[:, step * width : (step + 1) * width], TN)
        for block in range(32):
            gi[block // 8, block % 8 // 2, block % 2, :, step * width : (step + 1) * width] = grad[
                block * lead : (block + 1) * lead, :
            ].astype(bf16)
    move.keep(gi, gi_far)
    for g in range(4):
        grad = dot(context_rows[g].reshape(rows, GROUP), back_branch, TN)
        for zz in range(4):
            for cc in range(2):
                row = (zz * 2 + cc) * lead
                go[g, zz, cc] = grad[row : row + lead, :].astype(bf16)
        move.keep(go.at[g], go_far.at[g])

    long = column_sum(wide(back_inner[...]))
    for block in range(32):
        at_block = (block // 8, block % 8 // 2, block % 2)
        gs[at_block] = jnp.zeros((8, 128), f32)
        gs[at_block + (slice(0, 8), slice(0, lead))] = short[:, block * lead : (block + 1) * lead]
        gs[at_block + (slice(4, 5), slice(0, wide_piece))] = long[:, block * wide_piece : (block + 1) * wide_piece]
        gs[at_block + (slice(5, 6), slice(None))] = stat_row
    move.keep(gs, gs_far)
    for xx, cc in group:
        for yy in range(2):
            move.landed(back_context.at[yy, xx, :, cc], sem_back.at[xx * 2 + cc, yy])
    for k in range(1, 8):
        t = lax.rem(spot + 8 - k, 8)
        move.landed(output.at[t], sem_out.at[t])
    move.finish(range(2, len(move.local)))


def backward_kernel(
    gu, gi, go, gs, query, key, value, context, back_context, joint_weight, first_far, tok_own, back_residual, vectors,
    out_o, out_i, out_u, out_s, out_joint, tokens_gradient, late,
    send_sem, local_sem, sem1, sem2, sem3, sem4, sem_y, sem_z, sem_g, sem_c, sem_x, sem_t, sem_s,
    r1u, r1i, r1o, r1s, r2u, r2i, r2o, r2s, r3u, r3i, r3o, r3s, r4u, r4i, r4o, r4s, ou, oi, oo, os_,
    joint, sums, turned, first_low, back_first, rc, rx, gj, ry, rz, sj, joint_land, gradient_low, small, small_all,
):
    bf16, f32 = jnp.bfloat16, jnp.float32
    y, x, z, c = place()
    spot = y * 4 + z
    mine = x * 2 + c
    me = number(y, x, z, c)
    other_core = at(y, x, z, 1 - c)
    across = at(y, 1 - x, z, c)
    down = at(1 - y, x, z, c)
    y1, x1 = jnp.where(c == 0, y, 1 - y), jnp.where(c == 0, 1 - x, x)
    y2, x2 = jnp.where(c == 0, 1 - y, y), jnp.where(c == 0, x, 1 - x)
    first, second = at(y1, x1, z, c), at(y2, x2, z, c)
    line = [lax.rem(z + k, 4) for k in range(1, 4)]
    line_devices = [at(y, x, zz, c) for zz in line]
    own, near1, near2 = y * 2 + x, y1 * 2 + x1, y2 * 2 + x2
    far = (1 - y) * 2 + 1 - x
    order = (far, near1, near2, own)
    group = quad(x, c)
    others = []
    for k in range(1, 32):
        t = lax.rem(me + k, 32)
        others.append((t, (t // 8, lax.rem(t, 8))))
    meet([device for _, device in others])
    move = Mover(send_sem, local_sem, other_core)
    zero = move.zero
    parts = (gu, gi, go, gs)
    halves = (ou, oi, oo, os_)
    results = (out_u, out_i, out_o, out_s)
    r1, r2 = (r1u, r1i, r1o, r1s), (r2u, r2i, r2o, r2s)
    r3, r4 = (r3u, r3i, r3o, r3s), (r4u, r4i, r4o, r4s)
    for i in (0, 2, 3, 1):
        for quarter in order:
            move.push(
                parts[i].at[quarter, :, 1 - c], r1[i].at[quarter], sem1.at[i, quarter], other_core
            )
    for i in range(4):
        move.keep(parts[i].at[:, :, c], halves[i])
    move.keep(first_far, first_low)

    def gather(i, quarter):
        move.landed(r1[i].at[quarter], sem1.at[zero + i, quarter])
        r1[i][quarter] = (wide(r1[i][quarter]) + wide(halves[i][quarter])).astype(r1[i].dtype)

    def stage2(i):
        for slot, quarter in ((1, far), (0, near1)):
            gather(i, quarter)
            move.push_made(
                lambda slot=slot, quarter=quarter: (
                    r1[i].at[quarter], r2[i].at[zero + slot], sem2.at[zero + i, zero + slot]
                ),
                first,
            )

    def stage3(i):
        gather(i, near2)
        move.landed(r2[i].at[zero + 1], sem2.at[zero + i, zero + 1])
        r1[i][near2] = (wide(r1[i][near2]) + wide(r2[i][1])).astype(r1[i].dtype)
        move.push_made(lambda: (r1[i].at[near2], r3[i], sem3.at[zero + i]), second)

    def stage4(i):
        gather(i, own)
        move.landed(r2[i].at[zero], sem2.at[zero + i, zero])
        move.landed(r3[i], sem3.at[zero + i])
        r1[i][own] = (wide(r1[i][own]) + wide(r2[i][0]) + wide(r3[i][...])).astype(r1[i].dtype)
        for k in range(3):
            move.push_made(
                lambda k=k: (r1[i].at[own, line[k]], r4[i].at[zero + k], sem4.at[zero + i, zero + k]),
                line_devices[k],
            )

    def stage5(i):
        total = wide(r1[i][own, z])
        for k in range(3):
            move.landed(r4[i].at[k], sem4.at[i, k])
            total = total + wide(r4[i][k])
        results[i][...] = total

    rows_all = query.shape[1]
    piece = tok_own.shape[1]
    rows = tok_own.shape[0] * piece
    width = tok_own.shape[2]
    scale = DH ** (-0.5)
    eye = jnp.eye(DH, 2 * DH, dtype=bf16)
    side_lane = lax.broadcasted_iota(jnp.int32, (BACK_ROWS, DH), 1)
    per_head = rows_all // BACK_ROWS
    between = {
        1: lambda: stage2(0),
        2: lambda: (stage2(2), stage2(3)),
        3: lambda: stage2(1),
        6: lambda: stage3(0),
        7: lambda: (stage3(2), stage3(3)),
        9: lambda: stage4(0),
        10: lambda: (stage4(2), stage4(3)),
        11: lambda: stage3(1),
    }
    for n in range(4):
        move.kept(n)
    for h in range(3):
        for k in range(rows_all // KEY_ROWS):
            turned[k] = dot(eye, key[h, k * KEY_ROWS : (k + 1) * KEY_ROWS, :], NT).astype(bf16)
        sums[...] = jnp.zeros_like(sums)
        lanes = slice(h * DH, (h + 1) * DH)

        def block(i, _):
            here = pl.ds(i * BACK_ROWS, BACK_ROWS)
            queries = query[h, here, :]
            backs = back_context[i // 2, lax.rem(i, 2)].reshape(BACK_ROWS, GROUP)[:, lanes]
            spread = jnp.sum(wide(backs) * wide(context[here, lanes]), axis=1, keepdims=True)
            high, mid, low = three(spread)
            side = jnp.where(
                side_lane == 0, -high, jnp.where(side_lane == 1, -mid, jnp.where(side_lane == 2, -low, 0.0))
            )
            widened = jnp.concatenate([backs, side.astype(bf16)], axis=1)

            def part(k, back_query):
                keys = pl.ds(k * KEY_ROWS, KEY_ROWS)
                chances = jnp.exp(dot(key[h, keys, :], queries, NT))
                back_scores = (chances * dot(value[h, keys, :], widened, NT)).astype(bf16)
                sums[keys, :DH] += dot(back_scores, queries[:, :DH])
                sums[keys, DH:] += dot(chances.astype(bf16), backs)
                return back_query + dot(turned[k], back_scores)

            back_query = jnp.zeros((DH, BACK_ROWS), f32)
            back_query = lax.fori_loop(0, rows_all // KEY_ROWS, part, back_query)
            joint[here, lanes] = (back_query * scale).T.astype(bf16)
            for step, action in between.items():
                if step // per_head == h:

                    @pl.when(i == step % per_head)
                    def _(action=action):
                        action()

            return 0

        lax.fori_loop(0, per_head, block, 0)
        joint[:, GROUP + h * DH : GROUP + (h + 1) * DH] = sums[:, :DH].astype(bf16)
        joint[:, 2 * GROUP + h * DH : 2 * GROUP + (h + 1) * DH] = sums[:, DH:].astype(bf16)

    for k in range(2):
        for yy in range(2):
            xx = lax.rem(x + 1 + k, 2)
            here = pl.ds((yy * 2 + xx) * rows, rows)
            back_first[yy, xx] = dot(joint[here, :], joint_weight[...], NT).astype(bf16).reshape(4, 2, piece, width)
            move.push(back_first.at[yy, xx, :, 1 - c], rc.at[yy, xx], sem_c.at[yy, xx], other_core)
    move.kept(4)
    grad = dot(first_low[...], joint[...], TN)
    lead = width // 32
    for block_at in range(32):
        gj[block_at // 16, block_at // 8 % 2, block_at % 8 // 2, block_at % 2] = grad[
            block_at * lead : (block_at + 1) * lead, :
        ].astype(bf16)
    move.push(gj.at[1 - y], ry, sem_y, down)
    for yy in range(2):
        move.landed(rc.at[yy, 1 - x], sem_c.at[yy, 1 - x])
        rc[yy, 1 - x] = (wide(rc[yy, 1 - x]) + wide(back_first[yy, 1 - x, :, c])).astype(bf16)
        move.push(rc.at[yy, 1 - x], rx.at[yy], sem_x.at[yy], across)
    stage4(1)
    shifts = jnp.sum(wide(joint[...]), axis=0, keepdims=True)
    small[...] = jnp.zeros_like(small)
    for k in range(8):
        for row, kind in ((2, 0), (3, 2)):
            start = kind * GROUP + k * lead
            small[mine * 8 + k, row : row + 1, :lead] = shifts[:, start : start + lead]
    move.landed(ry, sem_y)
    ry[...] = (wide(ry[...]) + wide(gj[y])).astype(bf16)
    for k in range(3):
        move.push(ry.at[:, line[k]], rz.at[k], sem_z.at[k], line_devices[k])
    for yy in range(2):
        move.landed(rc.at[yy, x], sem_c.at[yy, x])

    inputs = wide(tok_own[...].reshape(rows, width))
    centered = inputs - mean_of(inputs)
    inverse = lax.rsqrt(mean_of(centered * centered) + EPS)
    unit = centered * inverse
    halves_rows = []
    for yy in range(2):
        move.landed(rx.at[yy], sem_x.at[yy])
        whole = wide(rc[yy, x]) + wide(back_first[yy, x, :, c]) + wide(rx[yy])
        halves_rows.append(whole.reshape(rows // 2, width))
    back_one = jnp.concatenate(halves_rows, axis=0)
    scaled = back_one * vectors[0:1, :]
    back_tokens = back_residual[...] + inverse * (scaled - mean_of(scaled) - unit * mean_of(scaled * unit))
    gradient_low[...] = back_tokens.astype(bf16).reshape(8, piece, width)
    for k in range(1, 8):
        yy, zz = column(lax.rem(spot + k, 8))
        move.push(gradient_low.at[yy * 4 + zz], tokens_gradient.at[spot], sem_t.at[spot], at(yy, x, zz, c))
    kept = [move.keep(gradient_low.at[spot], tokens_gradient.at[spot])]
    gains = jnp.concatenate(
        [jnp.sum(back_one * unit, axis=0, keepdims=True), jnp.sum(back_one, axis=0, keepdims=True)], axis=0
    )
    for block_at in range(32):
        small[block_at, 0:2, :lead] = gains[:, block_at * lead : (block_at + 1) * lead]
    for t, device in others:
        move.push(small.at[t], small_all.at[me], sem_s.at[me], device)
    kept.append(move.keep(small.at[me], small_all.at[me]))

    total = wide(ry[:, z])
    for k in range(3):
        move.landed(rz.at[k], sem_z.at[k])
        total = total + wide(rz[k])
    sj[...] = total
    for xx, cc in group:
        move.push(sj.at[xx, cc], joint_land.at[mine], sem_g.at[mine], at(y, xx, z, cc))
    gone = move.keep(sj.at[x, c], joint_land.at[mine])
    for i in (0, 2, 3, 1):
        stage5(i)
    move.kept(gone)
    for xx, cc in group:
        move.landed(joint_land.at[xx * 2 + cc], sem_g.at[xx * 2 + cc])
    for g in range(4):
        for kind in range(3):
            start = kind * width + g * GROUP
            out_joint[:, start : start + GROUP] = joint_land[g, :, kind * GROUP : (kind + 1) * GROUP]
    for spot_kept in kept:
        move.kept(spot_kept)
    for t, _ in others:
        move.landed(small_all.at[t], sem_s.at[t])
    late[...] = jnp.sum(small_all[...], axis=0)
    for k in range(1, 8):
        t = lax.rem(spot + 8 - k, 8)
        move.landed(tokens_gradient.at[t], sem_t.at[t])
    move.finish()


def owner_device(
    tokens,
    lengths,
    first_gain,
    first_bias,
    joint_weight,
    query_bias,
    value_bias,
    output_weight,
    output_bias,
    second_gain,
    second_bias,
    inner_weight,
    inner_bias,
    outer_weight,
    outer_bias,
    cotangent,
):
    bf16, f32 = jnp.bfloat16, jnp.float32
    y, x, z, c = place()
    mine = x * 2 + c
    slots, piece, width = tokens.shape
    ff = inner_weight.shape[1]
    short = jnp.stack(
        [first_gain, first_bias, query_bias, value_bias, output_bias, second_gain, second_bias, outer_bias]
    )
    lead = short.shape[1]
    ff_piece = inner_bias.shape[0]
    small = jnp.concatenate(
        [
            jnp.pad(short, ((0, 0), (0, ff_piece - lead))),
            jnp.broadcast_to(inner_bias, (8, ff_piece)),
        ],
        axis=0,
    )
    hbm, vmem = pltpu.HBM, pltpu.VMEM
    dma, regular = pltpu.SemaphoreType.DMA, pltpu.SemaphoreType.REGULAR
    rows_all = 32 * piece
    natural = (2, 2, 4, 2, piece)
    length = lax.dynamic_slice(lengths, (y * 4 + z,), (1,))
    joint_four = jnp.transpose(joint_weight.reshape(lead, 3, 4, GROUP), (2, 0, 1, 3)).reshape(4, lead, 3 * GROUP)
    forward_outs = [
        ((rows_all, width), bf16, vmem),
        ((3, rows_all, 2 * DH), bf16, vmem),
        ((3, rows_all, 2 * DH), bf16, vmem),
        ((3, rows_all, 2 * DH), bf16, vmem),
        ((rows_all, GROUP), bf16, vmem),
        ((4, 2, 4, piece, GROUP), bf16, vmem),
        ((8, piece, width), bf16, hbm),
        ((8, piece, width), bf16, hbm),
        ((32,) + output_weight.shape, bf16, hbm),
        ((32,) + inner_weight.shape, bf16, hbm),
        ((32,) + outer_weight.shape, bf16, hbm),
        ((32,) + small.shape, bf16, vmem),
        ((width, 3 * GROUP), bf16, vmem),
    ]
    (
        first_low, query, key, value, context, context_rows, cot_own, tok_own, wo_all, wi_all, wu_all, small_all, joint_here
    ) = comm_call(
        forward_kernel,
        forward_outs,
        (length, tokens, cotangent, joint_four, output_weight, inner_weight, outer_weight, small),
        220, 16,
        [(32,), (8,), (3, 32), (32,), (4,), (4,), (4,), (8, 2), (4, 8), (8,)],
        [
            vmem((32, piece, width), bf16),
            vmem((2, 2, 4, 2, lead, 3 * GROUP), bf16),
            vmem((8, width), f32),
            vmem((3, 72, rows_all), bf16),
            vmem(natural + (GROUP,), bf16),
        ],
        0,
        [pltpu.SMEM, hbm, hbm, hbm, hbm, hbm, hbm, hbm],
    )
    vectors = jnp.transpose(small_all[:, :2, :lead], (1, 0, 2)).reshape(2, width).astype(f32)
    rows = 8 * piece
    grid = (4, 4, 2)
    kinds = [
        (outer_weight.shape, bf16),
        (inner_weight.shape, bf16),
        (output_weight.shape, bf16),
        ((8, 128), f32),
    ]
    gu, gi, go, gs, output, back_context, back_residual = comm_call(
        feed_kernel,
        [(grid + shape, dtype, hbm) for shape, dtype in kinds]
        + [
            (tokens.shape, bf16, hbm),
            (natural + (GROUP,), bf16, vmem),
            ((rows, width), f32, vmem),
        ],
        (
            length, context_rows.reshape(4, 8, piece, GROUP), tok_own, cot_own, wo_all.reshape(width, width), small_all,
            wi_all.reshape(width, ff), wu_all.reshape(grid + outer_weight.shape),
        ),
        20, 20, [(8,), (4, 2)],
        [vmem(grid + shape, dtype) for shape, dtype in kinds]
        + [
            vmem((width, ff), bf16),
            vmem((4, 8, piece, GROUP), bf16),
            vmem((8, width), f32),
            vmem((1, ff), f32),
            vmem((rows, ff), bf16),
            vmem((rows, ff), bf16),
            vmem((8, piece, width), bf16),
        ],
        1,
        [pltpu.SMEM] + [vmem] * 5 + [hbm] * 2,
    )
    out_o, out_i, out_u, out_s, joint_shard, tokens_gradient, late = comm_call(
        backward_kernel,
        [
            (output_weight.shape, f32, vmem),
            (inner_weight.shape, f32, vmem),
            (outer_weight.shape, f32, vmem),
            ((8, 128), f32, vmem),
            (joint_weight.shape, f32, vmem),
            (tokens.shape, bf16, hbm),
            ((8, 128), f32, vmem),
        ],
        (
            gu, gi, go, gs, query, key, value, context, back_context, joint_here, first_low, tok_own, back_residual, vectors,
        ),
        110, 16,
        [(4, 4), (4, 2), (4,), (4, 3), (), (3,), (4,), (2, 2), (2,), (8,), (32,)],
        [vmem((4, 4) + shape, dtype) for shape, dtype in kinds]
        + [vmem((2, 4) + shape, dtype) for shape, dtype in kinds]
        + [vmem((4,) + shape, dtype) for shape, dtype in kinds]
        + [vmem((3,) + shape, dtype) for shape, dtype in kinds]
        + [vmem((4, 4) + shape, dtype) for shape, dtype in kinds]
        + [
            vmem((rows_all, 3 * GROUP), bf16),
            vmem((rows_all, 2 * DH), f32),
            vmem((rows_all // KEY_ROWS, DH, KEY_ROWS), bf16),
            vmem((rows_all, width), bf16),
            vmem(natural + (width,), bf16),
            vmem((2, 2, 4, piece, width), bf16),
            vmem((2, 4, piece, width), bf16),
            vmem((2, 2, 4, 2, lead, 3 * GROUP), bf16),
            vmem((2, 4, 2, lead, 3 * GROUP), bf16),
            vmem((3, 2, 2, lead, 3 * GROUP), bf16),
            vmem((2, 2, lead, 3 * GROUP), f32),
            vmem((4, lead, 3 * GROUP), f32),
            vmem((8, piece, width), bf16),
            vmem((32, 8, 128), f32),
            vmem((32, 8, 128), f32),
        ],
        2,
        [hbm] * 4 + [vmem] * 6 + [hbm] + [vmem] * 3,
    )
    count = jnp.sum(lengths).astype(f32) * width
    stats = jnp.sqrt(out_s[5, :3] / count + 1e-06)
    return (
        output,
        tokens_gradient,
        late[0, :lead],
        late[1, :lead],
        joint_shard,
        late[2, :lead],
        late[3, :lead],
        out_o,
        out_s[3, :lead],
        out_s[1, :lead],
        out_s[2, :lead],
        out_i,
        out_s[4, : inner_bias.shape[0]],
        out_u,
        out_s[0, :lead],
        stats,
    )


def solution(mesh):
    in_specs = (
        P(None, ("head", "blk"), None),
        P(),
        P(("head", "blk")),
        P(("head", "blk")),
        P(("head", "blk"), None),
        P(("head", "blk")),
        P(("head", "blk")),
        P(("head", "blk"), None),
        P(("head", "blk")),
        P(("head", "blk")),
        P(("head", "blk")),
        P(("head", "blk"), None),
        P(("head", "blk")),
        P(("head", "blk"), None),
        P(("head", "blk")),
        P(None, ("head", "blk"), None),
    )
    out_specs = (
        P(None, ("head", "blk"), None),
        P(None, ("head", "blk"), None),
        P(("head", "blk")),
        P(("head", "blk")),
        P(("head", "blk"), None),
        P(("head", "blk")),
        P(("head", "blk")),
        P(("head", "blk"), None),
        P(("head", "blk")),
        P(("head", "blk")),
        P(("head", "blk")),
        P(("head", "blk"), None),
        P(("head", "blk")),
        P(("head", "blk"), None),
        P(("head", "blk")),
        P(),
    )
    small_slice = dict(mesh.shape) == {"head": 4, "blk": 8}
    device_work = owner_device if small_slice else on_device
    return jax.shard_map(
        device_work, mesh=mesh, in_specs=in_specs, out_specs=out_specs, check_vma=False
    )
```

```python
import jax
import jax.numpy as jnp
from jax import lax
from jax.experimental import pallas as pl
from jax.experimental.pallas import tpu as pltpu
from jax.sharding import PartitionSpec as P

H = 12
DH = 64


EPS = 1e-12
NEG = -1e30


def passed_along(value, axis, steps):
    count = lax.axis_size(axis)
    pairs = [(source, (source + steps) % count) for source in range(count)]
    return lax.ppermute(value, axis, pairs)


def normalize(values, gain, shift):
    average = jnp.mean(values, axis=-1, keepdims=True)
    centered = values - average
    inverse = lax.rsqrt(jnp.mean(centered * centered, axis=-1, keepdims=True) + EPS)
    normed = centered * inverse
    return (normed * gain + shift, normed, inverse)


def normalize_back(incoming, normed, inverse, gain):
    scaled = incoming * gain
    inner = (
        scaled
        - jnp.mean(scaled, axis=-1, keepdims=True)
        - normed * jnp.mean(scaled * normed, axis=-1, keepdims=True)
    )
    return (
        inner * inverse,
        jnp.sum(incoming * normed, axis=(0, 1)),
        jnp.sum(incoming, axis=(0, 1)),
    )


def gelu_exact(values):
    return jax.nn.gelu(values, approximate=False)


def key_mask(lengths, source, piece_rows, block_count, head_count):
    rows_here = jnp.arange(head_count * piece_rows, dtype=jnp.int32)
    position = (
        rows_here // piece_rows * block_count + source
    ) * piece_rows + rows_here % piece_rows
    return position[None, :] < lengths[:, None]


def attend(query_part, state, keys_block, values_block, mask):
    best, total, running = state
    scores = jnp.einsum(
        "sqhd,skhd->sqhk", query_part, keys_block, preferred_element_type=jnp.float32
    ) * DH ** (-0.5)
    scores = jnp.where(mask[:, None, None, :], scores, NEG)
    fresh = jnp.maximum(best, jnp.max(scores, axis=-1))
    decay = jnp.exp(best - fresh)
    weights = jnp.exp(scores - fresh[..., None])
    total = total * decay + jnp.sum(weights, axis=-1)
    running = running * decay[..., None] + jnp.einsum(
        "sqhk,skhd->sqhd",
        weights.astype(jnp.bfloat16),
        values_block,
        preferred_element_type=jnp.float32,
    )
    return (fresh, total, running)


def block_grads(query_part, back_part, total_part, spread_part, keys_block, values_block, mask):
    scale = DH ** (-0.5)
    scores = (
        jnp.einsum("sqhd,skhd->sqhk", query_part, keys_block, preferred_element_type=jnp.float32)
        * scale
    )
    scores = jnp.where(mask[:, None, None, :], scores, NEG)
    chances = jnp.exp(scores - total_part[..., None])
    back_chances = jnp.einsum(
        "sqhd,skhd->sqhk", back_part, values_block, preferred_element_type=jnp.float32
    )
    back_scores = (chances * (back_chances - spread_part[..., None])).astype(jnp.bfloat16)
    query_step = (
        jnp.einsum("sqhk,skhd->sqhd", back_scores, keys_block, preferred_element_type=jnp.float32)
        * scale
    )
    key_step = (
        jnp.einsum("sqhk,sqhd->skhd", back_scores, query_part, preferred_element_type=jnp.float32)
        * scale
    )
    value_step = jnp.einsum(
        "sqhk,sqhd->skhd",
        chances.astype(jnp.bfloat16),
        back_part,
        preferred_element_type=jnp.float32,
    )
    return (query_step, key_step, value_step)


def on_device(
    tokens,
    lengths,
    first_gain,
    first_bias,
    joint_weight,
    query_bias,
    value_bias,
    output_weight,
    output_bias,
    second_gain,
    second_bias,
    inner_weight,
    inner_bias,
    outer_weight,
    outer_bias,
    cotangent,
):
    head_count = lax.axis_size("head")
    block_count = lax.axis_size("blk")
    block = lax.axis_index("blk")
    quarter = lax.axis_index("head")
    (
        gain_one,
        shift_one,
        joint_full,
        query_shift,
        value_shift,
        output_full,
        output_shift,
        gain_two,
        shift_two,
        inner_full,
        inner_shift,
        outer_full,
        outer_shift,
    ) = (
        lax.all_gather(first_gain, ("head", "blk"), axis=0, tiled=True),
        lax.all_gather(first_bias, ("head", "blk"), axis=0, tiled=True),
        lax.all_gather(joint_weight, ("head", "blk"), axis=0, tiled=True),
        lax.all_gather(query_bias, ("head", "blk"), axis=0, tiled=True),
        lax.all_gather(value_bias, ("head", "blk"), axis=0, tiled=True),
        lax.all_gather(output_weight, ("head", "blk"), axis=0, tiled=True),
        lax.all_gather(output_bias, ("head", "blk"), axis=0, tiled=True),
        lax.all_gather(second_gain, ("head", "blk"), axis=0, tiled=True),
        lax.all_gather(second_bias, ("head", "blk"), axis=0, tiled=True),
        lax.all_gather(inner_weight, ("head", "blk"), axis=0, tiled=True),
        lax.all_gather(inner_bias, ("head", "blk"), axis=0, tiled=True),
        lax.all_gather(outer_weight, ("head", "blk"), axis=0, tiled=True),
        lax.all_gather(outer_bias, ("head", "blk"), axis=0, tiled=True),
    )
    sequences, piece_rows, width = tokens.shape
    heads_here = H // head_count
    head_width = heads_here * DH
    rows = head_count * piece_rows
    shape_heads = (sequences, rows, heads_here, DH)
    shape_flat = (sequences, rows, head_width)
    own_position = (quarter * block_count + block) * piece_rows + jnp.arange(
        piece_rows, dtype=jnp.int32
    )
    valid = own_position[None, :] < lengths[:, None]
    keep = valid[..., None]
    inputs = tokens.astype(jnp.float32)
    gain_one_wide = gain_one.astype(jnp.float32)
    gain_two_wide = gain_two.astype(jnp.float32)
    first_out, first_unit, first_scale = normalize(
        inputs, gain_one_wide, shift_one.astype(jnp.float32)
    )
    first_low = first_out.astype(jnp.bfloat16)
    joint = jnp.einsum("scd,de->sce", first_low, joint_full, preferred_element_type=jnp.float32)
    query_flat = (joint[..., :width] + query_shift.astype(jnp.float32)).astype(jnp.bfloat16)
    key_flat = joint[..., width : 2 * width].astype(jnp.bfloat16)
    value_flat = (joint[..., 2 * width :] + value_shift.astype(jnp.float32)).astype(jnp.bfloat16)
    query_flat, key_flat, value_flat = (
        lax.all_to_all(query_flat, "head", split_axis=2, concat_axis=1, tiled=True),
        lax.all_to_all(key_flat, "head", split_axis=2, concat_axis=1, tiled=True),
        lax.all_to_all(value_flat, "head", split_axis=2, concat_axis=1, tiled=True),
    )
    query_rows = query_flat.reshape(shape_heads)
    key_rows = key_flat.reshape(shape_heads)
    value_rows = value_flat.reshape(shape_heads)

    def visit(carry):
        keys_block, values_block, source, state = carry
        keys_block, values_block = passed_along((keys_block, values_block), "blk", 1)
        source = (source - 1) % block_count
        mask = key_mask(lengths, source, piece_rows, block_count, head_count)
        return (
            keys_block,
            values_block,
            source,
            attend(query_rows, state, keys_block, values_block, mask),
        )

    start_state = (
        jnp.full((sequences, rows, heads_here), NEG, jnp.float32),
        jnp.zeros((sequences, rows, heads_here), jnp.float32),
        jnp.zeros(shape_heads, jnp.float32),
    )
    first_state = attend(
        query_rows,
        start_state,
        key_rows,
        value_rows,
        key_mask(lengths, block, piece_rows, block_count, head_count),
    )
    carry = (key_rows, value_rows, block, first_state)
    carry = lax.fori_loop(0, block_count // 2 - 1, lambda turn, state: visit(visit(state)), carry)
    best, total, running = visit(carry)[3]
    context = running / total[..., None]
    log_total = best + jnp.log(total)
    context_low = context.astype(jnp.bfloat16).reshape(shape_flat)
    context_tokens = lax.all_to_all(context_low, "head", split_axis=1, concat_axis=2, tiled=True)
    branch = jnp.einsum(
        "sce,ed->scd", context_tokens, output_full, preferred_element_type=jnp.float32
    ) + output_shift.astype(jnp.float32)
    residual = inputs + branch
    second_out, second_unit, second_scale = normalize(
        residual, gain_two_wide, shift_two.astype(jnp.float32)
    )
    second_low = second_out.astype(jnp.bfloat16)
    inner = jnp.einsum(
        "scd,df->scf", second_low, inner_full, preferred_element_type=jnp.float32
    ) + inner_shift.astype(jnp.float32)
    activated = gelu_exact(inner).astype(jnp.bfloat16)
    feed = jnp.einsum(
        "scf,fd->scd", activated, outer_full, preferred_element_type=jnp.float32
    ) + outer_shift.astype(jnp.float32)
    result = residual + feed
    output = jnp.where(keep, result, 0.0).astype(jnp.bfloat16)
    sums = lax.psum(
        (
            jnp.sum(jnp.where(keep, result * result, 0.0)),
            jnp.sum(jnp.where(keep, branch * branch, 0.0)),
            jnp.sum(jnp.where(keep, feed * feed, 0.0)),
        ),
        ("head", "blk"),
    )
    count = jnp.sum(lengths).astype(jnp.float32) * width
    stats = jnp.sqrt(jnp.stack(sums) / count + 1e-06)
    back_result = jnp.where(keep, cotangent.astype(jnp.float32), 0.0)
    back_feed = back_result.astype(jnp.bfloat16)
    outer_gradient = jnp.einsum(
        "scf,scd->fd", activated, back_feed, preferred_element_type=jnp.float32
    )
    outer_shift_gradient = jnp.sum(back_feed.astype(jnp.float32), axis=(0, 1))
    back_active = jnp.einsum(
        "scd,fd->scf", back_feed, outer_full, preferred_element_type=jnp.float32
    )
    back_inner = jax.vjp(gelu_exact, inner)[1](back_active)[0].astype(jnp.bfloat16)
    inner_gradient = jnp.einsum(
        "scd,scf->df", second_low, back_inner, preferred_element_type=jnp.float32
    )
    inner_shift_gradient = jnp.sum(back_inner.astype(jnp.float32), axis=(0, 1))
    back_second = jnp.einsum(
        "scf,df->scd", back_inner, inner_full, preferred_element_type=jnp.float32
    )
    back_norm_two, gain_two_gradient, shift_two_gradient = normalize_back(
        back_second, second_unit, second_scale, gain_two_wide
    )
    back_residual = back_result + back_norm_two
    back_branch = back_residual.astype(jnp.bfloat16)
    output_gradient = jnp.einsum(
        "sce,scd->ed", context_tokens, back_branch, preferred_element_type=jnp.float32
    )
    output_shift_gradient = jnp.sum(back_branch.astype(jnp.float32), axis=(0, 1))
    back_context = jnp.einsum(
        "scd,ed->sce", back_branch, output_full, preferred_element_type=jnp.float32
    ).astype(jnp.bfloat16)
    back_context = lax.all_to_all(back_context, "head", split_axis=2, concat_axis=1, tiled=True)
    back_heads = back_context.reshape(shape_heads)
    spread = jnp.sum(back_heads.astype(jnp.float32) * context, axis=-1)
    zero_heads = jnp.zeros(shape_heads, jnp.float32)

    def pass_keys(carry):
        keys_block, values_block, key_sum, value_sum, query_sum, source = carry
        mask = key_mask(lengths, source, piece_rows, block_count, head_count)
        query_step, key_step, value_step = block_grads(
            query_rows, back_heads, log_total, spread, keys_block, values_block, mask
        )
        keys_block, values_block = passed_along((keys_block, values_block), "blk", 1)
        key_sum, value_sum = passed_along((key_sum + key_step, value_sum + value_step), "blk", 1)
        return (
            keys_block,
            values_block,
            key_sum,
            value_sum,
            query_sum + query_step,
            (source - 1) % block_count,
        )

    carry = (key_rows, value_rows, zero_heads, zero_heads, zero_heads, block)
    carry = lax.fori_loop(
        0, block_count // 2, lambda turn, state: pass_keys(pass_keys(state)), carry
    )
    key_sum, value_sum, query_sum = (carry[2], carry[3], carry[4])
    back_query, back_key, back_value = (
        lax.all_to_all(
            query_sum.astype(jnp.bfloat16).reshape(shape_flat),
            "head",
            split_axis=1,
            concat_axis=2,
            tiled=True,
        ),
        lax.all_to_all(
            key_sum.astype(jnp.bfloat16).reshape(shape_flat),
            "head",
            split_axis=1,
            concat_axis=2,
            tiled=True,
        ),
        lax.all_to_all(
            value_sum.astype(jnp.bfloat16).reshape(shape_flat),
            "head",
            split_axis=1,
            concat_axis=2,
            tiled=True,
        ),
    )
    back_joint = jnp.concatenate([back_query, back_key, back_value], axis=-1)
    joint_gradient = jnp.einsum(
        "scd,sce->de", first_low, back_joint, preferred_element_type=jnp.float32
    )
    query_shift_gradient = jnp.sum(back_query.astype(jnp.float32), axis=(0, 1))
    value_shift_gradient = jnp.sum(back_value.astype(jnp.float32), axis=(0, 1))
    back_first = jnp.einsum(
        "sce,de->scd", back_joint, joint_full, preferred_element_type=jnp.float32
    )
    back_norm_one, gain_one_gradient, shift_one_gradient = normalize_back(
        back_first, first_unit, first_scale, gain_one_wide
    )
    tokens_gradient = (back_residual + back_norm_one).astype(jnp.bfloat16)
    shards = (
        lax.psum_scatter(gain_one_gradient, ("head", "blk"), scatter_dimension=0, tiled=True),
        lax.psum_scatter(shift_one_gradient, ("head", "blk"), scatter_dimension=0, tiled=True),
        lax.psum_scatter(joint_gradient, ("head", "blk"), scatter_dimension=0, tiled=True),
        lax.psum_scatter(query_shift_gradient, ("head", "blk"), scatter_dimension=0, tiled=True),
        lax.psum_scatter(value_shift_gradient, ("head", "blk"), scatter_dimension=0, tiled=True),
        lax.psum_scatter(output_gradient, ("head", "blk"), scatter_dimension=0, tiled=True),
        lax.psum_scatter(output_shift_gradient, ("head", "blk"), scatter_dimension=0, tiled=True),
        lax.psum_scatter(gain_two_gradient, ("head", "blk"), scatter_dimension=0, tiled=True),
        lax.psum_scatter(shift_two_gradient, ("head", "blk"), scatter_dimension=0, tiled=True),
        lax.psum_scatter(inner_gradient, ("head", "blk"), scatter_dimension=0, tiled=True),
        lax.psum_scatter(inner_shift_gradient, ("head", "blk"), scatter_dimension=0, tiled=True),
        lax.psum_scatter(outer_gradient, ("head", "blk"), scatter_dimension=0, tiled=True),
        lax.psum_scatter(outer_shift_gradient, ("head", "blk"), scatter_dimension=0, tiled=True),
    )
    return (
        output,
        tokens_gradient,
        shards[0],
        shards[1],
        shards[2],
        shards[3],
        shards[4],
        shards[5],
        shards[6],
        shards[7],
        shards[8],
        shards[9],
        shards[10],
        shards[11],
        shards[12],
        stats,
    )


MESH = pl.DeviceIdType.MESH
WIDTH = H * DH
GROUP = 3 * DH
NT = (((1,), (1,)), ((), ()))
NN = (((1,), (0,)), ((), ()))


def place():
    head = lax.axis_index("head")
    blk = lax.axis_index("blk")
    return head // 2, lax.rem(head, 2), blk // 2, lax.rem(blk, 2)


def at(y, x, z, c):
    return (y * 2 + x, z * 2 + c)


def number(y, x, z, c):
    return y * 16 + x * 8 + z * 2 + c


def column(t):
    return t // 4, lax.rem(t, 4)


def meet(peers):
    barrier = pltpu.get_barrier_semaphore()
    for peer in peers:
        pl.semaphore_signal(barrier, inc=1, device_id=peer, device_id_type=MESH)
    pl.semaphore_wait(barrier, len(peers))


class Mover:
    def __init__(self, send_sem, local_sem, anyone):
        self.send_sem = send_sem
        self.local_sem = local_sem
        self.anyone = anyone
        self.zero = anyone[0] * 0
        self.sent = []
        self.local = []

    def push(self, source, target, sem, device):
        self.push_made(lambda: (source, target, sem), device)

    def push_made(self, make, device, when=None):
        spot = len(self.sent)
        self.sent.append((make, spot, device, when))
        under(when, lambda: self.copy(make, spot, device).start())

    def copy(self, make, spot, device):
        source, target, sem = make()
        return remote(source, target, self.send_sem.at[self.zero + spot], sem, device)

    def keep(self, source, target):
        parts = (source, target, self.local_sem.at[len(self.local)])
        pltpu.make_async_copy(*parts).start()
        self.local.append(parts)
        return len(self.local) - 1

    def kept(self, spot):
        pltpu.make_async_copy(*self.local[spot]).wait()

    def landed(self, target, sem):
        remote(target, target, self.send_sem.at[self.zero], sem, self.anyone).wait_recv()

    def finish(self, kept=()):
        for make, spot, device, when in self.sent:
            under(when, lambda: self.copy(make, spot, device).wait_send())
        for spot in kept:
            self.kept(spot)


def under(when, action):
    if when is None:
        action()
    else:

        @pl.when(when)
        def _():
            action()


def remote(source, target, send_sem, recv_sem, device):
    return pltpu.make_async_remote_copy(
        src_ref=source,
        dst_ref=target,
        send_sem=send_sem,
        recv_sem=recv_sem,
        device_id=device,
        device_id_type=MESH,
    )


def unpack(small_all, vectors):
    for block in range(32):
        tile = wide(small_all[block])
        vectors[:, block * 24 : block * 24 + 24] = tile[:8, :24]


def forward_kernel(
    length, tokens, cotangent, wj, wo, wi, wu, small,
    first_far, query_far, key_far, value_far, context, context_rows, cot_own, tok_own, wo_all, wi_all, wu_all, small_all, wj_flat,
    send_sem, local_sem, tok_sem, cot_sem, weight_sem, small_sem, wja_sem, wjb_sem, wjc_sem, ctx_send, ctx_recv,
    ctx_local, tok_all, wj_all, vectors, turned, mixed_low, score_a, score_b, straight_low, first_low, query, key, value,
):
    y, x, z, c = place()
    mine = number(y, x, z, c)
    quarter = x * 2 + c
    spot = y * 4 + z
    other_core = at(y, x, z, 1 - c)
    across = at(y, 1 - x, z, c)
    diagonal = at(y, 1 - x, z, 1 - c)
    down = at(1 - y, x, z, c)
    y1, x1 = jnp.where(c == 0, y, 1 - y), jnp.where(c == 0, 1 - x, x)
    y2, x2 = jnp.where(c == 0, 1 - y, y), jnp.where(c == 0, x, 1 - x)
    first, second = at(y1, x1, z, c), at(y2, x2, z, c)
    spots = [column(lax.rem(spot + k, 8)) for k in range(1, 8)]
    back_spots = [column(lax.rem(spot + 8 - k, 8)) for k in range(1, 8)]
    ahead = [at(y, x, lax.rem(z + k, 4), c) for k in range(1, 4)]
    inside = jnp.logical_or(z == 1, z == 2)
    lines = [
        z,
        jnp.where(z == 0, 1, z - 1),
        jnp.where(z == 0, 2, jnp.where(z == 3, 1, z + 1)),
        jnp.where(z < 2, 3, 0),
    ]
    onward = [z + 1, z - 1, jnp.where(z == 1, 0, 3)]
    away, back = at(y, x, jnp.where(z < 3, z + 1, z - 1), c), at(y, x, jnp.maximum(z - 1, 0), c)
    onward = [at(y, x, lax.rem(zz + 4, 4), c) for zz in onward]
    line_blocks = [number(y, x, zz, c) for zz in lines]
    first_blocks = [number(y1, x1, zz, c) for zz in lines]
    second_blocks = [number(yy, xx, zz, c) for zz in lines for yy, xx in ((y2, x2), (1 - y, 1 - x))]
    core_blocks = [number(yy, xx, zz, 1 - c) for yy in range(2) for xx in range(2) for zz in range(4)]
    group = quad(x, c)
    meet([at(yy, x, zz, c) for yy, zz in spots] + [across, other_core, diagonal])
    move = Mover(send_sem, local_sem, other_core)
    sources = (wo, wi, wu)
    wholes = (wo_all, wi_all, wu_all)

    def hand(block, own, device, when=None):
        for i in range(3):
            move.push_made(
                lambda i=i: (
                    sources[i] if own else wholes[i].at[block],
                    wholes[i].at[block],
                    weight_sem.at[move.zero + i, block],
                ),
                device,
                when,
            )

    def arrive(block):
        for i in range(3):
            move.landed(wholes[i].at[block], weight_sem.at[i, block])

    def pass_small(blocks, devices):
        for block in blocks:
            move.landed(small_all.at[block], small_sem.at[block])
            for device in devices:
                move.push(small_all.at[block], small_all.at[block], small_sem.at[block], device)

    def spread(block, own):
        for device in (first, second, other_core):
            hand(block, own, device)

    def line_arrived(k):
        arrive(line_blocks[k])
        hand(line_blocks[k], False, onward[k - 1], inside)
        spread(line_blocks[k], False)

    def second_hand(k):
        arrive(first_blocks[k])
        hand(first_blocks[k], False, second)
        hand(first_blocks[k], False, other_core)

    def last_hand(k):
        for b in second_blocks[2 * k : 2 * k + 2]:
            arrive(b)
            hand(b, False, other_core)

    for device in ahead + [first, second, other_core]:
        move.push(small, small_all.at[mine], small_sem.at[mine], device)
    for xx, cc in group:
        move.push(wj.at[xx * 2 + cc], wj_all.at[y, x, z, c], wja_sem.at[quarter], at(y, xx, z, cc))
    move.keep(wj.at[quarter], wj_all.at[y, x, z, c])
    move.keep(tokens.at[spot], tok_all.at[mine])
    move.keep(small, small_all.at[mine])
    for yy, zz in spots:
        move.push(tokens.at[yy * 4 + zz], tok_all.at[mine], tok_sem.at[mine], at(yy, x, zz, c))
    for device in (across, other_core):
        move.push(tokens.at[spot], tok_all.at[mine], tok_sem.at[mine], device)
    spread(mine, True)
    for source, whole in zip(sources, wholes):
        move.keep(source, whole.at[mine])

    def slice_onward(zz, device, when):
        move.push_made(lambda: (wj_all.at[y, :, zz], wj_all.at[y, :, zz], wjb_sem.at[zz]), device, when)

    for xx, cc in group:
        move.landed(wj_all.at[y, xx, z, cc], wja_sem.at[xx * 2 + cc])
    move.kept(0)
    slice_onward(z, away, None)
    slice_onward(z, back, inside)
    move.push(wj_all.at[y, :, z], wj_all.at[y, :, z], wjc_sem.at[z], down)
    pass_small(line_blocks[1:], (first, second, other_core))
    pass_small(first_blocks, (second, other_core))
    for k in range(1, 4):
        zz = lines[k]
        move.landed(wj_all.at[y, :, zz], wjb_sem.at[zz])
        slice_onward(zz, onward[k - 1], inside)
        move.push(wj_all.at[y, :, zz], wj_all.at[y, :, zz], wjc_sem.at[zz], down)
    pass_small(second_blocks, (other_core,))
    for yy, zz in back_spots:
        block = number(yy, x, zz, c)
        move.landed(tok_all.at[block], tok_sem.at[block])
        move.push(tok_all.at[block], tok_all.at[block], tok_sem.at[block], across)
        move.push(tok_all.at[block], tok_all.at[block], tok_sem.at[block], other_core)
    hand(mine, True, away)
    hand(mine, True, back, inside)
    second_hand(0)
    for yy, zz in [(y, z)] + back_spots:
        block = number(yy, 1 - x, zz, c)
        move.landed(tok_all.at[block], tok_sem.at[block])
        move.push(tok_all.at[block], tok_all.at[block], tok_sem.at[block], other_core)
    for block in core_blocks:
        move.landed(small_all.at[block], small_sem.at[block])
    for zz in lines:
        move.landed(wj_all.at[1 - y, :, zz], wjc_sem.at[zz])
    line_arrived(1)
    for yy, zz in spots:
        move.push(cotangent.at[yy * 4 + zz], cot_own.at[spot], cot_sem.at[spot], at(yy, x, zz, c))
    move.keep(cotangent.at[spot], cot_own.at[spot])
    for yy, zz in [(y, z)] + back_spots:
        for xx in (x, 1 - x):
            block = number(yy, xx, zz, 1 - c)
            move.landed(tok_all.at[block], tok_sem.at[block])
    move.kept(1)
    move.kept(2)

    unpack(small_all, vectors)
    rows = query.shape[1]
    for yy in range(2):
        for xx in range(2):
            for zz in range(4):
                pair = jnp.concatenate([wide(wj_all[yy, xx, zz, cc]) for cc in range(2)], axis=0)
                row = number(yy, xx, zz, 0) * 24
                wj_flat[row : row + 48, :] = pair.astype(jnp.bfloat16)
    lane = lax.broadcasted_iota(jnp.int32, (ROWS, DH), 1)
    row_at = lax.broadcasted_iota(jnp.int32, (ROWS, DH), 0)
    one_lane = jnp.where(lane == 0, 1.0, 0.0).astype(jnp.bfloat16)
    three_lanes = jnp.where(lane < 3, 1.0, 0.0).astype(jnp.bfloat16)
    gain, shift = vectors[0:1, :], vectors[1:2, :]
    query_all, value_all = vectors[2:3, :], vectors[3:4, :]

    def chosen(whole):
        total = jnp.zeros((1, GROUP), jnp.float32)
        for q in range(4):
            total = jnp.where(quarter == q, whole[:, q * GROUP : (q + 1) * GROUP], total)
        return total

    query_shift, value_shift = chosen(query_all), chosen(value_all)
    blocks = ROWS // tokens.shape[1]

    def project(i, _):
        here = pl.ds(i * ROWS, ROWS)
        raw = tok_all[pl.ds(i * blocks, blocks)].reshape(ROWS, WIDTH)
        normed = normalize(wide(raw), gain, shift)[0].astype(jnp.bfloat16)
        first_low[here, :] = normed
        joint = dot(normed, wj_flat[...])
        low_q = ((joint[:, :GROUP] + query_shift).astype(jnp.bfloat16) * DH ** (-0.5)).astype(jnp.bfloat16)
        low_k = joint[:, GROUP : 2 * GROUP].astype(jnp.bfloat16)
        low_v = (joint[:, 2 * GROUP :] + value_shift).astype(jnp.bfloat16)
        mask = jnp.where(row_at + i * ROWS < length[0], 0.0, NEG)
        key_side = jnp.where(lane == 0, mask, jnp.where(lane < 4, 1.0, 0.0)).astype(jnp.bfloat16)
        for h in range(3):
            here_h = slice(h * DH, (h + 1) * DH)
            query[h, here, :] = jnp.concatenate([low_q[:, here_h], one_lane], axis=1)
            key[h, here, :] = jnp.concatenate([low_k[:, here_h], key_side], axis=1)
            value[h, here, :] = jnp.concatenate([low_v[:, here_h], three_lanes], axis=1)
        return 0

    for i in range(rows // ROWS):
        project(i, 0)
    for source, target in ((first_low, first_far), (key, key_far), (value, value_far)):
        move.keep(source, target)
    eye = jnp.eye(72, 2 * DH, dtype=jnp.bfloat16)
    for h in range(3):
        turned[h] = dot(eye, value[h], NT).astype(jnp.bfloat16)
    wider = score_a.shape[1]
    side = lax.broadcasted_iota(jnp.int32, (DH, wider), 0)
    chunk = 512
    units = 3 * rows // wider

    def ctx_copy(j, cc, for_local, for_remote):
        yy, xx = j // 2, lax.rem(j, 2)
        source, target = mixed_low.at[yy, xx, :, cc], context_rows.at[quarter, yy]
        here = jnp.logical_and(xx == x, c == cc)

        @pl.when(here)
        def _():
            for_local(pltpu.make_async_copy(source, target, ctx_local.at[j]))

        @pl.when(jnp.logical_not(here))
        def _():
            for_remote(remote(source, target, ctx_send.at[j, cc], ctx_recv.at[quarter, j], at(y, xx, z, cc)))

    def score_chunk(held, h, queries, k, best):
        fresh = dot(key[h, k * chunk : (k + 1) * chunk, :], queries, NT)
        held[k * chunk : (k + 1) * chunk, :] = fresh
        return jnp.maximum(best, jnp.max(fresh, axis=0, keepdims=True))

    lowest = jnp.full((1, wider), -jnp.inf, jnp.float32)
    start = lowest
    for k in range(rows // chunk):
        start = score_chunk(score_a, 0, query[0, :wider, :], k, start)

    def unit(u, best, held, fresh):
        j = u // 3
        h = u - 3 * j
        u_next = jnp.minimum(u + 1, units - 1)
        j_next = u_next // 3
        h_next = u_next - 3 * j_next
        here = pl.ds(j * wider, wider)
        queries = query[h_next, pl.ds(j_next * wider, wider), :]
        best_next = lowest
        mixed = jnp.zeros((72, wider), jnp.float32)
        for k in range(rows // chunk):
            keys = slice(k * chunk, (k + 1) * chunk)
            weights = jnp.exp(held[keys, :] - best).astype(jnp.bfloat16)
            mixed = mixed + dot(turned[h, :, keys], weights)
            best_next = score_chunk(fresh, h_next, queries, k, best_next)
        total = mixed[DH : DH + 1, :]
        mixed = mixed[:DH, :] / total
        high, mid, low = three(best + jnp.log(total))
        extra = jnp.where(
            side == 0, 1.0, jnp.where(side == 1, -high, jnp.where(side == 2, -mid, jnp.where(side == 3, -low, 0.0)))
        )
        straight = jnp.concatenate([mixed, extra], axis=0).T
        query[h, here, DH:] = straight[:, DH:].astype(jnp.bfloat16)
        straight_low[h] = straight[:, :DH].astype(jnp.bfloat16)

        @pl.when(h == 2)
        def _():
            whole = jnp.concatenate([straight_low[k] for k in range(3)], axis=1)
            context[here, :] = whole
            mixed_low[j // 2, lax.rem(j, 2)] = whole.reshape(4, 2, tokens.shape[1], GROUP)
            for cc in range(2):
                ctx_copy(j, cc, lambda copy: copy.start(), lambda copy: copy.start())

        return best_next

    def pair(p, best):
        best = unit(2 * p, best, score_a, score_b)
        best = unit(2 * p + 1, best, score_b, score_a)
        for when, action in (
            (0, lambda: second_hand(1)),
            (1, lambda: line_arrived(2)),
            (2, lambda: (second_hand(2), last_hand(0))),
            (3, lambda: line_arrived(3)),
            (4, lambda: (second_hand(3), last_hand(1))),
        ):

            @pl.when(p == when)
            def _(action=action):
                action()

        return best

    lax.fori_loop(0, units // 2, pair, start)
    move.keep(query, query_far)
    last_hand(2)
    last_hand(3)
    for yy, zz in back_spots:
        move.landed(cot_own.at[yy * 4 + zz], cot_sem.at[yy * 4 + zz])
    for b in core_blocks:
        arrive(b)
    tok_copies = []
    for i in range(8):
        yy, zz = i // 4, i % 4
        tok_copies.append(pltpu.make_async_copy(tok_all.at[number(yy, x, zz, c)], tok_own.at[i], local_sem.at[8 + i]))
        tok_copies[-1].start()

    def settle(j, _):
        for cc in range(2):
            ctx_copy(j, cc, lambda copy: copy.wait(), lambda copy: copy.wait_send())
        return 0

    lax.fori_loop(0, 4, settle, 0)
    for xx, cc in group:
        for yy in range(2):
            move.landed(context_rows.at[xx * 2 + cc, yy], ctx_recv.at[xx * 2 + cc, yy * 2 + x])
    move.finish(range(3, len(move.local)))
    for copy in tok_copies:
        copy.wait()


def comm_call(kernel, outs, args, sends, locals_, sems, scratch, ident, space=None):
    space = space or [pltpu.HBM] * len(args)
    return pl.pallas_call(
        kernel,
        out_shape=[jax.ShapeDtypeStruct(shape, dtype) for shape, dtype, _ in outs],
        in_specs=[pl.BlockSpec(memory_space=one) for one in space],
        out_specs=[pl.BlockSpec(memory_space=one) for _, _, one in outs],
        scratch_shapes=[
            pltpu.SemaphoreType.DMA((sends,)),
            pltpu.SemaphoreType.DMA((max(locals_, 1),)),
            *[pltpu.SemaphoreType.DMA(shape) for shape in sems],
            *scratch,
        ],
        compiler_params=pltpu.CompilerParams(
            collective_id=ident, has_side_effects=True, vmem_limit_bytes=61 * 1024 * 1024
        ),
    )(*args)


def quad(x, c):
    return [(lax.rem(x + dx, 2), lax.rem(c + dc, 2)) for dx, dc in ((0, 1), (1, 0), (1, 1))]


def wide(value):
    return value.astype(jnp.float32)


def dot(a, b, dims=NN):
    return lax.dot_general(a, b, dims, preferred_element_type=jnp.float32)


ROWS = 256


TN = (((0,), (0,)), ((), ()))
BACK_ROWS = 512
KEY_ROWS = 1024


def three(value):
    high = value.astype(jnp.bfloat16).astype(jnp.float32)
    middle = (value - high).astype(jnp.bfloat16).astype(jnp.float32)
    return high, middle, value - high - middle


def mean_of(value):
    return jnp.mean(value, axis=-1, keepdims=True)


TN = (((0,), (0,)), ((), ()))
BACK_ROWS = 512
KEY_ROWS = 1024


def three(value):
    high = value.astype(jnp.bfloat16).astype(jnp.float32)
    middle = (value - high).astype(jnp.bfloat16).astype(jnp.float32)
    return high, middle, value - high - middle


def mean_of(value):
    return jnp.mean(value, axis=-1, keepdims=True)


def feed_kernel(
    length, context_rows, tok_own, cot_own, wo, small_all, wi_far, wu_far,
    gu_far, gi_far, go_far, gs_far, output, back_context, back_residual,
    send_sem, local_sem, sem_out, sem_back,
    gu, gi, go, gs, wi, back_near, vectors, inner_shift, active, back_inner, output_low,
):
    bf16, f32 = jnp.bfloat16, jnp.float32
    y, x, z, c = place()
    spot = y * 4 + z
    mine = x * 2 + c
    other_core = at(y, x, z, 1 - c)
    across = at(y, 1 - x, z, c)
    diagonal = at(y, 1 - x, z, 1 - c)
    spots = [column(lax.rem(spot + k, 8)) for k in range(1, 8)]
    group = quad(x, c)
    meet([at(yy, x, zz, c) for yy, zz in spots] + [across, other_core, diagonal])
    move = Mover(send_sem, local_sem, other_core)
    width = wo.shape[0]
    ff = wi.shape[1]
    move.keep(wi_far, wi)
    move.keep(wu_far, gu)

    piece = tok_own.shape[1]
    rows = tok_own.shape[0] * piece
    steps = ff // width
    unpack(small_all, vectors)
    ff_piece = ff // 32
    for block in range(32):
        inner_shift[:, block * ff_piece : (block + 1) * ff_piece] = wide(small_all[block])[8:9, :ff_piece]

    spot_at = lax.broadcasted_iota(jnp.int32, (8, piece, 1), 0)
    position = number(spot_at // 4, x, lax.rem(spot_at, 4), c) * piece
    position = position + lax.broadcasted_iota(jnp.int32, (8, piece, 1), 1)
    keep = jnp.where(position < length[0], 1.0, 0.0).reshape(rows, 1) > 0.5

    def column_sum(item):
        return jnp.sum(item, axis=0, keepdims=True)

    def square(item):
        return jnp.sum(item * item)

    branch = vectors[4:5, :] + dot(context_rows[0].reshape(rows, GROUP), wo[:GROUP, :])
    for g in range(1, 4):
        branch = branch + dot(context_rows[g].reshape(rows, GROUP), wo[g * GROUP : (g + 1) * GROUP, :])
    residual = wide(tok_own[...].reshape(rows, width)) + branch
    branch_total = square(jnp.where(keep, branch, 0.0))
    average = mean_of(residual)
    centered = residual - average
    inverse = lax.rsqrt(mean_of(centered * centered) + EPS)
    unit = centered * inverse
    second_low = (unit * vectors[5:6, :] + vectors[6:7, :]).astype(bf16)
    back_result = jnp.where(keep, wide(cot_own[...].reshape(rows, width)), 0.0)
    back_feed = back_result.astype(bf16)
    move.kept(0)
    move.kept(1)

    def middle(step, sums_here):
        back_second, feed = sums_here
        cols = pl.ds(pl.multiple_of(step * width, width), width)
        wi_here = wi[:, cols]
        inner = dot(second_low, wi_here) + inner_shift[:, cols]
        chance = 0.5 * (1.0 + lax.erf(inner * 0.7071067811865476))
        low = (inner * chance).astype(bf16)
        active[:, cols] = low
        wu_here = gu[step].reshape(width, width)
        slope = chance + inner * jnp.exp(inner * inner * -0.5) * 0.3989422804014327
        back = (dot(back_feed, wu_here, NT) * slope).astype(bf16)
        back_inner[:, cols] = back
        return back_second + dot(back, wi_here, NT), feed + dot(low, wu_here)

    zero = jnp.zeros((rows, width), f32)
    back_second, feed = lax.fori_loop(0, steps, middle, (zero, zero))
    scaled = back_second * vectors[5:6, :]
    back_res = back_result + inverse * (scaled - mean_of(scaled) - unit * mean_of(scaled * unit))
    back_residual[...] = back_res
    back_branch = back_res.astype(bf16)
    short = jnp.concatenate(
        [
            column_sum(wide(back_feed)), column_sum(back_second * unit), column_sum(back_second),
            column_sum(wide(back_branch)), jnp.zeros((4, width), f32),
        ],
        axis=0,
    )
    for g in range(4):
        back_near[g] = dot(back_branch, wo[g * GROUP : (g + 1) * GROUP, :], NT).astype(bf16).reshape(8, piece, GROUP)
    for xx, cc in group[::-1]:
        for yy in range(2):
            move.push(
                back_near.at[xx * 2 + cc, pl.ds(yy * 4, 4)],
                back_context.at[yy, x, :, c],
                sem_back.at[mine, yy],
                at(y, xx, z, cc),
            )
    for yy in range(2):
        move.keep(back_near.at[mine, pl.ds(yy * 4, 4)], back_context.at[yy, x, :, c])

    feed = feed + vectors[7:8, :]
    result = jnp.where(keep, residual + feed, 0.0)
    output_low[...] = result.astype(bf16).reshape(8, piece, width)
    for yy, zz in spots:
        move.push(output_low.at[yy * 4 + zz], output.at[spot], sem_out.at[spot], at(yy, x, zz, c))
    move.keep(output_low.at[spot], output.at[spot])

    totals = (square(result), branch_total, square(jnp.where(keep, feed, 0.0)))
    lane = lax.broadcasted_iota(jnp.int32, (1, 128), 1)
    stat_row = jnp.where(lane == 0, totals[0], jnp.where(lane == 1, totals[1], jnp.where(lane == 2, totals[2], 0.0)))
    lead = width // 32
    wide_piece = ff // 32
    for step in range(steps):
        grad = dot(active[:, step * width : (step + 1) * width], back_feed, TN).astype(bf16)
        for zz in range(4):
            for cc in range(2):
                row = (zz * 2 + cc) * wide_piece
                gu[step, zz, cc] = grad[row : row + wide_piece, :]
        move.keep(gu.at[step], gu_far.at[step])
    for step in range(steps):
        grad = dot(second_low, back_inner[:, step * width : (step + 1) * width], TN)
        for block in range(32):
            gi[block // 8, block % 8 // 2, block % 2, :, step * width : (step + 1) * width] = grad[
                block * lead : (block + 1) * lead, :
            ].astype(bf16)
    move.keep(gi, gi_far)
    for g in range(4):
        grad = dot(context_rows[g].reshape(rows, GROUP), back_branch, TN)
        for zz in range(4):
            for cc in range(2):
                row = (zz * 2 + cc) * lead
                go[g, zz, cc] = grad[row : row + lead, :].astype(bf16)
        move.keep(go.at[g], go_far.at[g])

    long = column_sum(wide(back_inner[...]))
    for block in range(32):
        at_block = (block // 8, block % 8 // 2, block % 2)
        gs[at_block] = jnp.zeros((8, 128), f32)
        gs[at_block + (slice(0, 8), slice(0, lead))] = short[:, block * lead : (block + 1) * lead]
        gs[at_block + (slice(4, 5), slice(0, wide_piece))] = long[:, block * wide_piece : (block + 1) * wide_piece]
        gs[at_block + (slice(5, 6), slice(None))] = stat_row
    move.keep(gs, gs_far)
    for xx, cc in group:
        for yy in range(2):
            move.landed(back_context.at[yy, xx, :, cc], sem_back.at[xx * 2 + cc, yy])
    for k in range(1, 8):
        t = lax.rem(spot + 8 - k, 8)
        move.landed(output.at[t], sem_out.at[t])
    move.finish(range(2, len(move.local)))


def backward_kernel(
    gu, gi, go, gs, query, key, value, context, back_context, joint_weight, first_far, tok_own, back_residual, vectors,
    out_o, out_i, out_u, out_s, out_joint, tokens_gradient, late,
    send_sem, local_sem, sem1, sem2, sem3, sem4, sem_y, sem_z, sem_g, sem_c, sem_x, sem_t, sem_s,
    r1u, r1i, r1o, r1s, r2u, r2i, r2o, r2s, r3u, r3i, r3o, r3s, r4u, r4i, r4o, r4s, ou, oi, oo, os_,
    joint, sums, turned, first_low, back_first, rc, rx, gj, ry, rz, sj, joint_land, gradient_low, small, small_all,
):
    bf16, f32 = jnp.bfloat16, jnp.float32
    y, x, z, c = place()
    spot = y * 4 + z
    mine = x * 2 + c
    me = number(y, x, z, c)
    other_core = at(y, x, z, 1 - c)
    across = at(y, 1 - x, z, c)
    down = at(1 - y, x, z, c)
    y1, x1 = jnp.where(c == 0, y, 1 - y), jnp.where(c == 0, 1 - x, x)
    y2, x2 = jnp.where(c == 0, 1 - y, y), jnp.where(c == 0, x, 1 - x)
    first, second = at(y1, x1, z, c), at(y2, x2, z, c)
    line = [lax.rem(z + k, 4) for k in range(1, 4)]
    line_devices = [at(y, x, zz, c) for zz in line]
    own, near1, near2 = y * 2 + x, y1 * 2 + x1, y2 * 2 + x2
    far = (1 - y) * 2 + 1 - x
    order = (far, near1, near2, own)
    group = quad(x, c)
    others = []
    for k in range(1, 32):
        t = lax.rem(me + k, 32)
        others.append((t, (t // 8, lax.rem(t, 8))))
    meet([device for _, device in others])
    move = Mover(send_sem, local_sem, other_core)
    zero = move.zero
    parts = (gu, gi, go, gs)
    halves = (ou, oi, oo, os_)
    results = (out_u, out_i, out_o, out_s)
    r1, r2 = (r1u, r1i, r1o, r1s), (r2u, r2i, r2o, r2s)
    r3, r4 = (r3u, r3i, r3o, r3s), (r4u, r4i, r4o, r4s)
    for i in (0, 2, 3, 1):
        for quarter in order:
            move.push(
                parts[i].at[quarter, :, 1 - c], r1[i].at[quarter], sem1.at[i, quarter], other_core
            )
    for i in range(4):
        move.keep(parts[i].at[:, :, c], halves[i])
    move.keep(first_far, first_low)

    def gather(i, quarter):
        move.landed(r1[i].at[quarter], sem1.at[zero + i, quarter])
        r1[i][quarter] = (wide(r1[i][quarter]) + wide(halves[i][quarter])).astype(r1[i].dtype)

    def stage2(i):
        for slot, quarter in ((1, far), (0, near1)):
            gather(i, quarter)
            move.push_made(
                lambda slot=slot, quarter=quarter: (
                    r1[i].at[quarter], r2[i].at[zero + slot], sem2.at[zero + i, zero + slot]
                ),
                first,
            )

    def stage3(i):
        gather(i, near2)
        move.landed(r2[i].at[zero + 1], sem2.at[zero + i, zero + 1])
        r1[i][near2] = (wide(r1[i][near2]) + wide(r2[i][1])).astype(r1[i].dtype)
        move.push_made(lambda: (r1[i].at[near2], r3[i], sem3.at[zero + i]), second)

    def stage4(i):
        gather(i, own)
        move.landed(r2[i].at[zero], sem2.at[zero + i, zero])
        move.landed(r3[i], sem3.at[zero + i])
        r1[i][own] = (wide(r1[i][own]) + wide(r2[i][0]) + wide(r3[i][...])).astype(r1[i].dtype)
        for k in range(3):
            move.push_made(
                lambda k=k: (r1[i].at[own, line[k]], r4[i].at[zero + k], sem4.at[zero + i, zero + k]),
                line_devices[k],
            )

    def stage5(i):
        total = wide(r1[i][own, z])
        for k in range(3):
            move.landed(r4[i].at[k], sem4.at[i, k])
            total = total + wide(r4[i][k])
        results[i][...] = total

    rows_all = query.shape[1]
    piece = tok_own.shape[1]
    rows = tok_own.shape[0] * piece
    width = tok_own.shape[2]
    scale = DH ** (-0.5)
    eye = jnp.eye(DH, 2 * DH, dtype=bf16)
    side_lane = lax.broadcasted_iota(jnp.int32, (BACK_ROWS, DH), 1)
    per_head = rows_all // BACK_ROWS
    between = {
        1: lambda: stage2(0),
        2: lambda: (stage2(2), stage2(3)),
        3: lambda: stage2(1),
        6: lambda: stage3(0),
        7: lambda: (stage3(2), stage3(3)),
        9: lambda: stage4(0),
        10: lambda: (stage4(2), stage4(3)),
        11: lambda: stage3(1),
    }
    for n in range(4):
        move.kept(n)
    for h in range(3):
        for k in range(rows_all // KEY_ROWS):
            turned[k] = dot(eye, key[h, k * KEY_ROWS : (k + 1) * KEY_ROWS, :], NT).astype(bf16)
        sums[...] = jnp.zeros_like(sums)
        lanes = slice(h * DH, (h + 1) * DH)

        def block(i, _):
            here = pl.ds(i * BACK_ROWS, BACK_ROWS)
            queries = query[h, here, :]
            backs = back_context[i // 2, lax.rem(i, 2)].reshape(BACK_ROWS, GROUP)[:, lanes]
            spread = jnp.sum(wide(backs) * wide(context[here, lanes]), axis=1, keepdims=True)
            high, mid, low = three(spread)
            side = jnp.where(
                side_lane == 0, -high, jnp.where(side_lane == 1, -mid, jnp.where(side_lane == 2, -low, 0.0))
            )
            widened = jnp.concatenate([backs, side.astype(bf16)], axis=1)

            def part(k, back_query):
                keys = pl.ds(k * KEY_ROWS, KEY_ROWS)
                chances = jnp.exp(dot(key[h, keys, :], queries, NT))
                back_scores = (chances * dot(value[h, keys, :], widened, NT)).astype(bf16)
                sums[keys, :DH] += dot(back_scores, queries[:, :DH])
                sums[keys, DH:] += dot(chances.astype(bf16), backs)
                return back_query + dot(turned[k], back_scores)

            back_query = jnp.zeros((DH, BACK_ROWS), f32)
            back_query = lax.fori_loop(0, rows_all // KEY_ROWS, part, back_query)
            joint[here, lanes] = (back_query * scale).T.astype(bf16)
            for step, action in between.items():
                if step // per_head == h:

                    @pl.when(i == step % per_head)
                    def _(action=action):
                        action()

            return 0

        lax.fori_loop(0, per_head, block, 0)
        joint[:, GROUP + h * DH : GROUP + (h + 1) * DH] = sums[:, :DH].astype(bf16)
        joint[:, 2 * GROUP + h * DH : 2 * GROUP + (h + 1) * DH] = sums[:, DH:].astype(bf16)

    for k in range(2):
        for yy in range(2):
            xx = lax.rem(x + 1 + k, 2)
            here = pl.ds((yy * 2 + xx) * rows, rows)
            back_first[yy, xx] = dot(joint[here, :], joint_weight[...], NT).astype(bf16).reshape(4, 2, piece, width)
            move.push(back_first.at[yy, xx, :, 1 - c], rc.at[yy, xx], sem_c.at[yy, xx], other_core)
    move.kept(4)
    grad = dot(first_low[...], joint[...], TN)
    lead = width // 32
    for block_at in range(32):
        gj[block_at // 16, block_at // 8 % 2, block_at % 8 // 2, block_at % 2] = grad[
            block_at * lead : (block_at + 1) * lead, :
        ].astype(bf16)
    move.push(gj.at[1 - y], ry, sem_y, down)
    for yy in range(2):
        move.landed(rc.at[yy, 1 - x], sem_c.at[yy, 1 - x])
        rc[yy, 1 - x] = (wide(rc[yy, 1 - x]) + wide(back_first[yy, 1 - x, :, c])).astype(bf16)
        move.push(rc.at[yy, 1 - x], rx.at[yy], sem_x.at[yy], across)
    stage4(1)
    shifts = jnp.sum(wide(joint[...]), axis=0, keepdims=True)
    small[...] = jnp.zeros_like(small)
    for k in range(8):
        for row, kind in ((2, 0), (3, 2)):
            start = kind * GROUP + k * lead
            small[mine * 8 + k, row : row + 1, :lead] = shifts[:, start : start + lead]
    move.landed(ry, sem_y)
    ry[...] = (wide(ry[...]) + wide(gj[y])).astype(bf16)
    for k in range(3):
        move.push(ry.at[:, line[k]], rz.at[k], sem_z.at[k], line_devices[k])
    for yy in range(2):
        move.landed(rc.at[yy, x], sem_c.at[yy, x])

    inputs = wide(tok_own[...].reshape(rows, width))
    centered = inputs - mean_of(inputs)
    inverse = lax.rsqrt(mean_of(centered * centered) + EPS)
    unit = centered * inverse
    halves_rows = []
    for yy in range(2):
        move.landed(rx.at[yy], sem_x.at[yy])
        whole = wide(rc[yy, x]) + wide(back_first[yy, x, :, c]) + wide(rx[yy])
        halves_rows.append(whole.reshape(rows // 2, width))
    back_one = jnp.concatenate(halves_rows, axis=0)
    scaled = back_one * vectors[0:1, :]
    back_tokens = back_residual[...] + inverse * (scaled - mean_of(scaled) - unit * mean_of(scaled * unit))
    gradient_low[...] = back_tokens.astype(bf16).reshape(8, piece, width)
    for k in range(1, 8):
        yy, zz = column(lax.rem(spot + k, 8))
        move.push(gradient_low.at[yy * 4 + zz], tokens_gradient.at[spot], sem_t.at[spot], at(yy, x, zz, c))
    kept = [move.keep(gradient_low.at[spot], tokens_gradient.at[spot])]
    gains = jnp.concatenate(
        [jnp.sum(back_one * unit, axis=0, keepdims=True), jnp.sum(back_one, axis=0, keepdims=True)], axis=0
    )
    for block_at in range(32):
        small[block_at, 0:2, :lead] = gains[:, block_at * lead : (block_at + 1) * lead]
    for t, device in others:
        move.push(small.at[t], small_all.at[me], sem_s.at[me], device)
    kept.append(move.keep(small.at[me], small_all.at[me]))

    total = wide(ry[:, z])
    for k in range(3):
        move.landed(rz.at[k], sem_z.at[k])
        total = total + wide(rz[k])
    sj[...] = total
    for xx, cc in group:
        move.push(sj.at[xx, cc], joint_land.at[mine], sem_g.at[mine], at(y, xx, z, cc))
    gone = move.keep(sj.at[x, c], joint_land.at[mine])
    for i in (0, 2, 3, 1):
        stage5(i)
    move.kept(gone)
    for xx, cc in group:
        move.landed(joint_land.at[xx * 2 + cc], sem_g.at[xx * 2 + cc])
    for g in range(4):
        for kind in range(3):
            start = kind * width + g * GROUP
            out_joint[:, start : start + GROUP] = joint_land[g, :, kind * GROUP : (kind + 1) * GROUP]
    for spot_kept in kept:
        move.kept(spot_kept)
    for t, _ in others:
        move.landed(small_all.at[t], sem_s.at[t])
    late[...] = jnp.sum(small_all[...], axis=0)
    for k in range(1, 8):
        t = lax.rem(spot + 8 - k, 8)
        move.landed(tokens_gradient.at[t], sem_t.at[t])
    move.finish()


def owner_device(
    tokens,
    lengths,
    first_gain,
    first_bias,
    joint_weight,
    query_bias,
    value_bias,
    output_weight,
    output_bias,
    second_gain,
    second_bias,
    inner_weight,
    inner_bias,
    outer_weight,
    outer_bias,
    cotangent,
):
    bf16, f32 = jnp.bfloat16, jnp.float32
    y, x, z, c = place()
    mine = x * 2 + c
    slots, piece, width = tokens.shape
    ff = inner_weight.shape[1]
    short = jnp.stack(
        [first_gain, first_bias, query_bias, value_bias, output_bias, second_gain, second_bias, outer_bias]
    )
    lead = short.shape[1]
    ff_piece = inner_bias.shape[0]
    small = jnp.concatenate(
        [
            jnp.pad(short, ((0, 0), (0, ff_piece - lead))),
            jnp.broadcast_to(inner_bias, (8, ff_piece)),
        ],
        axis=0,
    )
    hbm, vmem = pltpu.HBM, pltpu.VMEM
    dma, regular = pltpu.SemaphoreType.DMA, pltpu.SemaphoreType.REGULAR
    rows_all = 32 * piece
    natural = (2, 2, 4, 2, piece)
    length = lax.dynamic_slice(lengths, (y * 4 + z,), (1,))
    joint_four = jnp.transpose(joint_weight.reshape(lead, 3, 4, GROUP), (2, 0, 1, 3)).reshape(4, lead, 3 * GROUP)
    forward_outs = [
        ((rows_all, width), bf16, hbm),
        ((3, rows_all, 2 * DH), bf16, hbm),
        ((3, rows_all, 2 * DH), bf16, hbm),
        ((3, rows_all, 2 * DH), bf16, hbm),
        ((rows_all, GROUP), bf16, vmem),
        ((4, 2, 4, piece, GROUP), bf16, vmem),
        ((8, piece, width), bf16, hbm),
        ((8, piece, width), bf16, hbm),
        ((32,) + output_weight.shape, bf16, hbm),
        ((32,) + inner_weight.shape, bf16, hbm),
        ((32,) + outer_weight.shape, bf16, hbm),
        ((32,) + small.shape, bf16, vmem),
        ((width, 3 * GROUP), bf16, vmem),
    ]
    (
        first_low, query, key, value, context, context_rows, cot_own, tok_own, wo_all, wi_all, wu_all, small_all, joint_here
    ) = comm_call(
        forward_kernel,
        forward_outs,
        (length, tokens, cotangent, joint_four, output_weight, inner_weight, outer_weight, small),
        220, 24,
        [(32,), (8,), (3, 32), (32,), (4,), (4,), (4,), (4, 2), (4, 4), (4,)],
        [
            vmem((32, piece, width), bf16),
            vmem((2, 2, 4, 2, lead, 3 * GROUP), bf16),
            vmem((8, width), f32),
            vmem((3, 72, rows_all), bf16),
            vmem(natural + (GROUP,), bf16),
            vmem((rows_all, 512), f32),
            vmem((rows_all, 512), f32),
            vmem((3, 512, DH), bf16),
            vmem((rows_all, width), bf16),
            vmem((3, rows_all, 2 * DH), bf16),
            vmem((3, rows_all, 2 * DH), bf16),
            vmem((3, rows_all, 2 * DH), bf16),
        ],
        0,
        [pltpu.SMEM, hbm, hbm, hbm, hbm, hbm, hbm, hbm],
    )
    vectors = jnp.transpose(small_all[:, :2, :lead], (1, 0, 2)).reshape(2, width).astype(f32)
    rows = 8 * piece
    grid = (4, 4, 2)
    kinds = [
        (outer_weight.shape, bf16),
        (inner_weight.shape, bf16),
        (output_weight.shape, bf16),
        ((8, 128), f32),
    ]
    gu, gi, go, gs, output, back_context, back_residual = comm_call(
        feed_kernel,
        [(grid + shape, dtype, hbm) for shape, dtype in kinds]
        + [
            (tokens.shape, bf16, hbm),
            (natural + (GROUP,), bf16, vmem),
            ((rows, width), f32, vmem),
        ],
        (
            length, context_rows.reshape(4, 8, piece, GROUP), tok_own, cot_own, wo_all.reshape(width, width), small_all,
            wi_all.reshape(width, ff), wu_all.reshape(grid + outer_weight.shape),
        ),
        20, 20, [(8,), (4, 2)],
        [vmem(grid + shape, dtype) for shape, dtype in kinds]
        + [
            vmem((width, ff), bf16),
            vmem((4, 8, piece, GROUP), bf16),
            vmem((8, width), f32),
            vmem((1, ff), f32),
            vmem((rows, ff), bf16),
            vmem((rows, ff), bf16),
            vmem((8, piece, width), bf16),
        ],
        1,
        [pltpu.SMEM] + [vmem] * 5 + [hbm] * 2,
    )
    out_o, out_i, out_u, out_s, joint_shard, tokens_gradient, late = comm_call(
        backward_kernel,
        [
            (output_weight.shape, f32, vmem),
            (inner_weight.shape, f32, vmem),
            (outer_weight.shape, f32, vmem),
            ((8, 128), f32, vmem),
            (joint_weight.shape, f32, vmem),
            (tokens.shape, bf16, hbm),
            ((8, 128), f32, vmem),
        ],
        (
            gu, gi, go, gs, query, key, value, context, back_context, joint_here, first_low, tok_own, back_residual, vectors,
        ),
        110, 16,
        [(4, 4), (4, 2), (4,), (4, 3), (), (3,), (4,), (2, 2), (2,), (8,), (32,)],
        [vmem((4, 4) + shape, dtype) for shape, dtype in kinds]
        + [vmem((2, 4) + shape, dtype) for shape, dtype in kinds]
        + [vmem((4,) + shape, dtype) for shape, dtype in kinds]
        + [vmem((3,) + shape, dtype) for shape, dtype in kinds]
        + [vmem((4, 4) + shape, dtype) for shape, dtype in kinds]
        + [
            vmem((rows_all, 3 * GROUP), bf16),
            vmem((rows_all, 2 * DH), f32),
            vmem((rows_all // KEY_ROWS, DH, KEY_ROWS), bf16),
            vmem((rows_all, width), bf16),
            vmem(natural + (width,), bf16),
            vmem((2, 2, 4, piece, width), bf16),
            vmem((2, 4, piece, width), bf16),
            vmem((2, 2, 4, 2, lead, 3 * GROUP), bf16),
            vmem((2, 4, 2, lead, 3 * GROUP), bf16),
            vmem((3, 2, 2, lead, 3 * GROUP), bf16),
            vmem((2, 2, lead, 3 * GROUP), f32),
            vmem((4, lead, 3 * GROUP), f32),
            vmem((8, piece, width), bf16),
            vmem((32, 8, 128), f32),
            vmem((32, 8, 128), f32),
        ],
        2,
        [hbm] * 4 + [vmem] * 6 + [hbm] + [vmem] * 3,
    )
    count = jnp.sum(lengths).astype(f32) * width
    stats = jnp.sqrt(out_s[5, :3] / count + 1e-06)
    return (
        output,
        tokens_gradient,
        late[0, :lead],
        late[1, :lead],
        joint_shard,
        late[2, :lead],
        late[3, :lead],
        out_o,
        out_s[3, :lead],
        out_s[1, :lead],
        out_s[2, :lead],
        out_i,
        out_s[4, : inner_bias.shape[0]],
        out_u,
        out_s[0, :lead],
        stats,
    )


def solution(mesh):
    in_specs = (
        P(None, ("head", "blk"), None),
        P(),
        P(("head", "blk")),
        P(("head", "blk")),
        P(("head", "blk"), None),
        P(("head", "blk")),
        P(("head", "blk")),
        P(("head", "blk"), None),
        P(("head", "blk")),
        P(("head", "blk")),
        P(("head", "blk")),
        P(("head", "blk"), None),
        P(("head", "blk")),
        P(("head", "blk"), None),
        P(("head", "blk")),
        P(None, ("head", "blk"), None),
    )
    out_specs = (
        P(None, ("head", "blk"), None),
        P(None, ("head", "blk"), None),
        P(("head", "blk")),
        P(("head", "blk")),
        P(("head", "blk"), None),
        P(("head", "blk")),
        P(("head", "blk")),
        P(("head", "blk"), None),
        P(("head", "blk")),
        P(("head", "blk")),
        P(("head", "blk")),
        P(("head", "blk"), None),
        P(("head", "blk")),
        P(("head", "blk"), None),
        P(("head", "blk")),
        P(),
    )
    small_slice = dict(mesh.shape) == {"head": 4, "blk": 8}
    device_work = owner_device if small_slice else on_device
    return jax.shard_map(
        device_work, mesh=mesh, in_specs=in_specs, out_specs=out_specs, check_vma=False
    )
```

```python
import jax
import jax.numpy as jnp
from jax import lax
from jax.experimental import pallas as pl
from jax.experimental.pallas import tpu as pltpu
from jax.sharding import PartitionSpec as P

H = 12
DH = 64


EPS = 1e-12
NEG = -1e30


def passed_along(value, axis, steps):
    count = lax.axis_size(axis)
    pairs = [(source, (source + steps) % count) for source in range(count)]
    return lax.ppermute(value, axis, pairs)


def normalize(values, gain, shift):
    average = jnp.mean(values, axis=-1, keepdims=True)
    centered = values - average
    inverse = lax.rsqrt(jnp.mean(centered * centered, axis=-1, keepdims=True) + EPS)
    normed = centered * inverse
    return (normed * gain + shift, normed, inverse)


def normalize_back(incoming, normed, inverse, gain):
    scaled = incoming * gain
    inner = (
        scaled
        - jnp.mean(scaled, axis=-1, keepdims=True)
        - normed * jnp.mean(scaled * normed, axis=-1, keepdims=True)
    )
    return (
        inner * inverse,
        jnp.sum(incoming * normed, axis=(0, 1)),
        jnp.sum(incoming, axis=(0, 1)),
    )


def gelu_exact(values):
    return jax.nn.gelu(values, approximate=False)


def key_mask(lengths, source, piece_rows, block_count, head_count):
    rows_here = jnp.arange(head_count * piece_rows, dtype=jnp.int32)
    position = (
        rows_here // piece_rows * block_count + source
    ) * piece_rows + rows_here % piece_rows
    return position[None, :] < lengths[:, None]


def attend(query_part, state, keys_block, values_block, mask):
    best, total, running = state
    scores = jnp.einsum(
        "sqhd,skhd->sqhk", query_part, keys_block, preferred_element_type=jnp.float32
    ) * DH ** (-0.5)
    scores = jnp.where(mask[:, None, None, :], scores, NEG)
    fresh = jnp.maximum(best, jnp.max(scores, axis=-1))
    decay = jnp.exp(best - fresh)
    weights = jnp.exp(scores - fresh[..., None])
    total = total * decay + jnp.sum(weights, axis=-1)
    running = running * decay[..., None] + jnp.einsum(
        "sqhk,skhd->sqhd",
        weights.astype(jnp.bfloat16),
        values_block,
        preferred_element_type=jnp.float32,
    )
    return (fresh, total, running)


def block_grads(query_part, back_part, total_part, spread_part, keys_block, values_block, mask):
    scale = DH ** (-0.5)
    scores = (
        jnp.einsum("sqhd,skhd->sqhk", query_part, keys_block, preferred_element_type=jnp.float32)
        * scale
    )
    scores = jnp.where(mask[:, None, None, :], scores, NEG)
    chances = jnp.exp(scores - total_part[..., None])
    back_chances = jnp.einsum(
        "sqhd,skhd->sqhk", back_part, values_block, preferred_element_type=jnp.float32
    )
    back_scores = (chances * (back_chances - spread_part[..., None])).astype(jnp.bfloat16)
    query_step = (
        jnp.einsum("sqhk,skhd->sqhd", back_scores, keys_block, preferred_element_type=jnp.float32)
        * scale
    )
    key_step = (
        jnp.einsum("sqhk,sqhd->skhd", back_scores, query_part, preferred_element_type=jnp.float32)
        * scale
    )
    value_step = jnp.einsum(
        "sqhk,sqhd->skhd",
        chances.astype(jnp.bfloat16),
        back_part,
        preferred_element_type=jnp.float32,
    )
    return (query_step, key_step, value_step)


def on_device(
    tokens,
    lengths,
    first_gain,
    first_bias,
    joint_weight,
    query_bias,
    value_bias,
    output_weight,
    output_bias,
    second_gain,
    second_bias,
    inner_weight,
    inner_bias,
    outer_weight,
    outer_bias,
    cotangent,
):
    head_count = lax.axis_size("head")
    block_count = lax.axis_size("blk")
    block = lax.axis_index("blk")
    quarter = lax.axis_index("head")
    (
        gain_one,
        shift_one,
        joint_full,
        query_shift,
        value_shift,
        output_full,
        output_shift,
        gain_two,
        shift_two,
        inner_full,
        inner_shift,
        outer_full,
        outer_shift,
    ) = (
        lax.all_gather(first_gain, ("head", "blk"), axis=0, tiled=True),
        lax.all_gather(first_bias, ("head", "blk"), axis=0, tiled=True),
        lax.all_gather(joint_weight, ("head", "blk"), axis=0, tiled=True),
        lax.all_gather(query_bias, ("head", "blk"), axis=0, tiled=True),
        lax.all_gather(value_bias, ("head", "blk"), axis=0, tiled=True),
        lax.all_gather(output_weight, ("head", "blk"), axis=0, tiled=True),
        lax.all_gather(output_bias, ("head", "blk"), axis=0, tiled=True),
        lax.all_gather(second_gain, ("head", "blk"), axis=0, tiled=True),
        lax.all_gather(second_bias, ("head", "blk"), axis=0, tiled=True),
        lax.all_gather(inner_weight, ("head", "blk"), axis=0, tiled=True),
        lax.all_gather(inner_bias, ("head", "blk"), axis=0, tiled=True),
        lax.all_gather(outer_weight, ("head", "blk"), axis=0, tiled=True),
        lax.all_gather(outer_bias, ("head", "blk"), axis=0, tiled=True),
    )
    sequences, piece_rows, width = tokens.shape
    heads_here = H // head_count
    head_width = heads_here * DH
    rows = head_count * piece_rows
    shape_heads = (sequences, rows, heads_here, DH)
    shape_flat = (sequences, rows, head_width)
    own_position = (quarter * block_count + block) * piece_rows + jnp.arange(
        piece_rows, dtype=jnp.int32
    )
    valid = own_position[None, :] < lengths[:, None]
    keep = valid[..., None]
    inputs = tokens.astype(jnp.float32)
    gain_one_wide = gain_one.astype(jnp.float32)
    gain_two_wide = gain_two.astype(jnp.float32)
    first_out, first_unit, first_scale = normalize(
        inputs, gain_one_wide, shift_one.astype(jnp.float32)
    )
    first_low = first_out.astype(jnp.bfloat16)
    joint = jnp.einsum("scd,de->sce", first_low, joint_full, preferred_element_type=jnp.float32)
    query_flat = (joint[..., :width] + query_shift.astype(jnp.float32)).astype(jnp.bfloat16)
    key_flat = joint[..., width : 2 * width].astype(jnp.bfloat16)
    value_flat = (joint[..., 2 * width :] + value_shift.astype(jnp.float32)).astype(jnp.bfloat16)
    query_flat, key_flat, value_flat = (
        lax.all_to_all(query_flat, "head", split_axis=2, concat_axis=1, tiled=True),
        lax.all_to_all(key_flat, "head", split_axis=2, concat_axis=1, tiled=True),
        lax.all_to_all(value_flat, "head", split_axis=2, concat_axis=1, tiled=True),
    )
    query_rows = query_flat.reshape(shape_heads)
    key_rows = key_flat.reshape(shape_heads)
    value_rows = value_flat.reshape(shape_heads)

    def visit(carry):
        keys_block, values_block, source, state = carry
        keys_block, values_block = passed_along((keys_block, values_block), "blk", 1)
        source = (source - 1) % block_count
        mask = key_mask(lengths, source, piece_rows, block_count, head_count)
        return (
            keys_block,
            values_block,
            source,
            attend(query_rows, state, keys_block, values_block, mask),
        )

    start_state = (
        jnp.full((sequences, rows, heads_here), NEG, jnp.float32),
        jnp.zeros((sequences, rows, heads_here), jnp.float32),
        jnp.zeros(shape_heads, jnp.float32),
    )
    first_state = attend(
        query_rows,
        start_state,
        key_rows,
        value_rows,
        key_mask(lengths, block, piece_rows, block_count, head_count),
    )
    carry = (key_rows, value_rows, block, first_state)
    carry = lax.fori_loop(0, block_count // 2 - 1, lambda turn, state: visit(visit(state)), carry)
    best, total, running = visit(carry)[3]
    context = running / total[..., None]
    log_total = best + jnp.log(total)
    context_low = context.astype(jnp.bfloat16).reshape(shape_flat)
    context_tokens = lax.all_to_all(context_low, "head", split_axis=1, concat_axis=2, tiled=True)
    branch = jnp.einsum(
        "sce,ed->scd", context_tokens, output_full, preferred_element_type=jnp.float32
    ) + output_shift.astype(jnp.float32)
    residual = inputs + branch
    second_out, second_unit, second_scale = normalize(
        residual, gain_two_wide, shift_two.astype(jnp.float32)
    )
    second_low = second_out.astype(jnp.bfloat16)
    inner = jnp.einsum(
        "scd,df->scf", second_low, inner_full, preferred_element_type=jnp.float32
    ) + inner_shift.astype(jnp.float32)
    activated = gelu_exact(inner).astype(jnp.bfloat16)
    feed = jnp.einsum(
        "scf,fd->scd", activated, outer_full, preferred_element_type=jnp.float32
    ) + outer_shift.astype(jnp.float32)
    result = residual + feed
    output = jnp.where(keep, result, 0.0).astype(jnp.bfloat16)
    sums = lax.psum(
        (
            jnp.sum(jnp.where(keep, result * result, 0.0)),
            jnp.sum(jnp.where(keep, branch * branch, 0.0)),
            jnp.sum(jnp.where(keep, feed * feed, 0.0)),
        ),
        ("head", "blk"),
    )
    count = jnp.sum(lengths).astype(jnp.float32) * width
    stats = jnp.sqrt(jnp.stack(sums) / count + 1e-06)
    back_result = jnp.where(keep, cotangent.astype(jnp.float32), 0.0)
    back_feed = back_result.astype(jnp.bfloat16)
    outer_gradient = jnp.einsum(
        "scf,scd->fd", activated, back_feed, preferred_element_type=jnp.float32
    )
    outer_shift_gradient = jnp.sum(back_feed.astype(jnp.float32), axis=(0, 1))
    back_active = jnp.einsum(
        "scd,fd->scf", back_feed, outer_full, preferred_element_type=jnp.float32
    )
    back_inner = jax.vjp(gelu_exact, inner)[1](back_active)[0].astype(jnp.bfloat16)
    inner_gradient = jnp.einsum(
        "scd,scf->df", second_low, back_inner, preferred_element_type=jnp.float32
    )
    inner_shift_gradient = jnp.sum(back_inner.astype(jnp.float32), axis=(0, 1))
    back_second = jnp.einsum(
        "scf,df->scd", back_inner, inner_full, preferred_element_type=jnp.float32
    )
    back_norm_two, gain_two_gradient, shift_two_gradient = normalize_back(
        back_second, second_unit, second_scale, gain_two_wide
    )
    back_residual = back_result + back_norm_two
    back_branch = back_residual.astype(jnp.bfloat16)
    output_gradient = jnp.einsum(
        "sce,scd->ed", context_tokens, back_branch, preferred_element_type=jnp.float32
    )
    output_shift_gradient = jnp.sum(back_branch.astype(jnp.float32), axis=(0, 1))
    back_context = jnp.einsum(
        "scd,ed->sce", back_branch, output_full, preferred_element_type=jnp.float32
    ).astype(jnp.bfloat16)
    back_context = lax.all_to_all(back_context, "head", split_axis=2, concat_axis=1, tiled=True)
    back_heads = back_context.reshape(shape_heads)
    spread = jnp.sum(back_heads.astype(jnp.float32) * context, axis=-1)
    zero_heads = jnp.zeros(shape_heads, jnp.float32)

    def pass_keys(carry):
        keys_block, values_block, key_sum, value_sum, query_sum, source = carry
        mask = key_mask(lengths, source, piece_rows, block_count, head_count)
        query_step, key_step, value_step = block_grads(
            query_rows, back_heads, log_total, spread, keys_block, values_block, mask
        )
        keys_block, values_block = passed_along((keys_block, values_block), "blk", 1)
        key_sum, value_sum = passed_along((key_sum + key_step, value_sum + value_step), "blk", 1)
        return (
            keys_block,
            values_block,
            key_sum,
            value_sum,
            query_sum + query_step,
            (source - 1) % block_count,
        )

    carry = (key_rows, value_rows, zero_heads, zero_heads, zero_heads, block)
    carry = lax.fori_loop(
        0, block_count // 2, lambda turn, state: pass_keys(pass_keys(state)), carry
    )
    key_sum, value_sum, query_sum = (carry[2], carry[3], carry[4])
    back_query, back_key, back_value = (
        lax.all_to_all(
            query_sum.astype(jnp.bfloat16).reshape(shape_flat),
            "head",
            split_axis=1,
            concat_axis=2,
            tiled=True,
        ),
        lax.all_to_all(
            key_sum.astype(jnp.bfloat16).reshape(shape_flat),
            "head",
            split_axis=1,
            concat_axis=2,
            tiled=True,
        ),
        lax.all_to_all(
            value_sum.astype(jnp.bfloat16).reshape(shape_flat),
            "head",
            split_axis=1,
            concat_axis=2,
            tiled=True,
        ),
    )
    back_joint = jnp.concatenate([back_query, back_key, back_value], axis=-1)
    joint_gradient = jnp.einsum(
        "scd,sce->de", first_low, back_joint, preferred_element_type=jnp.float32
    )
    query_shift_gradient = jnp.sum(back_query.astype(jnp.float32), axis=(0, 1))
    value_shift_gradient = jnp.sum(back_value.astype(jnp.float32), axis=(0, 1))
    back_first = jnp.einsum(
        "sce,de->scd", back_joint, joint_full, preferred_element_type=jnp.float32
    )
    back_norm_one, gain_one_gradient, shift_one_gradient = normalize_back(
        back_first, first_unit, first_scale, gain_one_wide
    )
    tokens_gradient = (back_residual + back_norm_one).astype(jnp.bfloat16)
    shards = (
        lax.psum_scatter(gain_one_gradient, ("head", "blk"), scatter_dimension=0, tiled=True),
        lax.psum_scatter(shift_one_gradient, ("head", "blk"), scatter_dimension=0, tiled=True),
        lax.psum_scatter(joint_gradient, ("head", "blk"), scatter_dimension=0, tiled=True),
        lax.psum_scatter(query_shift_gradient, ("head", "blk"), scatter_dimension=0, tiled=True),
        lax.psum_scatter(value_shift_gradient, ("head", "blk"), scatter_dimension=0, tiled=True),
        lax.psum_scatter(output_gradient, ("head", "blk"), scatter_dimension=0, tiled=True),
        lax.psum_scatter(output_shift_gradient, ("head", "blk"), scatter_dimension=0, tiled=True),
        lax.psum_scatter(gain_two_gradient, ("head", "blk"), scatter_dimension=0, tiled=True),
        lax.psum_scatter(shift_two_gradient, ("head", "blk"), scatter_dimension=0, tiled=True),
        lax.psum_scatter(inner_gradient, ("head", "blk"), scatter_dimension=0, tiled=True),
        lax.psum_scatter(inner_shift_gradient, ("head", "blk"), scatter_dimension=0, tiled=True),
        lax.psum_scatter(outer_gradient, ("head", "blk"), scatter_dimension=0, tiled=True),
        lax.psum_scatter(outer_shift_gradient, ("head", "blk"), scatter_dimension=0, tiled=True),
    )
    return (
        output,
        tokens_gradient,
        shards[0],
        shards[1],
        shards[2],
        shards[3],
        shards[4],
        shards[5],
        shards[6],
        shards[7],
        shards[8],
        shards[9],
        shards[10],
        shards[11],
        shards[12],
        stats,
    )


MESH = pl.DeviceIdType.MESH
WIDTH = H * DH
GROUP = 3 * DH
NT = (((1,), (1,)), ((), ()))
NN = (((1,), (0,)), ((), ()))


def place():
    head = lax.axis_index("head")
    blk = lax.axis_index("blk")
    return head // 2, lax.rem(head, 2), blk // 2, lax.rem(blk, 2)


def at(y, x, z, c):
    return (y * 2 + x, z * 2 + c)


def number(y, x, z, c):
    return y * 16 + x * 8 + z * 2 + c


def column(t):
    return t // 4, lax.rem(t, 4)


def meet(peers):
    barrier = pltpu.get_barrier_semaphore()
    for peer in peers:
        pl.semaphore_signal(barrier, inc=1, device_id=peer, device_id_type=MESH)
    pl.semaphore_wait(barrier, len(peers))


class Mover:
    def __init__(self, send_sem, local_sem, anyone):
        self.send_sem = send_sem
        self.local_sem = local_sem
        self.anyone = anyone
        self.zero = anyone[0] * 0
        self.sent = []
        self.local = []

    def push(self, source, target, sem, device):
        self.push_made(lambda: (source, target, sem), device)

    def push_made(self, make, device, when=None):
        spot = len(self.sent)
        self.sent.append((make, spot, device, when))
        under(when, lambda: self.copy(make, spot, device).start())

    def copy(self, make, spot, device):
        source, target, sem = make()
        return remote(source, target, self.send_sem.at[self.zero + spot], sem, device)

    def keep(self, source, target):
        parts = (source, target, self.local_sem.at[len(self.local)])
        pltpu.make_async_copy(*parts).start()
        self.local.append(parts)
        return len(self.local) - 1

    def kept(self, spot):
        pltpu.make_async_copy(*self.local[spot]).wait()

    def landed(self, target, sem):
        remote(target, target, self.send_sem.at[self.zero], sem, self.anyone).wait_recv()

    def finish(self, kept=()):
        for make, spot, device, when in self.sent:
            under(when, lambda: self.copy(make, spot, device).wait_send())
        for spot in kept:
            self.kept(spot)


def under(when, action):
    if when is None:
        action()
    else:

        @pl.when(when)
        def _():
            action()


def remote(source, target, send_sem, recv_sem, device):
    return pltpu.make_async_remote_copy(
        src_ref=source,
        dst_ref=target,
        send_sem=send_sem,
        recv_sem=recv_sem,
        device_id=device,
        device_id_type=MESH,
    )


def unpack(small_all, vectors):
    for block in range(32):
        tile = wide(small_all[block])
        vectors[:, block * 24 : block * 24 + 24] = tile[:8, :24]


def forward_kernel(
    length, tokens, cotangent, wj, wo, wi, wu, small,
    first_far, query_far, key_far, value_far, context, context_rows, cot_own, tok_own, wo_all, wi_all, wu_all, small_all, wj_flat,
    send_sem, local_sem, tok_sem, cot_sem, weight_sem, small_sem, wja_sem, wjb_sem, wjc_sem, ctx_send, ctx_recv,
    ctx_local, tok_all, wj_all, vectors, turned, mixed_low, score_a, score_b, straight_low, first_low, query, key, value,
):
    y, x, z, c = place()
    mine = number(y, x, z, c)
    quarter = x * 2 + c
    spot = y * 4 + z
    other_core = at(y, x, z, 1 - c)
    across = at(y, 1 - x, z, c)
    diagonal = at(y, 1 - x, z, 1 - c)
    down = at(1 - y, x, z, c)
    y1, x1 = jnp.where(c == 0, y, 1 - y), jnp.where(c == 0, 1 - x, x)
    y2, x2 = jnp.where(c == 0, 1 - y, y), jnp.where(c == 0, x, 1 - x)
    first, second = at(y1, x1, z, c), at(y2, x2, z, c)
    spots = [column(lax.rem(spot + k, 8)) for k in range(1, 8)]
    back_spots = [column(lax.rem(spot + 8 - k, 8)) for k in range(1, 8)]
    ahead = [at(y, x, lax.rem(z + k, 4), c) for k in range(1, 4)]
    inside = jnp.logical_or(z == 1, z == 2)
    lines = [
        z,
        jnp.where(z == 0, 1, z - 1),
        jnp.where(z == 0, 2, jnp.where(z == 3, 1, z + 1)),
        jnp.where(z < 2, 3, 0),
    ]
    onward = [z + 1, z - 1, jnp.where(z == 1, 0, 3)]
    away, back = at(y, x, jnp.where(z < 3, z + 1, z - 1), c), at(y, x, jnp.maximum(z - 1, 0), c)
    onward = [at(y, x, lax.rem(zz + 4, 4), c) for zz in onward]
    line_blocks = [number(y, x, zz, c) for zz in lines]
    first_blocks = [number(y1, x1, zz, c) for zz in lines]
    second_blocks = [number(yy, xx, zz, c) for zz in lines for yy, xx in ((y2, x2), (1 - y, 1 - x))]
    core_blocks = [number(yy, xx, zz, 1 - c) for yy in range(2) for xx in range(2) for zz in range(4)]
    group = quad(x, c)
    meet([at(yy, x, zz, c) for yy, zz in spots] + [across, other_core, diagonal])
    move = Mover(send_sem, local_sem, other_core)
    sources = (wo, wi, wu)
    wholes = (wo_all, wi_all, wu_all)

    def hand(block, own, device, when=None):
        for i in range(3):
            move.push_made(
                lambda i=i: (
                    sources[i] if own else wholes[i].at[block],
                    wholes[i].at[block],
                    weight_sem.at[move.zero + i, block],
                ),
                device,
                when,
            )

    def arrive(block):
        for i in range(3):
            move.landed(wholes[i].at[block], weight_sem.at[i, block])

    def pass_small(blocks, devices):
        for block in blocks:
            move.landed(small_all.at[block], small_sem.at[block])
            for device in devices:
                move.push(small_all.at[block], small_all.at[block], small_sem.at[block], device)

    def spread(block, own):
        for device in (first, second, other_core):
            hand(block, own, device)

    def line_arrived(k):
        arrive(line_blocks[k])
        hand(line_blocks[k], False, onward[k - 1], inside)
        spread(line_blocks[k], False)

    def second_hand(k):
        arrive(first_blocks[k])
        hand(first_blocks[k], False, second)
        hand(first_blocks[k], False, other_core)

    def last_hand(k):
        for b in second_blocks[2 * k : 2 * k + 2]:
            arrive(b)
            hand(b, False, other_core)

    for device in ahead + [first, second, other_core]:
        move.push(small, small_all.at[mine], small_sem.at[mine], device)
    for xx, cc in group:
        move.push(wj.at[xx * 2 + cc], wj_all.at[y, x, z, c], wja_sem.at[quarter], at(y, xx, z, cc))
    move.keep(wj.at[quarter], wj_all.at[y, x, z, c])
    move.keep(tokens.at[spot], tok_all.at[mine])
    move.keep(small, small_all.at[mine])
    for yy, zz in spots:
        move.push(tokens.at[yy * 4 + zz], tok_all.at[mine], tok_sem.at[mine], at(yy, x, zz, c))
    for device in (across, other_core):
        move.push(tokens.at[spot], tok_all.at[mine], tok_sem.at[mine], device)
    spread(mine, True)
    for source, whole in zip(sources, wholes):
        move.keep(source, whole.at[mine])

    def slice_onward(zz, device, when):
        move.push_made(lambda: (wj_all.at[y, :, zz], wj_all.at[y, :, zz], wjb_sem.at[zz]), device, when)

    for xx, cc in group:
        move.landed(wj_all.at[y, xx, z, cc], wja_sem.at[xx * 2 + cc])
    move.kept(0)
    slice_onward(z, away, None)
    slice_onward(z, back, inside)
    move.push(wj_all.at[y, :, z], wj_all.at[y, :, z], wjc_sem.at[z], down)
    pass_small(line_blocks[1:], (first, second, other_core))
    pass_small(first_blocks, (second, other_core))
    for k in range(1, 4):
        zz = lines[k]
        move.landed(wj_all.at[y, :, zz], wjb_sem.at[zz])
        slice_onward(zz, onward[k - 1], inside)
        move.push(wj_all.at[y, :, zz], wj_all.at[y, :, zz], wjc_sem.at[zz], down)
    pass_small(second_blocks, (other_core,))
    for yy, zz in back_spots:
        block = number(yy, x, zz, c)
        move.landed(tok_all.at[block], tok_sem.at[block])
        move.push(tok_all.at[block], tok_all.at[block], tok_sem.at[block], across)
        move.push(tok_all.at[block], tok_all.at[block], tok_sem.at[block], other_core)
    hand(mine, True, away)
    hand(mine, True, back, inside)
    second_hand(0)
    for yy, zz in [(y, z)] + back_spots:
        block = number(yy, 1 - x, zz, c)
        move.landed(tok_all.at[block], tok_sem.at[block])
        move.push(tok_all.at[block], tok_all.at[block], tok_sem.at[block], other_core)
    for block in core_blocks:
        move.landed(small_all.at[block], small_sem.at[block])
    for zz in lines:
        move.landed(wj_all.at[1 - y, :, zz], wjc_sem.at[zz])
    line_arrived(1)
    for yy, zz in spots:
        move.push(cotangent.at[yy * 4 + zz], cot_own.at[spot], cot_sem.at[spot], at(yy, x, zz, c))
    move.keep(cotangent.at[spot], cot_own.at[spot])
    for yy, zz in [(y, z)] + back_spots:
        for xx in (x, 1 - x):
            block = number(yy, xx, zz, 1 - c)
            move.landed(tok_all.at[block], tok_sem.at[block])
    move.kept(1)
    move.kept(2)

    unpack(small_all, vectors)
    rows = query.shape[1]
    for yy in range(2):
        for xx in range(2):
            for zz in range(4):
                pair = jnp.concatenate([wide(wj_all[yy, xx, zz, cc]) for cc in range(2)], axis=0)
                row = number(yy, xx, zz, 0) * 24
                wj_flat[row : row + 48, :] = pair.astype(jnp.bfloat16)
    lane = lax.broadcasted_iota(jnp.int32, (ROWS, DH), 1)
    row_at = lax.broadcasted_iota(jnp.int32, (ROWS, DH), 0)
    one_lane = jnp.where(lane == 0, 1.0, 0.0).astype(jnp.bfloat16)
    three_lanes = jnp.where(lane < 3, 1.0, 0.0).astype(jnp.bfloat16)
    gain, shift = vectors[0:1, :], vectors[1:2, :]
    query_all, value_all = vectors[2:3, :], vectors[3:4, :]

    def chosen(whole):
        total = jnp.zeros((1, GROUP), jnp.float32)
        for q in range(4):
            total = jnp.where(quarter == q, whole[:, q * GROUP : (q + 1) * GROUP], total)
        return total

    query_shift, value_shift = chosen(query_all), chosen(value_all)
    blocks = ROWS // tokens.shape[1]

    def project(i, _):
        here = pl.ds(i * ROWS, ROWS)
        raw = tok_all[pl.ds(i * blocks, blocks)].reshape(ROWS, WIDTH)
        normed = normalize(wide(raw), gain, shift)[0].astype(jnp.bfloat16)
        first_low[here, :] = normed
        joint = dot(normed, wj_flat[...])
        low_q = ((joint[:, :GROUP] + query_shift).astype(jnp.bfloat16) * DH ** (-0.5)).astype(jnp.bfloat16)
        low_k = joint[:, GROUP : 2 * GROUP].astype(jnp.bfloat16)
        low_v = (joint[:, 2 * GROUP :] + value_shift).astype(jnp.bfloat16)
        mask = jnp.where(row_at + i * ROWS < length[0], 0.0, NEG)
        key_side = jnp.where(lane == 0, mask, jnp.where(lane < 4, 1.0, 0.0)).astype(jnp.bfloat16)
        for h in range(3):
            here_h = slice(h * DH, (h + 1) * DH)
            query[h, here, :] = jnp.concatenate([low_q[:, here_h], one_lane], axis=1)
            key[h, here, :] = jnp.concatenate([low_k[:, here_h], key_side], axis=1)
            value[h, here, :] = jnp.concatenate([low_v[:, here_h], three_lanes], axis=1)
        return 0

    for i in range(rows // ROWS):
        project(i, 0)
    for source, target in ((first_low, first_far), (key, key_far), (value, value_far)):
        move.keep(source, target)
    eye = jnp.eye(72, 2 * DH, dtype=jnp.bfloat16)
    for h in range(3):
        turned[h] = dot(eye, value[h], NT).astype(jnp.bfloat16)
    wider = score_a.shape[1]
    side = lax.broadcasted_iota(jnp.int32, (DH, wider), 0)
    chunk = 512
    units = 3 * rows // wider

    def ctx_copy(j, cc, for_local, for_remote):
        yy, xx = j // 2, lax.rem(j, 2)
        source, target = mixed_low.at[yy, xx, :, cc], context_rows.at[quarter, yy]
        here = jnp.logical_and(xx == x, c == cc)

        @pl.when(here)
        def _():
            for_local(pltpu.make_async_copy(source, target, ctx_local.at[j]))

        @pl.when(jnp.logical_not(here))
        def _():
            for_remote(remote(source, target, ctx_send.at[j, cc], ctx_recv.at[quarter, j], at(y, xx, z, cc)))

    def score_chunk(held, h, queries, k, best):
        fresh = dot(key[h, k * chunk : (k + 1) * chunk, :], queries, NT)
        held[k * chunk : (k + 1) * chunk, :] = fresh
        return jnp.maximum(best, jnp.max(fresh, axis=0, keepdims=True))

    lowest = jnp.full((1, wider), -jnp.inf, jnp.float32)
    start = lowest
    for k in range(rows // chunk):
        start = score_chunk(score_a, 0, query[0, :wider, :], k, start)

    def unit(u, best, held, fresh):
        j = u // 3
        h = u - 3 * j
        u_next = jnp.minimum(u + 1, units - 1)
        j_next = u_next // 3
        h_next = u_next - 3 * j_next
        here = pl.ds(j * wider, wider)
        queries = query[h_next, pl.ds(j_next * wider, wider), :]
        best_next = lowest
        mixed = jnp.zeros((72, wider), jnp.float32)
        for k in range(rows // chunk):
            keys = slice(k * chunk, (k + 1) * chunk)
            weights = jnp.exp(held[keys, :] - best).astype(jnp.bfloat16)
            mixed = mixed + dot(turned[h, :, keys], weights)
            best_next = score_chunk(fresh, h_next, queries, k, best_next)
        total = mixed[DH : DH + 1, :]
        mixed = mixed[:DH, :] / total
        high, mid, low = three(best + jnp.log(total))
        extra = jnp.where(
            side == 0, 1.0, jnp.where(side == 1, -high, jnp.where(side == 2, -mid, jnp.where(side == 3, -low, 0.0)))
        )
        straight = jnp.concatenate([mixed, extra], axis=0).T
        query[h, here, DH:] = straight[:, DH:].astype(jnp.bfloat16)
        straight_low[h] = straight[:, :DH].astype(jnp.bfloat16)

        @pl.when(h == 2)
        def _():
            whole = jnp.concatenate([straight_low[k] for k in range(3)], axis=1)
            context[here, :] = whole
            mixed_low[j // 2, lax.rem(j, 2)] = whole.reshape(4, 2, tokens.shape[1], GROUP)
            for cc in range(2):
                ctx_copy(j, cc, lambda copy: copy.start(), lambda copy: copy.start())

        return best_next

    def pair(p, best):
        best = unit(2 * p, best, score_a, score_b)
        best = unit(2 * p + 1, best, score_b, score_a)
        for when, action in (
            (0, lambda: second_hand(1)),
            (1, lambda: line_arrived(2)),
            (2, lambda: (second_hand(2), last_hand(0))),
            (3, lambda: line_arrived(3)),
            (4, lambda: (second_hand(3), last_hand(1))),
        ):

            @pl.when(p == when)
            def _(action=action):
                action()

        return best

    lax.fori_loop(0, units // 2, pair, start)
    move.keep(query, query_far)
    last_hand(2)
    last_hand(3)
    for yy, zz in back_spots:
        move.landed(cot_own.at[yy * 4 + zz], cot_sem.at[yy * 4 + zz])
    for b in core_blocks:
        arrive(b)
    tok_copies = []
    for i in range(8):
        yy, zz = i // 4, i % 4
        tok_copies.append(pltpu.make_async_copy(tok_all.at[number(yy, x, zz, c)], tok_own.at[i], local_sem.at[8 + i]))
        tok_copies[-1].start()

    def settle(j, _):
        for cc in range(2):
            ctx_copy(j, cc, lambda copy: copy.wait(), lambda copy: copy.wait_send())
        return 0

    lax.fori_loop(0, 4, settle, 0)
    for xx, cc in group:
        for yy in range(2):
            move.landed(context_rows.at[xx * 2 + cc, yy], ctx_recv.at[xx * 2 + cc, yy * 2 + x])
    move.finish(range(3, len(move.local)))
    for copy in tok_copies:
        copy.wait()


def comm_call(kernel, outs, args, sends, locals_, sems, scratch, ident, space=None):
    space = space or [pltpu.HBM] * len(args)
    return pl.pallas_call(
        kernel,
        out_shape=[jax.ShapeDtypeStruct(shape, dtype) for shape, dtype, _ in outs],
        in_specs=[pl.BlockSpec(memory_space=one) for one in space],
        out_specs=[pl.BlockSpec(memory_space=one) for _, _, one in outs],
        scratch_shapes=[
            pltpu.SemaphoreType.DMA((sends,)),
            pltpu.SemaphoreType.DMA((max(locals_, 1),)),
            *[pltpu.SemaphoreType.DMA(shape) for shape in sems],
            *scratch,
        ],
        compiler_params=pltpu.CompilerParams(
            collective_id=ident, has_side_effects=True, vmem_limit_bytes=61 * 1024 * 1024
        ),
    )(*args)


def quad(x, c):
    return [(lax.rem(x + dx, 2), lax.rem(c + dc, 2)) for dx, dc in ((0, 1), (1, 0), (1, 1))]


def wide(value):
    return value.astype(jnp.float32)


def dot(a, b, dims=NN):
    return lax.dot_general(a, b, dims, preferred_element_type=jnp.float32)


ROWS = 256


TN = (((0,), (0,)), ((), ()))
BACK_ROWS = 1024
KEY_ROWS = 512


def three(value):
    high = value.astype(jnp.bfloat16).astype(jnp.float32)
    middle = (value - high).astype(jnp.bfloat16).astype(jnp.float32)
    return high, middle, value - high - middle


def mean_of(value):
    return jnp.mean(value, axis=-1, keepdims=True)


TN = (((0,), (0,)), ((), ()))
BACK_ROWS = 512
KEY_ROWS = 1024


def three(value):
    high = value.astype(jnp.bfloat16).astype(jnp.float32)
    middle = (value - high).astype(jnp.bfloat16).astype(jnp.float32)
    return high, middle, value - high - middle


def mean_of(value):
    return jnp.mean(value, axis=-1, keepdims=True)


def feed_kernel(
    length, context_rows_far, tok_far, cot_far, wo_far, small_all, wi_far, wu_far,
    hu_far, hi_far, ho_far, hs_far, output, back_context, back_residual,
    send_sem, local_sem, sem1, sem2, sem_out, sem_back,
    gu, gi, go, gs, wi, back_near, vectors, inner_shift, active, back_inner, output_low,
    r1u, r1i, r1o, r1s, r2u, context_rows, tok_own, cot_own, wo, load_sem,
):
    bf16, f32 = jnp.bfloat16, jnp.float32
    y, x, z, c = place()
    spot = y * 4 + z
    mine = x * 2 + c
    other_core = at(y, x, z, 1 - c)
    across = at(y, 1 - x, z, c)
    diagonal = at(y, 1 - x, z, 1 - c)
    spots = [column(lax.rem(spot + k, 8)) for k in range(1, 8)]
    y1, x1 = jnp.where(c == 0, y, 1 - y), jnp.where(c == 0, 1 - x, x)
    y2, x2 = jnp.where(c == 0, 1 - y, y), jnp.where(c == 0, x, 1 - x)
    first = at(y1, x1, z, c)
    own, near1, near2 = y * 2 + x, y1 * 2 + x1, y2 * 2 + x2
    far = (1 - y) * 2 + 1 - x
    order = (far, near1, near2, own)
    parts = (gu, gi, go, gs)
    r1 = (r1u, r1i, r1o, r1s)
    group = quad(x, c)
    move = Mover(send_sem, local_sem, other_core)
    width = wo.shape[0]
    ff = wi.shape[1]
    steps = ff // width
    for source, target in ((context_rows_far, context_rows), (wo_far, wo), (tok_far, tok_own), (cot_far, cot_own)):
        move.keep(source, target)

    def weights_load(step):
        cols = pl.ds(pl.multiple_of(step * width, width), width)
        return (
            pltpu.make_async_copy(wi_far.at[:, cols], wi.at[:, cols], load_sem.at[step, 0]),
            pltpu.make_async_copy(wu_far.at[step], gu.at[step], load_sem.at[step, 1]),
        )

    def load(step, _):
        for copy in weights_load(step):
            copy.start()
        return 0

    lax.fori_loop(0, steps, load, 0)
    meet([at(yy, x, zz, c) for yy, zz in spots] + [across, other_core, diagonal])

    piece = tok_own.shape[1]
    rows = tok_own.shape[0] * piece
    unpack(small_all, vectors)
    ff_piece = ff // 32
    for block in range(32):
        inner_shift[:, block * ff_piece : (block + 1) * ff_piece] = wide(small_all[block])[8:9, :ff_piece]

    spot_at = lax.broadcasted_iota(jnp.int32, (8, piece, 1), 0)
    position = number(spot_at // 4, x, lax.rem(spot_at, 4), c) * piece
    position = position + lax.broadcasted_iota(jnp.int32, (8, piece, 1), 1)
    keep = jnp.where(position < length[0], 1.0, 0.0).reshape(rows, 1) > 0.5

    def column_sum(item):
        return jnp.sum(item, axis=0, keepdims=True)

    def square(item):
        return jnp.sum(item * item)

    for n in range(4):
        move.kept(n)
    branch = vectors[4:5, :] + dot(context_rows[0].reshape(rows, GROUP), wo[:GROUP, :])
    for g in range(1, 4):
        branch = branch + dot(context_rows[g].reshape(rows, GROUP), wo[g * GROUP : (g + 1) * GROUP, :])
    residual = wide(tok_own[...].reshape(rows, width)) + branch
    branch_total = square(jnp.where(keep, branch, 0.0))
    average = mean_of(residual)
    centered = residual - average
    inverse = lax.rsqrt(mean_of(centered * centered) + EPS)
    unit = centered * inverse
    second_low = (unit * vectors[5:6, :] + vectors[6:7, :]).astype(bf16)
    back_result = jnp.where(keep, wide(cot_own[...].reshape(rows, width)), 0.0)
    back_feed = back_result.astype(bf16)

    def middle(step, sums_here):
        back_second, feed = sums_here
        for copy in weights_load(step):
            copy.wait()
        cols = pl.ds(pl.multiple_of(step * width, width), width)
        wi_here = wi[:, cols]
        inner = dot(second_low, wi_here) + inner_shift[:, cols]
        chance = 0.5 * (1.0 + lax.erf(inner * 0.7071067811865476))
        low = (inner * chance).astype(bf16)
        active[:, cols] = low
        wu_here = gu[step].reshape(width, width)
        slope = chance + inner * jnp.exp(inner * inner * -0.5) * 0.3989422804014327
        back = (dot(back_feed, wu_here, NT) * slope).astype(bf16)
        back_inner[:, cols] = back
        return back_second + dot(back, wi_here, NT), feed + dot(low, wu_here)

    zero = jnp.zeros((rows, width), f32)
    back_second, feed = lax.fori_loop(0, steps, middle, (zero, zero))
    scaled = back_second * vectors[5:6, :]
    back_res = back_result + inverse * (scaled - mean_of(scaled) - unit * mean_of(scaled * unit))
    back_residual[...] = back_res
    back_branch = back_res.astype(bf16)
    short = jnp.concatenate(
        [
            column_sum(wide(back_feed)), column_sum(back_second * unit), column_sum(back_second),
            column_sum(wide(back_branch)), jnp.zeros((4, width), f32),
        ],
        axis=0,
    )
    for g in range(4):
        back_near[g] = dot(back_branch, wo[g * GROUP : (g + 1) * GROUP, :], NT).astype(bf16).reshape(8, piece, GROUP)
    for xx, cc in group[::-1]:
        for yy in range(2):
            move.push(
                back_near.at[xx * 2 + cc, pl.ds(yy * 4, 4)],
                back_context.at[yy, x, :, c],
                sem_back.at[mine, yy],
                at(y, xx, z, cc),
            )
    for yy in range(2):
        move.keep(back_near.at[mine, pl.ds(yy * 4, 4)], back_context.at[yy, x, :, c])

    feed = feed + vectors[7:8, :]
    result = jnp.where(keep, residual + feed, 0.0)
    output_low[...] = result.astype(bf16).reshape(8, piece, width)
    for yy, zz in spots:
        move.push(output_low.at[yy * 4 + zz], output.at[spot], sem_out.at[spot], at(yy, x, zz, c))
    move.keep(output_low.at[spot], output.at[spot])

    totals = (square(result), branch_total, square(jnp.where(keep, feed, 0.0)))
    lane = lax.broadcasted_iota(jnp.int32, (1, 128), 1)
    stat_row = jnp.where(lane == 0, totals[0], jnp.where(lane == 1, totals[1], jnp.where(lane == 2, totals[2], 0.0)))
    def to_core(i, quarter):
        move.push(parts[i].at[quarter, :, 1 - c], r1[i].at[quarter], sem1.at[i, quarter], other_core)

    def gather(i, quarter):
        move.landed(r1[i].at[quarter], sem1.at[i, quarter])
        r1[i][quarter] = r1[i][quarter] + parts[i][quarter, :, c]

    lead = width // 32
    wide_piece = ff // 32
    for step in range(steps):
        grad = dot(active[:, step * width : (step + 1) * width], back_feed, TN).astype(bf16)
        for zz in range(4):
            for cc in range(2):
                row = (zz * 2 + cc) * wide_piece
                gu[step, zz, cc] = grad[row : row + wide_piece, :]
        to_core(0, step)
    for step in range(steps):
        grad = dot(second_low, back_inner[:, step * width : (step + 1) * width], TN)
        for block in range(32):
            gi[block // 8, block % 8 // 2, block % 2, :, step * width : (step + 1) * width] = grad[
                block * lead : (block + 1) * lead, :
            ].astype(bf16)
    for quarter in order:
        to_core(1, quarter)
    for slot, quarter in ((1, far), (0, near1)):
        gather(0, quarter)
        move.push(r1u.at[quarter], r2u.at[slot], sem2.at[slot], first)
    for quarter in (near2, own):
        gather(0, quarter)
    for g in range(4):
        grad = dot(context_rows[g].reshape(rows, GROUP), back_branch, TN)
        for zz in range(4):
            for cc in range(2):
                row = (zz * 2 + cc) * lead
                go[g, zz, cc] = grad[row : row + lead, :].astype(bf16)
        to_core(2, g)

    long = column_sum(wide(back_inner[...]))
    for block in range(32):
        at_block = (block // 8, block % 8 // 2, block % 2)
        gs[at_block] = jnp.zeros((8, 128), f32)
        gs[at_block + (slice(0, 8), slice(0, lead))] = short[:, block * lead : (block + 1) * lead]
        gs[at_block + (slice(4, 5), slice(0, wide_piece))] = long[:, block * wide_piece : (block + 1) * wide_piece]
        gs[at_block + (slice(5, 6), slice(None))] = stat_row
    for quarter in order:
        to_core(3, quarter)
    for i in (1, 2, 3):
        for quarter in order:
            gather(i, quarter)
    for slot, quarter in ((1, near2), (0, own)):
        move.landed(r2u.at[slot], sem2.at[slot])
        r1u[quarter] = r1u[quarter] + r2u[slot]
    for source, target in zip(r1, (hu_far, hi_far, ho_far, hs_far)):
        move.keep(source, target)
    for xx, cc in group:
        for yy in range(2):
            move.landed(back_context.at[yy, xx, :, cc], sem_back.at[xx * 2 + cc, yy])
    for k in range(1, 8):
        t = lax.rem(spot + 8 - k, 8)
        move.landed(output.at[t], sem_out.at[t])
    move.finish(range(4, len(move.local)))


def backward_kernel(
    hu, hi, ho, hs, query_far, key_far, value_far, context_far, back_far, weight_far, first_far, tok_far, residual_far, vectors,
    out_o, out_i, out_u, out_s, out_joint, tokens_gradient, late,
    send_sem, local_sem, sem2, sem3, sem4, sem_y, sem_z, sem_g, sem_c, sem_x, sem_t, sem_s,
    r1u, r1i, r1o, r1s, r2u, r2i, r2o, r2s, r3u, r3i, r3o, r3s, r4u, r4i, r4o, r4s,
    joint, back_query, widened, query, key, value, context, back_context, joint_weight, tok_own, back_residual,
    first_low, back_first, rc, rx, gj, ry, rz, sj, joint_land, gradient_low, small, small_all,
):
    bf16, f32 = jnp.bfloat16, jnp.float32
    y, x, z, c = place()
    spot = y * 4 + z
    mine = x * 2 + c
    me = number(y, x, z, c)
    other_core = at(y, x, z, 1 - c)
    across = at(y, 1 - x, z, c)
    down = at(1 - y, x, z, c)
    y1, x1 = jnp.where(c == 0, y, 1 - y), jnp.where(c == 0, 1 - x, x)
    y2, x2 = jnp.where(c == 0, 1 - y, y), jnp.where(c == 0, x, 1 - x)
    first, second = at(y1, x1, z, c), at(y2, x2, z, c)
    line = [lax.rem(z + k, 4) for k in range(1, 4)]
    line_devices = [at(y, x, zz, c) for zz in line]
    own, near1, near2 = y * 2 + x, y1 * 2 + x1, y2 * 2 + x2
    far = (1 - y) * 2 + 1 - x
    order = (far, near1, near2, own)
    group = quad(x, c)
    others = []
    for k in range(1, 32):
        t = lax.rem(me + k, 32)
        others.append((t, (t // 8, lax.rem(t, 8))))
    move = Mover(send_sem, local_sem, other_core)
    move.keep(back_far, back_context)
    move.keep(context_far, context)
    for h in range(3):
        for source, target in ((key_far, key), (query_far, query), (value_far, value)):
            move.keep(source.at[h], target.at[h])
    meet([device for _, device in others])
    zero = move.zero
    sources = (hu, hi, ho, hs)
    results = (out_u, out_i, out_o, out_s)
    r1, r2 = (r1u, r1i, r1o, r1s), (r2u, r2i, r2o, r2s)
    r3, r4 = (r3u, r3i, r3o, r3s), (r4u, r4i, r4o, r4s)
    for i in range(4):
        move.keep(sources[i], r1[i])
    for source, target in (
        (weight_far, joint_weight), (first_far, first_low), (tok_far, tok_own), (residual_far, back_residual)
    ):
        move.keep(source, target)

    def stage2(i):
        for slot, quarter in ((1, far), (0, near1)):
            move.push_made(
                lambda slot=slot, quarter=quarter: (
                    sources[i].at[quarter], r2[i].at[zero + slot], sem2.at[zero + i, zero + slot]
                ),
                first,
            )

    def stage3(i):
        if i:
            move.landed(r2[i].at[zero + 1], sem2.at[zero + i, zero + 1])
            r1[i][near2] = r1[i][near2] + r2[i][1]
        source = r1[i] if i else sources[i]
        move.push_made(lambda: (source.at[near2], r3[i], sem3.at[zero + i]), second)

    def stage4(i):
        total = wide(r1[i][own])
        if i:
            move.landed(r2[i].at[zero], sem2.at[zero + i, zero])
            total = total + wide(r2[i][0])
        move.landed(r3[i], sem3.at[zero + i])
        r1[i][own] = (total + wide(r3[i][...])).astype(r1[i].dtype)
        for k in range(3):
            move.push_made(
                lambda k=k: (r1[i].at[own, line[k]], r4[i].at[zero + k], sem4.at[zero + i, zero + k]),
                line_devices[k],
            )

    def stage5(i):
        total = wide(r1[i][own, z])
        for k in range(3):
            move.landed(r4[i].at[k], sem4.at[i, k])
            total = total + wide(r4[i][k])
        results[i][...] = total

    rows_all = query.shape[1]
    piece = tok_own.shape[1]
    rows = tok_own.shape[0] * piece
    width = tok_own.shape[2]
    scale = DH ** (-0.5)
    eye = jnp.eye(DH, 2 * DH, dtype=bf16)
    side_lane = lax.broadcasted_iota(jnp.int32, (rows, DH), 1)
    per_head = rows_all // KEY_ROWS
    between = {
        0: lambda: (stage4(0), stage3(2), stage3(3)),
        1: lambda: (stage3(1), stage4(2), stage4(3)),
        2: lambda: None,
    }
    stage3(0)
    stage2(2)
    stage2(3)
    stage2(1)
    move.kept(0)
    move.kept(1)
    for h in range(3):
        for n in range(3):
            move.kept(2 + 3 * h + n)
        if h == 0:
            for n in range(11, 15):
                move.kept(n)
        lanes = slice(h * DH, (h + 1) * DH)
        for q in range(4):
            here = slice(q * rows, (q + 1) * rows)
            backs = back_context[q // 2, q % 2].reshape(rows, GROUP)[:, lanes]
            spread = jnp.sum(wide(backs) * wide(context[here, lanes]), axis=1, keepdims=True)
            high, mid, low = three(spread)
            side = jnp.where(
                side_lane == 0, -high, jnp.where(side_lane == 1, -mid, jnp.where(side_lane == 2, -low, 0.0))
            )
            widened[here, :] = jnp.concatenate([backs, side.astype(bf16)], axis=1)
        back_query[...] = jnp.zeros_like(back_query)

        def block(i, _):
            keys = pl.ds(i * KEY_ROWS, KEY_ROWS)
            key_here, value_here = key[h, keys, :], value[h, keys, :]
            turned = dot(eye, key_here, NT).astype(bf16)
            back_key = jnp.zeros((KEY_ROWS, DH), f32)
            back_value = jnp.zeros((KEY_ROWS, DH), f32)
            for q in range(rows_all // BACK_ROWS):
                here = slice(q * BACK_ROWS, (q + 1) * BACK_ROWS)
                queries, backs = query[h, here, :], widened[here, :]
                chances = jnp.exp(dot(key_here, queries, NT))
                back_scores = (chances * dot(value_here, backs, NT)).astype(bf16)
                back_key = back_key + dot(back_scores, queries[:, :DH])
                back_value = back_value + dot(chances.astype(bf16), backs[:, :DH])
                back_query[:, here] += dot(turned, back_scores)
            joint[keys, GROUP + h * DH : GROUP + (h + 1) * DH] = back_key.astype(bf16)
            joint[keys, 2 * GROUP + h * DH : 2 * GROUP + (h + 1) * DH] = back_value.astype(bf16)
            return 0

        lax.fori_loop(0, per_head, block, 0)
        joint[:, lanes] = (back_query[...] * scale).T.astype(bf16)
        between[h]()

    move.kept(15)
    for k in range(2):
        for yy in range(2):
            xx = lax.rem(x + 1 + k, 2)
            here = pl.ds((yy * 2 + xx) * rows, rows)
            back_first[yy, xx] = dot(joint[here, :], joint_weight[...], NT).astype(bf16).reshape(4, 2, piece, width)
            move.push(back_first.at[yy, xx, :, 1 - c], rc.at[yy, xx], sem_c.at[yy, xx], other_core)
    for yy in range(2):
        move.landed(rc.at[yy, 1 - x], sem_c.at[yy, 1 - x])
        rc[yy, 1 - x] = rc[yy, 1 - x] + back_first[yy, 1 - x, :, c]
        move.push(rc.at[yy, 1 - x], rx.at[yy], sem_x.at[yy], across)
    move.kept(16)
    grad = dot(first_low[...], joint[...], TN)
    lead = width // 32
    for block_at in range(32):
        gj[block_at // 16, block_at // 8 % 2, block_at % 8 // 2, block_at % 2] = grad[
            block_at * lead : (block_at + 1) * lead, :
        ].astype(bf16)
    move.push(gj.at[1 - y], ry, sem_y, down)
    move.kept(17)
    move.kept(18)
    stage4(1)
    shifts = jnp.sum(wide(joint[...]), axis=0, keepdims=True)
    small[...] = jnp.zeros_like(small)
    for k in range(8):
        for row, kind in ((2, 0), (3, 2)):
            start = kind * GROUP + k * lead
            small[mine * 8 + k, row : row + 1, :lead] = shifts[:, start : start + lead]
    move.landed(ry, sem_y)
    ry[...] = ry[...] + gj[y]
    for k in range(3):
        move.push(ry.at[:, line[k]], rz.at[k], sem_z.at[k], line_devices[k])
    for yy in range(2):
        move.landed(rc.at[yy, x], sem_c.at[yy, x])

    kept = []
    gains = jnp.zeros((2, width), f32)
    half = rows // 2
    for yy in range(2):
        inputs = wide(tok_own[yy * 4 : yy * 4 + 4].reshape(half, width))
        centered = inputs - mean_of(inputs)
        inverse = lax.rsqrt(mean_of(centered * centered) + EPS)
        unit = centered * inverse
        move.landed(rx.at[yy], sem_x.at[yy])
        whole = wide(rc[yy, x]) + wide(back_first[yy, x, :, c]) + wide(rx[yy])
        back_one = whole.reshape(half, width)
        scaled = back_one * vectors[0:1, :]
        back_tokens = back_residual[yy * half : (yy + 1) * half, :] + inverse * (
            scaled - mean_of(scaled) - unit * mean_of(scaled * unit)
        )
        gradient_low[yy * 4 : yy * 4 + 4] = back_tokens.astype(bf16).reshape(4, piece, width)
        for zz in [lax.rem(z + k, 4) for k in range(4)]:
            there = y * 0 + yy
            move.push_made(
                lambda zz=zz, yy=yy: (gradient_low.at[yy * 4 + zz], tokens_gradient.at[spot], sem_t.at[spot]),
                at(there, x, zz, c),
                jnp.logical_or(y != yy, z != zz),
            )
        gains = gains + jnp.concatenate(
            [jnp.sum(back_one * unit, axis=0, keepdims=True), jnp.sum(back_one, axis=0, keepdims=True)], axis=0
        )
    kept.append(move.keep(gradient_low.at[spot], tokens_gradient.at[spot]))
    for block_at in range(32):
        small[block_at, 0:2, :lead] = gains[:, block_at * lead : (block_at + 1) * lead]
    for t, device in others:
        move.push(small.at[t], small_all.at[me], sem_s.at[me], device)
    kept.append(move.keep(small.at[me], small_all.at[me]))

    total = wide(ry[:, z])
    for k in range(3):
        move.landed(rz.at[k], sem_z.at[k])
        total = total + wide(rz[k])
    sj[...] = total
    for xx, cc in group:
        move.push(sj.at[xx, cc], joint_land.at[mine], sem_g.at[mine], at(y, xx, z, cc))
    gone = move.keep(sj.at[x, c], joint_land.at[mine])
    for i in (0, 2, 3, 1):
        stage5(i)
    move.kept(gone)
    for xx, cc in group:
        move.landed(joint_land.at[xx * 2 + cc], sem_g.at[xx * 2 + cc])
    for g in range(4):
        for kind in range(3):
            start = kind * width + g * GROUP
            out_joint[:, start : start + GROUP] = joint_land[g, :, kind * GROUP : (kind + 1) * GROUP]
    for spot_kept in kept:
        move.kept(spot_kept)
    for t, _ in others:
        move.landed(small_all.at[t], sem_s.at[t])
    late[...] = jnp.sum(small_all[...], axis=0)
    for k in range(1, 8):
        t = lax.rem(spot + 8 - k, 8)
        move.landed(tokens_gradient.at[t], sem_t.at[t])
    move.finish()


def owner_device(
    tokens,
    lengths,
    first_gain,
    first_bias,
    joint_weight,
    query_bias,
    value_bias,
    output_weight,
    output_bias,
    second_gain,
    second_bias,
    inner_weight,
    inner_bias,
    outer_weight,
    outer_bias,
    cotangent,
):
    bf16, f32 = jnp.bfloat16, jnp.float32
    y, x, z, c = place()
    mine = x * 2 + c
    slots, piece, width = tokens.shape
    ff = inner_weight.shape[1]
    short = jnp.stack(
        [first_gain, first_bias, query_bias, value_bias, output_bias, second_gain, second_bias, outer_bias]
    )
    lead = short.shape[1]
    ff_piece = inner_bias.shape[0]
    small = jnp.concatenate(
        [
            jnp.pad(short, ((0, 0), (0, ff_piece - lead))),
            jnp.broadcast_to(inner_bias, (8, ff_piece)),
        ],
        axis=0,
    )
    hbm, vmem = pltpu.HBM, pltpu.VMEM
    dma, regular = pltpu.SemaphoreType.DMA, pltpu.SemaphoreType.REGULAR
    rows_all = 32 * piece
    natural = (2, 2, 4, 2, piece)
    length = lax.dynamic_slice(lengths, (y * 4 + z,), (1,))
    joint_four = jnp.transpose(joint_weight.reshape(lead, 3, 4, GROUP), (2, 0, 1, 3)).reshape(4, lead, 3 * GROUP)
    forward_outs = [
        ((rows_all, width), bf16, hbm),
        ((3, rows_all, 2 * DH), bf16, hbm),
        ((3, rows_all, 2 * DH), bf16, hbm),
        ((3, rows_all, 2 * DH), bf16, hbm),
        ((rows_all, GROUP), bf16, vmem),
        ((4, 2, 4, piece, GROUP), bf16, vmem),
        ((8, piece, width), bf16, hbm),
        ((8, piece, width), bf16, hbm),
        ((32,) + output_weight.shape, bf16, hbm),
        ((32,) + inner_weight.shape, bf16, hbm),
        ((32,) + outer_weight.shape, bf16, hbm),
        ((32,) + small.shape, bf16, vmem),
        ((width, 3 * GROUP), bf16, vmem),
    ]
    (
        first_low, query, key, value, context, context_rows, cot_own, tok_own, wo_all, wi_all, wu_all, small_all, joint_here
    ) = comm_call(
        forward_kernel,
        forward_outs,
        (length, tokens, cotangent, joint_four, output_weight, inner_weight, outer_weight, small),
        220, 24,
        [(32,), (8,), (3, 32), (32,), (4,), (4,), (4,), (4, 2), (4, 4), (4,)],
        [
            vmem((32, piece, width), bf16),
            vmem((2, 2, 4, 2, lead, 3 * GROUP), bf16),
            vmem((8, width), f32),
            vmem((3, 72, rows_all), bf16),
            vmem(natural + (GROUP,), bf16),
            vmem((rows_all, 512), f32),
            vmem((rows_all, 512), f32),
            vmem((3, 512, DH), bf16),
            vmem((rows_all, width), bf16),
            vmem((3, rows_all, 2 * DH), bf16),
            vmem((3, rows_all, 2 * DH), bf16),
            vmem((3, rows_all, 2 * DH), bf16),
        ],
        0,
        [pltpu.SMEM, hbm, hbm, hbm, hbm, hbm, hbm, hbm],
    )
    vectors = jnp.transpose(small_all[:, :2, :lead], (1, 0, 2)).reshape(2, width).astype(f32)
    rows = 8 * piece
    grid = (4, 4, 2)
    kinds = [
        (outer_weight.shape, bf16),
        (inner_weight.shape, bf16),
        (output_weight.shape, bf16),
        ((8, 128), f32),
    ]
    hu, hi, ho, hs, output, back_context, back_residual = comm_call(
        feed_kernel,
        [((4, 4) + shape, dtype, hbm) for shape, dtype in kinds]
        + [
            (tokens.shape, bf16, hbm),
            (natural + (GROUP,), bf16, vmem),
            ((rows, width), f32, vmem),
        ],
        (
            length, context_rows.reshape(4, 8, piece, GROUP), tok_own, cot_own, wo_all.reshape(width, width), small_all,
            wi_all.reshape(width, ff), wu_all.reshape(grid + outer_weight.shape),
        ),
        48, 24, [(4, 4), (2,), (8,), (4, 2)],
        [vmem(grid + shape, dtype) for shape, dtype in kinds]
        + [
            vmem((width, ff), bf16),
            vmem((4, 8, piece, GROUP), bf16),
            vmem((8, width), f32),
            vmem((1, ff), f32),
            vmem((rows, ff), bf16),
            vmem((rows, ff), bf16),
            vmem((8, piece, width), bf16),
        ]
        + [vmem((4, 4) + shape, dtype) for shape, dtype in kinds]
        + [
            vmem((2, 4) + outer_weight.shape, bf16),
            vmem((4, 8, piece, GROUP), bf16),
            vmem((8, piece, width), bf16),
            vmem((8, piece, width), bf16),
            vmem((width, width), bf16),
            dma((4, 2)),
        ],
        1,
        [pltpu.SMEM] + [hbm] * 4 + [vmem] + [hbm] * 2,
    )
    out_o, out_i, out_u, out_s, joint_shard, tokens_gradient, late = comm_call(
        backward_kernel,
        [
            (output_weight.shape, f32, vmem),
            (inner_weight.shape, f32, vmem),
            (outer_weight.shape, f32, vmem),
            ((8, 128), f32, vmem),
            (joint_weight.shape, f32, vmem),
            (tokens.shape, bf16, hbm),
            ((8, 128), f32, vmem),
        ],
        (
            hu, hi, ho, hs, query, key, value, context, back_context, joint_here, first_low, tok_own, back_residual, vectors,
        ),
        110, 32,
        [(4, 2), (4,), (4, 3), (), (3,), (4,), (2, 2), (2,), (8,), (32,)],
        [vmem((4, 4) + shape, dtype) for shape, dtype in kinds]
        + [vmem((2, 4) + shape, dtype) for shape, dtype in kinds]
        + [vmem((4,) + shape, dtype) for shape, dtype in kinds]
        + [vmem((3,) + shape, dtype) for shape, dtype in kinds]
        + [
            vmem((rows_all, 3 * GROUP), bf16),
            vmem((DH, rows_all), f32),
            vmem((rows_all, 2 * DH), bf16),
            vmem(query.shape, bf16),
            vmem(key.shape, bf16),
            vmem(value.shape, bf16),
            vmem(context.shape, bf16),
            vmem(back_context.shape, bf16),
            vmem(joint_here.shape, bf16),
            vmem(tok_own.shape, bf16),
            vmem(back_residual.shape, f32),
            vmem((rows_all, width), bf16),
            vmem(natural + (width,), bf16),
            vmem((2, 2, 4, piece, width), bf16),
            vmem((2, 4, piece, width), bf16),
            vmem((2, 2, 4, 2, lead, 3 * GROUP), bf16),
            vmem((2, 4, 2, lead, 3 * GROUP), bf16),
            vmem((3, 2, 2, lead, 3 * GROUP), bf16),
            vmem((2, 2, lead, 3 * GROUP), f32),
            vmem((4, lead, 3 * GROUP), f32),
            vmem((8, piece, width), bf16),
            vmem((32, 8, 128), f32),
            vmem((32, 8, 128), f32),
        ],
        2,
        [hbm] * 13 + [vmem],
    )
    count = jnp.sum(lengths).astype(f32) * width
    stats = jnp.sqrt(out_s[5, :3] / count + 1e-06)
    return (
        output,
        tokens_gradient,
        late[0, :lead],
        late[1, :lead],
        joint_shard,
        late[2, :lead],
        late[3, :lead],
        out_o,
        out_s[3, :lead],
        out_s[1, :lead],
        out_s[2, :lead],
        out_i,
        out_s[4, : inner_bias.shape[0]],
        out_u,
        out_s[0, :lead],
        stats,
    )


def solution(mesh):
    in_specs = (
        P(None, ("head", "blk"), None),
        P(),
        P(("head", "blk")),
        P(("head", "blk")),
        P(("head", "blk"), None),
        P(("head", "blk")),
        P(("head", "blk")),
        P(("head", "blk"), None),
        P(("head", "blk")),
        P(("head", "blk")),
        P(("head", "blk")),
        P(("head", "blk"), None),
        P(("head", "blk")),
        P(("head", "blk"), None),
        P(("head", "blk")),
        P(None, ("head", "blk"), None),
    )
    out_specs = (
        P(None, ("head", "blk"), None),
        P(None, ("head", "blk"), None),
        P(("head", "blk")),
        P(("head", "blk")),
        P(("head", "blk"), None),
        P(("head", "blk")),
        P(("head", "blk")),
        P(("head", "blk"), None),
        P(("head", "blk")),
        P(("head", "blk")),
        P(("head", "blk")),
        P(("head", "blk"), None),
        P(("head", "blk")),
        P(("head", "blk"), None),
        P(("head", "blk")),
        P(),
    )
    small_slice = dict(mesh.shape) == {"head": 4, "blk": 8}
    device_work = owner_device if small_slice else on_device
    return jax.shard_map(
        device_work, mesh=mesh, in_specs=in_specs, out_specs=out_specs, check_vma=False
    )
```

```python
import jax
import jax.numpy as jnp
from jax import lax
from jax.experimental import pallas as pl
from jax.experimental.pallas import tpu as pltpu
from jax.sharding import PartitionSpec as P

H = 12
DH = 64


EPS = 1e-12
NEG = -1e30


def passed_along(value, axis, steps):
    count = lax.axis_size(axis)
    pairs = [(source, (source + steps) % count) for source in range(count)]
    return lax.ppermute(value, axis, pairs)


def normalize(values, gain, shift):
    average = jnp.mean(values, axis=-1, keepdims=True)
    centered = values - average
    inverse = lax.rsqrt(jnp.mean(centered * centered, axis=-1, keepdims=True) + EPS)
    normed = centered * inverse
    return (normed * gain + shift, normed, inverse)


def normalize_back(incoming, normed, inverse, gain):
    scaled = incoming * gain
    inner = (
        scaled
        - jnp.mean(scaled, axis=-1, keepdims=True)
        - normed * jnp.mean(scaled * normed, axis=-1, keepdims=True)
    )
    return (
        inner * inverse,
        jnp.sum(incoming * normed, axis=(0, 1)),
        jnp.sum(incoming, axis=(0, 1)),
    )


def gelu_exact(values):
    return jax.nn.gelu(values, approximate=False)


def key_mask(lengths, source, piece_rows, block_count, head_count):
    rows_here = jnp.arange(head_count * piece_rows, dtype=jnp.int32)
    position = (
        rows_here // piece_rows * block_count + source
    ) * piece_rows + rows_here % piece_rows
    return position[None, :] < lengths[:, None]


def attend(query_part, state, keys_block, values_block, mask):
    best, total, running = state
    scores = jnp.einsum(
        "sqhd,skhd->sqhk", query_part, keys_block, preferred_element_type=jnp.float32
    ) * DH ** (-0.5)
    scores = jnp.where(mask[:, None, None, :], scores, NEG)
    fresh = jnp.maximum(best, jnp.max(scores, axis=-1))
    decay = jnp.exp(best - fresh)
    weights = jnp.exp(scores - fresh[..., None])
    total = total * decay + jnp.sum(weights, axis=-1)
    running = running * decay[..., None] + jnp.einsum(
        "sqhk,skhd->sqhd",
        weights.astype(jnp.bfloat16),
        values_block,
        preferred_element_type=jnp.float32,
    )
    return (fresh, total, running)


def block_grads(query_part, back_part, total_part, spread_part, keys_block, values_block, mask):
    scale = DH ** (-0.5)
    scores = (
        jnp.einsum("sqhd,skhd->sqhk", query_part, keys_block, preferred_element_type=jnp.float32)
        * scale
    )
    scores = jnp.where(mask[:, None, None, :], scores, NEG)
    chances = jnp.exp(scores - total_part[..., None])
    back_chances = jnp.einsum(
        "sqhd,skhd->sqhk", back_part, values_block, preferred_element_type=jnp.float32
    )
    back_scores = (chances * (back_chances - spread_part[..., None])).astype(jnp.bfloat16)
    query_step = (
        jnp.einsum("sqhk,skhd->sqhd", back_scores, keys_block, preferred_element_type=jnp.float32)
        * scale
    )
    key_step = (
        jnp.einsum("sqhk,sqhd->skhd", back_scores, query_part, preferred_element_type=jnp.float32)
        * scale
    )
    value_step = jnp.einsum(
        "sqhk,sqhd->skhd",
        chances.astype(jnp.bfloat16),
        back_part,
        preferred_element_type=jnp.float32,
    )
    return (query_step, key_step, value_step)


def on_device(
    tokens,
    lengths,
    first_gain,
    first_bias,
    joint_weight,
    query_bias,
    value_bias,
    output_weight,
    output_bias,
    second_gain,
    second_bias,
    inner_weight,
    inner_bias,
    outer_weight,
    outer_bias,
    cotangent,
):
    head_count = lax.axis_size("head")
    block_count = lax.axis_size("blk")
    block = lax.axis_index("blk")
    quarter = lax.axis_index("head")
    (
        gain_one,
        shift_one,
        joint_full,
        query_shift,
        value_shift,
        output_full,
        output_shift,
        gain_two,
        shift_two,
        inner_full,
        inner_shift,
        outer_full,
        outer_shift,
    ) = (
        lax.all_gather(first_gain, ("head", "blk"), axis=0, tiled=True),
        lax.all_gather(first_bias, ("head", "blk"), axis=0, tiled=True),
        lax.all_gather(joint_weight, ("head", "blk"), axis=0, tiled=True),
        lax.all_gather(query_bias, ("head", "blk"), axis=0, tiled=True),
        lax.all_gather(value_bias, ("head", "blk"), axis=0, tiled=True),
        lax.all_gather(output_weight, ("head", "blk"), axis=0, tiled=True),
        lax.all_gather(output_bias, ("head", "blk"), axis=0, tiled=True),
        lax.all_gather(second_gain, ("head", "blk"), axis=0, tiled=True),
        lax.all_gather(second_bias, ("head", "blk"), axis=0, tiled=True),
        lax.all_gather(inner_weight, ("head", "blk"), axis=0, tiled=True),
        lax.all_gather(inner_bias, ("head", "blk"), axis=0, tiled=True),
        lax.all_gather(outer_weight, ("head", "blk"), axis=0, tiled=True),
        lax.all_gather(outer_bias, ("head", "blk"), axis=0, tiled=True),
    )
    sequences, piece_rows, width = tokens.shape
    heads_here = H // head_count
    head_width = heads_here * DH
    rows = head_count * piece_rows
    shape_heads = (sequences, rows, heads_here, DH)
    shape_flat = (sequences, rows, head_width)
    own_position = (quarter * block_count + block) * piece_rows + jnp.arange(
        piece_rows, dtype=jnp.int32
    )
    valid = own_position[None, :] < lengths[:, None]
    keep = valid[..., None]
    inputs = tokens.astype(jnp.float32)
    gain_one_wide = gain_one.astype(jnp.float32)
    gain_two_wide = gain_two.astype(jnp.float32)
    first_out, first_unit, first_scale = normalize(
        inputs, gain_one_wide, shift_one.astype(jnp.float32)
    )
    first_low = first_out.astype(jnp.bfloat16)
    joint = jnp.einsum("scd,de->sce", first_low, joint_full, preferred_element_type=jnp.float32)
    query_flat = (joint[..., :width] + query_shift.astype(jnp.float32)).astype(jnp.bfloat16)
    key_flat = joint[..., width : 2 * width].astype(jnp.bfloat16)
    value_flat = (joint[..., 2 * width :] + value_shift.astype(jnp.float32)).astype(jnp.bfloat16)
    query_flat, key_flat, value_flat = (
        lax.all_to_all(query_flat, "head", split_axis=2, concat_axis=1, tiled=True),
        lax.all_to_all(key_flat, "head", split_axis=2, concat_axis=1, tiled=True),
        lax.all_to_all(value_flat, "head", split_axis=2, concat_axis=1, tiled=True),
    )
    query_rows = query_flat.reshape(shape_heads)
    key_rows = key_flat.reshape(shape_heads)
    value_rows = value_flat.reshape(shape_heads)

    def visit(carry):
        keys_block, values_block, source, state = carry
        keys_block, values_block = passed_along((keys_block, values_block), "blk", 1)
        source = (source - 1) % block_count
        mask = key_mask(lengths, source, piece_rows, block_count, head_count)
        return (
            keys_block,
            values_block,
            source,
            attend(query_rows, state, keys_block, values_block, mask),
        )

    start_state = (
        jnp.full((sequences, rows, heads_here), NEG, jnp.float32),
        jnp.zeros((sequences, rows, heads_here), jnp.float32),
        jnp.zeros(shape_heads, jnp.float32),
    )
    first_state = attend(
        query_rows,
        start_state,
        key_rows,
        value_rows,
        key_mask(lengths, block, piece_rows, block_count, head_count),
    )
    carry = (key_rows, value_rows, block, first_state)
    carry = lax.fori_loop(0, block_count // 2 - 1, lambda turn, state: visit(visit(state)), carry)
    best, total, running = visit(carry)[3]
    context = running / total[..., None]
    log_total = best + jnp.log(total)
    context_low = context.astype(jnp.bfloat16).reshape(shape_flat)
    context_tokens = lax.all_to_all(context_low, "head", split_axis=1, concat_axis=2, tiled=True)
    branch = jnp.einsum(
        "sce,ed->scd", context_tokens, output_full, preferred_element_type=jnp.float32
    ) + output_shift.astype(jnp.float32)
    residual = inputs + branch
    second_out, second_unit, second_scale = normalize(
        residual, gain_two_wide, shift_two.astype(jnp.float32)
    )
    second_low = second_out.astype(jnp.bfloat16)
    inner = jnp.einsum(
        "scd,df->scf", second_low, inner_full, preferred_element_type=jnp.float32
    ) + inner_shift.astype(jnp.float32)
    activated = gelu_exact(inner).astype(jnp.bfloat16)
    feed = jnp.einsum(
        "scf,fd->scd", activated, outer_full, preferred_element_type=jnp.float32
    ) + outer_shift.astype(jnp.float32)
    result = residual + feed
    output = jnp.where(keep, result, 0.0).astype(jnp.bfloat16)
    sums = lax.psum(
        (
            jnp.sum(jnp.where(keep, result * result, 0.0)),
            jnp.sum(jnp.where(keep, branch * branch, 0.0)),
            jnp.sum(jnp.where(keep, feed * feed, 0.0)),
        ),
        ("head", "blk"),
    )
    count = jnp.sum(lengths).astype(jnp.float32) * width
    stats = jnp.sqrt(jnp.stack(sums) / count + 1e-06)
    back_result = jnp.where(keep, cotangent.astype(jnp.float32), 0.0)
    back_feed = back_result.astype(jnp.bfloat16)
    outer_gradient = jnp.einsum(
        "scf,scd->fd", activated, back_feed, preferred_element_type=jnp.float32
    )
    outer_shift_gradient = jnp.sum(back_feed.astype(jnp.float32), axis=(0, 1))
    back_active = jnp.einsum(
        "scd,fd->scf", back_feed, outer_full, preferred_element_type=jnp.float32
    )
    back_inner = jax.vjp(gelu_exact, inner)[1](back_active)[0].astype(jnp.bfloat16)
    inner_gradient = jnp.einsum(
        "scd,scf->df", second_low, back_inner, preferred_element_type=jnp.float32
    )
    inner_shift_gradient = jnp.sum(back_inner.astype(jnp.float32), axis=(0, 1))
    back_second = jnp.einsum(
        "scf,df->scd", back_inner, inner_full, preferred_element_type=jnp.float32
    )
    back_norm_two, gain_two_gradient, shift_two_gradient = normalize_back(
        back_second, second_unit, second_scale, gain_two_wide
    )
    back_residual = back_result + back_norm_two
    back_branch = back_residual.astype(jnp.bfloat16)
    output_gradient = jnp.einsum(
        "sce,scd->ed", context_tokens, back_branch, preferred_element_type=jnp.float32
    )
    output_shift_gradient = jnp.sum(back_branch.astype(jnp.float32), axis=(0, 1))
    back_context = jnp.einsum(
        "scd,ed->sce", back_branch, output_full, preferred_element_type=jnp.float32
    ).astype(jnp.bfloat16)
    back_context = lax.all_to_all(back_context, "head", split_axis=2, concat_axis=1, tiled=True)
    back_heads = back_context.reshape(shape_heads)
    spread = jnp.sum(back_heads.astype(jnp.float32) * context, axis=-1)
    zero_heads = jnp.zeros(shape_heads, jnp.float32)

    def pass_keys(carry):
        keys_block, values_block, key_sum, value_sum, query_sum, source = carry
        mask = key_mask(lengths, source, piece_rows, block_count, head_count)
        query_step, key_step, value_step = block_grads(
            query_rows, back_heads, log_total, spread, keys_block, values_block, mask
        )
        keys_block, values_block = passed_along((keys_block, values_block), "blk", 1)
        key_sum, value_sum = passed_along((key_sum + key_step, value_sum + value_step), "blk", 1)
        return (
            keys_block,
            values_block,
            key_sum,
            value_sum,
            query_sum + query_step,
            (source - 1) % block_count,
        )

    carry = (key_rows, value_rows, zero_heads, zero_heads, zero_heads, block)
    carry = lax.fori_loop(
        0, block_count // 2, lambda turn, state: pass_keys(pass_keys(state)), carry
    )
    key_sum, value_sum, query_sum = (carry[2], carry[3], carry[4])
    back_query, back_key, back_value = (
        lax.all_to_all(
            query_sum.astype(jnp.bfloat16).reshape(shape_flat),
            "head",
            split_axis=1,
            concat_axis=2,
            tiled=True,
        ),
        lax.all_to_all(
            key_sum.astype(jnp.bfloat16).reshape(shape_flat),
            "head",
            split_axis=1,
            concat_axis=2,
            tiled=True,
        ),
        lax.all_to_all(
            value_sum.astype(jnp.bfloat16).reshape(shape_flat),
            "head",
            split_axis=1,
            concat_axis=2,
            tiled=True,
        ),
    )
    back_joint = jnp.concatenate([back_query, back_key, back_value], axis=-1)
    joint_gradient = jnp.einsum(
        "scd,sce->de", first_low, back_joint, preferred_element_type=jnp.float32
    )
    query_shift_gradient = jnp.sum(back_query.astype(jnp.float32), axis=(0, 1))
    value_shift_gradient = jnp.sum(back_value.astype(jnp.float32), axis=(0, 1))
    back_first = jnp.einsum(
        "sce,de->scd", back_joint, joint_full, preferred_element_type=jnp.float32
    )
    back_norm_one, gain_one_gradient, shift_one_gradient = normalize_back(
        back_first, first_unit, first_scale, gain_one_wide
    )
    tokens_gradient = (back_residual + back_norm_one).astype(jnp.bfloat16)
    shards = (
        lax.psum_scatter(gain_one_gradient, ("head", "blk"), scatter_dimension=0, tiled=True),
        lax.psum_scatter(shift_one_gradient, ("head", "blk"), scatter_dimension=0, tiled=True),
        lax.psum_scatter(joint_gradient, ("head", "blk"), scatter_dimension=0, tiled=True),
        lax.psum_scatter(query_shift_gradient, ("head", "blk"), scatter_dimension=0, tiled=True),
        lax.psum_scatter(value_shift_gradient, ("head", "blk"), scatter_dimension=0, tiled=True),
        lax.psum_scatter(output_gradient, ("head", "blk"), scatter_dimension=0, tiled=True),
        lax.psum_scatter(output_shift_gradient, ("head", "blk"), scatter_dimension=0, tiled=True),
        lax.psum_scatter(gain_two_gradient, ("head", "blk"), scatter_dimension=0, tiled=True),
        lax.psum_scatter(shift_two_gradient, ("head", "blk"), scatter_dimension=0, tiled=True),
        lax.psum_scatter(inner_gradient, ("head", "blk"), scatter_dimension=0, tiled=True),
        lax.psum_scatter(inner_shift_gradient, ("head", "blk"), scatter_dimension=0, tiled=True),
        lax.psum_scatter(outer_gradient, ("head", "blk"), scatter_dimension=0, tiled=True),
        lax.psum_scatter(outer_shift_gradient, ("head", "blk"), scatter_dimension=0, tiled=True),
    )
    return (
        output,
        tokens_gradient,
        shards[0],
        shards[1],
        shards[2],
        shards[3],
        shards[4],
        shards[5],
        shards[6],
        shards[7],
        shards[8],
        shards[9],
        shards[10],
        shards[11],
        shards[12],
        stats,
    )


MESH = pl.DeviceIdType.MESH
WIDTH = H * DH
GROUP = 3 * DH
NT = (((1,), (1,)), ((), ()))
NN = (((1,), (0,)), ((), ()))


def place():
    head = lax.axis_index("head")
    blk = lax.axis_index("blk")
    return head // 2, lax.rem(head, 2), blk // 2, lax.rem(blk, 2)


def at(y, x, z, c):
    return (y * 2 + x, z * 2 + c)


def number(y, x, z, c):
    return y * 16 + x * 8 + z * 2 + c


def column(t):
    return t // 4, lax.rem(t, 4)


def meet(peers):
    barrier = pltpu.get_barrier_semaphore()
    for peer in peers:
        pl.semaphore_signal(barrier, inc=1, device_id=peer, device_id_type=MESH)
    pl.semaphore_wait(barrier, len(peers))


class Mover:
    def __init__(self, send_sem, local_sem, anyone):
        self.send_sem = send_sem
        self.local_sem = local_sem
        self.anyone = anyone
        self.zero = anyone[0] * 0
        self.sent = []
        self.local = []

    def push(self, source, target, sem, device):
        self.push_made(lambda: (source, target, sem), device)

    def push_made(self, make, device, when=None):
        spot = len(self.sent)
        self.sent.append((make, spot, device, when))
        under(when, lambda: self.copy(make, spot, device).start())

    def copy(self, make, spot, device):
        source, target, sem = make()
        return remote(source, target, self.send_sem.at[self.zero + spot], sem, device)

    def keep(self, source, target):
        parts = (source, target, self.local_sem.at[len(self.local)])
        pltpu.make_async_copy(*parts).start()
        self.local.append(parts)
        return len(self.local) - 1

    def kept(self, spot):
        pltpu.make_async_copy(*self.local[spot]).wait()

    def landed(self, target, sem):
        remote(target, target, self.send_sem.at[self.zero], sem, self.anyone).wait_recv()

    def finish(self, kept=()):
        for make, spot, device, when in self.sent:
            under(when, lambda: self.copy(make, spot, device).wait_send())
        for spot in kept:
            self.kept(spot)


def under(when, action):
    if when is None:
        action()
    else:

        @pl.when(when)
        def _():
            action()


def remote(source, target, send_sem, recv_sem, device):
    return pltpu.make_async_remote_copy(
        src_ref=source,
        dst_ref=target,
        send_sem=send_sem,
        recv_sem=recv_sem,
        device_id=device,
        device_id_type=MESH,
    )


def unpack(small_all, vectors):
    for block in range(32):
        tile = wide(small_all[block])
        vectors[:, block * 24 : block * 24 + 24] = tile[:8, :24]


def forward_kernel(
    length, tokens, cotangent, wj, wo, wi, wu, small,
    first_far, query_far, key_far, value_far, context_far, context_rows, cot_own, tok_own, wo_all, wi_all, wu_all, small_all, wj_far, vectors,
    send_sem, local_sem, tok_sem, cot_sem, weight_sem, small_sem, wja_sem, wjb_sem, wjc_sem, ctx_send, ctx_recv,
    ctx_local, tok_all, wj_all, turned, mixed_low, score_a, score_b, straight_low, first_low, query, key, value, context, wj_flat,
):
    y, x, z, c = place()
    mine = number(y, x, z, c)
    quarter = x * 2 + c
    spot = y * 4 + z
    other_core = at(y, x, z, 1 - c)
    across = at(y, 1 - x, z, c)
    diagonal = at(y, 1 - x, z, 1 - c)
    down = at(1 - y, x, z, c)
    y1, x1 = jnp.where(c == 0, y, 1 - y), jnp.where(c == 0, 1 - x, x)
    y2, x2 = jnp.where(c == 0, 1 - y, y), jnp.where(c == 0, x, 1 - x)
    first, second = at(y1, x1, z, c), at(y2, x2, z, c)
    spots = [column(lax.rem(spot + k, 8)) for k in range(1, 8)]
    back_spots = [column(lax.rem(spot + 8 - k, 8)) for k in range(1, 8)]
    ahead = [at(y, x, lax.rem(z + k, 4), c) for k in range(1, 4)]
    inside = jnp.logical_or(z == 1, z == 2)
    lines = [
        z,
        jnp.where(z == 0, 1, z - 1),
        jnp.where(z == 0, 2, jnp.where(z == 3, 1, z + 1)),
        jnp.where(z < 2, 3, 0),
    ]
    onward = [z + 1, z - 1, jnp.where(z == 1, 0, 3)]
    away, back = at(y, x, jnp.where(z < 3, z + 1, z - 1), c), at(y, x, jnp.maximum(z - 1, 0), c)
    onward = [at(y, x, lax.rem(zz + 4, 4), c) for zz in onward]
    line_blocks = [number(y, x, zz, c) for zz in lines]
    first_blocks = [number(y1, x1, zz, c) for zz in lines]
    second_blocks = [number(yy, xx, zz, c) for zz in lines for yy, xx in ((y2, x2), (1 - y, 1 - x))]
    core_blocks = [number(yy, xx, zz, 1 - c) for yy in range(2) for xx in range(2) for zz in range(4)]
    group = quad(x, c)
    meet([at(yy, x, zz, c) for yy, zz in spots] + [across, other_core, diagonal])
    move = Mover(send_sem, local_sem, other_core)
    sources = (wo, wi, wu)
    wholes = (wo_all, wi_all, wu_all)

    def hand(block, own, device, when=None):
        for i in range(3):
            move.push_made(
                lambda i=i: (
                    sources[i] if own else wholes[i].at[block],
                    wholes[i].at[block],
                    weight_sem.at[move.zero + i, block],
                ),
                device,
                when,
            )

    def arrive(block):
        for i in range(3):
            move.landed(wholes[i].at[block], weight_sem.at[i, block])

    def pass_small(blocks, devices):
        for block in blocks:
            move.landed(small_all.at[block], small_sem.at[block])
            for device in devices:
                move.push(small_all.at[block], small_all.at[block], small_sem.at[block], device)

    def spread(block, own):
        for device in (first, second, other_core):
            hand(block, own, device)

    def line_arrived(k):
        arrive(line_blocks[k])
        hand(line_blocks[k], False, onward[k - 1], inside)
        spread(line_blocks[k], False)

    def second_hand(k):
        arrive(first_blocks[k])
        hand(first_blocks[k], False, second)
        hand(first_blocks[k], False, other_core)

    def last_hand(k):
        for b in second_blocks[2 * k : 2 * k + 2]:
            arrive(b)
            hand(b, False, other_core)

    for device in ahead + [first, second, other_core]:
        move.push(small, small_all.at[mine], small_sem.at[mine], device)
    for xx, cc in group:
        move.push(wj.at[xx * 2 + cc], wj_all.at[y, x, z, c], wja_sem.at[quarter], at(y, xx, z, cc))
    move.keep(wj.at[quarter], wj_all.at[y, x, z, c])
    move.keep(tokens.at[spot], tok_all.at[mine])
    move.keep(small, small_all.at[mine])
    for yy, zz in spots:
        move.push(tokens.at[yy * 4 + zz], tok_all.at[mine], tok_sem.at[mine], at(yy, x, zz, c))
    for device in (across, other_core):
        move.push(tokens.at[spot], tok_all.at[mine], tok_sem.at[mine], device)
    spread(mine, True)
    for source, whole in zip(sources, wholes):
        move.keep(source, whole.at[mine])

    def slice_onward(zz, device, when):
        move.push_made(lambda: (wj_all.at[y, :, zz], wj_all.at[y, :, zz], wjb_sem.at[zz]), device, when)

    for xx, cc in group:
        move.landed(wj_all.at[y, xx, z, cc], wja_sem.at[xx * 2 + cc])
    move.kept(0)
    slice_onward(z, away, None)
    slice_onward(z, back, inside)
    move.push(wj_all.at[y, :, z], wj_all.at[y, :, z], wjc_sem.at[z], down)
    pass_small(line_blocks[1:], (first, second, other_core))
    pass_small(first_blocks, (second, other_core))
    for k in range(1, 4):
        zz = lines[k]
        move.landed(wj_all.at[y, :, zz], wjb_sem.at[zz])
        slice_onward(zz, onward[k - 1], inside)
        move.push(wj_all.at[y, :, zz], wj_all.at[y, :, zz], wjc_sem.at[zz], down)
    pass_small(second_blocks, (other_core,))
    for yy, zz in back_spots:
        block = number(yy, x, zz, c)
        move.landed(tok_all.at[block], tok_sem.at[block])
        move.push(tok_all.at[block], tok_all.at[block], tok_sem.at[block], across)
        move.push(tok_all.at[block], tok_all.at[block], tok_sem.at[block], other_core)
    hand(mine, True, away)
    hand(mine, True, back, inside)
    second_hand(0)
    for yy, zz in [(y, z)] + back_spots:
        block = number(yy, 1 - x, zz, c)
        move.landed(tok_all.at[block], tok_sem.at[block])
        move.push(tok_all.at[block], tok_all.at[block], tok_sem.at[block], other_core)
    for block in core_blocks:
        move.landed(small_all.at[block], small_sem.at[block])
    for zz in lines:
        move.landed(wj_all.at[1 - y, :, zz], wjc_sem.at[zz])
    line_arrived(1)
    for yy, zz in spots:
        move.push(cotangent.at[yy * 4 + zz], cot_own.at[spot], cot_sem.at[spot], at(yy, x, zz, c))
    move.keep(cotangent.at[spot], cot_own.at[spot])
    for yy, zz in [(y, z)] + back_spots:
        for xx in (x, 1 - x):
            block = number(yy, xx, zz, 1 - c)
            move.landed(tok_all.at[block], tok_sem.at[block])
    move.kept(1)
    move.kept(2)

    unpack(small_all, vectors)
    rows = query.shape[1]
    for yy in range(2):
        for xx in range(2):
            for zz in range(4):
                pair = jnp.concatenate([wide(wj_all[yy, xx, zz, cc]) for cc in range(2)], axis=0)
                row = number(yy, xx, zz, 0) * 24
                wj_flat[row : row + 48, :] = pair.astype(jnp.bfloat16)
    lane = lax.broadcasted_iota(jnp.int32, (ROWS, DH), 1)
    row_at = lax.broadcasted_iota(jnp.int32, (ROWS, DH), 0)
    one_lane = jnp.where(lane == 0, 1.0, 0.0).astype(jnp.bfloat16)
    three_lanes = jnp.where(lane < 3, 1.0, 0.0).astype(jnp.bfloat16)
    gain, shift = vectors[0:1, :], vectors[1:2, :]
    query_all, value_all = vectors[2:3, :], vectors[3:4, :]

    def chosen(whole):
        total = jnp.zeros((1, GROUP), jnp.float32)
        for q in range(4):
            total = jnp.where(quarter == q, whole[:, q * GROUP : (q + 1) * GROUP], total)
        return total

    query_shift, value_shift = chosen(query_all), chosen(value_all)
    blocks = ROWS // tokens.shape[1]

    def project(i, _):
        here = pl.ds(i * ROWS, ROWS)
        raw = tok_all[pl.ds(i * blocks, blocks)].reshape(ROWS, WIDTH)
        normed = normalize(wide(raw), gain, shift)[0].astype(jnp.bfloat16)
        first_low[here, :] = normed
        joint = dot(normed, wj_flat[...])
        low_q = ((joint[:, :GROUP] + query_shift).astype(jnp.bfloat16) * DH ** (-0.5)).astype(jnp.bfloat16)
        low_k = joint[:, GROUP : 2 * GROUP].astype(jnp.bfloat16)
        low_v = (joint[:, 2 * GROUP :] + value_shift).astype(jnp.bfloat16)
        mask = jnp.where(row_at + i * ROWS < length[spot], 0.0, NEG)
        key_side = jnp.where(lane == 0, mask, jnp.where(lane < 4, 1.0, 0.0)).astype(jnp.bfloat16)
        for h in range(3):
            here_h = slice(h * DH, (h + 1) * DH)
            query[h, here, :] = jnp.concatenate([low_q[:, here_h], one_lane], axis=1)
            key[h, here, :] = jnp.concatenate([low_k[:, here_h], key_side], axis=1)
            value[h, here, :] = jnp.concatenate([low_v[:, here_h], three_lanes], axis=1)
        return 0

    for i in range(rows // ROWS):
        project(i, 0)
    for source, target in ((first_low, first_far), (key, key_far), (value, value_far), (wj_flat, wj_far)):
        move.keep(source, target)
    eye = jnp.eye(72, 2 * DH, dtype=jnp.bfloat16)
    for h in range(3):
        turned[h] = dot(eye, value[h], NT).astype(jnp.bfloat16)
    wider = score_a.shape[1]
    side = lax.broadcasted_iota(jnp.int32, (DH, wider), 0)
    chunk = 512
    units = 3 * rows // wider

    def ctx_copy(j, cc, for_local, for_remote):
        yy, xx = j // 2, lax.rem(j, 2)
        source, target = mixed_low.at[yy, xx, :, cc], context_rows.at[quarter, yy]
        here = jnp.logical_and(xx == x, c == cc)

        @pl.when(here)
        def _():
            for_local(pltpu.make_async_copy(source, target, ctx_local.at[j]))

        @pl.when(jnp.logical_not(here))
        def _():
            for_remote(remote(source, target, ctx_send.at[j, cc], ctx_recv.at[quarter, j], at(y, xx, z, cc)))

    def score_chunk(held, h, queries, k, best):
        fresh = dot(key[h, k * chunk : (k + 1) * chunk, :], queries, NT)
        held[k * chunk : (k + 1) * chunk, :] = fresh
        return jnp.maximum(best, jnp.max(fresh, axis=0, keepdims=True))

    lowest = jnp.full((1, wider), -jnp.inf, jnp.float32)
    start = lowest
    for k in range(rows // chunk):
        start = score_chunk(score_a, 0, query[0, :wider, :], k, start)

    def unit(u, best, held, fresh):
        j = u // 3
        h = u - 3 * j
        u_next = jnp.minimum(u + 1, units - 1)
        j_next = u_next // 3
        h_next = u_next - 3 * j_next
        here = pl.ds(j * wider, wider)
        queries = query[h_next, pl.ds(j_next * wider, wider), :]
        best_next = lowest
        mixed = jnp.zeros((72, wider), jnp.float32)
        for k in range(rows // chunk):
            keys = slice(k * chunk, (k + 1) * chunk)
            weights = jnp.exp(held[keys, :] - best).astype(jnp.bfloat16)
            mixed = mixed + dot(turned[h, :, keys], weights)
            best_next = score_chunk(fresh, h_next, queries, k, best_next)
        total = mixed[DH : DH + 1, :]
        mixed = mixed[:DH, :] / total
        high, mid, low = three(best + jnp.log(total))
        extra = jnp.where(
            side == 0, 1.0, jnp.where(side == 1, -high, jnp.where(side == 2, -mid, jnp.where(side == 3, -low, 0.0)))
        )
        straight = jnp.concatenate([mixed, extra], axis=0).T
        query[h, here, DH:] = straight[:, DH:].astype(jnp.bfloat16)
        straight_low[h] = straight[:, :DH].astype(jnp.bfloat16)

        @pl.when(h == 2)
        def _():
            whole = jnp.concatenate([straight_low[k] for k in range(3)], axis=1)
            context[here, :] = whole
            mixed_low[j // 2, lax.rem(j, 2)] = whole.reshape(4, 2, tokens.shape[1], GROUP)
            for cc in range(2):
                ctx_copy(j, cc, lambda copy: copy.start(), lambda copy: copy.start())

        return best_next

    def pair(p, best):
        best = unit(2 * p, best, score_a, score_b)
        best = unit(2 * p + 1, best, score_b, score_a)
        for when, action in (
            (0, lambda: second_hand(1)),
            (1, lambda: line_arrived(2)),
            (2, lambda: (second_hand(2), last_hand(0))),
            (3, lambda: line_arrived(3)),
            (4, lambda: (second_hand(3), last_hand(1))),
        ):

            @pl.when(p == when)
            def _(action=action):
                action()

        return best

    lax.fori_loop(0, units // 2, pair, start)
    move.keep(query, query_far)
    move.keep(context, context_far)
    last_hand(2)
    last_hand(3)
    for yy, zz in back_spots:
        move.landed(cot_own.at[yy * 4 + zz], cot_sem.at[yy * 4 + zz])
    for b in core_blocks:
        arrive(b)
    tok_copies = []
    for i in range(8):
        yy, zz = i // 4, i % 4
        tok_copies.append(pltpu.make_async_copy(tok_all.at[number(yy, x, zz, c)], tok_own.at[i], local_sem.at[8 + i]))
        tok_copies[-1].start()

    def settle(j, _):
        for cc in range(2):
            ctx_copy(j, cc, lambda copy: copy.wait(), lambda copy: copy.wait_send())
        return 0

    lax.fori_loop(0, 4, settle, 0)
    for xx, cc in group:
        for yy in range(2):
            move.landed(context_rows.at[xx * 2 + cc, yy], ctx_recv.at[xx * 2 + cc, yy * 2 + x])
    move.finish(range(3, len(move.local)))
    for copy in tok_copies:
        copy.wait()


def comm_call(kernel, outs, args, sends, locals_, sems, scratch, ident, space=None):
    space = space or [pltpu.HBM] * len(args)
    return pl.pallas_call(
        kernel,
        out_shape=[jax.ShapeDtypeStruct(shape, dtype) for shape, dtype, _ in outs],
        in_specs=[pl.BlockSpec(memory_space=one) for one in space],
        out_specs=[pl.BlockSpec(memory_space=one) for _, _, one in outs],
        scratch_shapes=[
            pltpu.SemaphoreType.DMA((sends,)),
            pltpu.SemaphoreType.DMA((max(locals_, 1),)),
            *[pltpu.SemaphoreType.DMA(shape) for shape in sems],
            *scratch,
        ],
        compiler_params=pltpu.CompilerParams(
            collective_id=ident, has_side_effects=True, vmem_limit_bytes=61 * 1024 * 1024
        ),
    )(*args)


def quad(x, c):
    return [(lax.rem(x + dx, 2), lax.rem(c + dc, 2)) for dx, dc in ((0, 1), (1, 0), (1, 1))]


def wide(value):
    return value.astype(jnp.float32)


def dot(a, b, dims=NN):
    return lax.dot_general(a, b, dims, preferred_element_type=jnp.float32)


ROWS = 256


TN = (((0,), (0,)), ((), ()))
BACK_ROWS = 1024
KEY_ROWS = 512


def three(value):
    high = value.astype(jnp.bfloat16).astype(jnp.float32)
    middle = (value - high).astype(jnp.bfloat16).astype(jnp.float32)
    return high, middle, value - high - middle


def mean_of(value):
    return jnp.mean(value, axis=-1, keepdims=True)


TN = (((0,), (0,)), ((), ()))
BACK_ROWS = 512
KEY_ROWS = 1024


def three(value):
    high = value.astype(jnp.bfloat16).astype(jnp.float32)
    middle = (value - high).astype(jnp.bfloat16).astype(jnp.float32)
    return high, middle, value - high - middle


def mean_of(value):
    return jnp.mean(value, axis=-1, keepdims=True)


def feed_kernel(
    length, context_rows_far, tok_far, cot_far, wo_far, small_all, vectors, wi_far, wu_far,
    hu_far, hi_far, ho_far, hs_far, output, back_context, back_residual,
    send_sem, local_sem, sem1, sem2, sem_out, sem_back,
    gu, gi, go, gs, wi, back_near, inner_shift, active, back_inner, output_low,
    r1u, r1i, r1o, r1s, r2u, context_rows, tok_own, cot_own, wo, load_sem,
):
    bf16, f32 = jnp.bfloat16, jnp.float32
    y, x, z, c = place()
    spot = y * 4 + z
    mine = x * 2 + c
    other_core = at(y, x, z, 1 - c)
    across = at(y, 1 - x, z, c)
    diagonal = at(y, 1 - x, z, 1 - c)
    spots = [column(lax.rem(spot + k, 8)) for k in range(1, 8)]
    y1, x1 = jnp.where(c == 0, y, 1 - y), jnp.where(c == 0, 1 - x, x)
    y2, x2 = jnp.where(c == 0, 1 - y, y), jnp.where(c == 0, x, 1 - x)
    first = at(y1, x1, z, c)
    own, near1, near2 = y * 2 + x, y1 * 2 + x1, y2 * 2 + x2
    far = (1 - y) * 2 + 1 - x
    order = (far, near1, near2, own)
    parts = (gu, gi, go, gs)
    r1 = (r1u, r1i, r1o, r1s)
    group = quad(x, c)
    move = Mover(send_sem, local_sem, other_core)
    width = wo.shape[0]
    ff = wi.shape[1]
    steps = ff // width
    for source, target in ((context_rows_far, context_rows), (wo_far, wo), (tok_far, tok_own), (cot_far, cot_own)):
        move.keep(source, target)

    def weights_load(step):
        cols = pl.ds(pl.multiple_of(step * width, width), width)
        return (
            pltpu.make_async_copy(wi_far.at[:, cols], wi.at[:, cols], load_sem.at[step, 0]),
            pltpu.make_async_copy(wu_far.at[step], gu.at[step], load_sem.at[step, 1]),
        )

    def load(step, _):
        for copy in weights_load(step):
            copy.start()
        return 0

    lax.fori_loop(0, steps, load, 0)
    meet([at(yy, x, zz, c) for yy, zz in spots] + [across, other_core, diagonal])

    piece = tok_own.shape[1]
    rows = tok_own.shape[0] * piece
    ff_piece = ff // 32
    for block in range(32):
        inner_shift[:, block * ff_piece : (block + 1) * ff_piece] = wide(small_all[block])[8:9, :ff_piece]

    spot_at = lax.broadcasted_iota(jnp.int32, (8, piece, 1), 0)
    position = number(spot_at // 4, x, lax.rem(spot_at, 4), c) * piece
    position = position + lax.broadcasted_iota(jnp.int32, (8, piece, 1), 1)
    keep = jnp.where(position < length[spot], 1.0, 0.0).reshape(rows, 1) > 0.5

    def column_sum(item):
        return jnp.sum(item, axis=0, keepdims=True)

    def square(item):
        return jnp.sum(item * item)

    for n in range(4):
        move.kept(n)
    branch = vectors[4:5, :] + dot(context_rows[0].reshape(rows, GROUP), wo[:GROUP, :])
    for g in range(1, 4):
        branch = branch + dot(context_rows[g].reshape(rows, GROUP), wo[g * GROUP : (g + 1) * GROUP, :])
    residual = wide(tok_own[...].reshape(rows, width)) + branch
    branch_total = square(jnp.where(keep, branch, 0.0))
    average = mean_of(residual)
    centered = residual - average
    inverse = lax.rsqrt(mean_of(centered * centered) + EPS)
    unit = centered * inverse
    second_low = (unit * vectors[5:6, :] + vectors[6:7, :]).astype(bf16)
    back_result = jnp.where(keep, wide(cot_own[...].reshape(rows, width)), 0.0)
    back_feed = back_result.astype(bf16)

    def middle(step, sums_here):
        back_second, feed = sums_here
        for copy in weights_load(step):
            copy.wait()
        cols = pl.ds(pl.multiple_of(step * width, width), width)
        wi_here = wi[:, cols]
        inner = dot(second_low, wi_here) + inner_shift[:, cols]
        chance = 0.5 * (1.0 + lax.erf(inner * 0.7071067811865476))
        low = (inner * chance).astype(bf16)
        active[:, cols] = low
        wu_here = gu[step].reshape(width, width)
        slope = chance + inner * jnp.exp(inner * inner * -0.5) * 0.3989422804014327
        back = (dot(back_feed, wu_here, NT) * slope).astype(bf16)
        back_inner[:, cols] = back
        return back_second + dot(back, wi_here, NT), feed + dot(low, wu_here)

    zero = jnp.zeros((rows, width), f32)
    back_second, feed = lax.fori_loop(0, steps, middle, (zero, zero))
    scaled = back_second * vectors[5:6, :]
    back_res = back_result + inverse * (scaled - mean_of(scaled) - unit * mean_of(scaled * unit))
    back_residual[...] = back_res
    back_branch = back_res.astype(bf16)
    short = jnp.concatenate(
        [
            column_sum(wide(back_feed)), column_sum(back_second * unit), column_sum(back_second),
            column_sum(wide(back_branch)), jnp.zeros((4, width), f32),
        ],
        axis=0,
    )
    for g in range(4):
        back_near[g] = dot(back_branch, wo[g * GROUP : (g + 1) * GROUP, :], NT).astype(bf16).reshape(8, piece, GROUP)
    for xx, cc in group[::-1]:
        for yy in range(2):
            move.push(
                back_near.at[xx * 2 + cc, pl.ds(yy * 4, 4)],
                back_context.at[yy, x, :, c],
                sem_back.at[mine, yy],
                at(y, xx, z, cc),
            )
    for yy in range(2):
        move.keep(back_near.at[mine, pl.ds(yy * 4, 4)], back_context.at[yy, x, :, c])

    feed = feed + vectors[7:8, :]
    result = jnp.where(keep, residual + feed, 0.0)
    output_low[...] = result.astype(bf16).reshape(8, piece, width)
    for yy, zz in spots:
        move.push(output_low.at[yy * 4 + zz], output.at[spot], sem_out.at[spot], at(yy, x, zz, c))
    move.keep(output_low.at[spot], output.at[spot])

    totals = (square(result), branch_total, square(jnp.where(keep, feed, 0.0)))
    lane = lax.broadcasted_iota(jnp.int32, (1, 128), 1)
    stat_row = jnp.where(lane == 0, totals[0], jnp.where(lane == 1, totals[1], jnp.where(lane == 2, totals[2], 0.0)))
    def to_core(i, quarter):
        move.push(parts[i].at[quarter, :, 1 - c], r1[i].at[quarter], sem1.at[i, quarter], other_core)

    def gather(i, quarter):
        move.landed(r1[i].at[quarter], sem1.at[i, quarter])
        r1[i][quarter] = r1[i][quarter] + parts[i][quarter, :, c]

    lead = width // 32
    wide_piece = ff // 32
    for step in range(steps):
        grad = dot(active[:, step * width : (step + 1) * width], back_feed, TN).astype(bf16)
        for zz in range(4):
            for cc in range(2):
                row = (zz * 2 + cc) * wide_piece
                gu[step, zz, cc] = grad[row : row + wide_piece, :]
        to_core(0, step)
    for step in range(steps):
        grad = dot(second_low, back_inner[:, step * width : (step + 1) * width], TN)
        for block in range(32):
            gi[block // 8, block % 8 // 2, block % 2, :, step * width : (step + 1) * width] = grad[
                block * lead : (block + 1) * lead, :
            ].astype(bf16)
    for quarter in order:
        to_core(1, quarter)
    for slot, quarter in ((1, far), (0, near1)):
        gather(0, quarter)
        move.push(r1u.at[quarter], r2u.at[slot], sem2.at[slot], first)
    for quarter in (near2, own):
        gather(0, quarter)
    for g in range(4):
        grad = dot(context_rows[g].reshape(rows, GROUP), back_branch, TN)
        for zz in range(4):
            for cc in range(2):
                row = (zz * 2 + cc) * lead
                go[g, zz, cc] = grad[row : row + lead, :].astype(bf16)
        to_core(2, g)

    long = column_sum(wide(back_inner[...]))
    for block in range(32):
        at_block = (block // 8, block % 8 // 2, block % 2)
        gs[at_block] = jnp.zeros((8, 128), f32)
        gs[at_block + (slice(0, 8), slice(0, lead))] = short[:, block * lead : (block + 1) * lead]
        gs[at_block + (slice(4, 5), slice(0, wide_piece))] = long[:, block * wide_piece : (block + 1) * wide_piece]
        gs[at_block + (slice(5, 6), slice(None))] = stat_row
    for quarter in order:
        to_core(3, quarter)
    for i in (1, 2, 3):
        for quarter in order:
            gather(i, quarter)
    for slot, quarter in ((1, near2), (0, own)):
        move.landed(r2u.at[slot], sem2.at[slot])
        r1u[quarter] = r1u[quarter] + r2u[slot]
    for source, target in zip(r1, (hu_far, hi_far, ho_far, hs_far)):
        move.keep(source, target)
    for xx, cc in group:
        for yy in range(2):
            move.landed(back_context.at[yy, xx, :, cc], sem_back.at[xx * 2 + cc, yy])
    for k in range(1, 8):
        t = lax.rem(spot + 8 - k, 8)
        move.landed(output.at[t], sem_out.at[t])
    move.finish(range(4, len(move.local)))


def backward_kernel(
    hu, hi, ho, hs, query_far, key_far, value_far, context_far, back_far, weight_far, first_far, tok_far, residual_far, vectors,
    out_o, out_i, out_u, out_s, out_joint, tokens_gradient, late,
    send_sem, local_sem, sem2, sem3, sem4, sem_y, sem_z, sem_g, sem_c, sem_x, sem_t, sem_s,
    r1u, r1i, r1o, r1s, r2u, r2i, r2o, r2s, r3u, r3i, r3o, r3s, r4u, r4i, r4o, r4s,
    joint, back_query, widened, query, key, value, context, back_context, joint_weight, tok_own, back_residual,
    first_low, back_first, rc, rx, gj, ry, rz, sj, joint_land, gradient_low, small, small_all,
):
    bf16, f32 = jnp.bfloat16, jnp.float32
    y, x, z, c = place()
    spot = y * 4 + z
    mine = x * 2 + c
    me = number(y, x, z, c)
    other_core = at(y, x, z, 1 - c)
    across = at(y, 1 - x, z, c)
    down = at(1 - y, x, z, c)
    y1, x1 = jnp.where(c == 0, y, 1 - y), jnp.where(c == 0, 1 - x, x)
    y2, x2 = jnp.where(c == 0, 1 - y, y), jnp.where(c == 0, x, 1 - x)
    first, second = at(y1, x1, z, c), at(y2, x2, z, c)
    line = [lax.rem(z + k, 4) for k in range(1, 4)]
    line_devices = [at(y, x, zz, c) for zz in line]
    own, near1, near2 = y * 2 + x, y1 * 2 + x1, y2 * 2 + x2
    far = (1 - y) * 2 + 1 - x
    order = (far, near1, near2, own)
    group = quad(x, c)
    others = []
    for k in range(1, 32):
        t = lax.rem(me + k, 32)
        others.append((t, (t // 8, lax.rem(t, 8))))
    move = Mover(send_sem, local_sem, other_core)
    move.keep(back_far, back_context)
    move.keep(context_far, context)
    for h in range(3):
        for source, target in ((key_far, key), (query_far, query), (value_far, value)):
            move.keep(source.at[h], target.at[h])
    meet([device for _, device in others])
    zero = move.zero
    sources = (hu, hi, ho, hs)
    results = (out_u, out_i, out_o, out_s)
    r1, r2 = (r1u, r1i, r1o, r1s), (r2u, r2i, r2o, r2s)
    r3, r4 = (r3u, r3i, r3o, r3s), (r4u, r4i, r4o, r4s)
    for i in range(4):
        move.keep(sources[i], r1[i])
    for source, target in (
        (weight_far, joint_weight), (first_far, first_low), (tok_far, tok_own), (residual_far, back_residual)
    ):
        move.keep(source, target)

    def stage2(i):
        for slot, quarter in ((1, far), (0, near1)):
            move.push_made(
                lambda slot=slot, quarter=quarter: (
                    sources[i].at[quarter], r2[i].at[zero + slot], sem2.at[zero + i, zero + slot]
                ),
                first,
            )

    def stage3(i):
        if i:
            move.landed(r2[i].at[zero + 1], sem2.at[zero + i, zero + 1])
            r1[i][near2] = r1[i][near2] + r2[i][1]
        source = r1[i] if i else sources[i]
        move.push_made(lambda: (source.at[near2], r3[i], sem3.at[zero + i]), second)

    def stage4(i):
        total = wide(r1[i][own])
        if i:
            move.landed(r2[i].at[zero], sem2.at[zero + i, zero])
            total = total + wide(r2[i][0])
        move.landed(r3[i], sem3.at[zero + i])
        r1[i][own] = (total + wide(r3[i][...])).astype(r1[i].dtype)
        for k in range(3):
            move.push_made(
                lambda k=k: (r1[i].at[own, line[k]], r4[i].at[zero + k], sem4.at[zero + i, zero + k]),
                line_devices[k],
            )

    def stage5(i):
        total = wide(r1[i][own, z])
        for k in range(3):
            move.landed(r4[i].at[k], sem4.at[i, k])
            total = total + wide(r4[i][k])
        results[i][...] = total

    rows_all = query.shape[1]
    piece = tok_own.shape[1]
    rows = tok_own.shape[0] * piece
    width = tok_own.shape[2]
    scale = DH ** (-0.5)
    eye = jnp.eye(DH, 2 * DH, dtype=bf16)
    side_lane = lax.broadcasted_iota(jnp.int32, (rows, DH), 1)
    per_head = rows_all // KEY_ROWS
    between = {
        0: lambda: (stage4(0), stage3(2), stage3(3)),
        1: lambda: (stage3(1), stage4(2), stage4(3)),
        2: lambda: None,
    }
    stage3(0)
    stage2(2)
    stage2(3)
    stage2(1)
    move.kept(0)
    move.kept(1)
    for h in range(3):
        for n in range(3):
            move.kept(2 + 3 * h + n)
        if h == 0:
            for n in range(11, 15):
                move.kept(n)
        lanes = slice(h * DH, (h + 1) * DH)
        for q in range(4):
            here = slice(q * rows, (q + 1) * rows)
            backs = back_context[q // 2, q % 2].reshape(rows, GROUP)[:, lanes]
            spread = jnp.sum(wide(backs) * wide(context[here, lanes]), axis=1, keepdims=True)
            high, mid, low = three(spread)
            side = jnp.where(
                side_lane == 0, -high, jnp.where(side_lane == 1, -mid, jnp.where(side_lane == 2, -low, 0.0))
            )
            widened[here, :] = jnp.concatenate([backs, side.astype(bf16)], axis=1)
        back_query[...] = jnp.zeros_like(back_query)

        def block(i, _):
            keys = pl.ds(i * KEY_ROWS, KEY_ROWS)
            key_here, value_here = key[h, keys, :], value[h, keys, :]
            turned = dot(eye, key_here, NT).astype(bf16)
            back_key = jnp.zeros((KEY_ROWS, DH), f32)
            back_value = jnp.zeros((KEY_ROWS, DH), f32)
            for q in range(rows_all // BACK_ROWS):
                here = slice(q * BACK_ROWS, (q + 1) * BACK_ROWS)
                queries, backs = query[h, here, :], widened[here, :]
                chances = jnp.exp(dot(key_here, queries, NT))
                back_scores = (chances * dot(value_here, backs, NT)).astype(bf16)
                back_key = back_key + dot(back_scores, queries[:, :DH])
                back_value = back_value + dot(chances.astype(bf16), backs[:, :DH])
                back_query[:, here] += dot(turned, back_scores)
            joint[keys, GROUP + h * DH : GROUP + (h + 1) * DH] = back_key.astype(bf16)
            joint[keys, 2 * GROUP + h * DH : 2 * GROUP + (h + 1) * DH] = back_value.astype(bf16)
            return 0

        lax.fori_loop(0, per_head, block, 0)
        joint[:, lanes] = (back_query[...] * scale).T.astype(bf16)
        between[h]()

    move.kept(15)
    for k in range(2):
        for yy in range(2):
            xx = lax.rem(x + 1 + k, 2)
            here = pl.ds((yy * 2 + xx) * rows, rows)
            back_first[yy, xx] = dot(joint[here, :], joint_weight[...], NT).astype(bf16).reshape(4, 2, piece, width)
            move.push(back_first.at[yy, xx, :, 1 - c], rc.at[yy, xx], sem_c.at[yy, xx], other_core)
    for yy in range(2):
        move.landed(rc.at[yy, 1 - x], sem_c.at[yy, 1 - x])
        rc[yy, 1 - x] = rc[yy, 1 - x] + back_first[yy, 1 - x, :, c]
        move.push(rc.at[yy, 1 - x], rx.at[yy], sem_x.at[yy], across)
    move.kept(16)
    grad = dot(first_low[...], joint[...], TN)
    lead = width // 32
    for block_at in range(32):
        gj[block_at // 16, block_at // 8 % 2, block_at % 8 // 2, block_at % 2] = grad[
            block_at * lead : (block_at + 1) * lead, :
        ].astype(bf16)
    move.push(gj.at[1 - y], ry, sem_y, down)
    move.kept(17)
    move.kept(18)
    stage4(1)
    shifts = jnp.sum(wide(joint[...]), axis=0, keepdims=True)
    small[...] = jnp.zeros_like(small)
    for k in range(8):
        for row, kind in ((2, 0), (3, 2)):
            start = kind * GROUP + k * lead
            small[mine * 8 + k, row : row + 1, :lead] = shifts[:, start : start + lead]
    move.landed(ry, sem_y)
    ry[...] = ry[...] + gj[y]
    for k in range(3):
        move.push(ry.at[:, line[k]], rz.at[k], sem_z.at[k], line_devices[k])
    for yy in range(2):
        move.landed(rc.at[yy, x], sem_c.at[yy, x])

    kept = []
    gains = jnp.zeros((2, width), f32)
    half = rows // 2
    for yy in range(2):
        inputs = wide(tok_own[yy * 4 : yy * 4 + 4].reshape(half, width))
        centered = inputs - mean_of(inputs)
        inverse = lax.rsqrt(mean_of(centered * centered) + EPS)
        unit = centered * inverse
        move.landed(rx.at[yy], sem_x.at[yy])
        whole = wide(rc[yy, x]) + wide(back_first[yy, x, :, c]) + wide(rx[yy])
        back_one = whole.reshape(half, width)
        gains = gains + jnp.concatenate(
            [jnp.sum(back_one * unit, axis=0, keepdims=True), jnp.sum(back_one, axis=0, keepdims=True)], axis=0
        )
        if yy == 1:
            for block_at in range(32):
                small[block_at, 0:2, :lead] = gains[:, block_at * lead : (block_at + 1) * lead]
            for t, device in others:
                move.push(small.at[t], small_all.at[me], sem_s.at[me], device)
            kept.append(move.keep(small.at[me], small_all.at[me]))
        scaled = back_one * vectors[0:1, :]
        back_tokens = back_residual[yy * half : (yy + 1) * half, :] + inverse * (
            scaled - mean_of(scaled) - unit * mean_of(scaled * unit)
        )
        gradient_low[yy * 4 : yy * 4 + 4] = back_tokens.astype(bf16).reshape(4, piece, width)
        for zz in [lax.rem(z + k, 4) for k in range(4)]:
            there = y * 0 + yy
            move.push_made(
                lambda zz=zz, yy=yy: (gradient_low.at[yy * 4 + zz], tokens_gradient.at[spot], sem_t.at[spot]),
                at(there, x, zz, c),
                jnp.logical_or(y != yy, z != zz),
            )
    kept.append(move.keep(gradient_low.at[spot], tokens_gradient.at[spot]))

    total = wide(ry[:, z])
    for k in range(3):
        move.landed(rz.at[k], sem_z.at[k])
        total = total + wide(rz[k])
    sj[...] = total
    for xx, cc in group:
        move.push(sj.at[xx, cc], joint_land.at[mine], sem_g.at[mine], at(y, xx, z, cc))
    gone = move.keep(sj.at[x, c], joint_land.at[mine])
    for i in (0, 2, 3, 1):
        stage5(i)
    move.kept(gone)
    for xx, cc in group:
        move.landed(joint_land.at[xx * 2 + cc], sem_g.at[xx * 2 + cc])
    for g in range(4):
        for kind in range(3):
            start = kind * width + g * GROUP
            out_joint[:, start : start + GROUP] = joint_land[g, :, kind * GROUP : (kind + 1) * GROUP]
    for spot_kept in kept:
        move.kept(spot_kept)
    for t, _ in others:
        move.landed(small_all.at[t], sem_s.at[t])
    late[...] = jnp.sum(small_all[...], axis=0)
    for k in range(1, 8):
        t = lax.rem(spot + 8 - k, 8)
        move.landed(tokens_gradient.at[t], sem_t.at[t])
    move.finish()


def owner_device(
    tokens,
    lengths,
    first_gain,
    first_bias,
    joint_weight,
    query_bias,
    value_bias,
    output_weight,
    output_bias,
    second_gain,
    second_bias,
    inner_weight,
    inner_bias,
    outer_weight,
    outer_bias,
    cotangent,
):
    bf16, f32 = jnp.bfloat16, jnp.float32
    y, x, z, c = place()
    mine = x * 2 + c
    slots, piece, width = tokens.shape
    ff = inner_weight.shape[1]
    short = jnp.stack(
        [first_gain, first_bias, query_bias, value_bias, output_bias, second_gain, second_bias, outer_bias]
    )
    lead = short.shape[1]
    ff_piece = inner_bias.shape[0]
    small = jnp.concatenate(
        [
            jnp.pad(short, ((0, 0), (0, ff_piece - lead))),
            jnp.broadcast_to(inner_bias, (8, ff_piece)),
        ],
        axis=0,
    )
    hbm, vmem = pltpu.HBM, pltpu.VMEM
    dma, regular = pltpu.SemaphoreType.DMA, pltpu.SemaphoreType.REGULAR
    rows_all = 32 * piece
    natural = (2, 2, 4, 2, piece)
    joint_four = jnp.transpose(joint_weight.reshape(lead, 3, 4, GROUP), (2, 0, 1, 3)).reshape(4, lead, 3 * GROUP)
    forward_outs = [
        ((rows_all, width), bf16, hbm),
        ((3, rows_all, 2 * DH), bf16, hbm),
        ((3, rows_all, 2 * DH), bf16, hbm),
        ((3, rows_all, 2 * DH), bf16, hbm),
        ((rows_all, GROUP), bf16, hbm),
        ((4, 2, 4, piece, GROUP), bf16, vmem),
        ((8, piece, width), bf16, hbm),
        ((8, piece, width), bf16, hbm),
        ((32,) + output_weight.shape, bf16, hbm),
        ((32,) + inner_weight.shape, bf16, hbm),
        ((32,) + outer_weight.shape, bf16, hbm),
        ((32,) + small.shape, bf16, vmem),
        ((width, 3 * GROUP), bf16, hbm),
        ((8, width), f32, vmem),
    ]
    (
        first_low, query, key, value, context, context_rows, cot_own, tok_own, wo_all, wi_all, wu_all, small_all, joint_here, vectors
    ) = comm_call(
        forward_kernel,
        forward_outs,
        (lengths, tokens, cotangent, joint_four, output_weight, inner_weight, outer_weight, small),
        220, 24,
        [(32,), (8,), (3, 32), (32,), (4,), (4,), (4,), (4, 2), (4, 4), (4,)],
        [
            vmem((32, piece, width), bf16),
            vmem((2, 2, 4, 2, lead, 3 * GROUP), bf16),
            vmem((3, 72, rows_all), bf16),
            vmem(natural + (GROUP,), bf16),
            vmem((rows_all, 512), f32),
            vmem((rows_all, 512), f32),
            vmem((3, 512, DH), bf16),
            vmem((rows_all, width), bf16),
            vmem((3, rows_all, 2 * DH), bf16),
            vmem((3, rows_all, 2 * DH), bf16),
            vmem((3, rows_all, 2 * DH), bf16),
            vmem((rows_all, GROUP), bf16),
            vmem((width, 3 * GROUP), bf16),
        ],
        0,
        [pltpu.SMEM, hbm, hbm, hbm, hbm, hbm, hbm, hbm],
    )
    rows = 8 * piece
    grid = (4, 4, 2)
    kinds = [
        (outer_weight.shape, bf16),
        (inner_weight.shape, bf16),
        (output_weight.shape, bf16),
        ((8, 128), f32),
    ]
    hu, hi, ho, hs, output, back_context, back_residual = comm_call(
        feed_kernel,
        [((4, 4) + shape, dtype, hbm) for shape, dtype in kinds]
        + [
            (tokens.shape, bf16, hbm),
            (natural + (GROUP,), bf16, vmem),
            ((rows, width), f32, vmem),
        ],
        (
            lengths, context_rows.reshape(4, 8, piece, GROUP), tok_own, cot_own, wo_all.reshape(width, width), small_all, vectors,
            wi_all.reshape(width, ff), wu_all.reshape(grid + outer_weight.shape),
        ),
        48, 24, [(4, 4), (2,), (8,), (4, 2)],
        [vmem(grid + shape, dtype) for shape, dtype in kinds]
        + [
            vmem((width, ff), bf16),
            vmem((4, 8, piece, GROUP), bf16),
            vmem((1, ff), f32),
            vmem((rows, ff), bf16),
            vmem((rows, ff), bf16),
            vmem((8, piece, width), bf16),
        ]
        + [vmem((4, 4) + shape, dtype) for shape, dtype in kinds]
        + [
            vmem((2, 4) + outer_weight.shape, bf16),
            vmem((4, 8, piece, GROUP), bf16),
            vmem((8, piece, width), bf16),
            vmem((8, piece, width), bf16),
            vmem((width, width), bf16),
            dma((4, 2)),
        ],
        1,
        [pltpu.SMEM] + [hbm] * 4 + [vmem] * 2 + [hbm] * 2,
    )
    out_o, out_i, out_u, out_s, joint_shard, tokens_gradient, late = comm_call(
        backward_kernel,
        [
            (output_weight.shape, f32, vmem),
            (inner_weight.shape, f32, vmem),
            (outer_weight.shape, f32, vmem),
            ((8, 128), f32, vmem),
            (joint_weight.shape, f32, vmem),
            (tokens.shape, bf16, hbm),
            ((8, 128), f32, vmem),
        ],
        (
            hu, hi, ho, hs, query, key, value, context, back_context, joint_here, first_low, tok_own, back_residual, vectors,
        ),
        110, 32,
        [(4, 2), (4,), (4, 3), (), (3,), (4,), (2, 2), (2,), (8,), (32,)],
        [vmem((4, 4) + shape, dtype) for shape, dtype in kinds]
        + [vmem((2, 4) + shape, dtype) for shape, dtype in kinds]
        + [vmem((4,) + shape, dtype) for shape, dtype in kinds]
        + [vmem((3,) + shape, dtype) for shape, dtype in kinds]
        + [
            vmem((rows_all, 3 * GROUP), bf16),
            vmem((DH, rows_all), f32),
            vmem((rows_all, 2 * DH), bf16),
            vmem(query.shape, bf16),
            vmem(key.shape, bf16),
            vmem(value.shape, bf16),
            vmem(context.shape, bf16),
            vmem(back_context.shape, bf16),
            vmem(joint_here.shape, bf16),
            vmem(tok_own.shape, bf16),
            vmem(back_residual.shape, f32),
            vmem((rows_all, width), bf16),
            vmem(natural + (width,), bf16),
            vmem((2, 2, 4, piece, width), bf16),
            vmem((2, 4, piece, width), bf16),
            vmem((2, 2, 4, 2, lead, 3 * GROUP), bf16),
            vmem((2, 4, 2, lead, 3 * GROUP), bf16),
            vmem((3, 2, 2, lead, 3 * GROUP), bf16),
            vmem((2, 2, lead, 3 * GROUP), f32),
            vmem((4, lead, 3 * GROUP), f32),
            vmem((8, piece, width), bf16),
            vmem((32, 8, 128), f32),
            vmem((32, 8, 128), f32),
        ],
        2,
        [hbm] * 13 + [vmem],
    )
    count = jnp.sum(lengths).astype(f32) * width
    stats = jnp.sqrt(out_s[5, :3] / count + 1e-06)
    return (
        output,
        tokens_gradient,
        late[0, :lead],
        late[1, :lead],
        joint_shard,
        late[2, :lead],
        late[3, :lead],
        out_o,
        out_s[3, :lead],
        out_s[1, :lead],
        out_s[2, :lead],
        out_i,
        out_s[4, : inner_bias.shape[0]],
        out_u,
        out_s[0, :lead],
        stats,
    )


def solution(mesh):
    in_specs = (
        P(None, ("head", "blk"), None),
        P(),
        P(("head", "blk")),
        P(("head", "blk")),
        P(("head", "blk"), None),
        P(("head", "blk")),
        P(("head", "blk")),
        P(("head", "blk"), None),
        P(("head", "blk")),
        P(("head", "blk")),
        P(("head", "blk")),
        P(("head", "blk"), None),
        P(("head", "blk")),
        P(("head", "blk"), None),
        P(("head", "blk")),
        P(None, ("head", "blk"), None),
    )
    out_specs = (
        P(None, ("head", "blk"), None),
        P(None, ("head", "blk"), None),
        P(("head", "blk")),
        P(("head", "blk")),
        P(("head", "blk"), None),
        P(("head", "blk")),
        P(("head", "blk")),
        P(("head", "blk"), None),
        P(("head", "blk")),
        P(("head", "blk")),
        P(("head", "blk")),
        P(("head", "blk"), None),
        P(("head", "blk")),
        P(("head", "blk"), None),
        P(("head", "blk")),
        P(),
    )
    small_slice = dict(mesh.shape) == {"head": 4, "blk": 8}
    device_work = owner_device if small_slice else on_device
    return jax.shard_map(
        device_work, mesh=mesh, in_specs=in_specs, out_specs=out_specs, check_vma=False
    )
```

```python
import jax
import jax.numpy as jnp
from jax import lax
from jax.experimental import pallas as pl
from jax.experimental.pallas import tpu as pltpu
from jax.sharding import PartitionSpec as P

H = 12
DH = 64


EPS = 1e-12
NEG = -1e30


def passed_along(value, axis, steps):
    count = lax.axis_size(axis)
    pairs = [(source, (source + steps) % count) for source in range(count)]
    return lax.ppermute(value, axis, pairs)


def normalize(values, gain, shift):
    average = jnp.mean(values, axis=-1, keepdims=True)
    centered = values - average
    inverse = lax.rsqrt(jnp.mean(centered * centered, axis=-1, keepdims=True) + EPS)
    normed = centered * inverse
    return (normed * gain + shift, normed, inverse)


def normalize_back(incoming, normed, inverse, gain):
    scaled = incoming * gain
    inner = (
        scaled
        - jnp.mean(scaled, axis=-1, keepdims=True)
        - normed * jnp.mean(scaled * normed, axis=-1, keepdims=True)
    )
    return (
        inner * inverse,
        jnp.sum(incoming * normed, axis=(0, 1)),
        jnp.sum(incoming, axis=(0, 1)),
    )


def gelu_exact(values):
    return jax.nn.gelu(values, approximate=False)


def key_mask(lengths, source, piece_rows, block_count, head_count):
    rows_here = jnp.arange(head_count * piece_rows, dtype=jnp.int32)
    position = (
        rows_here // piece_rows * block_count + source
    ) * piece_rows + rows_here % piece_rows
    return position[None, :] < lengths[:, None]


def attend(query_part, state, keys_block, values_block, mask):
    best, total, running = state
    scores = jnp.einsum(
        "sqhd,skhd->sqhk", query_part, keys_block, preferred_element_type=jnp.float32
    ) * DH ** (-0.5)
    scores = jnp.where(mask[:, None, None, :], scores, NEG)
    fresh = jnp.maximum(best, jnp.max(scores, axis=-1))
    decay = jnp.exp(best - fresh)
    weights = jnp.exp(scores - fresh[..., None])
    total = total * decay + jnp.sum(weights, axis=-1)
    running = running * decay[..., None] + jnp.einsum(
        "sqhk,skhd->sqhd",
        weights.astype(jnp.bfloat16),
        values_block,
        preferred_element_type=jnp.float32,
    )
    return (fresh, total, running)


def block_grads(query_part, back_part, total_part, spread_part, keys_block, values_block, mask):
    scale = DH ** (-0.5)
    scores = (
        jnp.einsum("sqhd,skhd->sqhk", query_part, keys_block, preferred_element_type=jnp.float32)
        * scale
    )
    scores = jnp.where(mask[:, None, None, :], scores, NEG)
    chances = jnp.exp(scores - total_part[..., None])
    back_chances = jnp.einsum(
        "sqhd,skhd->sqhk", back_part, values_block, preferred_element_type=jnp.float32
    )
    back_scores = (chances * (back_chances - spread_part[..., None])).astype(jnp.bfloat16)
    query_step = (
        jnp.einsum("sqhk,skhd->sqhd", back_scores, keys_block, preferred_element_type=jnp.float32)
        * scale
    )
    key_step = (
        jnp.einsum("sqhk,sqhd->skhd", back_scores, query_part, preferred_element_type=jnp.float32)
        * scale
    )
    value_step = jnp.einsum(
        "sqhk,sqhd->skhd",
        chances.astype(jnp.bfloat16),
        back_part,
        preferred_element_type=jnp.float32,
    )
    return (query_step, key_step, value_step)


def on_device(
    tokens,
    lengths,
    first_gain,
    first_bias,
    joint_weight,
    query_bias,
    value_bias,
    output_weight,
    output_bias,
    second_gain,
    second_bias,
    inner_weight,
    inner_bias,
    outer_weight,
    outer_bias,
    cotangent,
):
    head_count = lax.axis_size("head")
    block_count = lax.axis_size("blk")
    block = lax.axis_index("blk")
    quarter = lax.axis_index("head")
    (
        gain_one,
        shift_one,
        joint_full,
        query_shift,
        value_shift,
        output_full,
        output_shift,
        gain_two,
        shift_two,
        inner_full,
        inner_shift,
        outer_full,
        outer_shift,
    ) = (
        lax.all_gather(first_gain, ("head", "blk"), axis=0, tiled=True),
        lax.all_gather(first_bias, ("head", "blk"), axis=0, tiled=True),
        lax.all_gather(joint_weight, ("head", "blk"), axis=0, tiled=True),
        lax.all_gather(query_bias, ("head", "blk"), axis=0, tiled=True),
        lax.all_gather(value_bias, ("head", "blk"), axis=0, tiled=True),
        lax.all_gather(output_weight, ("head", "blk"), axis=0, tiled=True),
        lax.all_gather(output_bias, ("head", "blk"), axis=0, tiled=True),
        lax.all_gather(second_gain, ("head", "blk"), axis=0, tiled=True),
        lax.all_gather(second_bias, ("head", "blk"), axis=0, tiled=True),
        lax.all_gather(inner_weight, ("head", "blk"), axis=0, tiled=True),
        lax.all_gather(inner_bias, ("head", "blk"), axis=0, tiled=True),
        lax.all_gather(outer_weight, ("head", "blk"), axis=0, tiled=True),
        lax.all_gather(outer_bias, ("head", "blk"), axis=0, tiled=True),
    )
    sequences, piece_rows, width = tokens.shape
    heads_here = H // head_count
    head_width = heads_here * DH
    rows = head_count * piece_rows
    shape_heads = (sequences, rows, heads_here, DH)
    shape_flat = (sequences, rows, head_width)
    own_position = (quarter * block_count + block) * piece_rows + jnp.arange(
        piece_rows, dtype=jnp.int32
    )
    valid = own_position[None, :] < lengths[:, None]
    keep = valid[..., None]
    inputs = tokens.astype(jnp.float32)
    gain_one_wide = gain_one.astype(jnp.float32)
    gain_two_wide = gain_two.astype(jnp.float32)
    first_out, first_unit, first_scale = normalize(
        inputs, gain_one_wide, shift_one.astype(jnp.float32)
    )
    first_low = first_out.astype(jnp.bfloat16)
    joint = jnp.einsum("scd,de->sce", first_low, joint_full, preferred_element_type=jnp.float32)
    query_flat = (joint[..., :width] + query_shift.astype(jnp.float32)).astype(jnp.bfloat16)
    key_flat = joint[..., width : 2 * width].astype(jnp.bfloat16)
    value_flat = (joint[..., 2 * width :] + value_shift.astype(jnp.float32)).astype(jnp.bfloat16)
    query_flat, key_flat, value_flat = (
        lax.all_to_all(query_flat, "head", split_axis=2, concat_axis=1, tiled=True),
        lax.all_to_all(key_flat, "head", split_axis=2, concat_axis=1, tiled=True),
        lax.all_to_all(value_flat, "head", split_axis=2, concat_axis=1, tiled=True),
    )
    query_rows = query_flat.reshape(shape_heads)
    key_rows = key_flat.reshape(shape_heads)
    value_rows = value_flat.reshape(shape_heads)

    def visit(carry):
        keys_block, values_block, source, state = carry
        keys_block, values_block = passed_along((keys_block, values_block), "blk", 1)
        source = (source - 1) % block_count
        mask = key_mask(lengths, source, piece_rows, block_count, head_count)
        return (
            keys_block,
            values_block,
            source,
            attend(query_rows, state, keys_block, values_block, mask),
        )

    start_state = (
        jnp.full((sequences, rows, heads_here), NEG, jnp.float32),
        jnp.zeros((sequences, rows, heads_here), jnp.float32),
        jnp.zeros(shape_heads, jnp.float32),
    )
    first_state = attend(
        query_rows,
        start_state,
        key_rows,
        value_rows,
        key_mask(lengths, block, piece_rows, block_count, head_count),
    )
    carry = (key_rows, value_rows, block, first_state)
    carry = lax.fori_loop(0, block_count // 2 - 1, lambda turn, state: visit(visit(state)), carry)
    best, total, running = visit(carry)[3]
    context = running / total[..., None]
    log_total = best + jnp.log(total)
    context_low = context.astype(jnp.bfloat16).reshape(shape_flat)
    context_tokens = lax.all_to_all(context_low, "head", split_axis=1, concat_axis=2, tiled=True)
    branch = jnp.einsum(
        "sce,ed->scd", context_tokens, output_full, preferred_element_type=jnp.float32
    ) + output_shift.astype(jnp.float32)
    residual = inputs + branch
    second_out, second_unit, second_scale = normalize(
        residual, gain_two_wide, shift_two.astype(jnp.float32)
    )
    second_low = second_out.astype(jnp.bfloat16)
    inner = jnp.einsum(
        "scd,df->scf", second_low, inner_full, preferred_element_type=jnp.float32
    ) + inner_shift.astype(jnp.float32)
    activated = gelu_exact(inner).astype(jnp.bfloat16)
    feed = jnp.einsum(
        "scf,fd->scd", activated, outer_full, preferred_element_type=jnp.float32
    ) + outer_shift.astype(jnp.float32)
    result = residual + feed
    output = jnp.where(keep, result, 0.0).astype(jnp.bfloat16)
    sums = lax.psum(
        (
            jnp.sum(jnp.where(keep, result * result, 0.0)),
            jnp.sum(jnp.where(keep, branch * branch, 0.0)),
            jnp.sum(jnp.where(keep, feed * feed, 0.0)),
        ),
        ("head", "blk"),
    )
    count = jnp.sum(lengths).astype(jnp.float32) * width
    stats = jnp.sqrt(jnp.stack(sums) / count + 1e-06)
    back_result = jnp.where(keep, cotangent.astype(jnp.float32), 0.0)
    back_feed = back_result.astype(jnp.bfloat16)
    outer_gradient = jnp.einsum(
        "scf,scd->fd", activated, back_feed, preferred_element_type=jnp.float32
    )
    outer_shift_gradient = jnp.sum(back_feed.astype(jnp.float32), axis=(0, 1))
    back_active = jnp.einsum(
        "scd,fd->scf", back_feed, outer_full, preferred_element_type=jnp.float32
    )
    back_inner = jax.vjp(gelu_exact, inner)[1](back_active)[0].astype(jnp.bfloat16)
    inner_gradient = jnp.einsum(
        "scd,scf->df", second_low, back_inner, preferred_element_type=jnp.float32
    )
    inner_shift_gradient = jnp.sum(back_inner.astype(jnp.float32), axis=(0, 1))
    back_second = jnp.einsum(
        "scf,df->scd", back_inner, inner_full, preferred_element_type=jnp.float32
    )
    back_norm_two, gain_two_gradient, shift_two_gradient = normalize_back(
        back_second, second_unit, second_scale, gain_two_wide
    )
    back_residual = back_result + back_norm_two
    back_branch = back_residual.astype(jnp.bfloat16)
    output_gradient = jnp.einsum(
        "sce,scd->ed", context_tokens, back_branch, preferred_element_type=jnp.float32
    )
    output_shift_gradient = jnp.sum(back_branch.astype(jnp.float32), axis=(0, 1))
    back_context = jnp.einsum(
        "scd,ed->sce", back_branch, output_full, preferred_element_type=jnp.float32
    ).astype(jnp.bfloat16)
    back_context = lax.all_to_all(back_context, "head", split_axis=2, concat_axis=1, tiled=True)
    back_heads = back_context.reshape(shape_heads)
    spread = jnp.sum(back_heads.astype(jnp.float32) * context, axis=-1)
    zero_heads = jnp.zeros(shape_heads, jnp.float32)

    def pass_keys(carry):
        keys_block, values_block, key_sum, value_sum, query_sum, source = carry
        mask = key_mask(lengths, source, piece_rows, block_count, head_count)
        query_step, key_step, value_step = block_grads(
            query_rows, back_heads, log_total, spread, keys_block, values_block, mask
        )
        keys_block, values_block = passed_along((keys_block, values_block), "blk", 1)
        key_sum, value_sum = passed_along((key_sum + key_step, value_sum + value_step), "blk", 1)
        return (
            keys_block,
            values_block,
            key_sum,
            value_sum,
            query_sum + query_step,
            (source - 1) % block_count,
        )

    carry = (key_rows, value_rows, zero_heads, zero_heads, zero_heads, block)
    carry = lax.fori_loop(
        0, block_count // 2, lambda turn, state: pass_keys(pass_keys(state)), carry
    )
    key_sum, value_sum, query_sum = (carry[2], carry[3], carry[4])
    back_query, back_key, back_value = (
        lax.all_to_all(
            query_sum.astype(jnp.bfloat16).reshape(shape_flat),
            "head",
            split_axis=1,
            concat_axis=2,
            tiled=True,
        ),
        lax.all_to_all(
            key_sum.astype(jnp.bfloat16).reshape(shape_flat),
            "head",
            split_axis=1,
            concat_axis=2,
            tiled=True,
        ),
        lax.all_to_all(
            value_sum.astype(jnp.bfloat16).reshape(shape_flat),
            "head",
            split_axis=1,
            concat_axis=2,
            tiled=True,
        ),
    )
    back_joint = jnp.concatenate([back_query, back_key, back_value], axis=-1)
    joint_gradient = jnp.einsum(
        "scd,sce->de", first_low, back_joint, preferred_element_type=jnp.float32
    )
    query_shift_gradient = jnp.sum(back_query.astype(jnp.float32), axis=(0, 1))
    value_shift_gradient = jnp.sum(back_value.astype(jnp.float32), axis=(0, 1))
    back_first = jnp.einsum(
        "sce,de->scd", back_joint, joint_full, preferred_element_type=jnp.float32
    )
    back_norm_one, gain_one_gradient, shift_one_gradient = normalize_back(
        back_first, first_unit, first_scale, gain_one_wide
    )
    tokens_gradient = (back_residual + back_norm_one).astype(jnp.bfloat16)
    shards = (
        lax.psum_scatter(gain_one_gradient, ("head", "blk"), scatter_dimension=0, tiled=True),
        lax.psum_scatter(shift_one_gradient, ("head", "blk"), scatter_dimension=0, tiled=True),
        lax.psum_scatter(joint_gradient, ("head", "blk"), scatter_dimension=0, tiled=True),
        lax.psum_scatter(query_shift_gradient, ("head", "blk"), scatter_dimension=0, tiled=True),
        lax.psum_scatter(value_shift_gradient, ("head", "blk"), scatter_dimension=0, tiled=True),
        lax.psum_scatter(output_gradient, ("head", "blk"), scatter_dimension=0, tiled=True),
        lax.psum_scatter(output_shift_gradient, ("head", "blk"), scatter_dimension=0, tiled=True),
        lax.psum_scatter(gain_two_gradient, ("head", "blk"), scatter_dimension=0, tiled=True),
        lax.psum_scatter(shift_two_gradient, ("head", "blk"), scatter_dimension=0, tiled=True),
        lax.psum_scatter(inner_gradient, ("head", "blk"), scatter_dimension=0, tiled=True),
        lax.psum_scatter(inner_shift_gradient, ("head", "blk"), scatter_dimension=0, tiled=True),
        lax.psum_scatter(outer_gradient, ("head", "blk"), scatter_dimension=0, tiled=True),
        lax.psum_scatter(outer_shift_gradient, ("head", "blk"), scatter_dimension=0, tiled=True),
    )
    return (
        output,
        tokens_gradient,
        shards[0],
        shards[1],
        shards[2],
        shards[3],
        shards[4],
        shards[5],
        shards[6],
        shards[7],
        shards[8],
        shards[9],
        shards[10],
        shards[11],
        shards[12],
        stats,
    )


MESH = pl.DeviceIdType.MESH
WIDTH = H * DH
GROUP = 3 * DH
NT = (((1,), (1,)), ((), ()))
NN = (((1,), (0,)), ((), ()))


def place():
    head = lax.axis_index("head")
    blk = lax.axis_index("blk")
    return head // 2, lax.rem(head, 2), blk // 2, lax.rem(blk, 2)


def at(y, x, z, c):
    return (y * 2 + x, z * 2 + c)


def number(y, x, z, c):
    return y * 16 + x * 8 + z * 2 + c


def column(t):
    return t // 4, lax.rem(t, 4)


def meet(peers):
    barrier = pltpu.get_barrier_semaphore()
    for peer in peers:
        pl.semaphore_signal(barrier, inc=1, device_id=peer, device_id_type=MESH)
    pl.semaphore_wait(barrier, len(peers))


class Mover:
    def __init__(self, send_sem, local_sem, anyone):
        self.send_sem = send_sem
        self.local_sem = local_sem
        self.anyone = anyone
        self.zero = anyone[0] * 0
        self.sent = []
        self.local = []

    def push(self, source, target, sem, device):
        self.push_made(lambda: (source, target, sem), device)

    def push_made(self, make, device, when=None):
        spot = len(self.sent)
        self.sent.append((make, spot, device, when))
        under(when, lambda: self.copy(make, spot, device).start())

    def copy(self, make, spot, device):
        source, target, sem = make()
        return remote(source, target, self.send_sem.at[self.zero + spot], sem, device)

    def keep(self, source, target):
        parts = (source, target, self.local_sem.at[len(self.local)])
        pltpu.make_async_copy(*parts).start()
        self.local.append(parts)
        return len(self.local) - 1

    def kept(self, spot):
        pltpu.make_async_copy(*self.local[spot]).wait()

    def landed(self, target, sem):
        remote(target, target, self.send_sem.at[self.zero], sem, self.anyone).wait_recv()

    def finish(self, kept=()):
        for make, spot, device, when in self.sent:
            under(when, lambda: self.copy(make, spot, device).wait_send())
        for spot in kept:
            self.kept(spot)


def under(when, action):
    if when is None:
        action()
    else:

        @pl.when(when)
        def _():
            action()


def remote(source, target, send_sem, recv_sem, device):
    return pltpu.make_async_remote_copy(
        src_ref=source,
        dst_ref=target,
        send_sem=send_sem,
        recv_sem=recv_sem,
        device_id=device,
        device_id_type=MESH,
    )


def unpack(small_all, vectors):
    for block in range(32):
        tile = wide(small_all[block])
        vectors[:, block * 24 : block * 24 + 24] = tile[:8, :24]


def forward_kernel(
    length, tokens, cotangent, wj, wo, wi, wu, small,
    first_far, query_far, key_far, value_far, context_far, context_rows, cot_own, tok_own, wo_all, wi_all, wu_all, small_all, wj_far, vectors,
    send_sem, local_sem, tok_sem, cot_sem, weight_sem, small_sem, wja_sem, wjb_sem, wjc_sem, ctx_send, ctx_recv,
    ctx_local, tok_all, wj_all, turned, mixed_low, score_a, score_b, straight_low, first_low, query, key, value, context, wj_flat,
):
    y, x, z, c = place()
    mine = number(y, x, z, c)
    quarter = x * 2 + c
    spot = y * 4 + z
    other_core = at(y, x, z, 1 - c)
    across = at(y, 1 - x, z, c)
    diagonal = at(y, 1 - x, z, 1 - c)
    down = at(1 - y, x, z, c)
    y1, x1 = jnp.where(c == 0, y, 1 - y), jnp.where(c == 0, 1 - x, x)
    y2, x2 = jnp.where(c == 0, 1 - y, y), jnp.where(c == 0, x, 1 - x)
    first, second = at(y1, x1, z, c), at(y2, x2, z, c)
    spots = [column(lax.rem(spot + k, 8)) for k in range(1, 8)]
    back_spots = [column(lax.rem(spot + 8 - k, 8)) for k in range(1, 8)]
    ahead = [at(y, x, lax.rem(z + k, 4), c) for k in range(1, 4)]
    inside = jnp.logical_or(z == 1, z == 2)
    lines = [
        z,
        jnp.where(z == 0, 1, z - 1),
        jnp.where(z == 0, 2, jnp.where(z == 3, 1, z + 1)),
        jnp.where(z < 2, 3, 0),
    ]
    onward = [z + 1, z - 1, jnp.where(z == 1, 0, 3)]
    away, back = at(y, x, jnp.where(z < 3, z + 1, z - 1), c), at(y, x, jnp.maximum(z - 1, 0), c)
    onward = [at(y, x, lax.rem(zz + 4, 4), c) for zz in onward]
    line_blocks = [number(y, x, zz, c) for zz in lines]
    first_blocks = [number(y1, x1, zz, c) for zz in lines]
    second_blocks = [number(yy, xx, zz, c) for zz in lines for yy, xx in ((y2, x2), (1 - y, 1 - x))]
    core_blocks = [number(yy, xx, zz, 1 - c) for yy in range(2) for xx in range(2) for zz in range(4)]
    group = quad(x, c)
    meet([at(yy, x, zz, c) for yy, zz in spots] + [across, other_core, diagonal])
    move = Mover(send_sem, local_sem, other_core)
    sources = (wo, wi, wu)
    wholes = (wo_all, wi_all, wu_all)

    def hand(block, own, device, when=None):
        for i in range(3):
            move.push_made(
                lambda i=i: (
                    sources[i] if own else wholes[i].at[block],
                    wholes[i].at[block],
                    weight_sem.at[move.zero + i, block],
                ),
                device,
                when,
            )

    def arrive(block):
        for i in range(3):
            move.landed(wholes[i].at[block], weight_sem.at[i, block])

    def pass_small(blocks, devices):
        for block in blocks:
            move.landed(small_all.at[block], small_sem.at[block])
            for device in devices:
                move.push(small_all.at[block], small_all.at[block], small_sem.at[block], device)

    def spread(block, own):
        for device in (first, second, other_core):
            hand(block, own, device)

    def line_arrived(k):
        arrive(line_blocks[k])
        hand(line_blocks[k], False, onward[k - 1], inside)
        spread(line_blocks[k], False)

    def second_hand(k):
        arrive(first_blocks[k])
        hand(first_blocks[k], False, second)
        hand(first_blocks[k], False, other_core)

    def last_hand(k):
        for b in second_blocks[2 * k : 2 * k + 2]:
            arrive(b)
            hand(b, False, other_core)

    for device in ahead + [first, second, other_core]:
        move.push(small, small_all.at[mine], small_sem.at[mine], device)
    for xx, cc in group:
        move.push(wj.at[xx * 2 + cc], wj_all.at[y, x, z, c], wja_sem.at[quarter], at(y, xx, z, cc))
    move.keep(wj.at[quarter], wj_all.at[y, x, z, c])
    move.keep(tokens.at[spot], tok_all.at[mine])
    move.keep(small, small_all.at[mine])
    for yy, zz in spots:
        move.push(tokens.at[yy * 4 + zz], tok_all.at[mine], tok_sem.at[mine], at(yy, x, zz, c))
    for device in (across, other_core):
        move.push(tokens.at[spot], tok_all.at[mine], tok_sem.at[mine], device)
    spread(mine, True)
    for source, whole in zip(sources, wholes):
        move.keep(source, whole.at[mine])

    def slice_onward(zz, device, when):
        move.push_made(lambda: (wj_all.at[y, :, zz], wj_all.at[y, :, zz], wjb_sem.at[zz]), device, when)

    for xx, cc in group:
        move.landed(wj_all.at[y, xx, z, cc], wja_sem.at[xx * 2 + cc])
    move.kept(0)
    slice_onward(z, away, None)
    slice_onward(z, back, inside)
    move.push(wj_all.at[y, :, z], wj_all.at[y, :, z], wjc_sem.at[z], down)
    pass_small(line_blocks[1:], (first, second, other_core))
    pass_small(first_blocks, (second, other_core))
    for k in range(1, 4):
        zz = lines[k]
        move.landed(wj_all.at[y, :, zz], wjb_sem.at[zz])
        slice_onward(zz, onward[k - 1], inside)
        move.push(wj_all.at[y, :, zz], wj_all.at[y, :, zz], wjc_sem.at[zz], down)
    pass_small(second_blocks, (other_core,))
    for yy, zz in back_spots:
        block = number(yy, x, zz, c)
        move.landed(tok_all.at[block], tok_sem.at[block])
        move.push(tok_all.at[block], tok_all.at[block], tok_sem.at[block], across)
        move.push(tok_all.at[block], tok_all.at[block], tok_sem.at[block], other_core)
    hand(mine, True, away)
    hand(mine, True, back, inside)
    second_hand(0)
    for yy, zz in [(y, z)] + back_spots:
        block = number(yy, 1 - x, zz, c)
        move.landed(tok_all.at[block], tok_sem.at[block])
        move.push(tok_all.at[block], tok_all.at[block], tok_sem.at[block], other_core)
    for block in core_blocks:
        move.landed(small_all.at[block], small_sem.at[block])
    for zz in lines:
        move.landed(wj_all.at[1 - y, :, zz], wjc_sem.at[zz])
    line_arrived(1)
    for yy, zz in spots:
        move.push(cotangent.at[yy * 4 + zz], cot_own.at[spot], cot_sem.at[spot], at(yy, x, zz, c))
    move.keep(cotangent.at[spot], cot_own.at[spot])
    for yy, zz in [(y, z)] + back_spots:
        for xx in (x, 1 - x):
            block = number(yy, xx, zz, 1 - c)
            move.landed(tok_all.at[block], tok_sem.at[block])
    move.kept(1)
    move.kept(2)

    unpack(small_all, vectors)
    rows = query.shape[1]
    for yy in range(2):
        for xx in range(2):
            for zz in range(4):
                pair = jnp.concatenate([wide(wj_all[yy, xx, zz, cc]) for cc in range(2)], axis=0)
                row = number(yy, xx, zz, 0) * 24
                wj_flat[row : row + 48, :] = pair.astype(jnp.bfloat16)
    lane = lax.broadcasted_iota(jnp.int32, (ROWS, DH), 1)
    row_at = lax.broadcasted_iota(jnp.int32, (ROWS, DH), 0)
    one_lane = jnp.where(lane == 0, 1.0, 0.0).astype(jnp.bfloat16)
    three_lanes = jnp.where(lane < 3, 1.0, 0.0).astype(jnp.bfloat16)
    gain, shift = vectors[0:1, :], vectors[1:2, :]
    query_all, value_all = vectors[2:3, :], vectors[3:4, :]

    def chosen(whole):
        total = jnp.zeros((1, GROUP), jnp.float32)
        for q in range(4):
            total = jnp.where(quarter == q, whole[:, q * GROUP : (q + 1) * GROUP], total)
        return total

    query_shift, value_shift = chosen(query_all), chosen(value_all)
    blocks = ROWS // tokens.shape[1]

    def project(i, _):
        here = pl.ds(i * ROWS, ROWS)
        raw = tok_all[pl.ds(i * blocks, blocks)].reshape(ROWS, WIDTH)
        normed = normalize(wide(raw), gain, shift)[0].astype(jnp.bfloat16)
        first_low[here, :] = normed
        joint = dot(normed, wj_flat[...])
        low_q = ((joint[:, :GROUP] + query_shift).astype(jnp.bfloat16) * DH ** (-0.5)).astype(jnp.bfloat16)
        low_k = joint[:, GROUP : 2 * GROUP].astype(jnp.bfloat16)
        low_v = (joint[:, 2 * GROUP :] + value_shift).astype(jnp.bfloat16)
        mask = jnp.where(row_at + i * ROWS < length[spot], 0.0, NEG)
        key_side = jnp.where(lane == 0, mask, jnp.where(lane < 4, 1.0, 0.0)).astype(jnp.bfloat16)
        for h in range(3):
            here_h = slice(h * DH, (h + 1) * DH)
            query[h, here, :] = jnp.concatenate([low_q[:, here_h], one_lane], axis=1)
            key[h, here, :] = jnp.concatenate([low_k[:, here_h], key_side], axis=1)
            value[h, here, :] = jnp.concatenate([low_v[:, here_h], three_lanes], axis=1)
        return 0

    for i in range(rows // ROWS):
        project(i, 0)
    for source, target in ((first_low, first_far), (key, key_far), (value, value_far), (wj_flat, wj_far)):
        move.keep(source, target)
    eye = jnp.eye(72, 2 * DH, dtype=jnp.bfloat16)
    for h in range(3):
        turned[h] = dot(eye, value[h], NT).astype(jnp.bfloat16)
    wider = score_a.shape[1]
    side = lax.broadcasted_iota(jnp.int32, (DH, wider), 0)
    chunk = 512
    units = 3 * rows // wider

    def ctx_copy(j, cc, for_local, for_remote):
        yy, xx = j // 2, lax.rem(j, 2)
        source, target = mixed_low.at[yy, xx, :, cc], context_rows.at[quarter, yy]
        here = jnp.logical_and(xx == x, c == cc)

        @pl.when(here)
        def _():
            for_local(pltpu.make_async_copy(source, target, ctx_local.at[j]))

        @pl.when(jnp.logical_not(here))
        def _():
            for_remote(remote(source, target, ctx_send.at[j, cc], ctx_recv.at[quarter, j], at(y, xx, z, cc)))

    def score_chunk(held, h, queries, k, best):
        fresh = dot(key[h, k * chunk : (k + 1) * chunk, :], queries, NT)
        held[k * chunk : (k + 1) * chunk, :] = fresh
        return jnp.maximum(best, jnp.max(fresh, axis=0, keepdims=True))

    lowest = jnp.full((1, wider), -jnp.inf, jnp.float32)
    start = lowest
    for k in range(rows // chunk):
        start = score_chunk(score_a, 0, query[0, :wider, :], k, start)

    def unit(u, best, held, fresh):
        j = u // 3
        h = u - 3 * j
        u_next = jnp.minimum(u + 1, units - 1)
        j_next = u_next // 3
        h_next = u_next - 3 * j_next
        here = pl.ds(j * wider, wider)
        queries = query[h_next, pl.ds(j_next * wider, wider), :]
        best_next = lowest
        mixed = jnp.zeros((72, wider), jnp.float32)
        for k in range(rows // chunk):
            keys = slice(k * chunk, (k + 1) * chunk)
            weights = jnp.exp(held[keys, :] - best).astype(jnp.bfloat16)
            mixed = mixed + dot(turned[h, :, keys], weights)
            best_next = score_chunk(fresh, h_next, queries, k, best_next)
        total = mixed[DH : DH + 1, :]
        mixed = mixed[:DH, :] / total
        high, mid, low = three(best + jnp.log(total))
        extra = jnp.where(
            side == 0, 1.0, jnp.where(side == 1, -high, jnp.where(side == 2, -mid, jnp.where(side == 3, -low, 0.0)))
        )
        straight = jnp.concatenate([mixed, extra], axis=0).T
        query[h, here, DH:] = straight[:, DH:].astype(jnp.bfloat16)
        straight_low[h] = straight[:, :DH].astype(jnp.bfloat16)

        @pl.when(h == 2)
        def _():
            whole = jnp.concatenate([straight_low[k] for k in range(3)], axis=1)
            context[here, :] = whole
            mixed_low[j // 2, lax.rem(j, 2)] = whole.reshape(4, 2, tokens.shape[1], GROUP)
            for cc in range(2):
                ctx_copy(j, cc, lambda copy: copy.start(), lambda copy: copy.start())

        return best_next

    def pair(p, best):
        best = unit(2 * p, best, score_a, score_b)
        best = unit(2 * p + 1, best, score_b, score_a)
        for when, action in (
            (0, lambda: second_hand(1)),
            (1, lambda: line_arrived(2)),
            (2, lambda: (second_hand(2), last_hand(0))),
            (3, lambda: line_arrived(3)),
            (4, lambda: (second_hand(3), last_hand(1))),
        ):

            @pl.when(p == when)
            def _(action=action):
                action()

        return best

    lax.fori_loop(0, units // 2, pair, start)
    move.keep(query, query_far)
    move.keep(context, context_far)
    last_hand(2)
    last_hand(3)
    for yy, zz in back_spots:
        move.landed(cot_own.at[yy * 4 + zz], cot_sem.at[yy * 4 + zz])
    for b in core_blocks:
        arrive(b)
    tok_copies = []
    for i in range(8):
        yy, zz = i // 4, i % 4
        tok_copies.append(pltpu.make_async_copy(tok_all.at[number(yy, x, zz, c)], tok_own.at[i], local_sem.at[8 + i]))
        tok_copies[-1].start()

    def settle(j, _):
        for cc in range(2):
            ctx_copy(j, cc, lambda copy: copy.wait(), lambda copy: copy.wait_send())
        return 0

    lax.fori_loop(0, 4, settle, 0)
    for xx, cc in group:
        for yy in range(2):
            move.landed(context_rows.at[xx * 2 + cc, yy], ctx_recv.at[xx * 2 + cc, yy * 2 + x])
    move.finish(range(3, len(move.local)))
    for copy in tok_copies:
        copy.wait()


def comm_call(kernel, outs, args, sends, locals_, sems, scratch, ident, space=None):
    space = space or [pltpu.HBM] * len(args)
    return pl.pallas_call(
        kernel,
        out_shape=[jax.ShapeDtypeStruct(shape, dtype) for shape, dtype, _ in outs],
        in_specs=[pl.BlockSpec(memory_space=one) for one in space],
        out_specs=[pl.BlockSpec(memory_space=one) for _, _, one in outs],
        scratch_shapes=[
            pltpu.SemaphoreType.DMA((sends,)),
            pltpu.SemaphoreType.DMA((max(locals_, 1),)),
            *[pltpu.SemaphoreType.DMA(shape) for shape in sems],
            *scratch,
        ],
        compiler_params=pltpu.CompilerParams(
            collective_id=ident, has_side_effects=True, vmem_limit_bytes=61 * 1024 * 1024
        ),
    )(*args)


def quad(x, c):
    return [(lax.rem(x + dx, 2), lax.rem(c + dc, 2)) for dx, dc in ((0, 1), (1, 0), (1, 1))]


def wide(value):
    return value.astype(jnp.float32)


def dot(a, b, dims=NN):
    return lax.dot_general(a, b, dims, preferred_element_type=jnp.float32)


ROWS = 256


TN = (((0,), (0,)), ((), ()))
BACK_ROWS = 1024
KEY_ROWS = 512


def three(value):
    high = value.astype(jnp.bfloat16).astype(jnp.float32)
    middle = (value - high).astype(jnp.bfloat16).astype(jnp.float32)
    return high, middle, value - high - middle


def mean_of(value):
    return jnp.mean(value, axis=-1, keepdims=True)


TN = (((0,), (0,)), ((), ()))
BACK_ROWS = 512
KEY_ROWS = 1024


def three(value):
    high = value.astype(jnp.bfloat16).astype(jnp.float32)
    middle = (value - high).astype(jnp.bfloat16).astype(jnp.float32)
    return high, middle, value - high - middle


def mean_of(value):
    return jnp.mean(value, axis=-1, keepdims=True)


def feed_kernel(
    length, context_rows_far, tok_far, cot_far, wo_far, small_all, vectors, wi_far, wu_far,
    hu_far, hi_far, ho_far, hs_far, output, back_context, back_residual,
    send_sem, local_sem, sem1, sem2, sem_out, sem_back,
    gu, gi, go, gs, wi, back_near, inner_shift, active, back_inner, output_low,
    r1u, r1i, r1o, r1s, r2u, context_rows, tok_own, cot_own, wo, load_sem,
):
    bf16, f32 = jnp.bfloat16, jnp.float32
    y, x, z, c = place()
    spot = y * 4 + z
    mine = x * 2 + c
    other_core = at(y, x, z, 1 - c)
    across = at(y, 1 - x, z, c)
    diagonal = at(y, 1 - x, z, 1 - c)
    spots = [column(lax.rem(spot + k, 8)) for k in range(1, 8)]
    y1, x1 = jnp.where(c == 0, y, 1 - y), jnp.where(c == 0, 1 - x, x)
    y2, x2 = jnp.where(c == 0, 1 - y, y), jnp.where(c == 0, x, 1 - x)
    first = at(y1, x1, z, c)
    own, near1, near2 = y * 2 + x, y1 * 2 + x1, y2 * 2 + x2
    far = (1 - y) * 2 + 1 - x
    order = (far, near1, near2, own)
    parts = (gu, gi, go, gs)
    r1 = (r1u, r1i, r1o, r1s)
    group = quad(x, c)
    move = Mover(send_sem, local_sem, other_core)
    width = wo.shape[0]
    ff = wi.shape[1]
    steps = ff // width
    for source, target in ((context_rows_far, context_rows), (wo_far, wo), (tok_far, tok_own), (cot_far, cot_own)):
        move.keep(source, target)

    def weights_load(step):
        cols = pl.ds(pl.multiple_of(step * width, width), width)
        return (
            pltpu.make_async_copy(wi_far.at[:, cols], wi.at[:, cols], load_sem.at[step, 0]),
            pltpu.make_async_copy(wu_far.at[step], gu.at[step], load_sem.at[step, 1]),
        )

    def load(step, _):
        for copy in weights_load(step):
            copy.start()
        return 0

    lax.fori_loop(0, steps, load, 0)
    meet([at(yy, x, zz, c) for yy, zz in spots] + [across, other_core, diagonal])

    piece = tok_own.shape[1]
    rows = tok_own.shape[0] * piece
    ff_piece = ff // 32
    for block in range(32):
        inner_shift[:, block * ff_piece : (block + 1) * ff_piece] = wide(small_all[block])[8:9, :ff_piece]

    spot_at = lax.broadcasted_iota(jnp.int32, (8, piece, 1), 0)
    position = number(spot_at // 4, x, lax.rem(spot_at, 4), c) * piece
    position = position + lax.broadcasted_iota(jnp.int32, (8, piece, 1), 1)
    keep = jnp.where(position < length[spot], 1.0, 0.0).reshape(rows, 1) > 0.5

    def column_sum(item):
        return jnp.sum(item, axis=0, keepdims=True)

    def square(item):
        return jnp.sum(item * item)

    for n in range(4):
        move.kept(n)
    branch = vectors[4:5, :] + dot(context_rows[0].reshape(rows, GROUP), wo[:GROUP, :])
    for g in range(1, 4):
        branch = branch + dot(context_rows[g].reshape(rows, GROUP), wo[g * GROUP : (g + 1) * GROUP, :])
    residual = wide(tok_own[...].reshape(rows, width)) + branch
    branch_total = square(jnp.where(keep, branch, 0.0))
    average = mean_of(residual)
    centered = residual - average
    inverse = lax.rsqrt(mean_of(centered * centered) + EPS)
    unit = centered * inverse
    second_low = (unit * vectors[5:6, :] + vectors[6:7, :]).astype(bf16)
    back_result = jnp.where(keep, wide(cot_own[...].reshape(rows, width)), 0.0)
    back_feed = back_result.astype(bf16)

    def middle(step, sums_here):
        back_second, feed = sums_here
        for copy in weights_load(step):
            copy.wait()
        cols = pl.ds(pl.multiple_of(step * width, width), width)
        wi_here = wi[:, cols]
        inner = dot(second_low, wi_here) + inner_shift[:, cols]
        chance = 0.5 * (1.0 + lax.erf(inner * 0.7071067811865476))
        low = (inner * chance).astype(bf16)
        active[:, cols] = low
        wu_here = gu[step].reshape(width, width)
        slope = chance + inner * jnp.exp(inner * inner * -0.5) * 0.3989422804014327
        back = (dot(back_feed, wu_here, NT) * slope).astype(bf16)
        back_inner[:, cols] = back
        return back_second + dot(back, wi_here, NT), feed + dot(low, wu_here)

    zero = jnp.zeros((rows, width), f32)
    back_second, feed = lax.fori_loop(0, steps, middle, (zero, zero), unroll=4)
    scaled = back_second * vectors[5:6, :]
    back_res = back_result + inverse * (scaled - mean_of(scaled) - unit * mean_of(scaled * unit))
    back_residual[...] = back_res
    back_branch = back_res.astype(bf16)
    short = jnp.concatenate(
        [
            column_sum(wide(back_feed)), column_sum(back_second * unit), column_sum(back_second),
            column_sum(wide(back_branch)), jnp.zeros((4, width), f32),
        ],
        axis=0,
    )
    for g in range(4):
        back_near[g] = dot(back_branch, wo[g * GROUP : (g + 1) * GROUP, :], NT).astype(bf16).reshape(8, piece, GROUP)
    for xx, cc in group[::-1]:
        for yy in range(2):
            move.push(
                back_near.at[xx * 2 + cc, pl.ds(yy * 4, 4)],
                back_context.at[yy, x, :, c],
                sem_back.at[mine, yy],
                at(y, xx, z, cc),
            )
    for yy in range(2):
        move.keep(back_near.at[mine, pl.ds(yy * 4, 4)], back_context.at[yy, x, :, c])

    feed = feed + vectors[7:8, :]
    result = jnp.where(keep, residual + feed, 0.0)
    output_low[...] = result.astype(bf16).reshape(8, piece, width)
    for yy, zz in spots:
        move.push(output_low.at[yy * 4 + zz], output.at[spot], sem_out.at[spot], at(yy, x, zz, c))
    move.keep(output_low.at[spot], output.at[spot])

    totals = (square(result), branch_total, square(jnp.where(keep, feed, 0.0)))
    lane = lax.broadcasted_iota(jnp.int32, (1, 128), 1)
    stat_row = jnp.where(lane == 0, totals[0], jnp.where(lane == 1, totals[1], jnp.where(lane == 2, totals[2], 0.0)))
    def to_core(i, quarter):
        move.push(parts[i].at[quarter, :, 1 - c], r1[i].at[quarter], sem1.at[i, quarter], other_core)

    def gather(i, quarter):
        move.landed(r1[i].at[quarter], sem1.at[i, quarter])
        r1[i][quarter] = r1[i][quarter] + parts[i][quarter, :, c]

    lead = width // 32
    wide_piece = ff // 32
    for step in range(steps):
        grad = dot(active[:, step * width : (step + 1) * width], back_feed, TN).astype(bf16)
        for zz in range(4):
            for cc in range(2):
                row = (zz * 2 + cc) * wide_piece
                gu[step, zz, cc] = grad[row : row + wide_piece, :]
        to_core(0, step)
    for step in range(steps):
        grad = dot(second_low, back_inner[:, step * width : (step + 1) * width], TN)
        for block in range(32):
            gi[block // 8, block % 8 // 2, block % 2, :, step * width : (step + 1) * width] = grad[
                block * lead : (block + 1) * lead, :
            ].astype(bf16)
    for quarter in order:
        to_core(1, quarter)
    for slot, quarter in ((1, far), (0, near1)):
        gather(0, quarter)
        move.push(r1u.at[quarter], r2u.at[slot], sem2.at[slot], first)
    for quarter in (near2, own):
        gather(0, quarter)
    for g in range(4):
        grad = dot(context_rows[g].reshape(rows, GROUP), back_branch, TN)
        for zz in range(4):
            for cc in range(2):
                row = (zz * 2 + cc) * lead
                go[g, zz, cc] = grad[row : row + lead, :].astype(bf16)
        to_core(2, g)

    long = column_sum(wide(back_inner[...]))
    for block in range(32):
        at_block = (block // 8, block % 8 // 2, block % 2)
        gs[at_block] = jnp.zeros((8, 128), f32)
        gs[at_block + (slice(0, 8), slice(0, lead))] = short[:, block * lead : (block + 1) * lead]
        gs[at_block + (slice(4, 5), slice(0, wide_piece))] = long[:, block * wide_piece : (block + 1) * wide_piece]
        gs[at_block + (slice(5, 6), slice(None))] = stat_row
    for quarter in order:
        to_core(3, quarter)
    for i in (1, 2, 3):
        for quarter in order:
            gather(i, quarter)
    for slot, quarter in ((1, near2), (0, own)):
        move.landed(r2u.at[slot], sem2.at[slot])
        r1u[quarter] = r1u[quarter] + r2u[slot]
    for source, target in zip(r1, (hu_far, hi_far, ho_far, hs_far)):
        move.keep(source, target)
    for xx, cc in group:
        for yy in range(2):
            move.landed(back_context.at[yy, xx, :, cc], sem_back.at[xx * 2 + cc, yy])
    for k in range(1, 8):
        t = lax.rem(spot + 8 - k, 8)
        move.landed(output.at[t], sem_out.at[t])
    move.finish(range(4, len(move.local)))


def backward_kernel(
    hu, hi, ho, hs, query_far, key_far, value_far, context_far, back_far, weight_far, first_far, tok_far, residual_far, vectors,
    out_o, out_i, out_u, out_s, out_joint, tokens_gradient, late,
    send_sem, local_sem, sem2, sem3, sem4, sem_y, sem_z, sem_g, sem_c, sem_x, sem_t, sem_s,
    r1u, r1i, r1o, r1s, r2u, r2i, r2o, r2s, r3u, r3i, r3o, r3s, r4u, r4i, r4o, r4s,
    joint, back_query, widened, query, key, value, context, back_context, joint_weight, tok_own, back_residual,
    first_low, back_first, rc, rx, gj, ry, rz, sj, joint_land, gradient_low, small, small_all,
):
    bf16, f32 = jnp.bfloat16, jnp.float32
    y, x, z, c = place()
    spot = y * 4 + z
    mine = x * 2 + c
    me = number(y, x, z, c)
    other_core = at(y, x, z, 1 - c)
    across = at(y, 1 - x, z, c)
    down = at(1 - y, x, z, c)
    y1, x1 = jnp.where(c == 0, y, 1 - y), jnp.where(c == 0, 1 - x, x)
    y2, x2 = jnp.where(c == 0, 1 - y, y), jnp.where(c == 0, x, 1 - x)
    first, second = at(y1, x1, z, c), at(y2, x2, z, c)
    line = [lax.rem(z + k, 4) for k in range(1, 4)]
    line_devices = [at(y, x, zz, c) for zz in line]
    own, near1, near2 = y * 2 + x, y1 * 2 + x1, y2 * 2 + x2
    far = (1 - y) * 2 + 1 - x
    order = (far, near1, near2, own)
    group = quad(x, c)
    others = []
    for k in range(1, 32):
        t = lax.rem(me + k, 32)
        others.append((t, (t // 8, lax.rem(t, 8))))
    move = Mover(send_sem, local_sem, other_core)
    move.keep(back_far, back_context)
    move.keep(context_far, context)
    for h in range(3):
        for source, target in ((key_far, key), (query_far, query), (value_far, value)):
            move.keep(source.at[h], target.at[h])
    meet([device for _, device in others])
    zero = move.zero
    sources = (hu, hi, ho, hs)
    results = (out_u, out_i, out_o, out_s)
    r1, r2 = (r1u, r1i, r1o, r1s), (r2u, r2i, r2o, r2s)
    r3, r4 = (r3u, r3i, r3o, r3s), (r4u, r4i, r4o, r4s)
    for i in range(4):
        move.keep(sources[i], r1[i])
    for source, target in (
        (weight_far, joint_weight), (first_far, first_low), (tok_far, tok_own), (residual_far, back_residual)
    ):
        move.keep(source, target)

    def stage2(i):
        for slot, quarter in ((1, far), (0, near1)):
            move.push_made(
                lambda slot=slot, quarter=quarter: (
                    sources[i].at[quarter], r2[i].at[zero + slot], sem2.at[zero + i, zero + slot]
                ),
                first,
            )

    def stage3(i):
        if i:
            move.landed(r2[i].at[zero + 1], sem2.at[zero + i, zero + 1])
            r1[i][near2] = r1[i][near2] + r2[i][1]
        source = r1[i] if i else sources[i]
        move.push_made(lambda: (source.at[near2], r3[i], sem3.at[zero + i]), second)

    def stage4(i):
        total = wide(r1[i][own])
        if i:
            move.landed(r2[i].at[zero], sem2.at[zero + i, zero])
            total = total + wide(r2[i][0])
        move.landed(r3[i], sem3.at[zero + i])
        r1[i][own] = (total + wide(r3[i][...])).astype(r1[i].dtype)
        for k in range(3):
            move.push_made(
                lambda k=k: (r1[i].at[own, line[k]], r4[i].at[zero + k], sem4.at[zero + i, zero + k]),
                line_devices[k],
            )

    def stage5(i):
        total = wide(r1[i][own, z])
        for k in range(3):
            move.landed(r4[i].at[k], sem4.at[i, k])
            total = total + wide(r4[i][k])
        results[i][...] = total

    rows_all = query.shape[1]
    piece = tok_own.shape[1]
    rows = tok_own.shape[0] * piece
    width = tok_own.shape[2]
    scale = DH ** (-0.5)
    eye = jnp.eye(DH, 2 * DH, dtype=bf16)
    side_lane = lax.broadcasted_iota(jnp.int32, (rows, DH), 1)
    per_head = rows_all // KEY_ROWS
    between = {
        0: lambda: (stage4(0), stage3(2), stage3(3)),
        1: lambda: (stage3(1), stage4(2), stage4(3)),
        2: lambda: None,
    }
    stage3(0)
    stage2(2)
    stage2(3)
    stage2(1)
    move.kept(0)
    move.kept(1)
    for h in range(3):
        for n in range(3):
            move.kept(2 + 3 * h + n)
        if h == 0:
            for n in range(11, 15):
                move.kept(n)
        lanes = slice(h * DH, (h + 1) * DH)
        for q in range(4):
            here = slice(q * rows, (q + 1) * rows)
            backs = back_context[q // 2, q % 2].reshape(rows, GROUP)[:, lanes]
            spread = jnp.sum(wide(backs) * wide(context[here, lanes]), axis=1, keepdims=True)
            high, mid, low = three(spread)
            side = jnp.where(
                side_lane == 0, -high, jnp.where(side_lane == 1, -mid, jnp.where(side_lane == 2, -low, 0.0))
            )
            widened[here, :] = jnp.concatenate([backs, side.astype(bf16)], axis=1)
        back_query[...] = jnp.zeros_like(back_query)

        def block(i, _):
            keys = pl.ds(i * KEY_ROWS, KEY_ROWS)
            key_here, value_here = key[h, keys, :], value[h, keys, :]
            turned = dot(eye, key_here, NT).astype(bf16)
            back_key = jnp.zeros((KEY_ROWS, DH), f32)
            back_value = jnp.zeros((KEY_ROWS, DH), f32)
            for q in range(rows_all // BACK_ROWS):
                here = slice(q * BACK_ROWS, (q + 1) * BACK_ROWS)
                queries, backs = query[h, here, :], widened[here, :]
                chances = jnp.exp(dot(key_here, queries, NT))
                back_scores = (chances * dot(value_here, backs, NT)).astype(bf16)
                back_key = back_key + dot(back_scores, queries[:, :DH])
                back_value = back_value + dot(chances.astype(bf16), backs[:, :DH])
                back_query[:, here] += dot(turned, back_scores)
            joint[keys, GROUP + h * DH : GROUP + (h + 1) * DH] = back_key.astype(bf16)
            joint[keys, 2 * GROUP + h * DH : 2 * GROUP + (h + 1) * DH] = back_value.astype(bf16)
            return 0

        lax.fori_loop(0, per_head, block, 0)
        joint[:, lanes] = (back_query[...] * scale).T.astype(bf16)
        between[h]()

    move.kept(15)
    for k in range(2):
        for yy in range(2):
            xx = lax.rem(x + 1 + k, 2)
            here = pl.ds((yy * 2 + xx) * rows, rows)
            back_first[yy, xx] = dot(joint[here, :], joint_weight[...], NT).astype(bf16).reshape(4, 2, piece, width)
            move.push(back_first.at[yy, xx, :, 1 - c], rc.at[yy, xx], sem_c.at[yy, xx], other_core)
    for yy in range(2):
        move.landed(rc.at[yy, 1 - x], sem_c.at[yy, 1 - x])
        rc[yy, 1 - x] = rc[yy, 1 - x] + back_first[yy, 1 - x, :, c]
        move.push(rc.at[yy, 1 - x], rx.at[yy], sem_x.at[yy], across)
    move.kept(16)
    grad = dot(first_low[...], joint[...], TN)
    lead = width // 32
    for block_at in range(32):
        gj[block_at // 16, block_at // 8 % 2, block_at % 8 // 2, block_at % 2] = grad[
            block_at * lead : (block_at + 1) * lead, :
        ].astype(bf16)
    move.push(gj.at[1 - y], ry, sem_y, down)
    move.kept(17)
    move.kept(18)
    stage4(1)
    shifts = jnp.sum(wide(joint[...]), axis=0, keepdims=True)
    small[...] = jnp.zeros_like(small)
    for k in range(8):
        for row, kind in ((2, 0), (3, 2)):
            start = kind * GROUP + k * lead
            small[mine * 8 + k, row : row + 1, :lead] = shifts[:, start : start + lead]
    move.landed(ry, sem_y)
    ry[...] = ry[...] + gj[y]
    for k in range(3):
        move.push(ry.at[:, line[k]], rz.at[k], sem_z.at[k], line_devices[k])
    for yy in range(2):
        move.landed(rc.at[yy, x], sem_c.at[yy, x])

    kept = []
    gains = jnp.zeros((2, width), f32)
    half = rows // 2
    for yy in range(2):
        inputs = wide(tok_own[yy * 4 : yy * 4 + 4].reshape(half, width))
        centered = inputs - mean_of(inputs)
        inverse = lax.rsqrt(mean_of(centered * centered) + EPS)
        unit = centered * inverse
        move.landed(rx.at[yy], sem_x.at[yy])
        whole = wide(rc[yy, x]) + wide(back_first[yy, x, :, c]) + wide(rx[yy])
        back_one = whole.reshape(half, width)
        gains = gains + jnp.concatenate(
            [jnp.sum(back_one * unit, axis=0, keepdims=True), jnp.sum(back_one, axis=0, keepdims=True)], axis=0
        )
        if yy == 1:
            for block_at in range(32):
                small[block_at, 0:2, :lead] = gains[:, block_at * lead : (block_at + 1) * lead]
            for t, device in others:
                move.push(small.at[t], small_all.at[me], sem_s.at[me], device)
            kept.append(move.keep(small.at[me], small_all.at[me]))
        scaled = back_one * vectors[0:1, :]
        back_tokens = back_residual[yy * half : (yy + 1) * half, :] + inverse * (
            scaled - mean_of(scaled) - unit * mean_of(scaled * unit)
        )
        gradient_low[yy * 4 : yy * 4 + 4] = back_tokens.astype(bf16).reshape(4, piece, width)
        for zz in [lax.rem(z + k, 4) for k in range(4)]:
            there = y * 0 + yy
            move.push_made(
                lambda zz=zz, yy=yy: (gradient_low.at[yy * 4 + zz], tokens_gradient.at[spot], sem_t.at[spot]),
                at(there, x, zz, c),
                jnp.logical_or(y != yy, z != zz),
            )
    kept.append(move.keep(gradient_low.at[spot], tokens_gradient.at[spot]))

    total = wide(ry[:, z])
    for k in range(3):
        move.landed(rz.at[k], sem_z.at[k])
        total = total + wide(rz[k])
    sj[...] = total
    for xx, cc in group:
        move.push(sj.at[xx, cc], joint_land.at[mine], sem_g.at[mine], at(y, xx, z, cc))
    gone = move.keep(sj.at[x, c], joint_land.at[mine])
    for i in (0, 2, 3, 1):
        stage5(i)
    move.kept(gone)
    for xx, cc in group:
        move.landed(joint_land.at[xx * 2 + cc], sem_g.at[xx * 2 + cc])
    for g in range(4):
        for kind in range(3):
            start = kind * width + g * GROUP
            out_joint[:, start : start + GROUP] = joint_land[g, :, kind * GROUP : (kind + 1) * GROUP]
    for spot_kept in kept:
        move.kept(spot_kept)
    for t, _ in others:
        move.landed(small_all.at[t], sem_s.at[t])
    late[...] = jnp.sum(small_all[...], axis=0)
    for k in range(1, 8):
        t = lax.rem(spot + 8 - k, 8)
        move.landed(tokens_gradient.at[t], sem_t.at[t])
    move.finish()


def owner_device(
    tokens,
    lengths,
    first_gain,
    first_bias,
    joint_weight,
    query_bias,
    value_bias,
    output_weight,
    output_bias,
    second_gain,
    second_bias,
    inner_weight,
    inner_bias,
    outer_weight,
    outer_bias,
    cotangent,
):
    bf16, f32 = jnp.bfloat16, jnp.float32
    y, x, z, c = place()
    mine = x * 2 + c
    slots, piece, width = tokens.shape
    ff = inner_weight.shape[1]
    short = jnp.stack(
        [first_gain, first_bias, query_bias, value_bias, output_bias, second_gain, second_bias, outer_bias]
    )
    lead = short.shape[1]
    ff_piece = inner_bias.shape[0]
    small = jnp.concatenate(
        [
            jnp.pad(short, ((0, 0), (0, ff_piece - lead))),
            jnp.broadcast_to(inner_bias, (8, ff_piece)),
        ],
        axis=0,
    )
    hbm, vmem = pltpu.HBM, pltpu.VMEM
    dma, regular = pltpu.SemaphoreType.DMA, pltpu.SemaphoreType.REGULAR
    rows_all = 32 * piece
    natural = (2, 2, 4, 2, piece)
    joint_four = jnp.transpose(joint_weight.reshape(lead, 3, 4, GROUP), (2, 0, 1, 3)).reshape(4, lead, 3 * GROUP)
    forward_outs = [
        ((rows_all, width), bf16, hbm),
        ((3, rows_all, 2 * DH), bf16, hbm),
        ((3, rows_all, 2 * DH), bf16, hbm),
        ((3, rows_all, 2 * DH), bf16, hbm),
        ((rows_all, GROUP), bf16, hbm),
        ((4, 2, 4, piece, GROUP), bf16, vmem),
        ((8, piece, width), bf16, hbm),
        ((8, piece, width), bf16, hbm),
        ((32,) + output_weight.shape, bf16, hbm),
        ((32,) + inner_weight.shape, bf16, hbm),
        ((32,) + outer_weight.shape, bf16, hbm),
        ((32,) + small.shape, bf16, vmem),
        ((width, 3 * GROUP), bf16, hbm),
        ((8, width), f32, vmem),
    ]
    (
        first_low, query, key, value, context, context_rows, cot_own, tok_own, wo_all, wi_all, wu_all, small_all, joint_here, vectors
    ) = comm_call(
        forward_kernel,
        forward_outs,
        (lengths, tokens, cotangent, joint_four, output_weight, inner_weight, outer_weight, small),
        220, 24,
        [(32,), (8,), (3, 32), (32,), (4,), (4,), (4,), (4, 2), (4, 4), (4,)],
        [
            vmem((32, piece, width), bf16),
            vmem((2, 2, 4, 2, lead, 3 * GROUP), bf16),
            vmem((3, 72, rows_all), bf16),
            vmem(natural + (GROUP,), bf16),
            vmem((rows_all, 512), f32),
            vmem((rows_all, 512), f32),
            vmem((3, 512, DH), bf16),
            vmem((rows_all, width), bf16),
            vmem((3, rows_all, 2 * DH), bf16),
            vmem((3, rows_all, 2 * DH), bf16),
            vmem((3, rows_all, 2 * DH), bf16),
            vmem((rows_all, GROUP), bf16),
            vmem((width, 3 * GROUP), bf16),
        ],
        0,
        [pltpu.SMEM, hbm, hbm, hbm, hbm, hbm, hbm, hbm],
    )
    rows = 8 * piece
    grid = (4, 4, 2)
    kinds = [
        (outer_weight.shape, bf16),
        (inner_weight.shape, bf16),
        (output_weight.shape, bf16),
        ((8, 128), f32),
    ]
    hu, hi, ho, hs, output, back_context, back_residual = comm_call(
        feed_kernel,
        [((4, 4) + shape, dtype, hbm) for shape, dtype in kinds]
        + [
            (tokens.shape, bf16, hbm),
            (natural + (GROUP,), bf16, vmem),
            ((rows, width), f32, vmem),
        ],
        (
            lengths, context_rows.reshape(4, 8, piece, GROUP), tok_own, cot_own, wo_all.reshape(width, width), small_all, vectors,
            wi_all.reshape(width, ff), wu_all.reshape(grid + outer_weight.shape),
        ),
        48, 24, [(4, 4), (2,), (8,), (4, 2)],
        [vmem(grid + shape, dtype) for shape, dtype in kinds]
        + [
            vmem((width, ff), bf16),
            vmem((4, 8, piece, GROUP), bf16),
            vmem((1, ff), f32),
            vmem((rows, ff), bf16),
            vmem((rows, ff), bf16),
            vmem((8, piece, width), bf16),
        ]
        + [vmem((4, 4) + shape, dtype) for shape, dtype in kinds]
        + [
            vmem((2, 4) + outer_weight.shape, bf16),
            vmem((4, 8, piece, GROUP), bf16),
            vmem((8, piece, width), bf16),
            vmem((8, piece, width), bf16),
            vmem((width, width), bf16),
            dma((4, 2)),
        ],
        1,
        [pltpu.SMEM] + [hbm] * 4 + [vmem] * 2 + [hbm] * 2,
    )
    out_o, out_i, out_u, out_s, joint_shard, tokens_gradient, late = comm_call(
        backward_kernel,
        [
            (output_weight.shape, f32, vmem),
            (inner_weight.shape, f32, vmem),
            (outer_weight.shape, f32, vmem),
            ((8, 128), f32, vmem),
            (joint_weight.shape, f32, vmem),
            (tokens.shape, bf16, hbm),
            ((8, 128), f32, vmem),
        ],
        (
            hu, hi, ho, hs, query, key, value, context, back_context, joint_here, first_low, tok_own, back_residual, vectors,
        ),
        110, 32,
        [(4, 2), (4,), (4, 3), (), (3,), (4,), (2, 2), (2,), (8,), (32,)],
        [vmem((4, 4) + shape, dtype) for shape, dtype in kinds]
        + [vmem((2, 4) + shape, dtype) for shape, dtype in kinds]
        + [vmem((4,) + shape, dtype) for shape, dtype in kinds]
        + [vmem((3,) + shape, dtype) for shape, dtype in kinds]
        + [
            vmem((rows_all, 3 * GROUP), bf16),
            vmem((DH, rows_all), f32),
            vmem((rows_all, 2 * DH), bf16),
            vmem(query.shape, bf16),
            vmem(key.shape, bf16),
            vmem(value.shape, bf16),
            vmem(context.shape, bf16),
            vmem(back_context.shape, bf16),
            vmem(joint_here.shape, bf16),
            vmem(tok_own.shape, bf16),
            vmem(back_residual.shape, f32),
            vmem((rows_all, width), bf16),
            vmem(natural + (width,), bf16),
            vmem((2, 2, 4, piece, width), bf16),
            vmem((2, 4, piece, width), bf16),
            vmem((2, 2, 4, 2, lead, 3 * GROUP), bf16),
            vmem((2, 4, 2, lead, 3 * GROUP), bf16),
            vmem((3, 2, 2, lead, 3 * GROUP), bf16),
            vmem((2, 2, lead, 3 * GROUP), f32),
            vmem((4, lead, 3 * GROUP), f32),
            vmem((8, piece, width), bf16),
            vmem((32, 8, 128), f32),
            vmem((32, 8, 128), f32),
        ],
        2,
        [hbm] * 13 + [vmem],
    )
    count = jnp.sum(lengths).astype(f32) * width
    stats = jnp.sqrt(out_s[5, :3] / count + 1e-06)
    return (
        output,
        tokens_gradient,
        late[0, :lead],
        late[1, :lead],
        joint_shard,
        late[2, :lead],
        late[3, :lead],
        out_o,
        out_s[3, :lead],
        out_s[1, :lead],
        out_s[2, :lead],
        out_i,
        out_s[4, : inner_bias.shape[0]],
        out_u,
        out_s[0, :lead],
        stats,
    )


def solution(mesh):
    in_specs = (
        P(None, ("head", "blk"), None),
        P(),
        P(("head", "blk")),
        P(("head", "blk")),
        P(("head", "blk"), None),
        P(("head", "blk")),
        P(("head", "blk")),
        P(("head", "blk"), None),
        P(("head", "blk")),
        P(("head", "blk")),
        P(("head", "blk")),
        P(("head", "blk"), None),
        P(("head", "blk")),
        P(("head", "blk"), None),
        P(("head", "blk")),
        P(None, ("head", "blk"), None),
    )
    out_specs = (
        P(None, ("head", "blk"), None),
        P(None, ("head", "blk"), None),
        P(("head", "blk")),
        P(("head", "blk")),
        P(("head", "blk"), None),
        P(("head", "blk")),
        P(("head", "blk")),
        P(("head", "blk"), None),
        P(("head", "blk")),
        P(("head", "blk")),
        P(("head", "blk")),
        P(("head", "blk"), None),
        P(("head", "blk")),
        P(("head", "blk"), None),
        P(("head", "blk")),
        P(),
    )
    small_slice = dict(mesh.shape) == {"head": 4, "blk": 8}
    device_work = owner_device if small_slice else on_device
    return jax.shard_map(
        device_work, mesh=mesh, in_specs=in_specs, out_specs=out_specs, check_vma=False
    )
```
